32 devices in a mesh: gx: 4 (over y, x), gy: 4 (over z), af: 2 (over core).
Axes of the slice: x: 2, y: 2, z: 4, core: 2. Of those that a mesh axis runs over, the one named last changes fastest.
Arguments:
- model: float32 [128, 128, 128], P('gx', 'gy'), may hold values from 0.5 to 2
- freq_sq: float32 [4], P('af'), may hold values from 0.5 to 3
- source: float32 [4, 2, 128, 128, 128], P('af', None, 'gx', 'gy'), may hold values from -20 to 20
- observed: float32 [4, 2, 128, 128], P('af', None, 'gx', 'gy'), may hold values from -6 to 6
- receiver_depth: int32 [128, 128], P('gx', 'gy'), may hold values from 0 to 3
Outputs:
- wavefield: float32 [4, 2, 128, 128, 128], P('af', None, 'gx', 'gy')
- gradient: float32 [128, 128, 128], P('gx', 'gy')
The draws below stay inside these ranges and needn't reach their ends.
Inputs may be any that keep to these rules, and one draw needn't show every extreme that they name: `receiver_depth`: every surface column holds one receiver, at the given depth index.
All inputs are finite; a program needn't handle non-finite values.
Results may differ from the reference program's by a relative error of at most 0.00012.
Values sent between devices are 32-bit elements; how exact they have to be, the bound alone decides.
No kernel may reach another device: no remote copies, remote signals or barrier semaphores. Data moves between devices by JAX's collectives and lax.ppermute only.
A program may use at most 64 MiB of HBM per device.

```python
import math
import jax
import jax.numpy as jnp

CZ = 128
ITERS = 2
RDEPTH = 4
NF = 4
NX = 128
NY = 128


def draw_source(key, part):
    first, second = jax.random.split(jax.random.fold_in(key, 11), 2)
    shape = (NF, 2, NX, NY, CZ)
    column = jnp.exp(jax.random.uniform(second, (NX, NY, 1), jnp.float32, -0.7, 0.7))
    base = jnp.clip(jax.random.normal(first, shape, jnp.float32), -3.0, 3.0)
    ramp = 1.0 + 2.0 * jnp.arange(NX, dtype=jnp.float32)[:, None, None] / max(NX - 1, 1)
    return (base * ramp * column).astype(jnp.float32)


def set_ends(entries, own_key, smallest, top_value):
    index_at = [jax.random.randint(jax.random.fold_in(own_key, axis), (), 0, length) for axis, length in enumerate(entries.shape)]
    longest = entries.shape.index(max(entries.shape))
    beside = index_at[:longest] + [(index_at[longest] + 1) % entries.shape[longest]] + index_at[longest + 1:]
    return entries.at[tuple(index_at)].set(smallest).at[tuple(beside)].set(top_value)


def steps_of(key, extent, pieces, least, largest):
    gain, own = 1.0, jax.random.fold_in(key, 6)
    for dim, shards_of in pieces:
        heights = jnp.exp(jax.random.uniform(jax.random.fold_in(own, dim), (shards_of,), jnp.float32, least / len(pieces), largest / len(pieces)))
        gain = gain * jnp.repeat(heights, extent[dim] // shards_of).reshape([-1 if axis == dim else 1 for axis in range(len(extent))])
    return gain


def noise(own_key, shape, scale, bound, cuts=(), kind=jnp.bfloat16):
    factor_of = steps_of(own_key, shape, cuts, -0.22, 0.18) if cuts else 1.0
    values = jax.random.normal(own_key, shape, jnp.float32) * scale * factor_of
    return jnp.minimum(jnp.maximum(values, -bound), bound).astype(kind)


def setup_inputs(seed: int = 0) -> dict:
    keys = jax.random.split(jax.random.key(seed), 6)
    return {
        "model": jnp.clip(jnp.exp(math.log(2.0) - 1.3862944 * jax.random.uniform(keys[0], (NX, NY, CZ), jnp.float32) ** steps_of(keys[0], (NX, NY, CZ), ((0, 4), (1, 4)), -0.2, 0.2)), 0.5, 2.0),
        "freq_sq": jnp.clip(jnp.exp(math.log(3.0) - 1.7917595 * jax.random.uniform(keys[1], (NF,), jnp.float32) ** steps_of(keys[1], (NF,), ((0, 2),), -0.2, 0.2)), 0.5, 3.0),
        "source": draw_source(jax.random.fold_in(keys[5], 71), 0),
        "observed": noise(keys[3], (NF, 2, NX, NY), 1.0, 6.0, ((0, 2), (2, 4), (3, 4)), jnp.float32),
        "receiver_depth": set_ends(jax.random.randint(keys[4], (NX, NY), 0, RDEPTH), jax.random.fold_in(keys[4], 1), 0, RDEPTH - 1).astype(jnp.int32),
    }


attenuation = 0.2
penalty = 4.0


def neighbours(field):
    padded = jnp.pad(field, ((0, 0), (1, 1), (1, 1), (1, 1)))
    total = padded[:, 2:, 1:-1, 1:-1] + padded[:, :-2, 1:-1, 1:-1]
    total = total + padded[:, 1:-1, 2:, 1:-1] + padded[:, 1:-1, :-2, 1:-1]
    total = total + padded[:, 1:-1, 1:-1, 2:] + padded[:, 1:-1, 1:-1, :-2]
    return total


def apply_coef(coef_real, coef_imag, field, sign):
    real_part = coef_real * field[0] - sign * coef_imag * field[1]
    imag_part = coef_real * field[1] + sign * coef_imag * field[0]
    return jnp.stack([real_part, imag_part])


def reference(model, freq_sq, source, observed, receiver_depth):
    levels = jax.lax.broadcasted_iota(jnp.int32, model.shape, 2)
    onehot = (levels == receiver_depth[:, :, None]).astype(jnp.float32)
    weights = penalty * onehot
    fields = []
    gradient = jnp.zeros(model.shape, jnp.float32)
    for freq in range(NF):
        squared = freq_sq[freq]
        coef_real = 6.0 - squared * model
        coef_imag = attenuation * squared * model

        def forward(field):
            return apply_coef(coef_real, coef_imag, field, 1.0) - neighbours(field)

        def adjoint(field):
            return apply_coef(coef_real, coef_imag, field, -1.0) - neighbours(field)

        def normal(field):
            return adjoint(forward(field)) + weights * field

        rhs = adjoint(source[freq]) + weights * observed[freq][:, :, :, None]
        field = jnp.zeros_like(rhs)
        resid = rhs
        direction = rhs
        norm_now = jnp.sum(resid * resid)
        for sweep in range(ITERS):
            image = normal(direction)
            alpha = norm_now / jnp.sum(direction * image)
            field = field + alpha * direction
            resid = resid - alpha * image
            norm_next = jnp.sum(resid * resid)
            direction = resid + (norm_next / norm_now) * direction
            norm_now = norm_next
        misfit = forward(field) - source[freq]
        deriv_real = -squared
        deriv_imag = attenuation * squared
        wave_real = deriv_real * field[0] - deriv_imag * field[1]
        wave_imag = deriv_real * field[1] + deriv_imag * field[0]
        gradient = gradient + (wave_real * misfit[0] + wave_imag * misfit[1])
        fields.append(field)
    return jnp.stack(fields), gradient
```

```python
import functools

import jax
import jax.numpy as jnp
from jax import lax
from jax.experimental import pallas as pl
from jax.experimental.pallas import tpu as pltpu
from jax.sharding import PartitionSpec as P

ITERS = 2
attenuation = 0.2
penalty = 4.0

HALO = 2 * ITERS
INNER = HALO - 1
F32 = jnp.float32
ANY = pl.BlockSpec(memory_space=pl.ANY)
VMEM = pl.BlockSpec(memory_space=pltpu.VMEM)
SMEM = pl.BlockSpec(memory_space=pltpu.SMEM)
MIB = 1 << 20


def params(mib):
    return pltpu.CompilerParams(vmem_limit_bytes=mib * MIB)


def parity(axis):
    return lax.rem(lax.axis_index(axis), 2) == 0


def run_all(copies):
    for copy in copies:
        copy.start()
    for copy in copies:
        copy.wait()


def pack_kernel(source, model, observed, depth, xe, xo, ye, yo, table, slab, sem):
    freqs, _, nx, ny, nz = source.shape
    fields = 2 * freqs
    for f in range(freqs):
        for p in range(2):
            table[2 * f + p, :, 0:nx] = observed[f, p].T
    table[fields, :, 0:nx] = depth[...].astype(F32).T
    lane = lax.broadcasted_iota(jnp.int32, (ny, nz), 1)
    even_x, even_y = parity("gx"), parity("gy")
    copies = []
    count = iter(range(64))

    def copy(src, dst):
        copies.append(pltpu.make_async_copy(src, dst, sem.at[next(count)]))
        copies[-1].start()

    for side, (xb, yb) in enumerate(((xe, ye), (xo, yo))):
        last_x = even_x if side == 0 else jnp.logical_not(even_x)
        last_y = even_y if side == 0 else jnp.logical_not(even_y)
        at_x = jnp.where(last_x, nx - HALO, 0)
        at_m = jnp.where(last_x, nx - INNER, 0)
        at_y = pl.multiple_of(jnp.where(last_y, ny - HALO, 0), HALO)
        for f in range(freqs):
            for p in range(2):
                k = 2 * f + p
                copy(source.at[f, p, pl.ds(at_x, HALO)], xb.at[pl.ds(k * HALO, HALO)])
                copy(
                    source.at[f, p, :, pl.ds(at_y, HALO), :],
                    yb.at[pl.ds(k * nx, nx)],
                )
        copy(model.at[pl.ds(at_m, INNER)], xb.at[pl.ds(fields * HALO, INNER)])
        copy(model.at[:, pl.ds(at_y, HALO), :], yb.at[pl.ds(fields * nx, nx)])
        copy(
            table.at[:, pl.ds(at_y, HALO), :],
            yb.at[pl.ds((fields + 1) * nx, fields + 1)],
        )
        lanes = jnp.zeros((ny, nz), F32)
        for k in range(fields + 1):
            inside = (lane >= 8 * k) & (lane < 8 * k + INNER)
            head = pltpu.roll(table[k], 8 * k, axis=1)
            tail = pltpu.roll(table[k], (8 * k - (nx - INNER)) % nz, axis=1)
            lanes = jnp.where(inside, jnp.where(last_x, tail, head), lanes)
        slab[side, 0] = lanes
        copy(slab.at[side], xb.at[pl.ds(fields * HALO + INNER, 1)])
    for c in copies:
        c.wait()


def pack(source, model, observed, depth):
    freqs, _, nx, ny, nz = source.shape
    fields = 2 * freqs
    xs = jax.ShapeDtypeStruct((fields * HALO + INNER + 1, ny, nz), F32)
    ys = jax.ShapeDtypeStruct(((fields + 1) * nx + fields + 1, HALO, nz), F32)
    return pl.pallas_call(
        pack_kernel,
        out_shape=(xs, xs, ys, ys, jax.ShapeDtypeStruct((fields + 1, ny, nz), F32)),
        in_specs=[ANY, ANY, VMEM, VMEM],
        out_specs=(ANY, ANY, ANY, ANY, VMEM),
        scratch_shapes=[
            pltpu.VMEM((2, 1, ny, nz), F32),
            pltpu.SemaphoreType.DMA((64,)),
        ],
        compiler_params=params(8),
        name="pack",
    )(source, model, observed, depth)


def corner_kernel(fields, nx, ye, yo, ce, co, sem):
    even_x = parity("gx")
    copies = []
    count = iter(range(64))
    size = (fields + 1) * HALO + fields + 1
    for side, cb in enumerate((ce, co)):
        last_x = even_x if side == 0 else jnp.logical_not(even_x)
        at_x = jnp.where(last_x, nx - HALO, 0)
        for half, yb in enumerate((ye, yo)):
            base = half * size
            for k in range(fields + 1):
                copies.append(
                    pltpu.make_async_copy(
                        yb.at[pl.ds(k * nx + at_x, HALO)],
                        cb.at[pl.ds(base + k * HALO, HALO)],
                        sem.at[next(count)],
                    )
                )
            copies.append(
                pltpu.make_async_copy(
                    yb.at[pl.ds((fields + 1) * nx, fields + 1)],
                    cb.at[pl.ds(base + (fields + 1) * HALO, fields + 1)],
                    sem.at[next(count)],
                )
            )
    run_all(copies)


def corners(fields, nx, ye, yo):
    size = (fields + 1) * HALO + fields + 1
    out = jax.ShapeDtypeStruct((2 * size, HALO, ye.shape[2]), F32)
    return pl.pallas_call(
        functools.partial(corner_kernel, fields, nx),
        out_shape=(out, out),
        in_specs=[ANY, ANY],
        out_specs=(ANY, ANY),
        scratch_shapes=[pltpu.SemaphoreType.DMA((64,))],
        compiler_params=params(4),
        name="corners",
    )(ye, yo)


class Sweep:
    def __init__(self, nx, ny, nz, freqs, freq_sq, refs):
        self.nx, self.ny, self.nz, self.freqs = nx, ny, nz, freqs
        self.xe, self.ye = nx + 2 * HALO, ny + 2 * HALO
        self.tiles = self.ye // 8
        self.freq_sq = freq_sq
        self.s, self.v0, self.u0, self.v1, self.u1, self.cr, self.ci, self.w = refs
        lane = lax.broadcasted_iota(jnp.int32, (8, nz), 1)
        self.first = lane == 0
        self.last = lane == nz - 1
        self.depths = lane.astype(F32)
        sub = lax.broadcasted_iota(jnp.int32, (8, nz), 0)
        self.sub = sub
        has_left = lax.axis_index("gy") > 0
        has_right = lax.axis_index("gy") < lax.axis_size("gy") - 1
        left = jnp.where(has_left, 1.0, 0.0)
        right = jnp.where(has_right, 1.0, 0.0)
        self.inside = []
        for t in range(self.tiles):
            y = sub * self.tiles + t
            self.inside.append(
                jnp.where(y < ny, 1.0, jnp.where(y < ny + HALO, right, left))
            )
        self.groups = {}
        for t in range(self.tiles):
            owned = -((t - ny) // self.tiles)
            self.groups.setdefault(owned, []).append(t)

    def rows(self, ref, f, p, i):
        return [
            ref[f, p, i, pl.ds(t, 8, stride=self.tiles), :] for t in range(self.tiles)
        ]

    def put(self, ref, f, p, i, values):
        for t in range(self.tiles):
            ref[f, p, i, pl.ds(t, 8, stride=self.tiles), :] = values[t]

    def around(self, ref, f, p, i, lo, hi):
        mid = self.rows(ref, f, p, i)
        below = self.rows(ref, f, p, lo)
        above = self.rows(ref, f, p, hi)
        total = []
        n = self.tiles
        for t in range(n):
            up = mid[t + 1] if t + 1 < n else pltpu.roll(mid[0], 7, axis=0)
            down = mid[t - 1] if t else pltpu.roll(mid[n - 1], 1, axis=0)
            left = jnp.where(self.first, 0.0, pltpu.roll(mid[t], 1, axis=1))
            right = jnp.where(self.last, 0.0, pltpu.roll(mid[t], self.nz - 1, axis=1))
            total.append(((below[t] + above[t]) + (up + down)) + (left + right))
        return mid, total

    def coef(self, f, i):
        return (
            [self.cr[f, i, t] for t in range(self.tiles)],
            [self.ci[f, i, t] for t in range(self.tiles)],
        )

    def apply(self, src, f, i, lo, hi, sign, coef):
        cr, ci = coef
        re, nre = self.around(src, f, 0, i, lo, hi)
        im, nim = self.around(src, f, 1, i, lo, hi)
        out_re, out_im = [], []
        for t in range(self.tiles):
            if sign > 0:
                out_re.append(cr[t] * re[t] - ci[t] * im[t] - nre[t])
                out_im.append(cr[t] * im[t] + ci[t] * re[t] - nim[t])
            else:
                out_re.append(cr[t] * re[t] + ci[t] * im[t] - nre[t])
                out_im.append(cr[t] * im[t] - ci[t] * re[t] - nim[t])
        return re, im, out_re, out_im

    def masks(self, scale):
        if scale is None:
            return self.inside
        return [m * scale for m in self.inside]

    def squares(self, re, im, weight=None):
        out = []
        for t in range(self.tiles):
            value = re[t] * re[t] + im[t] * im[t]
            out.append(value if weight is None else weight[t] * value)
        return out

    def gather(self, acc, values):
        return tuple(
            a + functools.reduce(jnp.add, [values[t] for t in ts])
            for a, ts in zip(acc, self.groups.values())
        )

    def zero(self):
        return tuple(jnp.zeros((8, self.nz), F32) for _ in self.groups)

    def total(self, acc):
        return functools.reduce(
            jnp.add,
            [jnp.where(self.sub < n, a, 0.0) for a, n in zip(acc, self.groups)],
        )

    def prepare(self, i, model_rows, column):
        depth = column(2 * self.freqs)
        weight, terms = [], []
        coefs = []
        for t in range(self.tiles):
            weight.append(jnp.where(self.depths == depth[t], penalty, 0.0))
            self.w[i, t] = weight[t]
        for f in range(self.freqs):
            cr, ci = [], []
            for t in range(self.tiles):
                scaled = self.freq_sq[f] * model_rows[t]
                cr.append(6.0 - scaled)
                ci.append(attenuation * scaled)
                self.cr[f, i, t] = cr[t]
                self.ci[f, i, t] = ci[t]
            coefs.append((cr, ci))
            parts = []
            for p in range(2):
                seen = column(2 * f + p)
                parts.append([weight[t] * seen[t] for t in range(self.tiles)])
            terms.append(parts)
        return coefs, terms

    def weights(self, i):
        return [self.w[i, t] for t in range(self.tiles)]

    def step_v0(self, f, i, lo, hi, coef, terms, scale=None):
        _, _, re, im = self.apply(self.s, f, i, lo, hi, -1, coef)
        mask = self.masks(scale)
        re = [(re[t] + terms[0][t]) * mask[t] for t in range(self.tiles)]
        im = [(im[t] + terms[1][t]) * mask[t] for t in range(self.tiles)]
        self.put(self.v0, f, 0, i, re)
        self.put(self.v0, f, 1, i, im)
        return self.squares(re, im)

    def step_u0(self, f, i, lo, hi, scale=None, own=True):
        vr, vi, re, im = self.apply(self.v0, f, i, lo, hi, 1, self.coef(f, i))
        mask = self.masks(scale)
        re = [re[t] * mask[t] for t in range(self.tiles)]
        im = [im[t] * mask[t] for t in range(self.tiles)]
        self.put(self.u0, f, 0, i, re)
        self.put(self.u0, f, 1, i, im)
        if not own:
            return None
        a = self.squares(re, im)
        b = self.squares(vr, vi, self.weights(i))
        return [a[t] + b[t] for t in range(self.tiles)]

    def step_v1(self, f, i, lo, hi, scale=None, own=True):
        _, _, re, im = self.apply(self.u0, f, i, lo, hi, -1, self.coef(f, i))
        mask = self.masks(scale)
        weight = self.weights(i)
        vr = self.rows(self.v0, f, 0, i)
        vi = self.rows(self.v0, f, 1, i)
        re = [(re[t] + weight[t] * vr[t]) * mask[t] for t in range(self.tiles)]
        im = [(im[t] + weight[t] * vi[t]) * mask[t] for t in range(self.tiles)]
        self.put(self.v1, f, 0, i, re)
        self.put(self.v1, f, 1, i, im)
        return self.squares(re, im) if own else None

    def step_u1(self, f, i, lo, hi):
        vr, vi, re, im = self.apply(self.v1, f, i, lo, hi, 1, self.coef(f, i))
        self.put(self.u1, f, 0, i, re)
        self.put(self.u1, f, 1, i, im)
        a = self.squares(re, im)
        b = self.squares(vr, vi, self.weights(i))
        return [a[t] + b[t] for t in range(self.tiles)]


def inner_kernel(
    freq_sq, source, model, table, ye, yo, *refs
):
    state, moments, (cells, aux, sem) = refs[:8], refs[8], refs[9:]
    freqs, _, nx, ny, nz = source.shape
    fields = 2 * freqs
    sweep = Sweep(nx, ny, nz, freqs, freq_sq, state)
    s = sweep.s
    even_y = parity("gy")
    copies = []
    count = iter(range(64))

    def copy(src, dst):
        copies.append(pltpu.make_async_copy(src, dst, sem.at[next(count)]))

    at_e = pl.multiple_of(jnp.where(even_y, ny, ny + HALO), HALO)
    at_o = pl.multiple_of(jnp.where(even_y, ny + HALO, ny), HALO)
    copy(model, cells.at[:, pl.ds(0, ny), :])
    copy(table, aux.at[:, pl.ds(0, ny), :])
    for yb, at in ((ye, at_e), (yo, at_o)):
        copy(yb.at[pl.ds(fields * nx, nx)], cells.at[:, pl.ds(at, HALO), :])
        copy(yb.at[pl.ds((fields + 1) * nx, fields + 1)], aux.at[:, pl.ds(at, HALO), :])
    for k in range(fields):
        f, p = k // 2, k % 2
        copy(source.at[f, p], s.at[f, p, pl.ds(0, nx), pl.ds(0, ny), :])
        for yb, at in ((ye, at_e), (yo, at_o)):
            copy(
                yb.at[pl.ds(k * nx, nx)],
                s.at[f, p, pl.ds(0, nx), pl.ds(at, HALO), :],
            )
    run_all(copies)

    tiles = sweep.tiles

    def prepare(i):
        def column(k):
            pick = jnp.full((8, nz), i, jnp.int32)
            return [
                jnp.take_along_axis(
                    aux[k, pl.ds(t, 8, stride=tiles), :], pick, axis=1
                )
                for t in range(tiles)
            ]

        rows = [cells[i, pl.ds(t, 8, stride=tiles), :] for t in range(tiles)]
        return sweep.prepare(i, rows, column)

    for i in (0, nx - 1):
        _, terms = prepare(i)
        for f in range(freqs):
            for p in range(2):
                sweep.put(sweep.v0, f, p, i, terms[f][p])

    def step(j, acc, active):
        acc = [list(a) for a in acc]
        if 3 in active:
            i = j - 6
            for f in range(freqs):
                acc[f][3] = sweep.gather(acc[f][3], sweep.step_u1(f, i, i - 1, i + 1))
        if 2 in active:
            i = j - 4
            for f in range(freqs):
                acc[f][2] = sweep.gather(acc[f][2], sweep.step_v1(f, i, i - 1, i + 1))
        if 1 in active:
            i = j - 2
            for f in range(freqs):
                acc[f][1] = sweep.gather(acc[f][1], sweep.step_u0(f, i, i - 1, i + 1))
        if 0 in active:
            coefs, terms = prepare(j)
            for f in range(freqs):
                acc[f][0] = sweep.gather(
                    acc[f][0], sweep.step_v0(f, j, j - 1, j + 1, coefs[f], terms[f])
                )
        return tuple(tuple(a) for a in acc)

    spans = [(1 + 3 * k, nx - 1 + k) for k in range(4)]
    edges = sorted({e for span in spans for e in span})
    acc = tuple(tuple(sweep.zero() for _ in range(4)) for _ in range(freqs))
    for lo, hi in zip(edges[:-1], edges[1:]):
        active = [k for k, (a, b) in enumerate(spans) if a <= lo and hi <= b]
        acc = lax.fori_loop(lo, hi, functools.partial(step, active=active), acc)
    for f in range(freqs):
        for m in range(4):
            moments[f, m] = sweep.total(acc[f][m])


def state_shapes(freqs, nx, ny, nz):
    xe, ye = nx + 2 * HALO, ny + 2 * HALO
    field = pltpu.VMEM((freqs, 2, xe, ye, nz), F32)
    coef = pltpu.VMEM((freqs, xe, ye // 8, 8, nz), F32)
    weight = pltpu.VMEM((xe, ye // 8, 8, nz), F32)
    return (field,) * 5 + (coef, coef, weight)


def inner_part(freq_sq, source, model, table, ye, yo):
    freqs, _, nx, ny, nz = source.shape
    return pl.pallas_call(
        inner_kernel,
        out_shape=state_shapes(freqs, nx, ny, nz)
        + (pltpu.VMEM((freqs, 4, 8, nz), F32),),
        in_specs=[SMEM, ANY, ANY, VMEM, ANY, ANY],
        scratch_shapes=[
            pltpu.VMEM((nx, ny + 2 * HALO, nz), F32),
            pltpu.VMEM((2 * freqs + 1, ny + 2 * HALO, nz), F32),
            pltpu.SemaphoreType.DMA((64,)),
        ],
        compiler_params=params(8),
        name="inner_part",
    )(freq_sq, source, model, table, ye, yo)


def edge_kernel(peers, nx, ny, freq_sq, xe, xo, ce, co, *refs):
    moments, part = refs[8], refs[17]
    state, (cells, aux, near, sem) = refs[9:17], refs[18:]
    freqs, _, _, _, nz = state[0].shape
    fields = 2 * freqs
    sweep = Sweep(nx, ny, nz, freqs, freq_sq, state)
    s, tiles = sweep.s, sweep.tiles
    even_x, even_y = parity("gx"), parity("gy")
    at_e = pl.multiple_of(jnp.where(even_y, ny, ny + HALO), HALO)
    at_o = pl.multiple_of(jnp.where(even_y, ny + HALO, ny), HALO)
    low_e = pl.multiple_of(jnp.where(even_y, 0, HALO), HALO)
    low_o = pl.multiple_of(jnp.where(even_y, HALO, 0), HALO)
    size = (fields + 1) * HALO + fields + 1
    copies = []
    count = iter(range(128))

    def copy(src, dst):
        copies.append(pltpu.make_async_copy(src, dst, sem.at[next(count)]))

    for side, (xb, cb) in enumerate(((xe, ce), (xo, co))):
        above = even_x if side == 0 else jnp.logical_not(even_x)
        slot = jnp.where(above, nx, nx + HALO)
        skip = jnp.where(above, 0, 1)
        half = jnp.where(above, 0, 1)
        for k in range(fields):
            f, p = k // 2, k % 2
            copy(
                xb.at[pl.ds(k * HALO, HALO)],
                s.at[f, p, pl.ds(slot, HALO), pl.ds(0, ny), :],
            )
            for h, at in enumerate((at_e, at_o)):
                copy(
                    cb.at[pl.ds(h * size + k * HALO, HALO)],
                    s.at[f, p, pl.ds(slot, HALO), pl.ds(at, HALO), :],
                )
        copy(
            xb.at[pl.ds(fields * HALO, INNER)],
            cells.at[half, pl.ds(0, INNER), pl.ds(0, ny), :],
        )
        copy(xb.at[fields * HALO + INNER], aux.at[half, pl.ds(0, ny), :])
        for h, (at, low) in enumerate(((at_e, low_e), (at_o, low_o))):
            copy(
                cb.at[pl.ds(h * size + fields * HALO + skip, INNER)],
                cells.at[half, pl.ds(0, INNER), pl.ds(at, HALO), :],
            )
            copy(
                cb.at[pl.ds(h * size + (fields + 1) * HALO, fields + 1)],
                near.at[half, :, pl.ds(low, HALO), :],
            )
    run_all(copies)

    lane = lax.broadcasted_iota(jnp.int32, (8, nz), 1)
    for half in range(2):
        base = 0 if half == 0 else nx - INNER
        lanes = jnp.zeros((8, nz), F32)
        for k in range(fields + 1):
            inside = (lane >= 8 * k) & (lane < 8 * k + INNER)
            moved = pltpu.roll(near[half, k], (8 * k - base) % nz, axis=1)
            lanes = jnp.where(inside, moved, lanes)
        aux[half, ny:, :] = lanes

    for half in range(2):
        for layer in range(INNER):
            i = nx + layer if half == 0 else nx + HALO + 1 + layer

            def column(k):
                pick = jnp.full((8, nz), 8 * k + layer, jnp.int32)
                return [
                    jnp.take_along_axis(
                        aux[half, pl.ds(t, 8, stride=tiles), :], pick, axis=1
                    )
                    for t in range(tiles)
                ]

            rows = [
                cells[half, layer, pl.ds(t, 8, stride=tiles), :] for t in range(tiles)
            ]
            _, terms = sweep.prepare(i, rows, column)
            for f in range(freqs):
                for p in range(2):
                    sweep.put(sweep.v0, f, p, i, terms[f][p])

    left = jnp.where(lax.axis_index("gx") > 0, 1.0, 0.0)
    right = jnp.where(lax.axis_index("gx") < lax.axis_size("gx") - 1, 1.0, 0.0)
    wrap = sweep.xe

    def place(x):
        return x % wrap, (x - 1) % wrap, (x + 1) % wrap

    def scale(x):
        return None if 0 <= x < nx else (left if x < 0 else right)

    acc = [[sweep.zero() for _ in range(4)] for _ in range(freqs)]
    for stage in range(4):
        for k in range(HALO):
            for x in (k - INNER + stage, nx - 1 - stage + k):
                i, lo, hi = place(x)
                own = 0 <= x < nx
                for f in range(freqs):
                    if stage == 0:
                        terms = [sweep.rows(sweep.v0, f, p, i) for p in range(2)]
                        got = sweep.step_v0(
                            f, i, lo, hi, sweep.coef(f, i), terms, scale(x)
                        )
                    elif stage == 1:
                        got = sweep.step_u0(f, i, lo, hi, scale(x), own)
                    elif stage == 2:
                        got = sweep.step_v1(f, i, lo, hi, scale(x), own)
                    else:
                        got = sweep.step_u1(f, i, lo, hi)
                    if own:
                        acc[f][stage] = sweep.gather(acc[f][stage], got)

    rows = []
    for f in range(freqs):
        for m in range(4):
            both = sweep.total(acc[f][m]) + moments[f, m]
            rows.append(jnp.sum(both, axis=0, keepdims=True))
    sums = jnp.sum(jnp.concatenate(rows, axis=0), axis=1, keepdims=True)
    sums = jnp.broadcast_to(sums, (4 * freqs, nz))
    for peer in range(peers):
        part[peer] = sums


def edge_part(peers, nx, ny, freq_sq, xe, xo, ce, co, state, moments):
    freqs, _, _, _, nz = state[0].shape
    outs = state_shapes(freqs, nx, ny, nz)
    return pl.pallas_call(
        functools.partial(edge_kernel, peers, nx, ny),
        out_shape=outs + (jax.ShapeDtypeStruct((peers, 4 * freqs, nz), F32),),
        in_specs=[SMEM] + [ANY] * 4 + [VMEM] * 9,
        input_output_aliases={5 + k: k for k in range(8)},
        scratch_shapes=[
            pltpu.VMEM((2, INNER, ny + 2 * HALO, nz), F32),
            pltpu.VMEM((2, ny + 2 * HALO, nz), F32),
            pltpu.VMEM((2, 2 * freqs + 1, 2 * HALO, nz), F32),
            pltpu.SemaphoreType.DMA((128,)),
        ],
        compiler_params=params(8),
        name="edge_part",
    )(freq_sq, xe, xo, ce, co, *state, moments)


def steps(sums, f):
    total = jnp.sum(sums[...], axis=0)
    shape = (8, total.shape[1])
    m0, m1, m2, m3 = (
        jnp.broadcast_to(total[4 * f + k : 4 * f + k + 1, :], shape) for k in range(4)
    )
    first = m0 / m1
    new = first * (first * m2 - m1)
    product = m1 - first * (2.0 * m2 - first * m3)
    ratio = new / m0
    second = new / (product - ratio * new / first)
    return first + second * (1.0 + ratio), -first * second


def gradient_kernel(nx, ny, freq_sq, sums, s, v0, u0, v1, u1, out):
    freqs = s.shape[0]
    weights = [steps(sums, f) for f in range(freqs)]

    def row(x, _):
        for y in range(0, ny, 8):
            at = pl.ds(y, 8)
            total = None
            for f in range(freqs):
                a, b = weights[f]
                wave_re = a * v0[f, 0, x, at, :] + b * v1[f, 0, x, at, :]
                wave_im = a * v0[f, 1, x, at, :] + b * v1[f, 1, x, at, :]
                miss_re = a * u0[f, 0, x, at, :] + b * u1[f, 0, x, at, :]
                miss_im = a * u0[f, 1, x, at, :] + b * u1[f, 1, x, at, :]
                miss_re = miss_re - s[f, 0, x, at, :]
                miss_im = miss_im - s[f, 1, x, at, :]
                left = (wave_re + attenuation * wave_im) * miss_re
                right = (wave_im - attenuation * wave_re) * miss_im
                term = -freq_sq[f] * (left + right)
                total = term if total is None else total + term
            out[x, at, :] = total
        return 0

    lax.fori_loop(0, nx, row, 0)


def wave_kernel(nx, ny, sums, v0, v1, out):
    step = pl.program_id(0)
    freqs = v0.shape[0]
    weights = [steps(sums, f) for f in range(freqs)]
    a, b = weights[0]
    f, p = step // 2, step % 2
    for k in range(1, freqs):
        a = jnp.where(f == k, weights[k][0], a)
        b = jnp.where(f == k, weights[k][1], b)

    def row(x, _):
        for y in range(0, ny, 8):
            at = pl.ds(y, 8)
            out[0, 0, x, at, :] = a * v0[f, p, x, at, :] + b * v1[f, p, x, at, :]
        return 0

    lax.fori_loop(0, nx, row, 0)


def results(nx, ny, freq_sq, sums, state):
    s, v0, u0, v1, u1 = state[:5]
    freqs, _, _, _, nz = s.shape
    gradient = pl.pallas_call(
        functools.partial(gradient_kernel, nx, ny),
        out_shape=jax.ShapeDtypeStruct((nx, ny, nz), F32),
        in_specs=[SMEM] + [VMEM] * 6,
        out_specs=VMEM,
        compiler_params=params(8),
        name="gradient_part",
    )(freq_sq, sums, s, v0, u0, v1, u1)
    wave = pl.pallas_call(
        functools.partial(wave_kernel, nx, ny),
        grid=(2 * freqs,),
        out_shape=jax.ShapeDtypeStruct((freqs, 2, nx, ny, nz), F32),
        in_specs=[VMEM] * 3,
        out_specs=pl.BlockSpec(
            (1, 1, nx, ny, nz), lambda k: (k // 2, k % 2, 0, 0, 0)
        ),
        compiler_params=params(8),
        name="wavefield",
    )(sums, v0, v1)
    return gradient, wave


def swap(cells, axis, odd):
    count = lax.axis_size(axis)
    pairs = []
    for i in range(odd, count - 1, 2):
        pairs += [(i, i + 1), (i + 1, i)]
    return lax.ppermute(cells, axis, pairs)


def on_device(model, freq_sq, source, observed, receiver_depth):
    nx, ny, nz = model.shape
    freqs = freq_sq.shape[0]
    xe, xo, ye, yo, table = pack(source, model, observed, receiver_depth)
    ye, yo = swap(ye, "gy", 0), swap(yo, "gy", 1)
    xe, xo = swap(xe, "gx", 0), swap(xo, "gx", 1)
    ce, co = corners(2 * freqs, nx, ye, yo)
    ce, co = swap(ce, "gx", 0), swap(co, "gx", 1)
    *state, moments = inner_part(freq_sq, source, model, table, ye, yo)
    peers = lax.axis_size("gx") * lax.axis_size("gy")
    *state, part = edge_part(peers, nx, ny, freq_sq, xe, xo, ce, co, state, moments)
    sums = lax.all_to_all(part, ("gx", "gy"), 0, 0)
    gradient, wave = results(nx, ny, freq_sq, sums, state)
    if lax.axis_size("af") == 2:
        gradient = gradient + lax.ppermute(gradient, "af", [(0, 1), (1, 0)])
    else:
        gradient = lax.psum(gradient, "af")
    return wave, gradient


def solution(mesh):
    in_specs = (
        P("gx", "gy", None),
        P("af"),
        P("af", None, "gx", "gy", None),
        P("af", None, "gx", "gy"),
        P("gx", "gy"),
    )
    out_specs = (P("af", None, "gx", "gy", None), P("gx", "gy", None))
    return jax.shard_map(
        on_device, mesh=mesh, in_specs=in_specs, out_specs=out_specs, check_vma=False
    )
```

```python
import functools

import jax
import jax.numpy as jnp
from jax import lax
from jax.experimental import pallas as pl
from jax.experimental.pallas import tpu as pltpu
from jax.sharding import PartitionSpec as P

ITERS = 2
attenuation = 0.2
penalty = 4.0

HALO = 2 * ITERS
INNER = HALO - 1
F32 = jnp.float32
ANY = pl.BlockSpec(memory_space=pl.ANY)
HBM = pl.BlockSpec(memory_space=pltpu.HBM)
VMEM = pl.BlockSpec(memory_space=pltpu.VMEM)
SMEM = pl.BlockSpec(memory_space=pltpu.SMEM)
MIB = 1 << 20
LOAD_MIB = 55
SHIFT = 2


def params(mib):
    return pltpu.CompilerParams(vmem_limit_bytes=mib * MIB)


def cost(us):
    return pl.CostEstimate(
        flops=int(us * 1e3), bytes_accessed=int(us * 1e3), transcendentals=0
    )


def parity(axis):
    return lax.rem(lax.axis_index(axis), 2) == 0


class Copies:
    def __init__(self, sem):
        self.sem, self.all = sem, []

    def add(self, src, dst):
        copy = pltpu.make_async_copy(src, dst, self.sem.at[len(self.all)])
        copy.start()
        self.all.append(copy)

    def wait(self):
        for copy in self.all:
            copy.wait()


def lane_slab(table, fields, skip, rows, nz):
    lane = lax.broadcasted_iota(jnp.int32, (rows, nz), 1)
    lanes = jnp.zeros((rows, nz), F32)
    for k in range(fields + 1):
        inside = (lane >= 8 * k) & (lane < 8 * k + INNER)
        shift = lax.rem(8 * k + nz - skip, nz)
        lanes = jnp.where(inside, pltpu.roll(table[k], shift, axis=1), lanes)
    return lanes


def load_kernel(source, model, observed, depth, *refs):
    freqs, _, nx, ny, nz = source.shape
    fields = 2 * freqs
    s, (cells, aux, xe, xo, ye, yo, seen, sunk, table, slab, sem) = refs[:freqs], refs[freqs:]
    small = Copies(sem.at[0])
    small.add(observed, seen)
    small.add(depth, sunk)
    large = Copies(sem.at[1])
    large.add(model, cells.at[:, pl.ds(0, ny), :])
    for f in range(freqs):
        for p in range(2):
            large.add(source.at[f, p], s[f].at[p, pl.ds(0, nx), pl.ds(0, ny), :])
    even_x, even_y = parity("gx"), parity("gy")
    small.wait()
    for f in range(freqs):
        for p in range(2):
            table[2 * f + p, :, 0:nx] = seen[f, p].T
    table[fields, :, 0:nx] = sunk[...].astype(F32).T
    copies = Copies(sem.at[2])
    copies.add(table, aux.at[:, pl.ds(0, ny), :])
    faces = []
    for side, xb in enumerate((xe, xo)):
        last = even_x if side == 0 else jnp.logical_not(even_x)
        skip = jnp.where(last, nx - INNER, 0)
        faces.append((xb, skip, jnp.where(last, nx - HALO, 0)))
        slab[side] = lane_slab(table, fields, skip, ny, nz)
        copies.add(
            slab.at[pl.ds(side, 1)], xb.at[pl.ds(fields * HALO + INNER, 1)]
        )
    places = []
    for side, yb in enumerate((ye, yo)):
        last = even_y if side == 0 else jnp.logical_not(even_y)
        at = pl.multiple_of(jnp.where(last, ny - HALO, 0), HALO)
        places.append((yb, at))
        copies.add(
            table.at[:, pl.ds(at, HALO), :],
            yb.at[pl.ds((fields + 1) * nx, fields + 1)],
        )
    large.all[0].wait()
    for yb, at in places:
        copies.add(cells.at[:, pl.ds(at, HALO), :], yb.at[pl.ds(fields * nx, nx)])
    for xb, skip, _ in faces:
        copies.add(
            cells.at[pl.ds(skip, INNER), pl.ds(0, ny), :],
            xb.at[pl.ds(fields * HALO, INNER)],
        )
    for k in range(fields):
        large.all[1 + k].wait()
        block = s[k // 2].at[k % 2]
        for yb, at in places:
            copies.add(
                block.at[pl.ds(0, nx), pl.ds(at, HALO), :], yb.at[pl.ds(k * nx, nx)]
            )
        for xb, _, at in faces:
            copies.add(
                block.at[pl.ds(at, HALO), pl.ds(0, ny), :],
                xb.at[pl.ds(k * HALO, HALO)],
            )
    copies.wait()


def load(source, model, observed, depth):
    freqs, _, nx, ny, nz = source.shape
    fields = 2 * freqs
    xs = pltpu.VMEM((fields * HALO + INNER + 1, ny, nz), F32)
    ys = pltpu.VMEM(((fields + 1) * nx + fields + 1, HALO, nz), F32)
    return pl.pallas_call(
        load_kernel,
        out_shape=(pltpu.VMEM((2, nx + 2 * HALO, ny + 2 * HALO, nz), F32),) * freqs
        + (
            pltpu.VMEM((nx, ny + 2 * HALO, nz), F32),
            pltpu.VMEM((fields + 1, ny + 2 * HALO, nz), F32),
            xs,
            xs,
            ys,
            ys,
        ),
        in_specs=[HBM] * 4,
        scratch_shapes=[
            pltpu.VMEM(observed.shape, F32),
            pltpu.VMEM(depth.shape, jnp.int32),
            pltpu.VMEM((fields + 1, ny, nz), F32),
            pltpu.VMEM((2, ny, nz), F32),
            pltpu.SemaphoreType.DMA((3, 32)),
        ],
        compiler_params=params(LOAD_MIB),
        name="load",
    )(source, model, observed, depth)


def halo_places(ny):
    even_y = parity("gy")
    at_e = pl.multiple_of(jnp.where(even_y, ny, ny + HALO), HALO)
    at_o = pl.multiple_of(jnp.where(even_y, ny + HALO, ny), HALO)
    return at_e, at_o


class Grid:
    def __init__(self, nx, ny, nz):
        self.nx, self.ny, self.nz = nx, ny, nz
        self.xe, self.ye = nx + 2 * HALO, ny + 2 * HALO
        self.tiles = self.ye // 8
        lane = lax.broadcasted_iota(jnp.int32, (8, nz), 1)
        self.first = lane == 0
        self.last = lane == nz - 1
        self.depths = lane.astype(F32)
        self.sub = lax.broadcasted_iota(jnp.int32, (8, nz), 0)
        has_left = lax.axis_index("gy") > 0
        has_right = lax.axis_index("gy") < lax.axis_size("gy") - 1
        self.cut_left = jnp.where(
            self.sub == 0, jnp.where(has_left, 1.0, 0.0), jnp.ones((8, nz), F32)
        )
        self.cut_tile = (ny - 1) % self.tiles
        self.cut_right = jnp.where(
            self.sub == (ny - 1) // self.tiles,
            jnp.where(has_right, 1.0, 0.0),
            jnp.ones((8, nz), F32),
        )
        self.groups = {}
        for t in range(self.tiles):
            owned = -((t - ny) // self.tiles)
            self.groups.setdefault(owned, []).append(t)

    def rows(self, ref, p, i):
        return [
            ref[p, i, pl.ds(t, 8, stride=self.tiles), :] for t in range(self.tiles)
        ]

    def put(self, ref, p, i, values):
        for t in range(self.tiles):
            ref[p, i, pl.ds(t, 8, stride=self.tiles), :] = values[t]

    def beside(self, mid):
        out = []
        for t in range(self.tiles):
            left = jnp.where(self.first, 0.0, pltpu.roll(mid[t], 1, axis=1))
            right = jnp.where(self.last, 0.0, pltpu.roll(mid[t], self.nz - 1, axis=1))
            out.append(left + right)
        return out

    def around(self, mid, below, above, beside):
        total = []
        n = self.tiles
        for t in range(n):
            up = mid[t + 1] if t + 1 < n else pltpu.roll(mid[0], 7, axis=0)
            down = mid[t - 1] if t else pltpu.roll(mid[n - 1], 1, axis=0)
            if t == 0:
                down = down * self.cut_left
            if t == self.cut_tile:
                up = up * self.cut_right
            total.append(((below[t] + above[t]) + (up + down)) + beside[t])
        return total

    def apply(self, src, i, lo, hi, sign, coef, mid_im, beside_im, cut=None):
        cr, ci = coef
        mid_re = self.rows(src, 0, i)
        total = []
        for p, mid, beside in (
            (0, mid_re, self.beside(mid_re)),
            (1, mid_im, beside_im),
        ):
            below, above = self.rows(src, p, lo), self.rows(src, p, hi)
            if cut is not None and cut[0] < 0:
                below = [b * cut[1] for b in below]
            if cut is not None and cut[0] > 0:
                above = [a * cut[1] for a in above]
            total.append(self.around(mid, below, above, beside))
        out_re, out_im = [], []
        for t in range(self.tiles):
            re, im = mid_re[t], mid_im[t]
            if sign > 0:
                out_re.append(cr[t] * re - ci[t] * im - total[0][t])
                out_im.append(cr[t] * im + ci[t] * re - total[1][t])
            else:
                out_re.append(cr[t] * re + ci[t] * im - total[0][t])
                out_im.append(cr[t] * im - ci[t] * re - total[1][t])
        return out_re, out_im

    def squares(self, re, im):
        return [re[t] * re[t] + im[t] * im[t] for t in range(self.tiles)]

    def gather(self, acc, values):
        return tuple(
            a + functools.reduce(jnp.add, [values[t] for t in ts])
            for a, ts in zip(acc, self.groups.values())
        )

    def zero(self):
        return tuple(jnp.zeros((8, self.nz), F32) for _ in self.groups)

    def total(self, acc):
        return functools.reduce(
            jnp.add,
            [jnp.where(self.sub < n, a, 0.0) for a, n in zip(acc, self.groups)],
        )

    def tile_list(self, ref, i):
        return [ref[i, t] for t in range(self.tiles)]

    def weigh(self, i, w, depth):
        for t in range(self.tiles):
            w[i, t] = jnp.where(self.depths == depth[t], penalty, 0.0)

    def coefs(self, i, freq_sq, cells, cr, ci):
        for t in range(self.tiles):
            scaled = freq_sq * cells[t]
            cr[i, t] = 6.0 - scaled
            ci[i, t] = attenuation * scaled


class Field:
    def __init__(self, grid, refs, w):
        self.grid = grid
        self.s, self.v0, self.u0, self.v1, self.u1, self.cr, self.ci = refs
        self.w = w

    def source_of(self, stage):
        return (self.s, self.v0, self.u0, self.v1)[stage]

    def target_of(self, stage):
        return (self.v0, self.u0, self.v1, self.u1)[stage]

    def step(self, stage, i, lo, hi, mid_im, beside_im, terms=None, cut=None, acc=None):
        g = self.grid
        tiles = range(g.tiles)
        coef = (g.tile_list(self.cr, i), g.tile_list(self.ci, i))
        sign = -1 if stage in (0, 2) else 1
        re, im = g.apply(
            self.source_of(stage), i, lo, hi, sign, coef, mid_im, beside_im, cut
        )
        weight = g.tile_list(self.w, i) if stage in (0, 2) else None
        if stage == 0:
            re = [re[t] + terms[0][t] for t in tiles]
            im = [im[t] + terms[1][t] for t in tiles]
        if stage == 2:
            old_re, old_im = g.rows(self.v0, 0, i), g.rows(self.v0, 1, i)
            re = [re[t] + weight[t] * old_re[t] for t in tiles]
            im = [im[t] + weight[t] * old_im[t] for t in tiles]
        g.put(self.target_of(stage), 0, i, re)
        g.put(self.target_of(stage), 1, i, im)
        if acc is None:
            return None
        acc = list(acc)
        squares = g.squares(re, im)
        acc[stage] = g.gather(acc[stage], squares)
        if stage in (0, 2):
            weighted = [weight[t] * squares[t] for t in tiles]
            acc[stage + 1] = g.gather(acc[stage + 1], weighted)
        return tuple(acc)


def corner_faces(freqs, nx, ny, s, cells, aux, ce, co, slab, sem):
    fields = 2 * freqs
    nz = cells.shape[2]
    even_x = parity("gx")
    out = Copies(sem)
    rows = pl.ds(ny, 2 * HALO)
    for side, cb in enumerate((ce, co)):
        last = even_x if side == 0 else jnp.logical_not(even_x)
        skip = jnp.where(last, nx - INNER, 0)
        at = jnp.where(last, nx - HALO, 0)
        for k in range(fields):
            out.add(
                s[k // 2].at[k % 2, pl.ds(at, HALO), rows, :],
                cb.at[pl.ds(k * HALO, HALO)],
            )
        out.add(cells.at[pl.ds(skip, INNER), rows, :], cb.at[pl.ds(fields * HALO, INNER)])
        near = [aux[k, ny:, :] for k in range(fields + 1)]
        slab[side] = lane_slab(near, fields, skip, 2 * HALO, nz)
        out.add(
            slab.at[pl.ds(side, 1)], cb.at[pl.ds(fields * HALO + INNER, 1)]
        )
    return out


def inner_kernel(freqs, nx, ny, half, freq_sq, *refs):
    if half == 0:
        ye, yo = refs[:2]
        refs = refs[2 + freqs + 2 :]
        s, (cells, aux), refs = refs[:freqs], refs[freqs : freqs + 2], refs[freqs + 2 :]
        state, (w, moments, ce, co, slab, sem) = refs[: 6 * freqs], refs[6 * freqs :]
    else:
        (cells, aux), s = refs[:2], refs[2 : 2 + freqs]
        partial = refs[2 + freqs + 6 * freqs + 1]
        refs = refs[2 + 7 * freqs + 2 :]
        state, (w, moments) = refs[: 6 * freqs], refs[6 * freqs :]
    nz = cells.shape[2]
    fields = 2 * freqs
    if half == 0:
        copies = Copies(sem.at[0])
        for yb, at in zip((ye, yo), halo_places(ny)):
            rows = pl.ds(at, HALO)
            copies.add(
                yb.at[pl.ds((fields + 1) * nx, fields + 1)], aux.at[:, rows, :]
            )
            copies.add(yb.at[pl.ds(fields * nx, nx)], cells.at[:, rows, :])
            for k in range(fields):
                copies.add(
                    yb.at[pl.ds(k * nx, nx)],
                    s[k // 2].at[k % 2, pl.ds(0, nx), rows, :],
                )
    grid = Grid(nx, ny, nz)
    if half == 0:
        copies.wait()
        out = corner_faces(freqs, nx, ny, s, cells, aux, ce, co, slab, sem.at[1])
    tiles = grid.tiles
    many = [Field(grid, (s[f], *state[6 * f : 6 * f + 6]), w) for f in range(freqs)]

    def prepare(i):
        def column(k):
            pick = jnp.full((8, nz), i, jnp.int32)
            return [
                jnp.take_along_axis(
                    aux[k, pl.ds(t, 8, stride=tiles), :], pick, axis=1
                )
                for t in range(tiles)
            ]

        rows = [cells[i, pl.ds(t, 8, stride=tiles), :] for t in range(tiles)]
        grid.weigh(i, w, column(fields))
        weight = grid.tile_list(w, i)
        out = []
        for f in range(freqs):
            grid.coefs(i, freq_sq[f], rows, many[f].cr, many[f].ci)
            terms = []
            for p in range(2):
                seen = column(2 * f + p)
                terms.append([weight[t] * seen[t] for t in range(tiles)])
            out.append(terms)
        return out

    if half == 0:
        for i in (0, nx - 1):
            terms = prepare(i)
            for f in range(freqs):
                for p in range(2):
                    grid.put(many[f].v0, p, i, terms[f][p])

    def step(j, acc, active):
        acc = list(acc)
        for k in reversed(active):
            i = j - 2 * k
            terms = prepare(i) if k == 0 else [None] * freqs
            for f in range(freqs):
                mid = grid.rows(many[f].source_of(k), 1, i)
                acc[f] = many[f].step(
                    k, i, i - 1, i + 1, mid, grid.beside(mid), terms[f], acc=acc[f]
                )
        return tuple(acc)

    spans = [(1 + 3 * k, nx - 1 + k) for k in range(4)]
    middle = nx // 2 + SHIFT
    edges = sorted({e for span in spans for e in span} | {middle})
    acc = tuple(tuple(grid.zero() for _ in range(4)) for _ in range(freqs))
    for lo, hi in zip(edges[:-1], edges[1:]):
        if (lo < middle) != (half == 0):
            continue
        active = [k for k, (a, b) in enumerate(spans) if a <= lo and hi <= b]
        acc = lax.fori_loop(lo, hi, functools.partial(step, active=active), acc)
    for f in range(freqs):
        for m in range(4):
            value = grid.total(acc[f][m])
            moments[f, m] = value if half == 0 else value + partial[f, m]
    if half == 0:
        out.wait()


def inner_part(nx, ny, freq_sq, ye, yo, s, cells, aux):
    _, xe, ye_rows, nz = s[0].shape
    freqs = len(s)
    slabs = 2 * freqs * HALO + INNER + 1
    field = pltpu.VMEM(s[0].shape, F32)
    coef = pltpu.VMEM((xe, ye_rows // 8, 8, nz), F32)
    corner = pltpu.VMEM((slabs, 2 * HALO, nz), F32)
    kept = (*s, cells, aux)
    news = ((field,) * 4 + (coef, coef)) * freqs + (
        coef,
        pltpu.VMEM((freqs, 4, 8, nz), F32),
    )
    got = pl.pallas_call(
        functools.partial(inner_kernel, freqs, nx, ny, 0),
        out_shape=tuple(pltpu.VMEM(k.shape, F32) for k in kept)
        + news
        + (corner, corner),
        in_specs=[SMEM, ANY, ANY] + [VMEM] * len(kept),
        input_output_aliases={3 + k: k for k in range(len(kept))},
        scratch_shapes=[
            pltpu.VMEM((2, 2 * HALO, nz), F32),
            pltpu.SemaphoreType.DMA((2, 16)),
        ],
        compiler_params=params(8),
        name="inner_first",
    )(freq_sq, ye, yo, *kept)
    s, cells, aux = got[:freqs], got[freqs], got[freqs + 1]
    news_got, (ce, co) = got[freqs + 2 : -2], got[-2:]

    def rest():
        again = pl.pallas_call(
            functools.partial(inner_kernel, freqs, nx, ny, 1),
            out_shape=news,
            in_specs=[SMEM] + [VMEM] * (2 + freqs + len(news)),
            input_output_aliases={3 + freqs + k: k for k in range(len(news))},
            compiler_params=params(8),
            name="inner_second",
        )(freq_sq, cells, aux, *s, *news_got)
        state = []
        for f in range(freqs):
            state += [s[f], *again[6 * f : 6 * f + 6]]
        return state + [again[-2]], again[-1]

    return ce, co, rest


def edge_kernel(peers, freqs, nx, ny, freq_sq, xe, xo, ce, co, *refs):
    count = 7 * freqs + 1
    moments, refs = refs[count], refs[count + 1 :]
    state, (part, cells, aux, sem) = refs[:count], refs[count:]
    fields = 2 * freqs
    nz = state[0].shape[3]
    w = state[-1]
    copies = Copies(sem)
    even_x = parity("gx")
    pieces = (
        (xe, 0, 0, ny),
        (xo, 1, 0, ny),
        (ce, 0, ny, 2 * HALO),
        (co, 1, ny, 2 * HALO),
    )
    for block, side, at, size in pieces:
        above = even_x if side == 0 else jnp.logical_not(even_x)
        slot = jnp.where(above, nx, nx + HALO)
        half = jnp.where(above, 0, 1)
        rows = pl.ds(at, size)
        for k in range(fields):
            copies.add(
                block.at[pl.ds(k * HALO, HALO)],
                state[7 * (k // 2)].at[k % 2, pl.ds(slot, HALO), rows, :],
            )
        copies.add(
            block.at[pl.ds(fields * HALO, INNER)], cells.at[half, :, rows, :]
        )
        copies.add(
            block.at[pl.ds(fields * HALO + INNER, 1)],
            aux.at[pl.ds(half, 1), rows, :],
        )
    grid = Grid(nx, ny, nz)
    copies.wait()
    tiles = grid.tiles
    many = [Field(grid, state[7 * f : 7 * f + 7], w) for f in range(freqs)]

    for half in range(2):
        for layer in range(INNER):
            i = nx + layer if half == 0 else nx + HALO + 1 + layer

            def column(k):
                pick = jnp.full((8, nz), 8 * k + layer, jnp.int32)
                return [
                    jnp.take_along_axis(
                        aux[half, pl.ds(t, 8, stride=tiles), :], pick, axis=1
                    )
                    for t in range(tiles)
                ]

            rows = [
                cells[half, layer, pl.ds(t, 8, stride=tiles), :] for t in range(tiles)
            ]
            grid.weigh(i, w, column(fields))
            weight = grid.tile_list(w, i)
            for f in range(freqs):
                grid.coefs(i, freq_sq[f], rows, many[f].cr, many[f].ci)
                for p in range(2):
                    seen = column(2 * f + p)
                    grid.put(
                        many[f].v0, p, i, [weight[t] * seen[t] for t in range(tiles)]
                    )

    left = jnp.where(lax.axis_index("gx") > 0, 1.0, 0.0)
    right = jnp.where(lax.axis_index("gx") < lax.axis_size("gx") - 1, 1.0, 0.0)
    wrap = grid.xe
    acc = [tuple(grid.zero() for _ in range(4)) for _ in range(freqs)]
    for stage in range(4):
        for k in range(HALO):
            jobs = [
                (x, f)
                for x in (k - INNER + stage, nx - 1 - stage + k)
                for f in range(freqs)
            ]
            mids = [many[f].source_of(stage) for _, f in jobs]
            mids = [grid.rows(ref, 1, x % wrap) for ref, (x, _) in zip(mids, jobs)]
            sums = [grid.beside(mid) for mid in mids]
            for (x, f), mid, beside in zip(jobs, mids, sums):
                i, lo, hi = x % wrap, (x - 1) % wrap, (x + 1) % wrap
                own = 0 <= x < nx
                cut = None
                if x == 0:
                    cut = (-1, left)
                if x == nx - 1:
                    cut = (1, right)
                terms = None
                if stage == 0:
                    terms = [grid.rows(many[f].v0, p, i) for p in range(2)]
                got = many[f].step(
                    stage, i, lo, hi, mid, beside, terms, cut, acc[f] if own else None
                )
                if own:
                    acc[f] = got

    rows = []
    for f in range(freqs):
        for m in range(4):
            both = grid.total(acc[f][m]) + moments[f, m]
            rows.append(jnp.sum(both, axis=0, keepdims=True))
    sums = jnp.sum(jnp.concatenate(rows, axis=0), axis=1, keepdims=True)
    sums = jnp.broadcast_to(sums, (4 * freqs, nz))
    for peer in range(peers):
        part[peer] = sums


def edge_part(peers, freqs, nx, ny, freq_sq, xe, xo, ce, co, state, moments):
    nz = state[0].shape[3]
    outs = tuple(pltpu.VMEM(k.shape, F32) for k in state)
    return pl.pallas_call(
        functools.partial(edge_kernel, peers, freqs, nx, ny),
        out_shape=outs + (jax.ShapeDtypeStruct((peers, 4 * freqs, nz), F32),),
        in_specs=[SMEM] + [ANY] * 4 + [VMEM] * (len(state) + 1),
        input_output_aliases={5 + k: k for k in range(len(state))},
        scratch_shapes=[
            pltpu.VMEM((2, INNER, ny + 2 * HALO, nz), F32),
            pltpu.VMEM((2, ny + 2 * HALO, nz), F32),
            pltpu.SemaphoreType.DMA((64,)),
        ],
        compiler_params=params(8),
        name="edge_part",
    )(freq_sq, xe, xo, ce, co, *state, moments)


def steps(sums, freqs):
    total = jnp.sum(sums[...], axis=0)
    shape = (8, total.shape[1])
    out = []
    for f in range(freqs):
        m0, m1, m2, m3 = (
            jnp.broadcast_to(total[4 * f + k : 4 * f + k + 1, :], shape)
            for k in range(4)
        )
        first = m0 / m1
        new = first * (first * m2 - m1)
        product = m1 - first * (2.0 * m2 - first * m3)
        ratio = new / m0
        second = new / (product - ratio * new / first)
        out.append((first + second * (1.0 + ratio), -first * second))
    return out


def gradient_kernel(freqs, nx, ny, freq_sq, sums, *refs):
    out = refs[-1]
    weights = steps(sums, freqs)

    def row(x, _):
        for y in range(0, ny, 8):
            at = pl.ds(y, 8)
            total = None
            for f in range(freqs):
                s, v0, u0, v1, u1 = refs[5 * f : 5 * f + 5]
                a, b = weights[f]
                wave_re = a * v0[0, x, at, :] + b * v1[0, x, at, :]
                wave_im = a * v0[1, x, at, :] + b * v1[1, x, at, :]
                miss_re = a * u0[0, x, at, :] + b * u1[0, x, at, :]
                miss_im = a * u0[1, x, at, :] + b * u1[1, x, at, :]
                miss_re = miss_re - s[0, x, at, :]
                miss_im = miss_im - s[1, x, at, :]
                left = (wave_re + attenuation * wave_im) * miss_re
                right = (wave_im - attenuation * wave_re) * miss_im
                term = -freq_sq[f] * (left + right)
                total = term if total is None else total + term
            out[x, at, :] = total
        return 0

    lax.fori_loop(0, nx, row, 0)


def wave_kernel(freqs, nx, ny, sums, *refs):
    out, block, sem = refs[2 * freqs :]
    weights = steps(sums, freqs)
    copies = Copies(sem)
    for f in range(freqs):
        a, b = weights[f]
        v0, v1 = refs[2 * f : 2 * f + 2]
        for p in range(2):
            k = 2 * f + p

            def row(x, _):
                for y in range(0, ny, 8):
                    at = pl.ds(y, 8)
                    block[k, x, at, :] = a * v0[p, x, at, :] + b * v1[p, x, at, :]
                return 0

            lax.fori_loop(0, nx, row, 0)
            copies.add(block.at[k], out.at[f, p])
    copies.wait()


def results(freqs, nx, ny, freq_sq, sums, state):
    nz = state[0].shape[3]
    fields, pairs = [], []
    for f in range(freqs):
        s, v0, u0, v1, u1 = state[7 * f : 7 * f + 5]
        fields += [s, v0, u0, v1, u1]
        pairs += [v0, v1]
    gradient = pl.pallas_call(
        functools.partial(gradient_kernel, freqs, nx, ny),
        out_shape=jax.ShapeDtypeStruct((nx, ny, nz), F32),
        in_specs=[SMEM] + [VMEM] * (1 + len(fields)),
        out_specs=VMEM,
        compiler_params=params(8),
        name="gradient_part",
    )(freq_sq, sums, *fields)
    wave = pl.pallas_call(
        functools.partial(wave_kernel, freqs, nx, ny),
        out_shape=jax.ShapeDtypeStruct((freqs, 2, nx, ny, nz), F32),
        in_specs=[VMEM] * (1 + len(pairs)),
        out_specs=HBM,
        scratch_shapes=[
            pltpu.VMEM((2 * freqs, nx, ny, nz), F32),
            pltpu.SemaphoreType.DMA((2 * freqs,)),
        ],
        compiler_params=params(8),
        name="wavefield",
    )(sums, *pairs)
    return gradient, wave


def swap(cells, axis, odd):
    count = lax.axis_size(axis)
    pairs = []
    for i in range(odd, count - 1, 2):
        pairs += [(i, i + 1), (i + 1, i)]
    return lax.ppermute(cells, axis, pairs)


def on_device(model, freq_sq, source, observed, receiver_depth):
    nx, ny, nz = model.shape
    freqs = freq_sq.shape[0]
    *s, cells, aux, xe, xo, ye, yo = load(source, model, observed, receiver_depth)
    ye, yo = swap(ye, "gy", 0), swap(yo, "gy", 1)
    xe, xo = swap(xe, "gx", 0), swap(xo, "gx", 1)
    ce, co, rest = inner_part(nx, ny, freq_sq, ye, yo, s, cells, aux)
    ce, co = swap(ce, "gx", 0), swap(co, "gx", 1)
    state, moments = rest()
    peers = lax.axis_size("gx") * lax.axis_size("gy")
    *state, part = edge_part(
        peers, freqs, nx, ny, freq_sq, xe, xo, ce, co, state, moments
    )
    sums = lax.all_to_all(part, ("gx", "gy"), 0, 0)
    gradient, wave = results(freqs, nx, ny, freq_sq, sums, state)
    if lax.axis_size("af") == 2:
        gradient = gradient + lax.ppermute(gradient, "af", [(0, 1), (1, 0)])
    else:
        gradient = lax.psum(gradient, "af")
    return wave, gradient


def solution(mesh):
    in_specs = (
        P("gx", "gy", None),
        P("af"),
        P("af", None, "gx", "gy", None),
        P("af", None, "gx", "gy"),
        P("gx", "gy"),
    )
    out_specs = (P("af", None, "gx", "gy", None), P("gx", "gy", None))
    return jax.shard_map(
        on_device, mesh=mesh, in_specs=in_specs, out_specs=out_specs, check_vma=False
    )
```

```python
import functools

import jax
import jax.numpy as jnp
from jax import lax
from jax.experimental import pallas as pl
from jax.experimental.pallas import tpu as pltpu
from jax.sharding import PartitionSpec as P

ITERS = 2
attenuation = 0.2
penalty = 4.0

HALO = 2 * ITERS
INNER = HALO - 1
F32 = jnp.float32
ANY = pl.BlockSpec(memory_space=pl.ANY)
HBM = pl.BlockSpec(memory_space=pltpu.HBM)
VMEM = pl.BlockSpec(memory_space=pltpu.VMEM)
SMEM = pl.BlockSpec(memory_space=pltpu.SMEM)
MIB = 1 << 20
LOAD_MIB = 55
SHIFT = 2


def params(mib):
    return pltpu.CompilerParams(vmem_limit_bytes=mib * MIB)


def cost(us):
    return pl.CostEstimate(
        flops=int(us * 1e3), bytes_accessed=int(us * 1e3), transcendentals=0
    )


def parity(axis):
    return lax.rem(lax.axis_index(axis), 2) == 0


class Copies:
    def __init__(self, sem):
        self.sem, self.all = sem, []

    def add(self, src, dst):
        copy = pltpu.make_async_copy(src, dst, self.sem.at[len(self.all)])
        copy.start()
        self.all.append(copy)

    def wait(self):
        for copy in self.all:
            copy.wait()


def lane_slab(table, fields, skip, rows, nz):
    lane = lax.broadcasted_iota(jnp.int32, (rows, nz), 1)
    lanes = jnp.zeros((rows, nz), F32)
    for k in range(fields + 1):
        inside = (lane >= 8 * k) & (lane < 8 * k + INNER)
        shift = lax.rem(8 * k + nz - skip, nz)
        lanes = jnp.where(inside, pltpu.roll(table[k], shift, axis=1), lanes)
    return lanes


def load_kernel(source, model, observed, depth, *refs):
    freqs, _, nx, ny, nz = source.shape
    fields = 2 * freqs
    s, (cells, aux, xe, xo, ye, yo, seen, sunk, table, slab, sem) = refs[:freqs], refs[freqs:]
    small = Copies(sem.at[0])
    small.add(observed, seen)
    small.add(depth, sunk)
    large = Copies(sem.at[1])
    large.add(model, cells.at[:, pl.ds(0, ny), :])
    for f in range(freqs):
        for p in range(2):
            large.add(source.at[f, p], s[f].at[p, pl.ds(0, nx), pl.ds(0, ny), :])
    even_x, even_y = parity("gx"), parity("gy")
    small.wait()
    for f in range(freqs):
        for p in range(2):
            table[2 * f + p, :, 0:nx] = seen[f, p].T
    table[fields, :, 0:nx] = sunk[...].astype(F32).T
    copies = Copies(sem.at[2])
    copies.add(table, aux.at[:, pl.ds(0, ny), :])
    faces = []
    for side, xb in enumerate((xe, xo)):
        last = even_x if side == 0 else jnp.logical_not(even_x)
        skip = jnp.where(last, nx - INNER, 0)
        faces.append((xb, skip, jnp.where(last, nx - HALO, 0)))
        slab[side] = lane_slab(table, fields, skip, ny, nz)
        copies.add(
            slab.at[pl.ds(side, 1)], xb.at[pl.ds(fields * HALO + INNER, 1)]
        )
    places = []
    for side, yb in enumerate((ye, yo)):
        last = even_y if side == 0 else jnp.logical_not(even_y)
        at = pl.multiple_of(jnp.where(last, ny - HALO, 0), HALO)
        places.append((yb, at))
        copies.add(
            table.at[:, pl.ds(at, HALO), :],
            yb.at[pl.ds((fields + 1) * nx, fields + 1)],
        )
    large.all[0].wait()
    for yb, at in places:
        copies.add(cells.at[:, pl.ds(at, HALO), :], yb.at[pl.ds(fields * nx, nx)])
    for xb, skip, _ in faces:
        copies.add(
            cells.at[pl.ds(skip, INNER), pl.ds(0, ny), :],
            xb.at[pl.ds(fields * HALO, INNER)],
        )
    for k in range(fields):
        large.all[1 + k].wait()
        block = s[k // 2].at[k % 2]
        for yb, at in places:
            copies.add(
                block.at[pl.ds(0, nx), pl.ds(at, HALO), :], yb.at[pl.ds(k * nx, nx)]
            )
        for xb, _, at in faces:
            copies.add(
                block.at[pl.ds(at, HALO), pl.ds(0, ny), :],
                xb.at[pl.ds(k * HALO, HALO)],
            )
    copies.wait()


def load(source, model, observed, depth):
    freqs, _, nx, ny, nz = source.shape
    fields = 2 * freqs
    xs = pltpu.VMEM((fields * HALO + INNER + 1, ny, nz), F32)
    ys = pltpu.VMEM(((fields + 1) * nx + fields + 1, HALO, nz), F32)
    return pl.pallas_call(
        load_kernel,
        out_shape=(pltpu.VMEM((2, nx + 2 * HALO, ny + 2 * HALO, nz), F32),) * freqs
        + (
            pltpu.VMEM((nx, ny + 2 * HALO, nz), F32),
            pltpu.VMEM((fields + 1, ny + 2 * HALO, nz), F32),
            xs,
            xs,
            ys,
            ys,
        ),
        in_specs=[HBM] * 4,
        scratch_shapes=[
            pltpu.VMEM(observed.shape, F32),
            pltpu.VMEM(depth.shape, jnp.int32),
            pltpu.VMEM((fields + 1, ny, nz), F32),
            pltpu.VMEM((2, ny, nz), F32),
            pltpu.SemaphoreType.DMA((3, 32)),
        ],
        compiler_params=params(LOAD_MIB),
        name="load",
    )(source, model, observed, depth)


def halo_places(ny):
    even_y = parity("gy")
    at_e = pl.multiple_of(jnp.where(even_y, ny, ny + HALO), HALO)
    at_o = pl.multiple_of(jnp.where(even_y, ny + HALO, ny), HALO)
    return at_e, at_o


class Grid:
    def __init__(self, nx, ny, nz):
        self.nx, self.ny, self.nz = nx, ny, nz
        self.xe, self.ye = nx + 2 * HALO, ny + 2 * HALO
        self.tiles = self.ye // 8
        lane = lax.broadcasted_iota(jnp.int32, (8, nz), 1)
        self.first = lane == 0
        self.last = lane == nz - 1
        self.depths = lane.astype(F32)
        self.sub = lax.broadcasted_iota(jnp.int32, (8, nz), 0)
        has_left = lax.axis_index("gy") > 0
        has_right = lax.axis_index("gy") < lax.axis_size("gy") - 1
        self.cut_left = jnp.where(
            self.sub == 0, jnp.where(has_left, 1.0, 0.0), jnp.ones((8, nz), F32)
        )
        self.cut_tile = (ny - 1) % self.tiles
        self.cut_right = jnp.where(
            self.sub == (ny - 1) // self.tiles,
            jnp.where(has_right, 1.0, 0.0),
            jnp.ones((8, nz), F32),
        )
        self.groups = {}
        for t in range(self.tiles):
            owned = -((t - ny) // self.tiles)
            self.groups.setdefault(owned, []).append(t)

    def rows(self, ref, p, i):
        return [
            ref[p, i, pl.ds(t, 8, stride=self.tiles), :] for t in range(self.tiles)
        ]

    def put(self, ref, p, i, values):
        for t in range(self.tiles):
            ref[p, i, pl.ds(t, 8, stride=self.tiles), :] = values[t]

    def beside(self, mid):
        out = []
        for t in range(self.tiles):
            left = jnp.where(self.first, 0.0, pltpu.roll(mid[t], 1, axis=1))
            right = jnp.where(self.last, 0.0, pltpu.roll(mid[t], self.nz - 1, axis=1))
            out.append(left + right)
        return out

    def around(self, mid, below, above, beside):
        total = []
        n = self.tiles
        for t in range(n):
            up = mid[t + 1] if t + 1 < n else pltpu.roll(mid[0], 7, axis=0)
            down = mid[t - 1] if t else pltpu.roll(mid[n - 1], 1, axis=0)
            if t == 0:
                down = down * self.cut_left
            if t == self.cut_tile:
                up = up * self.cut_right
            total.append(((below[t] + above[t]) + (up + down)) + beside[t])
        return total

    def apply(self, src, i, lo, hi, sign, coef, mid_im, beside_im, cut=None):
        cr, ci = coef
        mid_re = self.rows(src, 0, i)
        total = []
        for p, mid, beside in (
            (0, mid_re, self.beside(mid_re)),
            (1, mid_im, beside_im),
        ):
            below, above = self.rows(src, p, lo), self.rows(src, p, hi)
            if cut is not None and cut[0] < 0:
                below = [b * cut[1] for b in below]
            if cut is not None and cut[0] > 0:
                above = [a * cut[1] for a in above]
            total.append(self.around(mid, below, above, beside))
        out_re, out_im = [], []
        for t in range(self.tiles):
            re, im = mid_re[t], mid_im[t]
            if sign > 0:
                out_re.append(cr[t] * re - ci[t] * im - total[0][t])
                out_im.append(cr[t] * im + ci[t] * re - total[1][t])
            else:
                out_re.append(cr[t] * re + ci[t] * im - total[0][t])
                out_im.append(cr[t] * im - ci[t] * re - total[1][t])
        return out_re, out_im

    def squares(self, re, im):
        return [re[t] * re[t] + im[t] * im[t] for t in range(self.tiles)]

    def gather(self, acc, values):
        return tuple(
            a + functools.reduce(jnp.add, [values[t] for t in ts])
            for a, ts in zip(acc, self.groups.values())
        )

    def zero(self):
        return tuple(jnp.zeros((8, self.nz), F32) for _ in self.groups)

    def total(self, acc):
        return functools.reduce(
            jnp.add,
            [jnp.where(self.sub < n, a, 0.0) for a, n in zip(acc, self.groups)],
        )

    def tile_list(self, ref, i):
        return [ref[i, t] for t in range(self.tiles)]

    def weigh(self, i, w, depth):
        for t in range(self.tiles):
            w[i, t] = jnp.where(self.depths == depth[t], penalty, 0.0)

    def coefs(self, i, freq_sq, cells, cr, ci):
        for t in range(self.tiles):
            scaled = freq_sq * cells[t]
            cr[i, t] = 6.0 - scaled
            ci[i, t] = attenuation * scaled


class Field:
    def __init__(self, grid, refs, w):
        self.grid = grid
        self.s, self.v0, self.u0, self.v1, self.u1, self.cr, self.ci = refs
        self.w = w

    def source_of(self, stage):
        return (self.s, self.v0, self.u0, self.v1)[stage]

    def target_of(self, stage):
        return (self.v0, self.u0, self.v1, self.u1)[stage]

    def step(self, stage, i, lo, hi, mid_im, beside_im, terms=None, cut=None, acc=None):
        g = self.grid
        tiles = range(g.tiles)
        coef = (g.tile_list(self.cr, i), g.tile_list(self.ci, i))
        sign = -1 if stage in (0, 2) else 1
        re, im = g.apply(
            self.source_of(stage), i, lo, hi, sign, coef, mid_im, beside_im, cut
        )
        weight = g.tile_list(self.w, i) if stage in (0, 2) else None
        if stage == 0:
            re = [re[t] + terms[0][t] for t in tiles]
            im = [im[t] + terms[1][t] for t in tiles]
        if stage == 2:
            old_re, old_im = g.rows(self.v0, 0, i), g.rows(self.v0, 1, i)
            re = [re[t] + weight[t] * old_re[t] for t in tiles]
            im = [im[t] + weight[t] * old_im[t] for t in tiles]
        g.put(self.target_of(stage), 0, i, re)
        g.put(self.target_of(stage), 1, i, im)
        if acc is None:
            return None
        acc = list(acc)
        squares = g.squares(re, im)
        acc[stage] = g.gather(acc[stage], squares)
        if stage in (0, 2):
            weighted = [weight[t] * squares[t] for t in tiles]
            acc[stage + 1] = g.gather(acc[stage + 1], weighted)
        return tuple(acc)


def corner_faces(freqs, nx, ny, s, cells, aux, ce, co, slab, sem):
    fields = 2 * freqs
    nz = cells.shape[2]
    even_x = parity("gx")
    out = Copies(sem)
    rows = pl.ds(ny, 2 * HALO)
    for side, cb in enumerate((ce, co)):
        last = even_x if side == 0 else jnp.logical_not(even_x)
        skip = jnp.where(last, nx - INNER, 0)
        at = jnp.where(last, nx - HALO, 0)
        for k in range(fields):
            out.add(
                s[k // 2].at[k % 2, pl.ds(at, HALO), rows, :],
                cb.at[pl.ds(k * HALO, HALO)],
            )
        out.add(cells.at[pl.ds(skip, INNER), rows, :], cb.at[pl.ds(fields * HALO, INNER)])
        near = [aux[k, ny:, :] for k in range(fields + 1)]
        slab[side] = lane_slab(near, fields, skip, 2 * HALO, nz)
        out.add(
            slab.at[pl.ds(side, 1)], cb.at[pl.ds(fields * HALO + INNER, 1)]
        )
    return out


def inner_kernel(freqs, nx, ny, half, freq_sq, *refs):
    if half == 0:
        ye, yo = refs[:2]
        refs = refs[2 + freqs + 2 :]
        s, (cells, aux), refs = refs[:freqs], refs[freqs : freqs + 2], refs[freqs + 2 :]
        state, (w, moments, ce, co, slab, sem) = refs[: 6 * freqs], refs[6 * freqs :]
    else:
        (cells, aux), s = refs[:2], refs[2 : 2 + freqs]
        partial = refs[2 + freqs + 6 * freqs + 1]
        refs = refs[2 + 7 * freqs + 2 :]
        state, (w, moments) = refs[: 6 * freqs], refs[6 * freqs :]
    nz = cells.shape[2]
    fields = 2 * freqs
    if half == 0:
        copies = Copies(sem.at[0])
        for yb, at in zip((ye, yo), halo_places(ny)):
            rows = pl.ds(at, HALO)
            copies.add(
                yb.at[pl.ds((fields + 1) * nx, fields + 1)], aux.at[:, rows, :]
            )
            copies.add(yb.at[pl.ds(fields * nx, nx)], cells.at[:, rows, :])
            for k in range(fields):
                copies.add(
                    yb.at[pl.ds(k * nx, nx)],
                    s[k // 2].at[k % 2, pl.ds(0, nx), rows, :],
                )
    grid = Grid(nx, ny, nz)
    if half == 0:
        copies.wait()
        out = corner_faces(freqs, nx, ny, s, cells, aux, ce, co, slab, sem.at[1])
    tiles = grid.tiles
    many = [Field(grid, (s[f], *state[6 * f : 6 * f + 6]), w) for f in range(freqs)]

    def prepare(i):
        def column(k):
            pick = jnp.full((8, nz), i, jnp.int32)
            return [
                jnp.take_along_axis(
                    aux[k, pl.ds(t, 8, stride=tiles), :], pick, axis=1
                )
                for t in range(tiles)
            ]

        rows = [cells[i, pl.ds(t, 8, stride=tiles), :] for t in range(tiles)]
        grid.weigh(i, w, column(fields))
        weight = grid.tile_list(w, i)
        out = []
        for f in range(freqs):
            grid.coefs(i, freq_sq[f], rows, many[f].cr, many[f].ci)
            terms = []
            for p in range(2):
                seen = column(2 * f + p)
                terms.append([weight[t] * seen[t] for t in range(tiles)])
            out.append(terms)
        return out

    if half == 0:
        for i in (0, nx - 1):
            terms = prepare(i)
            for f in range(freqs):
                for p in range(2):
                    grid.put(many[f].v0, p, i, terms[f][p])

    def step(j, acc, active):
        acc = list(acc)
        for k in reversed(active):
            i = j - 2 * k
            terms = prepare(i) if k == 0 else [None] * freqs
            for f in range(freqs):
                mid = grid.rows(many[f].source_of(k), 1, i)
                acc[f] = many[f].step(
                    k, i, i - 1, i + 1, mid, grid.beside(mid), terms[f], acc=acc[f]
                )
        return tuple(acc)

    spans = [(1 + 3 * k, nx - 1 + k) for k in range(4)]
    middle = nx // 2 + SHIFT
    edges = sorted({e for span in spans for e in span} | {middle})
    acc = tuple(tuple(grid.zero() for _ in range(4)) for _ in range(freqs))
    for lo, hi in zip(edges[:-1], edges[1:]):
        if (lo < middle) != (half == 0):
            continue
        active = [k for k, (a, b) in enumerate(spans) if a <= lo and hi <= b]
        acc = lax.fori_loop(lo, hi, functools.partial(step, active=active), acc)
    for f in range(freqs):
        for m in range(4):
            value = grid.total(acc[f][m])
            moments[f, m] = value if half == 0 else value + partial[f, m]
    if half == 0:
        out.wait()


def inner_part(nx, ny, freq_sq, ye, yo, s, cells, aux):
    _, xe, ye_rows, nz = s[0].shape
    freqs = len(s)
    slabs = 2 * freqs * HALO + INNER + 1
    field = pltpu.VMEM(s[0].shape, F32)
    coef = pltpu.VMEM((xe, ye_rows // 8, 8, nz), F32)
    corner = pltpu.VMEM((slabs, 2 * HALO, nz), F32)
    kept = (*s, cells, aux)
    news = ((field,) * 4 + (coef, coef)) * freqs + (
        coef,
        pltpu.VMEM((freqs, 4, 8, nz), F32),
    )
    got = pl.pallas_call(
        functools.partial(inner_kernel, freqs, nx, ny, 0),
        out_shape=tuple(pltpu.VMEM(k.shape, F32) for k in kept)
        + news
        + (corner, corner),
        in_specs=[SMEM, ANY, ANY] + [VMEM] * len(kept),
        input_output_aliases={3 + k: k for k in range(len(kept))},
        scratch_shapes=[
            pltpu.VMEM((2, 2 * HALO, nz), F32),
            pltpu.SemaphoreType.DMA((2, 16)),
        ],
        compiler_params=params(8),
        name="inner_first",
    )(freq_sq, ye, yo, *kept)
    s, cells, aux = got[:freqs], got[freqs], got[freqs + 1]
    news_got, (ce, co) = got[freqs + 2 : -2], got[-2:]

    def rest():
        again = pl.pallas_call(
            functools.partial(inner_kernel, freqs, nx, ny, 1),
            out_shape=news,
            in_specs=[SMEM] + [VMEM] * (2 + freqs + len(news)),
            input_output_aliases={3 + freqs + k: k for k in range(len(news))},
            compiler_params=params(8),
            name="inner_second",
        )(freq_sq, cells, aux, *s, *news_got)
        state = []
        for f in range(freqs):
            state += [s[f], *again[6 * f : 6 * f + 6]]
        return state + [again[-2]], again[-1]

    return ce, co, rest


def edge_kernel(peers, freqs, nx, ny, freq_sq, xe, xo, ce, co, *refs):
    count = 7 * freqs + 1
    moments, refs = refs[count], refs[count + 1 :]
    state, (part, cells, aux, sem) = refs[:count], refs[count:]
    fields = 2 * freqs
    nz = state[0].shape[3]
    w = state[-1]
    copies = Copies(sem)
    even_x = parity("gx")
    pieces = (
        (xe, 0, 0, ny),
        (xo, 1, 0, ny),
        (ce, 0, ny, 2 * HALO),
        (co, 1, ny, 2 * HALO),
    )
    for block, side, at, size in pieces:
        above = even_x if side == 0 else jnp.logical_not(even_x)
        slot = jnp.where(above, nx, nx + HALO)
        half = jnp.where(above, 0, 1)
        rows = pl.ds(at, size)
        for k in range(fields):
            copies.add(
                block.at[pl.ds(k * HALO, HALO)],
                state[7 * (k // 2)].at[k % 2, pl.ds(slot, HALO), rows, :],
            )
        copies.add(
            block.at[pl.ds(fields * HALO, INNER)], cells.at[half, :, rows, :]
        )
        copies.add(
            block.at[pl.ds(fields * HALO + INNER, 1)],
            aux.at[pl.ds(half, 1), rows, :],
        )
    grid = Grid(nx, ny, nz)
    copies.wait()
    tiles = grid.tiles
    many = [Field(grid, state[7 * f : 7 * f + 7], w) for f in range(freqs)]

    for half in range(2):
        for layer in range(INNER):
            i = nx + layer if half == 0 else nx + HALO + 1 + layer

            def column(k):
                pick = jnp.full((8, nz), 8 * k + layer, jnp.int32)
                return [
                    jnp.take_along_axis(
                        aux[half, pl.ds(t, 8, stride=tiles), :], pick, axis=1
                    )
                    for t in range(tiles)
                ]

            rows = [
                cells[half, layer, pl.ds(t, 8, stride=tiles), :] for t in range(tiles)
            ]
            grid.weigh(i, w, column(fields))
            weight = grid.tile_list(w, i)
            for f in range(freqs):
                grid.coefs(i, freq_sq[f], rows, many[f].cr, many[f].ci)
                for p in range(2):
                    seen = column(2 * f + p)
                    grid.put(
                        many[f].v0, p, i, [weight[t] * seen[t] for t in range(tiles)]
                    )

    left = jnp.where(lax.axis_index("gx") > 0, 1.0, 0.0)
    right = jnp.where(lax.axis_index("gx") < lax.axis_size("gx") - 1, 1.0, 0.0)
    wrap = grid.xe
    acc = [tuple(grid.zero() for _ in range(4)) for _ in range(freqs)]
    for stage in range(4):
        for k in range(HALO):
            jobs = [
                (x, f)
                for x in (k - INNER + stage, nx - 1 - stage + k)
                for f in range(freqs)
            ]
            mids = [many[f].source_of(stage) for _, f in jobs]
            mids = [grid.rows(ref, 1, x % wrap) for ref, (x, _) in zip(mids, jobs)]
            sums = [grid.beside(mid) for mid in mids]
            for (x, f), mid, beside in zip(jobs, mids, sums):
                i, lo, hi = x % wrap, (x - 1) % wrap, (x + 1) % wrap
                own = 0 <= x < nx
                cut = None
                if x == 0:
                    cut = (-1, left)
                if x == nx - 1:
                    cut = (1, right)
                terms = None
                if stage == 0:
                    terms = [grid.rows(many[f].v0, p, i) for p in range(2)]
                got = many[f].step(
                    stage, i, lo, hi, mid, beside, terms, cut, acc[f] if own else None
                )
                if own:
                    acc[f] = got

    rows = []
    for f in range(freqs):
        for m in range(4):
            both = grid.total(acc[f][m]) + moments[f, m]
            rows.append(jnp.sum(both, axis=0, keepdims=True))
    sums = jnp.sum(jnp.concatenate(rows, axis=0), axis=1, keepdims=True)
    sums = jnp.broadcast_to(sums, (4 * freqs, nz))
    for peer in range(peers):
        part[peer] = sums


def edge_part(peers, freqs, nx, ny, freq_sq, xe, xo, ce, co, state, moments):
    nz = state[0].shape[3]
    outs = tuple(pltpu.VMEM(k.shape, F32) for k in state)
    return pl.pallas_call(
        functools.partial(edge_kernel, peers, freqs, nx, ny),
        out_shape=outs + (jax.ShapeDtypeStruct((peers, 4 * freqs, nz), F32),),
        in_specs=[SMEM] + [ANY] * 4 + [VMEM] * (len(state) + 1),
        input_output_aliases={5 + k: k for k in range(len(state))},
        scratch_shapes=[
            pltpu.VMEM((2, INNER, ny + 2 * HALO, nz), F32),
            pltpu.VMEM((2, ny + 2 * HALO, nz), F32),
            pltpu.SemaphoreType.DMA((64,)),
        ],
        compiler_params=params(8),
        name="edge_part",
    )(freq_sq, xe, xo, ce, co, *state, moments)


def steps(sums, freqs):
    total = jnp.sum(sums[...], axis=0)
    shape = (8, total.shape[1])
    out = []
    for f in range(freqs):
        m0, m1, m2, m3 = (
            jnp.broadcast_to(total[4 * f + k : 4 * f + k + 1, :], shape)
            for k in range(4)
        )
        first = m0 / m1
        new = first * (first * m2 - m1)
        product = m1 - first * (2.0 * m2 - first * m3)
        ratio = new / m0
        second = new / (product - ratio * new / first)
        out.append((first + second * (1.0 + ratio), -first * second))
    return out


def gradient_kernel(freqs, nx, ny, freq_sq, sums, *refs):
    out = refs[-1]
    weights = steps(sums, freqs)

    def row(x, _):
        for y in range(0, ny, 8):
            at = pl.ds(y, 8)
            total = None
            for f in range(freqs):
                s, v0, u0, v1, u1 = refs[5 * f : 5 * f + 5]
                a, b = weights[f]
                wave_re = a * v0[0, x, at, :] + b * v1[0, x, at, :]
                wave_im = a * v0[1, x, at, :] + b * v1[1, x, at, :]
                miss_re = a * u0[0, x, at, :] + b * u1[0, x, at, :]
                miss_im = a * u0[1, x, at, :] + b * u1[1, x, at, :]
                miss_re = miss_re - s[0, x, at, :]
                miss_im = miss_im - s[1, x, at, :]
                left = (wave_re + attenuation * wave_im) * miss_re
                right = (wave_im - attenuation * wave_re) * miss_im
                term = -freq_sq[f] * (left + right)
                total = term if total is None else total + term
            out[x, at, :] = total
        return 0

    lax.fori_loop(0, nx, row, 0)


def wave_kernel(freqs, nx, ny, sums, *refs):
    out, block, sem = refs[2 * freqs :]
    weights = steps(sums, freqs)
    copies = Copies(sem)
    for f in range(freqs):
        a, b = weights[f]
        v0, v1 = refs[2 * f : 2 * f + 2]
        for p in range(2):
            k = 2 * f + p

            def row(x, _):
                for y in range(0, ny, 8):
                    at = pl.ds(y, 8)
                    block[k, x, at, :] = a * v0[p, x, at, :] + b * v1[p, x, at, :]
                return 0

            lax.fori_loop(0, nx, row, 0)
            copies.add(block.at[k], out.at[f, p])
    copies.wait()


def results(freqs, nx, ny, freq_sq, sums, state):
    nz = state[0].shape[3]
    fields, pairs = [], []
    for f in range(freqs):
        s, v0, u0, v1, u1 = state[7 * f : 7 * f + 5]
        fields += [s, v0, u0, v1, u1]
        pairs += [v0, v1]
    gradient = pl.pallas_call(
        functools.partial(gradient_kernel, freqs, nx, ny),
        out_shape=jax.ShapeDtypeStruct((nx, ny, nz), F32),
        in_specs=[SMEM] + [VMEM] * (1 + len(fields)),
        out_specs=VMEM,
        compiler_params=params(8),
        name="gradient_part",
    )(freq_sq, sums, *fields)
    wave = pl.pallas_call(
        functools.partial(wave_kernel, freqs, nx, ny),
        out_shape=jax.ShapeDtypeStruct((freqs, 2, nx, ny, nz), F32),
        in_specs=[VMEM] * (1 + len(pairs)),
        out_specs=HBM,
        scratch_shapes=[
            pltpu.VMEM((2 * freqs, nx, ny, nz), F32),
            pltpu.SemaphoreType.DMA((2 * freqs,)),
        ],
        compiler_params=params(8),
        name="wavefield",
    )(sums, *pairs)
    return gradient, wave


def swap(cells, axis, odd):
    names = ("gx", "gy", "af")
    sizes = [lax.axis_size(name) for name in names]
    along = names.index(axis)
    pairs = []
    for flat in range(sizes[0] * sizes[1] * sizes[2]):
        place = [flat // (sizes[1] * sizes[2]), flat // sizes[2] % sizes[1], flat % sizes[2]]
        mate = ((place[along] + odd) ^ 1) - odd
        if 0 <= mate < sizes[along]:
            place[along] = mate
        elif sizes[2] % 2 == 0:
            place[2] ^= 1
        else:
            continue
        pairs.append((flat, (place[0] * sizes[1] + place[1]) * sizes[2] + place[2]))
    return lax.ppermute(cells, names, pairs)


def on_device(model, freq_sq, source, observed, receiver_depth):
    nx, ny, nz = model.shape
    freqs = freq_sq.shape[0]
    *s, cells, aux, xe, xo, ye, yo = load(source, model, observed, receiver_depth)
    ye, yo = swap(ye, "gy", 0), swap(yo, "gy", 1)
    xe, xo = swap(xe, "gx", 0), swap(xo, "gx", 1)
    ce, co, rest = inner_part(nx, ny, freq_sq, ye, yo, s, cells, aux)
    ce, co = swap(ce, "gx", 0), swap(co, "gx", 1)
    state, moments = rest()
    peers = lax.axis_size("gx") * lax.axis_size("gy")
    *state, part = edge_part(
        peers, freqs, nx, ny, freq_sq, xe, xo, ce, co, state, moments
    )
    sums = lax.all_to_all(part, ("gx", "gy"), 0, 0)
    gradient, wave = results(freqs, nx, ny, freq_sq, sums, state)
    if lax.axis_size("af") == 2:
        gradient = gradient + lax.ppermute(gradient, "af", [(0, 1), (1, 0)])
    else:
        gradient = lax.psum(gradient, "af")
    return wave, gradient


def solution(mesh):
    in_specs = (
        P("gx", "gy", None),
        P("af"),
        P("af", None, "gx", "gy", None),
        P("af", None, "gx", "gy"),
        P("gx", "gy"),
    )
    out_specs = (P("af", None, "gx", "gy", None), P("gx", "gy", None))
    return jax.shard_map(
        on_device, mesh=mesh, in_specs=in_specs, out_specs=out_specs, check_vma=False
    )
```

```python
import functools

import jax
import jax.numpy as jnp
from jax import lax
from jax.experimental import pallas as pl
from jax.experimental.pallas import tpu as pltpu
from jax.sharding import PartitionSpec as P

ITERS = 2
attenuation = 0.2
penalty = 4.0

HALO = 2 * ITERS
INNER = HALO - 1
F32 = jnp.float32
ANY = pl.BlockSpec(memory_space=pl.ANY)
HBM = pl.BlockSpec(memory_space=pltpu.HBM)
VMEM = pl.BlockSpec(memory_space=pltpu.VMEM)
SMEM = pl.BlockSpec(memory_space=pltpu.SMEM)
MIB = 1 << 20
LOAD_MIB = 55
SHIFT = 2


def params(mib):
    return pltpu.CompilerParams(vmem_limit_bytes=mib * MIB)


def cost(us):
    return pl.CostEstimate(
        flops=int(us * 1e3), bytes_accessed=int(us * 1e3), transcendentals=0
    )


def parity(axis):
    return lax.rem(lax.axis_index(axis), 2) == 0


class Copies:
    def __init__(self, sem):
        self.sem, self.all = sem, []

    def add(self, src, dst):
        copy = pltpu.make_async_copy(src, dst, self.sem.at[len(self.all)])
        copy.start()
        self.all.append(copy)

    def wait(self):
        for copy in self.all:
            copy.wait()


def lane_slab(table, fields, skip, rows, nz):
    lane = lax.broadcasted_iota(jnp.int32, (rows, nz), 1)
    lanes = jnp.zeros((rows, nz), F32)
    for k in range(fields + 1):
        inside = (lane >= 8 * k) & (lane < 8 * k + INNER)
        shift = lax.rem(8 * k + nz - skip, nz)
        lanes = jnp.where(inside, pltpu.roll(table[k], shift, axis=1), lanes)
    return lanes


def load_kernel(source, model, observed, depth, *refs):
    freqs, _, nx, ny, nz = source.shape
    fields = 2 * freqs
    s, (cells, aux, xe, xo, ye, yo, seen, sunk, table, slab, sem) = refs[:freqs], refs[freqs:]
    small = Copies(sem.at[0])
    small.add(observed, seen)
    small.add(depth, sunk)
    large = Copies(sem.at[1])
    large.add(model, cells.at[:, pl.ds(0, ny), :])
    for f in range(freqs):
        for p in range(2):
            large.add(source.at[f, p], s[f].at[p, pl.ds(0, nx), pl.ds(0, ny), :])
    even_x, even_y = parity("gx"), parity("gy")
    small.wait()
    for f in range(freqs):
        for p in range(2):
            table[2 * f + p, :, 0:nx] = seen[f, p].T
    table[fields, :, 0:nx] = sunk[...].astype(F32).T
    copies = Copies(sem.at[2])
    copies.add(table, aux.at[:, pl.ds(0, ny), :])
    faces = []
    for side, xb in enumerate((xe, xo)):
        last = even_x if side == 0 else jnp.logical_not(even_x)
        skip = jnp.where(last, nx - INNER, 0)
        faces.append((xb, skip, jnp.where(last, nx - HALO, 0)))
        slab[side] = lane_slab(table, fields, skip, ny, nz)
        copies.add(
            slab.at[pl.ds(side, 1)], xb.at[pl.ds(fields * HALO + INNER, 1)]
        )
    places = []
    for side, yb in enumerate((ye, yo)):
        last = even_y if side == 0 else jnp.logical_not(even_y)
        at = pl.multiple_of(jnp.where(last, ny - HALO, 0), HALO)
        places.append((yb, at))
        copies.add(
            table.at[:, pl.ds(at, HALO), :],
            yb.at[pl.ds((fields + 1) * nx, fields + 1)],
        )
    large.all[0].wait()
    for yb, at in places:
        copies.add(cells.at[:, pl.ds(at, HALO), :], yb.at[pl.ds(fields * nx, nx)])
    for xb, skip, _ in faces:
        copies.add(
            cells.at[pl.ds(skip, INNER), pl.ds(0, ny), :],
            xb.at[pl.ds(fields * HALO, INNER)],
        )
    for k in range(fields):
        large.all[1 + k].wait()
        block = s[k // 2].at[k % 2]
        for yb, at in places:
            copies.add(
                block.at[pl.ds(0, nx), pl.ds(at, HALO), :], yb.at[pl.ds(k * nx, nx)]
            )
        for xb, _, at in faces:
            copies.add(
                block.at[pl.ds(at, HALO), pl.ds(0, ny), :],
                xb.at[pl.ds(k * HALO, HALO)],
            )
    copies.wait()


def load(source, model, observed, depth):
    freqs, _, nx, ny, nz = source.shape
    fields = 2 * freqs
    xs = pltpu.VMEM((fields * HALO + INNER + 1, ny, nz), F32)
    ys = pltpu.VMEM(((fields + 1) * nx + fields + 1, HALO, nz), F32)
    return pl.pallas_call(
        load_kernel,
        out_shape=(pltpu.VMEM((2, nx + 2 * HALO, ny + 2 * HALO, nz), F32),) * freqs
        + (
            pltpu.VMEM((nx, ny + 2 * HALO, nz), F32),
            pltpu.VMEM((fields + 1, ny + 2 * HALO, nz), F32),
            xs,
            xs,
            ys,
            ys,
        ),
        in_specs=[HBM] * 4,
        scratch_shapes=[
            pltpu.VMEM(observed.shape, F32),
            pltpu.VMEM(depth.shape, jnp.int32),
            pltpu.VMEM((fields + 1, ny, nz), F32),
            pltpu.VMEM((2, ny, nz), F32),
            pltpu.SemaphoreType.DMA((3, 32)),
        ],
        compiler_params=params(LOAD_MIB),
        name="load",
    )(source, model, observed, depth)


def halo_places(ny):
    even_y = parity("gy")
    at_e = pl.multiple_of(jnp.where(even_y, ny, ny + HALO), HALO)
    at_o = pl.multiple_of(jnp.where(even_y, ny + HALO, ny), HALO)
    return at_e, at_o


class Grid:
    def __init__(self, nx, ny, nz):
        self.nx, self.ny, self.nz = nx, ny, nz
        self.xe = nx + 2 * HALO
        self.tiles = ny // 8
        self.own = range(self.tiles)
        self.both = range(self.tiles + 1)
        lane = lax.broadcasted_iota(jnp.int32, (8, nz), 1)
        self.first = lane == 0
        self.last = lane == nz - 1
        self.depths = lane.astype(F32)
        sub = lax.broadcasted_iota(jnp.int32, (8, nz), 0)
        self.top = sub == 7
        self.bottom = sub == 0
        has_left = lax.axis_index("gy") > 0
        has_right = lax.axis_index("gy") < lax.axis_size("gy") - 1
        self.left = jnp.where(has_left, 1.0, 0.0)
        self.right = jnp.where(has_right, 1.0, 0.0)

    def tile(self, t):
        if t < self.tiles:
            return pl.ds(t, 8, stride=self.tiles)
        return pl.ds(self.ny, 8)

    def rows(self, ref, p, i, tiles):
        return [ref[p, i, self.tile(t), :] for t in tiles]

    def put(self, ref, p, i, values, tiles):
        for t in tiles:
            ref[p, i, self.tile(t), :] = values[t]

    def beside(self, mid):
        left = jnp.where(self.first, 0.0, pltpu.roll(mid, 1, axis=1))
        right = jnp.where(self.last, 0.0, pltpu.roll(mid, self.nz - 1, axis=1))
        return left + right

    def around(self, mid, below, above, tiles):
        n = self.tiles
        halo = mid[n] if len(mid) > n else None
        first_up = pltpu.roll(mid[0], 7, axis=0)
        last_down = pltpu.roll(mid[n - 1], 1, axis=0)
        if halo is not None:
            halo_up = pltpu.roll(halo, 7, axis=0)
            halo_down = pltpu.roll(halo, 1, axis=0)
        total = {}
        for t in tiles:
            if t == n:
                up = jnp.where(self.top, first_up, halo_up)
                down = jnp.where(self.bottom, last_down, halo_down)
            else:
                up = mid[t + 1] if t + 1 < n else None
                down = mid[t - 1] if t else None
                if up is None:
                    edge = 0.0 if halo is None else halo_up * self.right
                    up = jnp.where(self.top, edge, first_up)
                if down is None:
                    edge = 0.0 if halo is None else halo_down * self.left
                    down = jnp.where(self.bottom, edge, last_down)
            total[t] = ((below[t] + above[t]) + (up + down)) + self.beside(mid[t])
        return total

    def apply(self, src, i, lo, hi, sign, coef, tiles, wide=True, cut=None):
        cr, ci = coef
        mids, totals = [], []
        for p in range(2):
            mid = self.rows(src, p, i, self.both if wide else self.own)
            below = {t: src[p, lo, self.tile(t), :] for t in tiles}
            above = {t: src[p, hi, self.tile(t), :] for t in tiles}
            if cut is not None and cut[0] < 0:
                below = {t: v * cut[1] for t, v in below.items()}
            if cut is not None and cut[0] > 0:
                above = {t: v * cut[1] for t, v in above.items()}
            mids.append(mid)
            totals.append(self.around(mid, below, above, tiles))
        out_re, out_im = {}, {}
        for t in tiles:
            re, im = mids[0][t], mids[1][t]
            if sign > 0:
                out_re[t] = cr[t] * re - ci[t] * im - totals[0][t]
                out_im[t] = cr[t] * im + ci[t] * re - totals[1][t]
            else:
                out_re[t] = cr[t] * re + ci[t] * im - totals[0][t]
                out_im[t] = cr[t] * im - ci[t] * re - totals[1][t]
        return mids, out_re, out_im

    def squares(self, re, im):
        return {t: re[t] * re[t] + im[t] * im[t] for t in self.own}

    def gather(self, values):
        return functools.reduce(jnp.add, [values[t] for t in self.own])

    def zero(self):
        return jnp.zeros((8, self.nz), F32)

    def prepare(self, i, tiles, freq_sq, w, many, cell, column):
        fields = 2 * len(many)
        weight = {}
        for t in tiles:
            depth = column(fields, t)
            weight[t] = jnp.where(self.depths == depth, penalty, 0.0)
            w[i, t] = weight[t]
        out = []
        for f, field in enumerate(many):
            for t in tiles:
                scaled = freq_sq[f] * cell(t)
                field.cr[i, t] = 6.0 - scaled
                field.ci[i, t] = attenuation * scaled
            out.append(
                [
                    {t: weight[t] * column(2 * f + p, t) for t in tiles}
                    for p in range(2)
                ]
            )
        return out

    def pick(self, ref, lead, t, lane):
        at = jnp.full((8, self.nz), lane, jnp.int32)
        return jnp.take_along_axis(ref[lead, self.tile(t), :], at, axis=1)


class Field:
    def __init__(self, grid, refs, w):
        self.grid = grid
        self.s, self.v0, self.u0, self.v1, self.u1, self.cr, self.ci = refs
        self.w = w

    def coef(self, i, tiles):
        return {t: self.cr[i, t] for t in tiles}, {t: self.ci[i, t] for t in tiles}

    def finish(self, i, tiles, wide, lo=None, hi=None, cut=None):
        g = self.grid
        _, re, im = g.apply(self.s, i, lo, hi, -1, self.coef(i, tiles), tiles, wide, cut)
        for p, value in enumerate((re, im)):
            for t in tiles:
                at = g.tile(t)
                self.v0[p, i, at, :] = self.v0[p, i, at, :] + value[t]

    def first_halo(self, i, terms):
        g = self.grid
        n = g.tiles
        coef = self.coef(i, [n])
        _, re, im = g.apply(self.s, i, i - 1, i + 1, -1, coef, [n])
        for p, value in enumerate((re, im)):
            self.v0[p, i, g.tile(n), :] = value[n] + terms[p][n]
            halo = self.s[p, i, g.tile(n), :]
            low = jnp.where(g.bottom, pltpu.roll(halo, 1, axis=0) * g.left, 0.0)
            high = jnp.where(g.top, pltpu.roll(halo, 7, axis=0) * g.right, 0.0)
            for t, change in ((0, low), (n - 1, high)):
                at = g.tile(t)
                self.v0[p, i, at, :] = self.v0[p, i, at, :] - change

    def step(self, stage, i, lo, hi, cut=None, acc=None):
        g = self.grid
        src = (None, self.v0, self.u0, self.v1)[stage]
        dst = (None, self.u0, self.v1, self.u1)[stage]
        tiles = g.own if stage == 3 else g.both
        sign = -1 if stage == 2 else 1
        mids, re, im = g.apply(src, i, lo, hi, sign, self.coef(i, tiles), tiles, True, cut)
        if stage != 3:
            weight = {t: self.w[i, t] for t in tiles}
        if stage == 2:
            for p, out in enumerate((re, im)):
                for t in tiles:
                    out[t] = out[t] + weight[t] * self.v0[p, i, g.tile(t), :]
        g.put(dst, 0, i, re, tiles)
        g.put(dst, 1, i, im, tiles)
        if acc is None:
            return None
        acc = list(acc)
        squares = g.squares(re, im)
        acc[stage] = acc[stage] + g.gather(squares)
        if stage == 1:
            squares = g.squares(*mids)
            acc[0] = acc[0] + g.gather(squares)
        if stage != 3:
            at = 1 if stage == 1 else 3
            weighted = {t: weight[t] * squares[t] for t in g.own}
            acc[at] = acc[at] + g.gather(weighted)
        return tuple(acc)


def early_kernel(freqs, nx, ny, freq_sq, *refs):
    s, (cells, aux), refs = refs[:freqs], refs[freqs : freqs + 2], refs[freqs + 2 :]
    w = refs[3 * freqs]
    nz = cells.shape[2]
    grid = Grid(nx, ny, nz)
    many = [
        Field(grid, (s[f], refs[3 * f], None, None, None, *refs[3 * f + 1 : 3 * f + 3]), w)
        for f in range(freqs)
    ]

    def prepare(i):
        return grid.prepare(
            i,
            grid.own,
            freq_sq,
            w,
            many,
            lambda t: cells[i, grid.tile(t), :],
            lambda k, t: grid.pick(aux, k, t, i),
        )

    for i in (0, nx - 1):
        terms = prepare(i)
        for f in range(freqs):
            for p in range(2):
                grid.put(many[f].v0, p, i, terms[f][p], grid.own)

    def row(i):
        terms = prepare(i)
        for f in range(freqs):
            field = many[f]
            _, re, im = grid.apply(
                field.s, i, i - 1, i + 1, -1, field.coef(i, grid.own), grid.own, False
            )
            for p, value in enumerate((re, im)):
                value = {t: value[t] + terms[f][p][t] for t in grid.own}
                grid.put(field.v0, p, i, value, grid.own)

    def pair(k, _):
        row(2 * k + 1)
        row(2 * k + 2)
        return 0

    lax.fori_loop(0, (nx - 2) // 2, pair, 0)


def early(nx, ny, freq_sq, s, cells, aux):
    freqs = len(s)
    _, xe, _, nz = s[0].shape
    field = pltpu.VMEM(s[0].shape, F32)
    coef = pltpu.VMEM((xe, ny // 8 + 1, 8, nz), F32)
    return pl.pallas_call(
        functools.partial(early_kernel, freqs, nx, ny),
        out_shape=(field, coef, coef) * freqs + (coef,),
        in_specs=[SMEM] + [VMEM] * (freqs + 2),
        compiler_params=params(8),
        name="early",
    )(freq_sq, *s, cells, aux)


def corner_faces(freqs, nx, ny, s, cells, aux, ce, co, slab, sem):
    fields = 2 * freqs
    nz = cells.shape[2]
    even_x = parity("gx")
    out = Copies(sem)
    rows = pl.ds(ny, 2 * HALO)
    for side, cb in enumerate((ce, co)):
        last = even_x if side == 0 else jnp.logical_not(even_x)
        skip = jnp.where(last, nx - INNER, 0)
        at = jnp.where(last, nx - HALO, 0)
        for k in range(fields):
            out.add(
                s[k // 2].at[k % 2, pl.ds(at, HALO), rows, :],
                cb.at[pl.ds(k * HALO, HALO)],
            )
        out.add(cells.at[pl.ds(skip, INNER), rows, :], cb.at[pl.ds(fields * HALO, INNER)])
        near = [aux[k, ny:, :] for k in range(fields + 1)]
        slab[side] = lane_slab(near, fields, skip, 2 * HALO, nz)
        out.add(
            slab.at[pl.ds(side, 1)], cb.at[pl.ds(fields * HALO + INNER, 1)]
        )
    return out


def inner_kernel(freqs, nx, ny, half, freq_sq, *refs):
    if half == 0:
        ye, yo = refs[:2]
        count = 4 * freqs + 3
        refs = refs[2 + count :]
        s, (cells, aux), refs = refs[:freqs], refs[freqs : freqs + 2], refs[freqs + 2 :]
        known, refs = refs[: 3 * freqs + 1], refs[3 * freqs + 1 :]
        news, (moments, ce, co, slab, sem) = refs[: 3 * freqs], refs[3 * freqs :]
    else:
        s, known = refs[:freqs], refs[freqs : 4 * freqs + 1]
        partial = refs[7 * freqs + 1]
        refs = refs[7 * freqs + 2 :]
        news, (moments,) = refs[: 3 * freqs], refs[3 * freqs :]
    nz = s[0].shape[3]
    fields = 2 * freqs
    w = known[3 * freqs]
    grid = Grid(nx, ny, nz)
    many = []
    for f in range(freqs):
        v0, cr, ci = known[3 * f : 3 * f + 3]
        u0, v1, u1 = news[3 * f : 3 * f + 3]
        many.append(Field(grid, (s[f], v0, u0, v1, u1, cr, ci), w))
    if half == 0:
        copies = Copies(sem.at[0])
        for yb, at in zip((ye, yo), halo_places(ny)):
            rows = pl.ds(at, HALO)
            copies.add(
                yb.at[pl.ds((fields + 1) * nx, fields + 1)], aux.at[:, rows, :]
            )
            copies.add(yb.at[pl.ds(fields * nx, nx)], cells.at[:, rows, :])
            for k in range(fields):
                copies.add(
                    yb.at[pl.ds(k * nx, nx)],
                    s[k // 2].at[k % 2, pl.ds(0, nx), rows, :],
                )
        copies.wait()
        out = corner_faces(freqs, nx, ny, s, cells, aux, ce, co, slab, sem.at[1])

    def prepare(i):
        return grid.prepare(
            i,
            [grid.tiles],
            freq_sq,
            w,
            many,
            lambda t: cells[i, grid.tile(t), :],
            lambda k, t: grid.pick(aux, k, t, i),
        )

    if half == 0:
        for i in (0, nx - 1):
            terms = prepare(i)
            for f in range(freqs):
                for p in range(2):
                    grid.put(many[f].v0, p, i, terms[f][p], [grid.tiles])

    def step(j, acc, active):
        acc = list(acc)
        for k in reversed(active):
            i = j - 2 * k
            if k == 0:
                terms = prepare(i)
            for f in range(freqs):
                if k == 0:
                    many[f].first_halo(i, terms[f])
                else:
                    acc[f] = many[f].step(k, i, i - 1, i + 1, acc=acc[f])
        return tuple(acc)

    def heads(i, _):
        terms = prepare(i)
        for f in range(freqs):
            many[f].first_halo(i, terms[f])
        return 0

    spans = [(1 + 3 * k, nx - 1 + k) for k in range(4)]
    middle = nx // 2 + SHIFT
    edges = sorted({e for span in spans for e in span} | {middle})
    acc = tuple(tuple(grid.zero() for _ in range(4)) for _ in range(freqs))
    if half == 0:
        lax.fori_loop(1, nx - 1, heads, 0, unroll=3)
    for lo, hi in zip(edges[:-1], edges[1:]):
        if (lo < middle) != (half == 0):
            continue
        active = [k for k, (a, b) in enumerate(spans) if k and a <= lo and hi <= b]
        if active:
            acc = lax.fori_loop(lo, hi, functools.partial(step, active=active), acc)
    for f in range(freqs):
        for m in range(4):
            value = acc[f][m]
            moments[f, m] = value if half == 0 else value + partial[f, m]
    if half == 0:
        out.wait()


def inner_part(nx, ny, freq_sq, ye, yo, s, cells, aux, known):
    freqs = len(s)
    nz = cells.shape[2]
    slabs = 2 * freqs * HALO + INNER + 1
    field = pltpu.VMEM(s[0].shape, F32)
    corner = pltpu.VMEM((slabs, 2 * HALO, nz), F32)
    kept = (*s, cells, aux, *known)
    news = (field,) * (3 * freqs) + (pltpu.VMEM((freqs, 4, 8, nz), F32),)
    got = pl.pallas_call(
        functools.partial(inner_kernel, freqs, nx, ny, 0),
        out_shape=tuple(pltpu.VMEM(k.shape, F32) for k in kept)
        + news
        + (corner, corner),
        in_specs=[SMEM, ANY, ANY] + [VMEM] * len(kept),
        input_output_aliases={3 + k: k for k in range(len(kept))},
        scratch_shapes=[
            pltpu.VMEM((2, 2 * HALO, nz), F32),
            pltpu.SemaphoreType.DMA((2, 16)),
        ],
        compiler_params=params(8),
        name="inner_first",
    )(freq_sq, ye, yo, *kept)
    s, known = got[:freqs], got[freqs + 2 : len(kept)]
    news_got, (ce, co) = got[len(kept) : -2], got[-2:]

    def rest():
        first = 1 + freqs + len(known)
        again = pl.pallas_call(
            functools.partial(inner_kernel, freqs, nx, ny, 1),
            out_shape=news,
            in_specs=[SMEM] + [VMEM] * (freqs + len(known) + len(news)),
            input_output_aliases={first + k: k for k in range(len(news))},
            compiler_params=params(8),
            name="inner_second",
        )(freq_sq, *s, *known, *news_got)
        state = []
        for f in range(freqs):
            v0, cr, ci = known[3 * f : 3 * f + 3]
            state += [s[f], v0, *again[3 * f : 3 * f + 3], cr, ci]
        return state + [known[-1]], again[-1]

    return ce, co, rest


def edge_kernel(peers, freqs, nx, ny, freq_sq, xe, xo, ce, co, *refs):
    count = 7 * freqs + 1
    moments, refs = refs[count], refs[count + 1 :]
    state, (part, cells, aux, sem) = refs[:count], refs[count:]
    fields = 2 * freqs
    nz = state[0].shape[3]
    w = state[-1]
    copies = Copies(sem)
    even_x = parity("gx")
    pieces = (
        (xe, 0, 0, ny),
        (xo, 1, 0, ny),
        (ce, 0, ny, 2 * HALO),
        (co, 1, ny, 2 * HALO),
    )
    for block, side, at, size in pieces:
        above = even_x if side == 0 else jnp.logical_not(even_x)
        slot = jnp.where(above, nx, nx + HALO)
        half = jnp.where(above, 0, 1)
        rows = pl.ds(at, size)
        for k in range(fields):
            copies.add(
                block.at[pl.ds(k * HALO, HALO)],
                state[7 * (k // 2)].at[k % 2, pl.ds(slot, HALO), rows, :],
            )
        copies.add(
            block.at[pl.ds(fields * HALO, INNER)], cells.at[half, :, rows, :]
        )
        copies.add(
            block.at[pl.ds(fields * HALO + INNER, 1)],
            aux.at[pl.ds(half, 1), rows, :],
        )
    grid = Grid(nx, ny, nz)
    copies.wait()
    many = [Field(grid, state[7 * f : 7 * f + 7], w) for f in range(freqs)]
    for half in range(2):
        for layer in range(INNER):
            i = nx + layer if half == 0 else nx + HALO + 1 + layer
            terms = grid.prepare(
                i,
                grid.both,
                freq_sq,
                w,
                many,
                lambda t: cells[half, layer, grid.tile(t), :],
                lambda k, t: grid.pick(aux, half, t, 8 * k + layer),
            )
            for f in range(freqs):
                for p in range(2):
                    grid.put(many[f].v0, p, i, terms[f][p], grid.both)

    left = jnp.where(lax.axis_index("gx") > 0, 1.0, 0.0)
    right = jnp.where(lax.axis_index("gx") < lax.axis_size("gx") - 1, 1.0, 0.0)
    wrap = grid.xe
    acc = [tuple(grid.zero() for _ in range(4)) for _ in range(freqs)]
    for stage in range(4):
        for k in range(HALO):
            for x in (k - INNER + stage, nx - 1 - stage + k):
                i, lo, hi = x % wrap, (x - 1) % wrap, (x + 1) % wrap
                own = 0 <= x < nx
                cut = None
                if x == 0:
                    cut = (-1, left)
                if x == nx - 1:
                    cut = (1, right)
                for f in range(freqs):
                    if stage == 0:
                        many[f].finish(i, grid.both, True, lo, hi, cut)
                        continue
                    got = many[f].step(
                        stage, i, lo, hi, cut, acc[f] if own else None
                    )
                    if own:
                        acc[f] = got

    rows = []
    for f in range(freqs):
        for m in range(4):
            both = acc[f][m] + moments[f, m]
            rows.append(jnp.sum(both, axis=0, keepdims=True))
    sums = jnp.sum(jnp.concatenate(rows, axis=0), axis=1, keepdims=True)
    sums = jnp.broadcast_to(sums, (4 * freqs, nz))
    for peer in range(peers):
        part[peer] = sums


def edge_part(peers, freqs, nx, ny, freq_sq, xe, xo, ce, co, state, moments):
    nz = state[0].shape[3]
    outs = tuple(pltpu.VMEM(k.shape, F32) for k in state)
    return pl.pallas_call(
        functools.partial(edge_kernel, peers, freqs, nx, ny),
        out_shape=outs + (jax.ShapeDtypeStruct((peers, 4 * freqs, nz), F32),),
        in_specs=[SMEM] + [ANY] * 4 + [VMEM] * (len(state) + 1),
        input_output_aliases={5 + k: k for k in range(len(state))},
        scratch_shapes=[
            pltpu.VMEM((2, INNER, ny + 2 * HALO, nz), F32),
            pltpu.VMEM((2, ny + 2 * HALO, nz), F32),
            pltpu.SemaphoreType.DMA((64,)),
        ],
        compiler_params=params(8),
        name="edge_part",
    )(freq_sq, xe, xo, ce, co, *state, moments)


def steps(sums, freqs):
    total = jnp.sum(sums[...], axis=0)
    shape = (8, total.shape[1])
    out = []
    for f in range(freqs):
        m0, m1, m2, m3 = (
            jnp.broadcast_to(total[4 * f + k : 4 * f + k + 1, :], shape)
            for k in range(4)
        )
        first = m0 / m1
        new = first * (first * m2 - m1)
        product = m1 - first * (2.0 * m2 - first * m3)
        ratio = new / m0
        second = new / (product - ratio * new / first)
        out.append((first + second * (1.0 + ratio), -first * second))
    return out


def gradient_kernel(freqs, nx, ny, freq_sq, sums, *refs):
    out = refs[-1]
    weights = steps(sums, freqs)

    def row(x, _):
        for y in range(0, ny, 8):
            at = pl.ds(y, 8)
            total = None
            for f in range(freqs):
                s, v0, u0, v1, u1 = refs[5 * f : 5 * f + 5]
                a, b = weights[f]
                wave_re = a * v0[0, x, at, :] + b * v1[0, x, at, :]
                wave_im = a * v0[1, x, at, :] + b * v1[1, x, at, :]
                miss_re = a * u0[0, x, at, :] + b * u1[0, x, at, :]
                miss_im = a * u0[1, x, at, :] + b * u1[1, x, at, :]
                miss_re = miss_re - s[0, x, at, :]
                miss_im = miss_im - s[1, x, at, :]
                left = (wave_re + attenuation * wave_im) * miss_re
                right = (wave_im - attenuation * wave_re) * miss_im
                term = -freq_sq[f] * (left + right)
                total = term if total is None else total + term
            out[x, at, :] = total
        return 0

    lax.fori_loop(0, nx, row, 0)


def wave_kernel(freqs, nx, ny, sums, *refs):
    out, block, sem = refs[2 * freqs :]
    weights = steps(sums, freqs)
    copies = Copies(sem)
    for f in range(freqs):
        a, b = weights[f]
        v0, v1 = refs[2 * f : 2 * f + 2]
        for p in range(2):
            k = 2 * f + p

            def row(x, _):
                for y in range(0, ny, 8):
                    at = pl.ds(y, 8)
                    block[k, x, at, :] = a * v0[p, x, at, :] + b * v1[p, x, at, :]
                return 0

            lax.fori_loop(0, nx, row, 0)
            copies.add(block.at[k], out.at[f, p])
    copies.wait()


def results(freqs, nx, ny, freq_sq, sums, state):
    nz = state[0].shape[3]
    fields, pairs = [], []
    for f in range(freqs):
        s, v0, u0, v1, u1 = state[7 * f : 7 * f + 5]
        fields += [s, v0, u0, v1, u1]
        pairs += [v0, v1]
    gradient = pl.pallas_call(
        functools.partial(gradient_kernel, freqs, nx, ny),
        out_shape=jax.ShapeDtypeStruct((nx, ny, nz), F32),
        in_specs=[SMEM] + [VMEM] * (1 + len(fields)),
        out_specs=VMEM,
        compiler_params=params(8),
        name="gradient_part",
    )(freq_sq, sums, *fields)
    wave = pl.pallas_call(
        functools.partial(wave_kernel, freqs, nx, ny),
        out_shape=jax.ShapeDtypeStruct((freqs, 2, nx, ny, nz), F32),
        in_specs=[VMEM] * (1 + len(pairs)),
        out_specs=HBM,
        scratch_shapes=[
            pltpu.VMEM((2 * freqs, nx, ny, nz), F32),
            pltpu.SemaphoreType.DMA((2 * freqs,)),
        ],
        compiler_params=params(8),
        name="wavefield",
    )(sums, *pairs)
    return gradient, wave


def swap(cells, axis, odd):
    names = ("gx", "gy", "af")
    sizes = [lax.axis_size(name) for name in names]
    along = names.index(axis)
    pairs = []
    for flat in range(sizes[0] * sizes[1] * sizes[2]):
        place = [flat // (sizes[1] * sizes[2]), flat // sizes[2] % sizes[1], flat % sizes[2]]
        mate = ((place[along] + odd) ^ 1) - odd
        if 0 <= mate < sizes[along]:
            place[along] = mate
        elif sizes[2] % 2 == 0:
            place[2] ^= 1
        else:
            continue
        pairs.append((flat, (place[0] * sizes[1] + place[1]) * sizes[2] + place[2]))
    return lax.ppermute(cells, names, pairs)


def on_device(model, freq_sq, source, observed, receiver_depth):
    nx, ny, nz = model.shape
    freqs = freq_sq.shape[0]
    *s, cells, aux, xe, xo, ye, yo = load(source, model, observed, receiver_depth)
    ye, yo = swap(ye, "gy", 0), swap(yo, "gy", 1)
    xe, xo = swap(xe, "gx", 0), swap(xo, "gx", 1)
    known = early(nx, ny, freq_sq, s, cells, aux)
    ce, co, rest = inner_part(nx, ny, freq_sq, ye, yo, s, cells, aux, known)
    ce, co = swap(ce, "gx", 0), swap(co, "gx", 1)
    state, moments = rest()
    peers = lax.axis_size("gx") * lax.axis_size("gy")
    *state, part = edge_part(
        peers, freqs, nx, ny, freq_sq, xe, xo, ce, co, state, moments
    )
    sums = lax.all_to_all(part, ("gx", "gy"), 0, 0)
    gradient, wave = results(freqs, nx, ny, freq_sq, sums, state)
    if lax.axis_size("af") == 2:
        gradient = gradient + lax.ppermute(gradient, "af", [(0, 1), (1, 0)])
    else:
        gradient = lax.psum(gradient, "af")
    return wave, gradient


def solution(mesh):
    in_specs = (
        P("gx", "gy", None),
        P("af"),
        P("af", None, "gx", "gy", None),
        P("af", None, "gx", "gy"),
        P("gx", "gy"),
    )
    out_specs = (P("af", None, "gx", "gy", None), P("gx", "gy", None))
    return jax.shard_map(
        on_device, mesh=mesh, in_specs=in_specs, out_specs=out_specs, check_vma=False
    )
```

```python
import functools

import jax
import jax.numpy as jnp
from jax import lax
from jax.experimental import pallas as pl
from jax.experimental.pallas import tpu as pltpu
from jax.sharding import PartitionSpec as P

ITERS = 2
attenuation = 0.2
penalty = 4.0

HALO = 2 * ITERS
INNER = HALO - 1
F32 = jnp.float32
ANY = pl.BlockSpec(memory_space=pl.ANY)
HBM = pl.BlockSpec(memory_space=pltpu.HBM)
VMEM = pl.BlockSpec(memory_space=pltpu.VMEM)
SMEM = pl.BlockSpec(memory_space=pltpu.SMEM)
MIB = 1 << 20
LOAD_MIB = 55
SHIFT = 2


def params(mib):
    return pltpu.CompilerParams(vmem_limit_bytes=mib * MIB)


def cost(us):
    return pl.CostEstimate(
        flops=int(us * 1e3), bytes_accessed=int(us * 1e3), transcendentals=0
    )


def parity(axis):
    return lax.rem(lax.axis_index(axis), 2) == 0


class Copies:
    def __init__(self, sem):
        self.sem, self.all = sem, []

    def add(self, src, dst):
        copy = pltpu.make_async_copy(src, dst, self.sem.at[len(self.all)])
        copy.start()
        self.all.append(copy)

    def wait(self):
        for copy in self.all:
            copy.wait()


def lane_slab(table, fields, skip, rows, nz):
    lane = lax.broadcasted_iota(jnp.int32, (rows, nz), 1)
    lanes = jnp.zeros((rows, nz), F32)
    for k in range(fields + 1):
        inside = (lane >= 8 * k) & (lane < 8 * k + INNER)
        shift = lax.rem(8 * k + nz - skip, nz)
        lanes = jnp.where(inside, pltpu.roll(table[k], shift, axis=1), lanes)
    return lanes


def load_kernel(source, model, observed, depth, *refs):
    freqs, _, nx, ny, nz = source.shape
    fields = 2 * freqs
    s, (cells, aux, xe, xo, ye, yo, seen, sunk, table, slab, sem) = refs[:freqs], refs[freqs:]
    small = Copies(sem.at[0])
    small.add(observed, seen)
    small.add(depth, sunk)
    large = Copies(sem.at[1])
    large.add(model, cells.at[:, pl.ds(0, ny), :])
    for f in range(freqs):
        for p in range(2):
            large.add(source.at[f, p], s[f].at[p, pl.ds(0, nx), pl.ds(0, ny), :])
    even_x, even_y = parity("gx"), parity("gy")
    small.wait()
    for f in range(freqs):
        for p in range(2):
            table[2 * f + p, :, 0:nx] = seen[f, p].T
    table[fields, :, 0:nx] = sunk[...].astype(F32).T
    copies = Copies(sem.at[2])
    copies.add(table, aux.at[:, pl.ds(0, ny), :])
    faces = []
    for side, xb in enumerate((xe, xo)):
        last = even_x if side == 0 else jnp.logical_not(even_x)
        skip = jnp.where(last, nx - INNER, 0)
        faces.append((xb, skip, jnp.where(last, nx - HALO, 0)))
        slab[side] = lane_slab(table, fields, skip, ny, nz)
        copies.add(
            slab.at[pl.ds(side, 1)], xb.at[pl.ds(fields * HALO + INNER, 1)]
        )
    swapped = jnp.broadcast_to(even_y, (HALO, nz))

    def y_faces(block, at):
        def row(x, _):
            head, tail = block[x, 0:HALO, :], block[x, ny - HALO : ny, :]
            ye[at + x] = jnp.where(swapped, tail, head)
            yo[at + x] = jnp.where(swapped, head, tail)
            return 0

        lax.fori_loop(0, nx, row, 0, unroll=8)

    def x_face(xb, to, block, at, layers):
        for layer in range(layers):
            for y in range(0, ny, 8):
                xb[to + layer, y : y + 8, :] = block[at + layer, y : y + 8, :]

    for k in range(fields + 1):
        head, tail = table[k, 0:HALO, :], table[k, ny - HALO : ny, :]
        ye[(fields + 1) * nx + k] = jnp.where(swapped, tail, head)
        yo[(fields + 1) * nx + k] = jnp.where(swapped, head, tail)
    large.all[0].wait()
    y_faces(cells, fields * nx)
    for xb, skip, _ in faces:
        x_face(xb, fields * HALO, cells, skip, INNER)
    for k in range(fields):
        large.all[1 + k].wait()
        block = s[k // 2].at[k % 2]
        y_faces(block, k * nx)
        for xb, _, at in faces:
            x_face(xb, k * HALO, block, at, HALO)
    copies.wait()


def load(source, model, observed, depth):
    freqs, _, nx, ny, nz = source.shape
    fields = 2 * freqs
    xs = pltpu.VMEM((fields * HALO + INNER + 1, ny, nz), F32)
    ys = pltpu.VMEM(((fields + 1) * nx + fields + 1, HALO, nz), F32)
    return pl.pallas_call(
        load_kernel,
        out_shape=(pltpu.VMEM((2, nx + 2 * HALO, ny + 2 * HALO, nz), F32),) * freqs
        + (
            pltpu.VMEM((nx, ny + 2 * HALO, nz), F32),
            pltpu.VMEM((fields + 1, ny + 2 * HALO, nz), F32),
            xs,
            xs,
            ys,
            ys,
        ),
        in_specs=[HBM] * 4,
        scratch_shapes=[
            pltpu.VMEM(observed.shape, F32),
            pltpu.VMEM(depth.shape, jnp.int32),
            pltpu.VMEM((fields + 1, ny, nz), F32),
            pltpu.VMEM((2, ny, nz), F32),
            pltpu.SemaphoreType.DMA((3, 32)),
        ],
        compiler_params=params(LOAD_MIB),
        name="load",
    )(source, model, observed, depth)


class Grid:
    def __init__(self, nx, ny, nz):
        self.nx, self.ny, self.nz = nx, ny, nz
        self.xe = nx + 2 * HALO
        self.tiles = ny // 8
        self.own = range(self.tiles)
        self.both = range(self.tiles + 1)
        lane = lax.broadcasted_iota(jnp.int32, (8, nz), 1)
        self.first = lane == 0
        self.last = lane == nz - 1
        self.depths = lane.astype(F32)
        sub = lax.broadcasted_iota(jnp.int32, (8, nz), 0)
        self.top = sub == 7
        self.bottom = sub == 0
        has_left = lax.axis_index("gy") > 0
        has_right = lax.axis_index("gy") < lax.axis_size("gy") - 1
        self.left = jnp.where(has_left, 1.0, 0.0)
        self.right = jnp.where(has_right, 1.0, 0.0)
        self.inside = jnp.where(sub < HALO, self.right, self.left)

    def tile(self, t):
        if t < self.tiles:
            return pl.ds(t, 8, stride=self.tiles)
        return pl.ds(self.ny, 8)

    def rows(self, ref, p, i, tiles):
        return [ref[p, i, self.tile(t), :] for t in tiles]

    def put(self, ref, p, i, values, tiles):
        for t in tiles:
            ref[p, i, self.tile(t), :] = values[t]

    def beside(self, mid):
        left = jnp.where(self.first, 0.0, pltpu.roll(mid, 1, axis=1))
        right = jnp.where(self.last, 0.0, pltpu.roll(mid, self.nz - 1, axis=1))
        return left + right

    def around(self, mid, below, above, tiles):
        n = self.tiles
        halo = mid[n] if len(mid) > n else None
        first_up = pltpu.roll(mid[0], 7, axis=0)
        last_down = pltpu.roll(mid[n - 1], 1, axis=0)
        if halo is not None:
            halo_up = pltpu.roll(halo, 7, axis=0)
            halo_down = pltpu.roll(halo, 1, axis=0)
        total = {}
        for t in tiles:
            if t == n:
                up = jnp.where(self.top, first_up, halo_up)
                down = jnp.where(self.bottom, last_down, halo_down)
            else:
                up = mid[t + 1] if t + 1 < n else None
                down = mid[t - 1] if t else None
                if up is None:
                    edge = 0.0 if halo is None else halo_up
                    up = jnp.where(self.top, edge, first_up)
                if down is None:
                    edge = 0.0 if halo is None else halo_down
                    down = jnp.where(self.bottom, edge, last_down)
            total[t] = ((below[t] + above[t]) + (up + down)) + self.beside(mid[t])
        return total

    def apply(self, src, i, lo, hi, sign, coef, tiles, wide=True, cut=None):
        cr, ci = coef
        mids, totals = [], []
        for p in range(2):
            mid = self.rows(src, p, i, self.both if wide else self.own)
            below = {t: src[p, lo, self.tile(t), :] for t in tiles}
            above = {t: src[p, hi, self.tile(t), :] for t in tiles}
            if cut is not None and cut[0] < 0:
                below = {t: v * cut[1] for t, v in below.items()}
            if cut is not None and cut[0] > 0:
                above = {t: v * cut[1] for t, v in above.items()}
            mids.append(mid)
            totals.append(self.around(mid, below, above, tiles))
        out_re, out_im = {}, {}
        for t in tiles:
            re, im = mids[0][t], mids[1][t]
            if sign > 0:
                out_re[t] = cr[t] * re - ci[t] * im - totals[0][t]
                out_im[t] = cr[t] * im + ci[t] * re - totals[1][t]
            else:
                out_re[t] = cr[t] * re + ci[t] * im - totals[0][t]
                out_im[t] = cr[t] * im - ci[t] * re - totals[1][t]
        return mids, out_re, out_im

    def squares(self, re, im):
        return {t: re[t] * re[t] + im[t] * im[t] for t in self.own}

    def gather(self, values):
        return functools.reduce(jnp.add, [values[t] for t in self.own])

    def zero(self):
        return jnp.zeros((8, self.nz), F32)

    def prepare(self, i, tiles, freq_sq, w, many, cell, column):
        fields = 2 * len(many)
        weight = {}
        for t in tiles:
            depth = column(fields, t)
            weight[t] = jnp.where(self.depths == depth, penalty, 0.0)
            w[i, t] = weight[t]
        out = []
        for f, field in enumerate(many):
            for t in tiles:
                scaled = freq_sq[f] * cell(t)
                field.cr[i, t] = 6.0 - scaled
                field.ci[i, t] = attenuation * scaled
            out.append(
                [
                    {t: weight[t] * column(2 * f + p, t) for t in tiles}
                    for p in range(2)
                ]
            )
        return out

    def pick(self, ref, lead, t, lane):
        at = jnp.full((8, self.nz), lane, jnp.int32)
        return jnp.take_along_axis(ref[lead, self.tile(t), :], at, axis=1)


class Field:
    def __init__(self, grid, refs, w):
        self.grid = grid
        self.s, self.v0, self.u0, self.v1, self.u1, self.cr, self.ci = refs
        self.w = w

    def coef(self, i, tiles):
        return {t: self.cr[i, t] for t in tiles}, {t: self.ci[i, t] for t in tiles}

    def finish(self, i, tiles, wide, lo=None, hi=None, cut=None):
        g = self.grid
        _, re, im = g.apply(self.s, i, lo, hi, -1, self.coef(i, tiles), tiles, wide, cut)
        for p, value in enumerate((re, im)):
            for t in tiles:
                at = g.tile(t)
                total = self.v0[p, i, at, :] + value[t]
                self.v0[p, i, at, :] = total * g.inside if t == g.tiles else total

    def first_halo(self, i, terms):
        g = self.grid
        n = g.tiles
        coef = self.coef(i, [n])
        _, re, im = g.apply(self.s, i, i - 1, i + 1, -1, coef, [n])
        for p, value in enumerate((re, im)):
            self.v0[p, i, g.tile(n), :] = (value[n] + terms[p][n]) * g.inside
            halo = self.s[p, i, g.tile(n), :]
            low = jnp.where(g.bottom, pltpu.roll(halo, 1, axis=0), 0.0)
            high = jnp.where(g.top, pltpu.roll(halo, 7, axis=0), 0.0)
            for t, change in ((0, low), (n - 1, high)):
                at = g.tile(t)
                self.v0[p, i, at, :] = self.v0[p, i, at, :] - change

    def step(self, stage, i, lo, hi, cut=None, acc=None):
        g = self.grid
        src = (None, self.v0, self.u0, self.v1)[stage]
        dst = (None, self.u0, self.v1, self.u1)[stage]
        tiles = g.own if stage == 3 else g.both
        sign = -1 if stage == 2 else 1
        mids, re, im = g.apply(src, i, lo, hi, sign, self.coef(i, tiles), tiles, True, cut)
        if stage != 3:
            weight = {t: self.w[i, t] for t in tiles}
        if stage == 2:
            for p, out in enumerate((re, im)):
                for t in tiles:
                    out[t] = out[t] + weight[t] * self.v0[p, i, g.tile(t), :]
        if stage != 3:
            re[g.tiles] = re[g.tiles] * g.inside
            im[g.tiles] = im[g.tiles] * g.inside
        g.put(dst, 0, i, re, tiles)
        g.put(dst, 1, i, im, tiles)
        if acc is None:
            return None
        acc = list(acc)
        squares = g.squares(re, im)
        acc[stage] = acc[stage] + g.gather(squares)
        if stage == 1:
            squares = g.squares(*mids)
            acc[0] = acc[0] + g.gather(squares)
        if stage != 3:
            at = 1 if stage == 1 else 3
            weighted = {t: weight[t] * squares[t] for t in g.own}
            acc[at] = acc[at] + g.gather(weighted)
        return tuple(acc)


def early_kernel(freqs, nx, ny, freq_sq, *refs):
    s, (cells, aux), refs = refs[:freqs], refs[freqs : freqs + 2], refs[freqs + 2 :]
    w = refs[3 * freqs]
    nz = cells.shape[2]
    grid = Grid(nx, ny, nz)
    many = [
        Field(grid, (s[f], refs[3 * f], None, None, None, *refs[3 * f + 1 : 3 * f + 3]), w)
        for f in range(freqs)
    ]

    def prepare(i):
        return grid.prepare(
            i,
            grid.own,
            freq_sq,
            w,
            many,
            lambda t: cells[i, grid.tile(t), :],
            lambda k, t: grid.pick(aux, k, t, i),
        )

    for i in (0, nx - 1):
        terms = prepare(i)
        for f in range(freqs):
            for p in range(2):
                grid.put(many[f].v0, p, i, terms[f][p], grid.own)

    def row(i):
        terms = prepare(i)
        for f in range(freqs):
            field = many[f]
            _, re, im = grid.apply(
                field.s, i, i - 1, i + 1, -1, field.coef(i, grid.own), grid.own, False
            )
            for p, value in enumerate((re, im)):
                value = {t: value[t] + terms[f][p][t] for t in grid.own}
                grid.put(field.v0, p, i, value, grid.own)

    def pair(k, _):
        row(2 * k + 1)
        row(2 * k + 2)
        return 0

    lax.fori_loop(0, (nx - 2) // 2, pair, 0)


def early(nx, ny, freq_sq, s, cells, aux):
    freqs = len(s)
    _, xe, _, nz = s[0].shape
    field = pltpu.VMEM(s[0].shape, F32)
    coef = pltpu.VMEM((xe, ny // 8 + 1, 8, nz), F32)
    return pl.pallas_call(
        functools.partial(early_kernel, freqs, nx, ny),
        out_shape=(field, coef, coef) * freqs + (coef,),
        in_specs=[SMEM] + [VMEM] * (freqs + 2),
        compiler_params=params(8),
        name="early",
    )(freq_sq, *s, cells, aux)


def corner_faces(freqs, nx, ny, s, cells, aux, ce, co, slab, sem):
    fields = 2 * freqs
    nz = cells.shape[2]
    even_x = parity("gx")
    out = Copies(sem)
    rows = pl.ds(ny, 2 * HALO)
    for side, cb in enumerate((ce, co)):
        last = even_x if side == 0 else jnp.logical_not(even_x)
        skip = jnp.where(last, nx - INNER, 0)
        at = jnp.where(last, nx - HALO, 0)
        for k in range(fields):
            out.add(
                s[k // 2].at[k % 2, pl.ds(at, HALO), rows, :],
                cb.at[pl.ds(k * HALO, HALO)],
            )
        out.add(cells.at[pl.ds(skip, INNER), rows, :], cb.at[pl.ds(fields * HALO, INNER)])
        near = [aux[k, ny:, :] for k in range(fields + 1)]
        slab[side] = lane_slab(near, fields, skip, 2 * HALO, nz)
        out.add(
            slab.at[pl.ds(side, 1)], cb.at[pl.ds(fields * HALO + INNER, 1)]
        )
    return out


def inner_kernel(freqs, nx, ny, half, freq_sq, *refs):
    if half == 0:
        ye, yo = refs[:2]
        count = 4 * freqs + 3
        refs = refs[2 + count :]
        s, (cells, aux), refs = refs[:freqs], refs[freqs : freqs + 2], refs[freqs + 2 :]
        known, refs = refs[: 3 * freqs + 1], refs[3 * freqs + 1 :]
        news, (moments, ce, co, slab, sem) = refs[: 3 * freqs], refs[3 * freqs :]
    else:
        s, known = refs[:freqs], refs[freqs : 4 * freqs + 1]
        partial = refs[7 * freqs + 1]
        refs = refs[7 * freqs + 2 :]
        news, (moments,) = refs[: 3 * freqs], refs[3 * freqs :]
    nz = s[0].shape[3]
    fields = 2 * freqs
    w = known[3 * freqs]
    grid = Grid(nx, ny, nz)
    many = []
    for f in range(freqs):
        v0, cr, ci = known[3 * f : 3 * f + 3]
        u0, v1, u1 = news[3 * f : 3 * f + 3]
        many.append(Field(grid, (s[f], v0, u0, v1, u1, cr, ci), w))
    if half == 0:
        swapped = jnp.broadcast_to(parity("gy"), (HALO, nz))

        def halo(at):
            even, odd = ye[at], yo[at]
            high = jnp.where(swapped, even, odd) * grid.right
            low = jnp.where(swapped, odd, even) * grid.left
            return jnp.concatenate([high, low], axis=0)

        def merge(x, _):
            cells[x, ny:, :] = halo(fields * nx + x)
            for k in range(fields):
                s[k // 2][k % 2, x, ny:, :] = halo(k * nx + x)
            return 0

        lax.fori_loop(0, nx, merge, 0, unroll=4)
        for k in range(fields + 1):
            aux[k, ny:, :] = halo((fields + 1) * nx + k)
        out = corner_faces(freqs, nx, ny, s, cells, aux, ce, co, slab, sem)

    def prepare(i):
        return grid.prepare(
            i,
            [grid.tiles],
            freq_sq,
            w,
            many,
            lambda t: cells[i, grid.tile(t), :],
            lambda k, t: grid.pick(aux, k, t, i),
        )

    if half == 0:
        for i in (0, nx - 1):
            terms = prepare(i)
            for f in range(freqs):
                for p in range(2):
                    grid.put(many[f].v0, p, i, terms[f][p], [grid.tiles])

    def step(j, acc, active):
        acc = list(acc)
        for k in reversed(active):
            i = j - 2 * k
            if k == 0:
                terms = prepare(i)
            for f in range(freqs):
                if k == 0:
                    many[f].first_halo(i, terms[f])
                else:
                    acc[f] = many[f].step(k, i, i - 1, i + 1, acc=acc[f])
        return tuple(acc)

    def heads(i, _):
        terms = prepare(i)
        for f in range(freqs):
            many[f].first_halo(i, terms[f])
        return 0

    spans = [(1 + 3 * k, nx - 1 + k) for k in range(4)]
    middle = nx // 2 + SHIFT
    edges = sorted({e for span in spans for e in span} | {middle})
    acc = tuple(tuple(grid.zero() for _ in range(4)) for _ in range(freqs))
    if half == 0:
        lax.fori_loop(1, nx - 1, heads, 0, unroll=3)
    for lo, hi in zip(edges[:-1], edges[1:]):
        if (lo < middle) != (half == 0):
            continue
        active = [k for k, (a, b) in enumerate(spans) if k and a <= lo and hi <= b]
        if active:
            acc = lax.fori_loop(lo, hi, functools.partial(step, active=active), acc)
    for f in range(freqs):
        for m in range(4):
            value = acc[f][m]
            moments[f, m] = value if half == 0 else value + partial[f, m]
    if half == 0:
        out.wait()


def inner_part(nx, ny, freq_sq, ye, yo, s, cells, aux, known):
    freqs = len(s)
    nz = cells.shape[2]
    slabs = 2 * freqs * HALO + INNER + 1
    field = pltpu.VMEM(s[0].shape, F32)
    corner = pltpu.VMEM((slabs, 2 * HALO, nz), F32)
    kept = (*s, cells, aux, *known)
    news = (field,) * (3 * freqs) + (pltpu.VMEM((freqs, 4, 8, nz), F32),)
    got = pl.pallas_call(
        functools.partial(inner_kernel, freqs, nx, ny, 0),
        out_shape=tuple(pltpu.VMEM(k.shape, F32) for k in kept)
        + news
        + (corner, corner),
        in_specs=[SMEM, VMEM, VMEM] + [VMEM] * len(kept),
        input_output_aliases={3 + k: k for k in range(len(kept))},
        scratch_shapes=[
            pltpu.VMEM((2, 2 * HALO, nz), F32),
            pltpu.SemaphoreType.DMA((16,)),
        ],
        compiler_params=params(8),
        name="inner_first",
    )(freq_sq, ye, yo, *kept)
    s, known = got[:freqs], got[freqs + 2 : len(kept)]
    news_got, (ce, co) = got[len(kept) : -2], got[-2:]

    def rest():
        first = 1 + freqs + len(known)
        again = pl.pallas_call(
            functools.partial(inner_kernel, freqs, nx, ny, 1),
            out_shape=news,
            in_specs=[SMEM] + [VMEM] * (freqs + len(known) + len(news)),
            input_output_aliases={first + k: k for k in range(len(news))},
            compiler_params=params(8),
            name="inner_second",
        )(freq_sq, *s, *known, *news_got)
        state = []
        for f in range(freqs):
            v0, cr, ci = known[3 * f : 3 * f + 3]
            state += [s[f], v0, *again[3 * f : 3 * f + 3], cr, ci]
        return state + [known[-1]], again[-1]

    return ce, co, rest


def edge_kernel(peers, freqs, nx, ny, freq_sq, xe, xo, ce, co, *refs):
    count = 7 * freqs + 1
    moments, refs = refs[count], refs[count + 1 :]
    state, (part, cells, aux) = refs[:count], refs[count:]
    fields = 2 * freqs
    nz = state[0].shape[3]
    w = state[-1]
    even_x = parity("gx")
    pieces = (
        (xe, 0, 0, ny),
        (xo, 1, 0, ny),
        (ce, 0, ny, 2 * HALO),
        (co, 1, ny, 2 * HALO),
    )
    for block, side, at, size in pieces:
        above = even_x if side == 0 else jnp.logical_not(even_x)
        slot = jnp.where(above, nx, nx + HALO)
        half = jnp.where(above, 0, 1)
        for y in range(0, size, 8):
            here, there = pl.ds(y, 8), pl.ds(at + y, 8)
            for k in range(fields):
                for layer in range(HALO):
                    state[7 * (k // 2)][k % 2, slot + layer, there, :] = block[
                        k * HALO + layer, here, :
                    ]
            for layer in range(INNER):
                cells[half, layer, there, :] = block[fields * HALO + layer, here, :]
            aux[half, there, :] = block[fields * HALO + INNER, here, :]
    grid = Grid(nx, ny, nz)
    many = [Field(grid, state[7 * f : 7 * f + 7], w) for f in range(freqs)]
    for half in range(2):
        for layer in range(INNER):
            i = nx + layer if half == 0 else nx + HALO + 1 + layer
            terms = grid.prepare(
                i,
                grid.both,
                freq_sq,
                w,
                many,
                lambda t: cells[half, layer, grid.tile(t), :],
                lambda k, t: grid.pick(aux, half, t, 8 * k + layer),
            )
            for f in range(freqs):
                for p in range(2):
                    grid.put(many[f].v0, p, i, terms[f][p], grid.both)

    left = jnp.where(lax.axis_index("gx") > 0, 1.0, 0.0)
    right = jnp.where(lax.axis_index("gx") < lax.axis_size("gx") - 1, 1.0, 0.0)
    wrap = grid.xe
    acc = [tuple(grid.zero() for _ in range(4)) for _ in range(freqs)]
    for stage in range(4):
        for k in range(HALO):
            for x in (k - INNER + stage, nx - 1 - stage + k):
                i, lo, hi = x % wrap, (x - 1) % wrap, (x + 1) % wrap
                own = 0 <= x < nx
                cut = None
                if x == 0:
                    cut = (-1, left)
                if x == nx - 1:
                    cut = (1, right)
                for f in range(freqs):
                    if stage == 0:
                        many[f].finish(i, grid.both, True, lo, hi, cut)
                        continue
                    got = many[f].step(
                        stage, i, lo, hi, cut, acc[f] if own else None
                    )
                    if own:
                        acc[f] = got

    rows = []
    for f in range(freqs):
        for m in range(4):
            both = acc[f][m] + moments[f, m]
            rows.append(jnp.sum(both, axis=0, keepdims=True))
    sums = jnp.sum(jnp.concatenate(rows, axis=0), axis=1, keepdims=True)
    sums = jnp.broadcast_to(sums, (4 * freqs, nz))
    for peer in range(peers):
        part[peer] = sums


def edge_part(peers, freqs, nx, ny, freq_sq, xe, xo, ce, co, state, moments):
    nz = state[0].shape[3]
    outs = tuple(pltpu.VMEM(k.shape, F32) for k in state)
    return pl.pallas_call(
        functools.partial(edge_kernel, peers, freqs, nx, ny),
        out_shape=outs + (jax.ShapeDtypeStruct((peers, 4 * freqs, nz), F32),),
        in_specs=[SMEM] + [VMEM] * (5 + len(state)),
        input_output_aliases={5 + k: k for k in range(len(state))},
        scratch_shapes=[
            pltpu.VMEM((2, INNER, ny + 2 * HALO, nz), F32),
            pltpu.VMEM((2, ny + 2 * HALO, nz), F32),
        ],
        compiler_params=params(8),
        name="edge_part",
    )(freq_sq, xe, xo, ce, co, *state, moments)


def steps(sums, freqs):
    total = jnp.sum(sums[...], axis=0)
    shape = (8, total.shape[1])
    out = []
    for f in range(freqs):
        m0, m1, m2, m3 = (
            jnp.broadcast_to(total[4 * f + k : 4 * f + k + 1, :], shape)
            for k in range(4)
        )
        first = m0 / m1
        new = first * (first * m2 - m1)
        product = m1 - first * (2.0 * m2 - first * m3)
        ratio = new / m0
        second = new / (product - ratio * new / first)
        out.append((first + second * (1.0 + ratio), -first * second))
    return out


def gradient_kernel(freqs, nx, ny, freq_sq, sums, *refs):
    out = refs[-1]
    weights = steps(sums, freqs)

    def row(x, _):
        for y in range(0, ny, 8):
            at = pl.ds(y, 8)
            total = None
            for f in range(freqs):
                s, v0, u0, v1, u1 = refs[5 * f : 5 * f + 5]
                a, b = weights[f]
                wave_re = a * v0[0, x, at, :] + b * v1[0, x, at, :]
                wave_im = a * v0[1, x, at, :] + b * v1[1, x, at, :]
                miss_re = a * u0[0, x, at, :] + b * u1[0, x, at, :]
                miss_im = a * u0[1, x, at, :] + b * u1[1, x, at, :]
                miss_re = miss_re - s[0, x, at, :]
                miss_im = miss_im - s[1, x, at, :]
                left = (wave_re + attenuation * wave_im) * miss_re
                right = (wave_im - attenuation * wave_re) * miss_im
                term = -freq_sq[f] * (left + right)
                total = term if total is None else total + term
            out[x, at, :] = total
        return 0

    lax.fori_loop(0, nx, row, 0, unroll=2)


def wave_kernel(freqs, nx, ny, sums, *refs):
    out, block, sem = refs[2 * freqs :]
    weights = steps(sums, freqs)
    copies = Copies(sem)
    for f in range(freqs):
        a, b = weights[f]
        v0, v1 = refs[2 * f : 2 * f + 2]
        for p in range(2):
            k = 2 * f + p

            def row(x, _):
                for y in range(0, ny, 8):
                    at = pl.ds(y, 8)
                    block[k, x, at, :] = a * v0[p, x, at, :] + b * v1[p, x, at, :]
                return 0

            lax.fori_loop(0, nx, row, 0, unroll=8)
            copies.add(block.at[k], out.at[f, p])
    copies.wait()


def results(freqs, nx, ny, freq_sq, sums, state):
    nz = state[0].shape[3]
    fields, pairs = [], []
    for f in range(freqs):
        s, v0, u0, v1, u1 = state[7 * f : 7 * f + 5]
        fields += [s, v0, u0, v1, u1]
        pairs += [v0, v1]
    gradient = pl.pallas_call(
        functools.partial(gradient_kernel, freqs, nx, ny),
        out_shape=jax.ShapeDtypeStruct((nx, ny, nz), F32),
        in_specs=[SMEM] + [VMEM] * (1 + len(fields)),
        out_specs=VMEM,
        compiler_params=params(8),
        name="gradient_part",
    )(freq_sq, sums, *fields)
    wave = pl.pallas_call(
        functools.partial(wave_kernel, freqs, nx, ny),
        out_shape=jax.ShapeDtypeStruct((freqs, 2, nx, ny, nz), F32),
        in_specs=[VMEM] * (1 + len(pairs)),
        out_specs=HBM,
        scratch_shapes=[
            pltpu.VMEM((2 * freqs, nx, ny, nz), F32),
            pltpu.SemaphoreType.DMA((2 * freqs,)),
        ],
        compiler_params=params(8),
        name="wavefield",
    )(sums, *pairs)
    return gradient, wave


def swap(cells, axis, odd):
    names = ("gx", "gy", "af")
    sizes = [lax.axis_size(name) for name in names]
    along = names.index(axis)
    pairs = []
    for flat in range(sizes[0] * sizes[1] * sizes[2]):
        place = [flat // (sizes[1] * sizes[2]), flat // sizes[2] % sizes[1], flat % sizes[2]]
        mate = ((place[along] + odd) ^ 1) - odd
        if 0 <= mate < sizes[along]:
            place[along] = mate
        elif sizes[2] % 2 == 0:
            place[2] ^= 1
        else:
            continue
        pairs.append((flat, (place[0] * sizes[1] + place[1]) * sizes[2] + place[2]))
    return lax.ppermute(cells, names, pairs)


def on_device(model, freq_sq, source, observed, receiver_depth):
    nx, ny, nz = model.shape
    freqs = freq_sq.shape[0]
    *s, cells, aux, xe, xo, ye, yo = load(source, model, observed, receiver_depth)
    ye, yo = swap(ye, "gy", 0), swap(yo, "gy", 1)
    xe, xo = swap(xe, "gx", 0), swap(xo, "gx", 1)
    known = early(nx, ny, freq_sq, s, cells, aux)
    ce, co, rest = inner_part(nx, ny, freq_sq, ye, yo, s, cells, aux, known)
    ce, co = swap(ce, "gx", 0), swap(co, "gx", 1)
    state, moments = rest()
    peers = lax.axis_size("gx") * lax.axis_size("gy")
    *state, part = edge_part(
        peers, freqs, nx, ny, freq_sq, xe, xo, ce, co, state, moments
    )
    sums = lax.all_to_all(part, ("gx", "gy"), 0, 0)
    gradient, wave = results(freqs, nx, ny, freq_sq, sums, state)
    if lax.axis_size("af") == 2:
        gradient = gradient + lax.ppermute(gradient, "af", [(0, 1), (1, 0)])
    else:
        gradient = lax.psum(gradient, "af")
    return wave, gradient


def solution(mesh):
    in_specs = (
        P("gx", "gy", None),
        P("af"),
        P("af", None, "gx", "gy", None),
        P("af", None, "gx", "gy"),
        P("gx", "gy"),
    )
    out_specs = (P("af", None, "gx", "gy", None), P("gx", "gy", None))
    return jax.shard_map(
        on_device, mesh=mesh, in_specs=in_specs, out_specs=out_specs, check_vma=False
    )
```

```python
import functools

import jax
import jax.numpy as jnp
from jax import lax
from jax.experimental import pallas as pl
from jax.experimental.pallas import tpu as pltpu
from jax.sharding import PartitionSpec as P

ITERS = 2
attenuation = 0.2
penalty = 4.0

HALO = 2 * ITERS
INNER = HALO - 1
F32 = jnp.float32
ANY = pl.BlockSpec(memory_space=pl.ANY)
HBM = pl.BlockSpec(memory_space=pltpu.HBM)
VMEM = pl.BlockSpec(memory_space=pltpu.VMEM)
SMEM = pl.BlockSpec(memory_space=pltpu.SMEM)
MIB = 1 << 20
LOAD_MIB = 55
SHIFT = 2


def params(mib):
    return pltpu.CompilerParams(vmem_limit_bytes=mib * MIB)


def cost(us):
    return pl.CostEstimate(
        flops=int(us * 1e3), bytes_accessed=int(us * 1e3), transcendentals=0
    )


def parity(axis):
    return lax.rem(lax.axis_index(axis), 2) == 0


class Copies:
    def __init__(self, sem):
        self.sem, self.all = sem, []

    def add(self, src, dst):
        copy = pltpu.make_async_copy(src, dst, self.sem.at[len(self.all)])
        copy.start()
        self.all.append(copy)

    def wait(self):
        for copy in self.all:
            copy.wait()


def lane_slab(table, fields, skip, rows, nz):
    lane = lax.broadcasted_iota(jnp.int32, (rows, nz), 1)
    lanes = jnp.zeros((rows, nz), F32)
    for k in range(fields + 1):
        inside = (lane >= INNER * k) & (lane < INNER * k + INNER)
        shift = lax.rem(INNER * k + nz - skip, nz)
        lanes = jnp.where(inside, pltpu.roll(table[k], shift, axis=1), lanes)
    return lanes


def fold(slab, nz):
    rows, width = slab.shape[0] // 8, nz // 8
    lane = lax.broadcasted_iota(jnp.int32, (rows, nz), 1)
    out = jnp.zeros((rows, nz), F32)
    for g in range(8):
        piece = slab[g * rows : (g + 1) * rows, :]
        inside = (lane >= g * width) & (lane < (g + 1) * width)
        out = jnp.where(inside, pltpu.roll(piece, g * width, axis=1), out)
    return out


def load_kernel(source, model, observed, depth, *refs):
    freqs, _, nx, ny, nz = source.shape
    fields = 2 * freqs
    s, (cells, aux, xe, xo, ye, yo, seen, sunk, table, sem) = refs[:freqs], refs[freqs:]
    small = Copies(sem.at[0])
    small.add(observed, seen)
    small.add(depth, sunk)
    large = Copies(sem.at[1])
    large.add(model, cells.at[:, pl.ds(0, ny), :])
    for f in range(freqs):
        for p in range(2):
            large.add(source.at[f, p], s[f].at[p, pl.ds(0, nx), pl.ds(0, ny), :])
    even_x, even_y = parity("gx"), parity("gy")
    small.wait()
    for f in range(freqs):
        for p in range(2):
            table[2 * f + p, :, 0:nx] = seen[f, p].T
    table[fields, :, 0:nx] = sunk[...].astype(F32).T
    copies = Copies(sem.at[2])
    copies.add(table, aux.at[:, pl.ds(0, ny), :])
    faces = []
    for side, xb in enumerate((xe, xo)):
        last = even_x if side == 0 else jnp.logical_not(even_x)
        skip = jnp.where(last, nx - INNER, 0)
        faces.append((xb, skip, jnp.where(last, nx - HALO, 0)))
        at = (fields * HALO + INNER) * ny
        xb[at : at + ny // 8, :] = fold(lane_slab(table, fields, skip, ny, nz), nz)
    swapped = jnp.broadcast_to(even_y, (HALO, nz))

    def y_faces(block, at):
        def row(x, _):
            head, tail = block[x, 0:HALO, :], block[x, ny - HALO : ny, :]
            ye[at + x] = jnp.where(swapped, tail, head)
            yo[at + x] = jnp.where(swapped, head, tail)
            return 0

        lax.fori_loop(0, nx, row, 0, unroll=8)

    def x_face(xb, to, block, at, layers):
        for layer in range(layers):
            for y in range(0, ny, 8):
                row = (to + layer) * ny + y
                xb[row : row + 8, :] = block[at + layer, y : y + 8, :]

    for k in range(fields + 1):
        head, tail = table[k, 0:HALO, :], table[k, ny - HALO : ny, :]
        ye[(fields + 1) * nx + k] = jnp.where(swapped, tail, head)
        yo[(fields + 1) * nx + k] = jnp.where(swapped, head, tail)
    large.all[0].wait()
    y_faces(cells, fields * nx)
    for xb, skip, _ in faces:
        x_face(xb, fields * HALO, cells, skip, INNER)
    for k in range(fields):
        large.all[1 + k].wait()
        block = s[k // 2].at[k % 2]
        y_faces(block, k * nx)
        for xb, _, at in faces:
            x_face(xb, k * HALO, block, at, HALO)
    copies.wait()


def load(source, model, observed, depth):
    freqs, _, nx, ny, nz = source.shape
    fields = 2 * freqs
    xs = pltpu.VMEM(((fields * HALO + INNER) * ny + 8, nz), F32)
    ys = pltpu.VMEM(((fields + 1) * nx + fields + 1, HALO, nz), F32)
    return pl.pallas_call(
        load_kernel,
        out_shape=(pltpu.VMEM((2, nx + 2 * HALO, ny + 2 * HALO, nz), F32),) * freqs
        + (
            pltpu.VMEM((nx, ny + 2 * HALO, nz), F32),
            pltpu.VMEM((fields + 1, ny + 2 * HALO, nz), F32),
            xs,
            xs,
            ys,
            ys,
        ),
        in_specs=[HBM] * 4,
        scratch_shapes=[
            pltpu.VMEM(observed.shape, F32),
            pltpu.VMEM(depth.shape, jnp.int32),
            pltpu.VMEM((fields + 1, ny, nz), F32),
            pltpu.SemaphoreType.DMA((3, 32)),
        ],
        compiler_params=params(LOAD_MIB),
        name="load",
    )(source, model, observed, depth)


class Grid:
    def __init__(self, nx, ny, nz):
        self.nx, self.ny, self.nz = nx, ny, nz
        self.xe = nx + 2 * HALO
        self.tiles = ny // 8
        self.own = range(self.tiles)
        self.both = range(self.tiles + 1)
        lane = lax.broadcasted_iota(jnp.int32, (8, nz), 1)
        self.first = lane == 0
        self.last = lane == nz - 1
        self.depths = lane.astype(F32)
        sub = lax.broadcasted_iota(jnp.int32, (8, nz), 0)
        self.top = sub == 7
        self.bottom = sub == 0
        has_left = lax.axis_index("gy") > 0
        has_right = lax.axis_index("gy") < lax.axis_size("gy") - 1
        self.left = jnp.where(has_left, 1.0, 0.0)
        self.right = jnp.where(has_right, 1.0, 0.0)
        self.inside = jnp.where(sub < HALO, self.right, self.left)

    def tile(self, t):
        if t < self.tiles:
            return pl.ds(t, 8, stride=self.tiles)
        return pl.ds(self.ny, 8)

    def rows(self, ref, p, i, tiles):
        return [ref[p, i, self.tile(t), :] for t in tiles]

    def put(self, ref, p, i, values, tiles):
        for t in tiles:
            ref[p, i, self.tile(t), :] = values[t]

    def beside(self, mid):
        left = jnp.where(self.first, 0.0, pltpu.roll(mid, 1, axis=1))
        right = jnp.where(self.last, 0.0, pltpu.roll(mid, self.nz - 1, axis=1))
        return left + right

    def around(self, mid, below, above, tiles):
        n = self.tiles
        halo = mid[n] if len(mid) > n else None
        first_up = pltpu.roll(mid[0], 7, axis=0)
        last_down = pltpu.roll(mid[n - 1], 1, axis=0)
        if halo is not None:
            halo_up = pltpu.roll(halo, 7, axis=0)
            halo_down = pltpu.roll(halo, 1, axis=0)
        total = {}
        for t in tiles:
            if t == n:
                up = jnp.where(self.top, first_up, halo_up)
                down = jnp.where(self.bottom, last_down, halo_down)
            else:
                up = mid[t + 1] if t + 1 < n else None
                down = mid[t - 1] if t else None
                if up is None:
                    edge = 0.0 if halo is None else halo_up
                    up = jnp.where(self.top, edge, first_up)
                if down is None:
                    edge = 0.0 if halo is None else halo_down
                    down = jnp.where(self.bottom, edge, last_down)
            total[t] = ((below[t] + above[t]) + (up + down)) + self.beside(mid[t])
        return total

    def apply(self, src, i, lo, hi, sign, coef, tiles, wide=True, cut=None):
        cr, ci = coef
        mids, totals = [], []
        for p in range(2):
            mid = self.rows(src, p, i, self.both if wide else self.own)
            below = {t: src[p, lo, self.tile(t), :] for t in tiles}
            above = {t: src[p, hi, self.tile(t), :] for t in tiles}
            if cut is not None and cut[0] < 0:
                below = {t: v * cut[1] for t, v in below.items()}
            if cut is not None and cut[0] > 0:
                above = {t: v * cut[1] for t, v in above.items()}
            mids.append(mid)
            totals.append(self.around(mid, below, above, tiles))
        out_re, out_im = {}, {}
        for t in tiles:
            re, im = mids[0][t], mids[1][t]
            if sign > 0:
                out_re[t] = cr[t] * re - ci[t] * im - totals[0][t]
                out_im[t] = cr[t] * im + ci[t] * re - totals[1][t]
            else:
                out_re[t] = cr[t] * re + ci[t] * im - totals[0][t]
                out_im[t] = cr[t] * im - ci[t] * re - totals[1][t]
        return mids, out_re, out_im

    def squares(self, re, im):
        return {t: re[t] * re[t] + im[t] * im[t] for t in self.own}

    def gather(self, values):
        return functools.reduce(jnp.add, [values[t] for t in self.own])

    def zero(self):
        return jnp.zeros((8, self.nz), F32)

    def prepare(self, i, tiles, freq_sq, w, many, cell, column):
        fields = 2 * len(many)
        weight = {}
        for t in tiles:
            depth = column(fields, t)
            weight[t] = jnp.where(self.depths == depth, penalty, 0.0)
            w[i, t] = weight[t]
        out = []
        for f, field in enumerate(many):
            for t in tiles:
                scaled = freq_sq[f] * cell(t)
                field.cr[i, t] = 6.0 - scaled
                field.ci[i, t] = attenuation * scaled
            out.append(
                [
                    {t: weight[t] * column(2 * f + p, t) for t in tiles}
                    for p in range(2)
                ]
            )
        return out

    def pick(self, ref, lead, t, lane):
        at = jnp.full((8, self.nz), lane, jnp.int32)
        return jnp.take_along_axis(ref[lead, self.tile(t), :], at, axis=1)


class Field:
    def __init__(self, grid, refs, w):
        self.grid = grid
        self.s, self.v0, self.u0, self.v1, self.u1, self.cr, self.ci = refs
        self.w = w

    def coef(self, i, tiles):
        return {t: self.cr[i, t] for t in tiles}, {t: self.ci[i, t] for t in tiles}

    def finish(self, i, tiles, wide, lo=None, hi=None, cut=None):
        g = self.grid
        _, re, im = g.apply(self.s, i, lo, hi, -1, self.coef(i, tiles), tiles, wide, cut)
        for p, value in enumerate((re, im)):
            for t in tiles:
                at = g.tile(t)
                total = self.v0[p, i, at, :] + value[t]
                self.v0[p, i, at, :] = total * g.inside if t == g.tiles else total

    def first_halo(self, i, terms):
        g = self.grid
        n = g.tiles
        coef = self.coef(i, [n])
        _, re, im = g.apply(self.s, i, i - 1, i + 1, -1, coef, [n])
        for p, value in enumerate((re, im)):
            self.v0[p, i, g.tile(n), :] = (value[n] + terms[p][n]) * g.inside
            halo = self.s[p, i, g.tile(n), :]
            low = jnp.where(g.bottom, pltpu.roll(halo, 1, axis=0), 0.0)
            high = jnp.where(g.top, pltpu.roll(halo, 7, axis=0), 0.0)
            for t, change in ((0, low), (n - 1, high)):
                at = g.tile(t)
                self.v0[p, i, at, :] = self.v0[p, i, at, :] - change

    def step(self, stage, i, lo, hi, cut=None, acc=None):
        g = self.grid
        src = (None, self.v0, self.u0, self.v1)[stage]
        dst = (None, self.u0, self.v1, self.u1)[stage]
        tiles = g.own if stage == 3 else g.both
        sign = -1 if stage == 2 else 1
        mids, re, im = g.apply(src, i, lo, hi, sign, self.coef(i, tiles), tiles, True, cut)
        if stage != 3:
            weight = {t: self.w[i, t] for t in tiles}
        if stage == 2:
            for p, out in enumerate((re, im)):
                for t in tiles:
                    out[t] = out[t] + weight[t] * self.v0[p, i, g.tile(t), :]
        if stage != 3:
            re[g.tiles] = re[g.tiles] * g.inside
            im[g.tiles] = im[g.tiles] * g.inside
        g.put(dst, 0, i, re, tiles)
        g.put(dst, 1, i, im, tiles)
        if acc is None:
            return None
        acc = list(acc)
        squares = g.squares(re, im)
        acc[stage] = acc[stage] + g.gather(squares)
        if stage == 1:
            squares = g.squares(*mids)
            acc[0] = acc[0] + g.gather(squares)
        if stage != 3:
            at = 1 if stage == 1 else 3
            weighted = {t: weight[t] * squares[t] for t in g.own}
            acc[at] = acc[at] + g.gather(weighted)
        return tuple(acc)


def early_kernel(freqs, nx, ny, freq_sq, *refs):
    s, (cells, aux), refs = refs[:freqs], refs[freqs : freqs + 2], refs[freqs + 2 :]
    w, splat = refs[3 * freqs :]
    nz = cells.shape[2]
    for f in range(freqs):
        splat[f] = jnp.full((8, nz), freq_sq[f], F32)
    grid = Grid(nx, ny, nz)
    many = [
        Field(grid, (s[f], refs[3 * f], None, None, None, *refs[3 * f + 1 : 3 * f + 3]), w)
        for f in range(freqs)
    ]

    def prepare(i):
        return grid.prepare(
            i,
            grid.own,
            freq_sq,
            w,
            many,
            lambda t: cells[i, grid.tile(t), :],
            lambda k, t: grid.pick(aux, k, t, i),
        )

    for i in (0, nx - 1):
        terms = prepare(i)
        for f in range(freqs):
            for p in range(2):
                grid.put(many[f].v0, p, i, terms[f][p], grid.own)

    def row(i):
        terms = prepare(i)
        for f in range(freqs):
            field = many[f]
            _, re, im = grid.apply(
                field.s, i, i - 1, i + 1, -1, field.coef(i, grid.own), grid.own, False
            )
            for p, value in enumerate((re, im)):
                value = {t: value[t] + terms[f][p][t] for t in grid.own}
                grid.put(field.v0, p, i, value, grid.own)

    def pair(k, _):
        row(2 * k + 1)
        row(2 * k + 2)
        return 0

    lax.fori_loop(0, (nx - 2) // 2, pair, 0)


def early(nx, ny, freq_sq, s, cells, aux):
    freqs = len(s)
    _, xe, _, nz = s[0].shape
    field = pltpu.VMEM(s[0].shape, F32)
    coef = pltpu.VMEM((xe, ny // 8 + 1, 8, nz), F32)
    return pl.pallas_call(
        functools.partial(early_kernel, freqs, nx, ny),
        out_shape=(field, coef, coef) * freqs
        + (coef, pltpu.VMEM((freqs, 8, nz), F32)),
        in_specs=[SMEM] + [VMEM] * (freqs + 2),
        compiler_params=params(8),
        name="early",
    )(freq_sq, *s, cells, aux)


def corner_faces(freqs, nx, ny, s, cells, aux, ce, co):
    fields = 2 * freqs
    nz = cells.shape[2]
    even_x = parity("gx")
    near = [aux[k, ny:, :] for k in range(fields + 1)]
    for side, cb in enumerate((ce, co)):
        last = even_x if side == 0 else jnp.logical_not(even_x)
        at = jnp.where(last, nx - INNER, 0)
        for layer in range(INNER):
            for k in range(fields):
                cb[k * INNER + layer] = s[k // 2][k % 2, at + layer, ny:, :]
            cb[fields * INNER + layer] = cells[at + layer, ny:, :]
        cb[(fields + 1) * INNER] = lane_slab(near, fields, at, 2 * HALO, nz)


def inner_kernel(freqs, nx, ny, half, freq_sq, *refs):
    if half == 0:
        ye, yo = refs[:2]
        count = 4 * freqs + 3
        refs = refs[2 + count :]
        s, (cells, aux), refs = refs[:freqs], refs[freqs : freqs + 2], refs[freqs + 2 :]
        known, refs = refs[: 3 * freqs + 1], refs[3 * freqs + 1 :]
        news, (moments, ce, co) = refs[: 3 * freqs], refs[3 * freqs :]
    else:
        s, known = refs[:freqs], refs[freqs : 4 * freqs + 1]
        partial = refs[7 * freqs + 1]
        refs = refs[7 * freqs + 2 :]
        news, (moments,) = refs[: 3 * freqs], refs[3 * freqs :]
    nz = s[0].shape[3]
    fields = 2 * freqs
    w = known[3 * freqs]
    grid = Grid(nx, ny, nz)
    many = []
    for f in range(freqs):
        v0, cr, ci = known[3 * f : 3 * f + 3]
        u0, v1, u1 = news[3 * f : 3 * f + 3]
        many.append(Field(grid, (s[f], v0, u0, v1, u1, cr, ci), w))
    if half == 0:
        swapped = jnp.broadcast_to(parity("gy"), (HALO, nz))

        def halo(at):
            even, odd = ye[at], yo[at]
            high = jnp.where(swapped, even, odd) * grid.right
            low = jnp.where(swapped, odd, even) * grid.left
            return jnp.concatenate([high, low], axis=0)

        def merge(x, _):
            cells[x, ny:, :] = halo(fields * nx + x)
            for k in range(fields):
                s[k // 2][k % 2, x, ny:, :] = halo(k * nx + x)
            return 0

        lax.fori_loop(0, nx, merge, 0, unroll=4)
        for k in range(fields + 1):
            aux[k, ny:, :] = halo((fields + 1) * nx + k)
        corner_faces(freqs, nx, ny, s, cells, aux, ce, co)

    def prepare(i):
        return grid.prepare(
            i,
            [grid.tiles],
            freq_sq,
            w,
            many,
            lambda t: cells[i, grid.tile(t), :],
            lambda k, t: grid.pick(aux, k, t, i),
        )

    if half == 0:
        for i in (0, nx - 1):
            terms = prepare(i)
            for f in range(freqs):
                for p in range(2):
                    grid.put(many[f].v0, p, i, terms[f][p], [grid.tiles])

    def step(j, acc, active):
        acc = list(acc)
        for k in reversed(active):
            i = j - 2 * k
            if k == 0:
                terms = prepare(i)
            for f in range(freqs):
                if k == 0:
                    many[f].first_halo(i, terms[f])
                else:
                    acc[f] = many[f].step(k, i, i - 1, i + 1, acc=acc[f])
        return tuple(acc)

    def heads(i, _):
        terms = prepare(i)
        for f in range(freqs):
            many[f].first_halo(i, terms[f])
        return 0

    spans = [(1 + 3 * k, nx - 1 + k) for k in range(4)]
    middle = nx // 2 + SHIFT
    edges = sorted({e for span in spans for e in span} | {middle})
    acc = tuple(tuple(grid.zero() for _ in range(4)) for _ in range(freqs))
    if half == 0:
        lax.fori_loop(1, nx - 1, heads, 0, unroll=3)
    for lo, hi in zip(edges[:-1], edges[1:]):
        if (lo < middle) != (half == 0):
            continue
        active = [k for k, (a, b) in enumerate(spans) if k and a <= lo and hi <= b]
        if active:
            acc = lax.fori_loop(lo, hi, functools.partial(step, active=active), acc)
    for f in range(freqs):
        for m in range(4):
            value = acc[f][m]
            moments[f, m] = value if half == 0 else value + partial[f, m]


def inner_part(nx, ny, freq_sq, ye, yo, s, cells, aux, known):
    freqs = len(s)
    nz = cells.shape[2]
    slabs = (2 * freqs + 1) * INNER + 1
    field = pltpu.VMEM(s[0].shape, F32)
    corner = pltpu.VMEM((slabs, 2 * HALO, nz), F32)
    kept = (*s, cells, aux, *known)
    news = (field,) * (3 * freqs) + (pltpu.VMEM((freqs, 4, 8, nz), F32),)
    got = pl.pallas_call(
        functools.partial(inner_kernel, freqs, nx, ny, 0),
        out_shape=tuple(pltpu.VMEM(k.shape, F32) for k in kept)
        + news
        + (corner, corner),
        in_specs=[VMEM] * (3 + len(kept)),
        input_output_aliases={3 + k: k for k in range(len(kept))},
        compiler_params=params(8),
        name="inner_first",
    )(freq_sq, ye, yo, *kept)
    s, known = got[:freqs], got[freqs + 2 : len(kept)]
    news_got, (ce, co) = got[len(kept) : -2], got[-2:]

    def rest():
        first = freqs + len(known)
        again = pl.pallas_call(
            functools.partial(inner_kernel, freqs, nx, ny, 1, None),
            out_shape=news,
            in_specs=[VMEM] * (freqs + len(known) + len(news)),
            input_output_aliases={first + k: k for k in range(len(news))},
            compiler_params=params(8),
            name="inner_second",
        )(*s, *known, *news_got)
        state = []
        for f in range(freqs):
            v0, cr, ci = known[3 * f : 3 * f + 3]
            state += [s[f], v0, *again[3 * f : 3 * f + 3], cr, ci]
        return state + [known[-1]], again[-1]

    return ce, co, rest


def edge_kernel(peers, freqs, nx, ny, freq_sq, xe, xo, ce, co, *refs):
    count = 7 * freqs + 1
    moments, refs = refs[count], refs[count + 1 :]
    state, (part, cells, aux) = refs[:count], refs[count:]
    fields = 2 * freqs
    nz = state[0].shape[3]
    w = state[-1]
    even_x = parity("gx")
    group = nz // 8
    for side, (xb, cb) in enumerate(((xe, ce), (xo, co))):
        above = even_x if side == 0 else jnp.logical_not(even_x)
        slot = jnp.where(above, nx, nx + HALO)
        near = jnp.where(above, nx, nx + HALO + 1)
        half = jnp.where(above, 0, 1)
        for layer in range(HALO):
            for k in range(fields):
                block = state[7 * (k // 2)]
                for y in range(0, ny, 8):
                    row = (k * HALO + layer) * ny + y
                    block[k % 2, slot + layer, y : y + 8, :] = xb[row : row + 8, :]
                if layer < INNER:
                    block[k % 2, near + layer, ny:, :] = cb[k * INNER + layer]
            if layer < INNER:
                for y in range(0, ny, 8):
                    row = (fields * HALO + layer) * ny + y
                    cells[half, layer, y : y + 8, :] = xb[row : row + 8, :]
                cells[half, layer, ny:, :] = cb[fields * INNER + layer]
        at = (fields * HALO + INNER) * ny
        folded = xb[at : at + ny // 8, :]
        for g in range(8):
            rows = pl.ds(g * (ny // 8), ny // 8)
            aux[half, rows, :] = pltpu.roll(folded, (nz - g * group) % nz, axis=1)
        aux[half, ny:, :] = cb[(fields + 1) * INNER]
    for k in range(fields):
        for i in (nx + HALO - 1, nx + HALO):
            state[7 * (k // 2)][k % 2, i, ny:, :] = jnp.zeros((2 * HALO, nz), F32)
    grid = Grid(nx, ny, nz)
    many = [Field(grid, state[7 * f : 7 * f + 7], w) for f in range(freqs)]
    for half in range(2):
        for layer in range(INNER):
            i = nx + layer if half == 0 else nx + HALO + 1 + layer
            terms = grid.prepare(
                i,
                grid.both,
                freq_sq,
                w,
                many,
                lambda t: cells[half, layer, grid.tile(t), :],
                lambda k, t: grid.pick(aux, half, t, INNER * k + layer),
            )
            for f in range(freqs):
                for p in range(2):
                    grid.put(many[f].v0, p, i, terms[f][p], grid.both)

    left = jnp.where(lax.axis_index("gx") > 0, 1.0, 0.0)
    right = jnp.where(lax.axis_index("gx") < lax.axis_size("gx") - 1, 1.0, 0.0)
    wrap = grid.xe
    acc = [tuple(grid.zero() for _ in range(4)) for _ in range(freqs)]
    for stage in range(4):
        for k in range(HALO):
            for x in (k - INNER + stage, nx - 1 - stage + k):
                i, lo, hi = x % wrap, (x - 1) % wrap, (x + 1) % wrap
                own = 0 <= x < nx
                cut = None
                if x == 0:
                    cut = (-1, left)
                if x == nx - 1:
                    cut = (1, right)
                for f in range(freqs):
                    if stage == 0:
                        many[f].finish(i, grid.both, True, lo, hi, cut)
                        continue
                    got = many[f].step(
                        stage, i, lo, hi, cut, acc[f] if own else None
                    )
                    if own:
                        acc[f] = got

    rows = []
    for f in range(freqs):
        for m in range(4):
            both = acc[f][m] + moments[f, m]
            rows.append(jnp.sum(both, axis=0, keepdims=True))
    sums = jnp.sum(jnp.concatenate(rows, axis=0), axis=1, keepdims=True)
    sums = jnp.broadcast_to(sums, (4 * freqs, nz))
    for peer in range(peers):
        part[peer] = sums


def edge_part(peers, freqs, nx, ny, freq_sq, xe, xo, ce, co, state, moments):
    nz = state[0].shape[3]
    outs = tuple(pltpu.VMEM(k.shape, F32) for k in state)
    return pl.pallas_call(
        functools.partial(edge_kernel, peers, freqs, nx, ny),
        out_shape=outs + (jax.ShapeDtypeStruct((peers, 4 * freqs, nz), F32),),
        in_specs=[VMEM] * (6 + len(state)),
        input_output_aliases={5 + k: k for k in range(len(state))},
        scratch_shapes=[
            pltpu.VMEM((2, INNER, ny + 2 * HALO, nz), F32),
            pltpu.VMEM((2, ny + 2 * HALO, nz), F32),
        ],
        compiler_params=params(8),
        name="edge_part",
    )(freq_sq, xe, xo, ce, co, *state, moments)


def steps(sums, freqs):
    total = jnp.sum(sums[...], axis=0)
    shape = (8, total.shape[1])
    out = []
    for f in range(freqs):
        m0, m1, m2, m3 = (
            jnp.broadcast_to(total[4 * f + k : 4 * f + k + 1, :], shape)
            for k in range(4)
        )
        first = m0 / m1
        new = first * (first * m2 - m1)
        product = m1 - first * (2.0 * m2 - first * m3)
        ratio = new / m0
        second = new / (product - ratio * new / first)
        out.append((first + second * (1.0 + ratio), -first * second))
    return out


def gradient_kernel(freqs, nx, ny, freq_sq, sums, *refs):
    out = refs[-1]
    weights = steps(sums, freqs)
    scale = [-freq_sq[f] for f in range(freqs)]

    def row(x, _):
        for y in range(0, ny, 8):
            at = pl.ds(y, 8)
            total = None
            for f in range(freqs):
                s, v0, u0, v1, u1 = refs[5 * f : 5 * f + 5]
                a, b = weights[f]
                wave_re = a * v0[0, x, at, :] + b * v1[0, x, at, :]
                wave_im = a * v0[1, x, at, :] + b * v1[1, x, at, :]
                miss_re = a * u0[0, x, at, :] + b * u1[0, x, at, :]
                miss_im = a * u0[1, x, at, :] + b * u1[1, x, at, :]
                miss_re = miss_re - s[0, x, at, :]
                miss_im = miss_im - s[1, x, at, :]
                left = (wave_re + attenuation * wave_im) * miss_re
                right = (wave_im - attenuation * wave_re) * miss_im
                term = scale[f] * (left + right)
                total = term if total is None else total + term
            out[x, at, :] = total
        return 0

    lax.fori_loop(0, nx, row, 0, unroll=2)


def wave_kernel(freqs, nx, ny, sums, *refs):
    out, block, sem = refs[2 * freqs :]
    weights = steps(sums, freqs)
    copies = Copies(sem)
    for f in range(freqs):
        a, b = weights[f]
        v0, v1 = refs[2 * f : 2 * f + 2]
        for p in range(2):
            k = 2 * f + p

            def row(x, _):
                for y in range(0, ny, 8):
                    at = pl.ds(y, 8)
                    block[k, x, at, :] = a * v0[p, x, at, :] + b * v1[p, x, at, :]
                return 0

            lax.fori_loop(0, nx, row, 0, unroll=8)
            copies.add(block.at[k], out.at[f, p])
    copies.wait()


def results(freqs, nx, ny, freq_sq, sums, state):
    nz = state[0].shape[3]
    fields, pairs = [], []
    for f in range(freqs):
        s, v0, u0, v1, u1 = state[7 * f : 7 * f + 5]
        fields += [s, v0, u0, v1, u1]
        pairs += [v0, v1]
    gradient = pl.pallas_call(
        functools.partial(gradient_kernel, freqs, nx, ny),
        out_shape=jax.ShapeDtypeStruct((nx, ny, nz), F32),
        in_specs=[VMEM] * (2 + len(fields)),
        out_specs=VMEM,
        compiler_params=params(8),
        name="gradient_part",
    )(freq_sq, sums, *fields)
    wave = pl.pallas_call(
        functools.partial(wave_kernel, freqs, nx, ny),
        out_shape=jax.ShapeDtypeStruct((freqs, 2, nx, ny, nz), F32),
        in_specs=[VMEM] * (1 + len(pairs)),
        out_specs=HBM,
        scratch_shapes=[
            pltpu.VMEM((2 * freqs, nx, ny, nz), F32),
            pltpu.SemaphoreType.DMA((2 * freqs,)),
        ],
        compiler_params=params(8),
        name="wavefield",
    )(sums, *pairs)
    return gradient, wave


def swap(cells, axis, odd):
    names = ("gx", "gy", "af")
    sizes = [lax.axis_size(name) for name in names]
    along = names.index(axis)
    pairs = []
    for flat in range(sizes[0] * sizes[1] * sizes[2]):
        place = [flat // (sizes[1] * sizes[2]), flat // sizes[2] % sizes[1], flat % sizes[2]]
        mate = ((place[along] + odd) ^ 1) - odd
        if 0 <= mate < sizes[along]:
            place[along] = mate
        elif sizes[2] % 2 == 0:
            place[2] ^= 1
        else:
            continue
        pairs.append((flat, (place[0] * sizes[1] + place[1]) * sizes[2] + place[2]))
    return lax.ppermute(cells, names, pairs)


def on_device(model, freq_sq, source, observed, receiver_depth):
    nx, ny, nz = model.shape
    freqs = freq_sq.shape[0]
    *s, cells, aux, xe, xo, ye, yo = load(source, model, observed, receiver_depth)
    ye, yo = swap(ye, "gy", 0), swap(yo, "gy", 1)
    xe, xo = swap(xe, "gx", 0), swap(xo, "gx", 1)
    *known, splat = early(nx, ny, freq_sq, s, cells, aux)
    ce, co, rest = inner_part(nx, ny, splat, ye, yo, s, cells, aux, known)
    ce, co = swap(ce, "gx", 0), swap(co, "gx", 1)
    state, moments = rest()
    peers = lax.axis_size("gx") * lax.axis_size("gy")
    *state, part = edge_part(
        peers, freqs, nx, ny, splat, xe, xo, ce, co, state, moments
    )
    sums = lax.all_to_all(part, ("gx", "gy"), 0, 0)
    gradient, wave = results(freqs, nx, ny, splat, sums, state)
    if lax.axis_size("af") == 2:
        gradient = gradient + lax.ppermute(gradient, "af", [(0, 1), (1, 0)])
    else:
        gradient = lax.psum(gradient, "af")
    return wave, gradient


def solution(mesh):
    in_specs = (
        P("gx", "gy", None),
        P("af"),
        P("af", None, "gx", "gy", None),
        P("af", None, "gx", "gy"),
        P("gx", "gy"),
    )
    out_specs = (P("af", None, "gx", "gy", None), P("gx", "gy", None))
    return jax.shard_map(
        on_device, mesh=mesh, in_specs=in_specs, out_specs=out_specs, check_vma=False
    )
```

```python
import functools

import jax
import jax.numpy as jnp
from jax import lax
from jax.experimental import pallas as pl
from jax.experimental.pallas import tpu as pltpu
from jax.sharding import PartitionSpec as P

ITERS = 2
attenuation = 0.2
penalty = 4.0

HALO = 2 * ITERS
INNER = HALO - 1
F32 = jnp.float32
ANY = pl.BlockSpec(memory_space=pl.ANY)
HBM = pl.BlockSpec(memory_space=pltpu.HBM)
VMEM = pl.BlockSpec(memory_space=pltpu.VMEM)
SMEM = pl.BlockSpec(memory_space=pltpu.SMEM)
MIB = 1 << 20
LOAD_MIB = 55
SHIFT = 2


def params(mib):
    return pltpu.CompilerParams(vmem_limit_bytes=mib * MIB)


def cost(us):
    return pl.CostEstimate(
        flops=int(us * 1e3), bytes_accessed=int(us * 1e3), transcendentals=0
    )


def parity(axis):
    return lax.rem(lax.axis_index(axis), 2) == 0


class Copies:
    def __init__(self, sem):
        self.sem, self.all = sem, []

    def add(self, src, dst):
        copy = pltpu.make_async_copy(src, dst, self.sem.at[len(self.all)])
        copy.start()
        self.all.append(copy)

    def wait(self):
        for copy in self.all:
            copy.wait()


def lane_slab(table, fields, skip, rows, nz):
    lane = lax.broadcasted_iota(jnp.int32, (rows, nz), 1)
    lanes = jnp.zeros((rows, nz), F32)
    for k in range(fields + 1):
        inside = (lane >= INNER * k) & (lane < INNER * k + INNER)
        shift = lax.rem(INNER * k + nz - skip, nz)
        lanes = jnp.where(inside, pltpu.roll(table[k], shift, axis=1), lanes)
    return lanes


def fold(slab, nz):
    rows, width = slab.shape[0] // 8, nz // 8
    lane = lax.broadcasted_iota(jnp.int32, (rows, nz), 1)
    out = jnp.zeros((rows, nz), F32)
    for g in range(8):
        piece = slab[g * rows : (g + 1) * rows, :]
        inside = (lane >= g * width) & (lane < (g + 1) * width)
        out = jnp.where(inside, pltpu.roll(piece, g * width, axis=1), out)
    return out


def load_kernel(source, model, observed, depth, *refs):
    freqs, _, nx, ny, nz = source.shape
    fields = 2 * freqs
    s, (cells, aux, xe, xo, ye, yo, seen, sunk, table, sem) = refs[:freqs], refs[freqs:]
    small = Copies(sem.at[0])
    small.add(observed, seen)
    small.add(depth, sunk)
    large = Copies(sem.at[1])
    large.add(model, cells.at[:, pl.ds(0, ny), :])
    for f in range(freqs):
        for p in range(2):
            large.add(source.at[f, p], s[f].at[p, pl.ds(0, nx), pl.ds(0, ny), :])
    even_x, even_y = parity("gx"), parity("gy")
    small.wait()
    for f in range(freqs):
        for p in range(2):
            table[2 * f + p, :, 0:nx] = seen[f, p].T
    table[fields, :, 0:nx] = sunk[...].astype(F32).T
    copies = Copies(sem.at[2])
    copies.add(table, aux.at[:, pl.ds(0, ny), :])
    faces = []
    for side, xb in enumerate((xe, xo)):
        last = even_x if side == 0 else jnp.logical_not(even_x)
        skip = jnp.where(last, nx - INNER, 0)
        faces.append((xb, skip, jnp.where(last, nx - HALO, 0)))
        at = (fields * HALO + INNER) * ny
        xb[at : at + ny // 8, :] = fold(lane_slab(table, fields, skip, ny, nz), nz)
    swapped = jnp.broadcast_to(even_y, (HALO, nz))

    def y_faces(block, at):
        def row(x, _):
            head, tail = block[x, 0:HALO, :], block[x, ny - HALO : ny, :]
            ye[at + x] = jnp.where(swapped, tail, head)
            yo[at + x] = jnp.where(swapped, head, tail)
            return 0

        lax.fori_loop(0, nx, row, 0, unroll=8)

    def x_face(xb, to, block, at, layers):
        for layer in range(layers):
            for y in range(0, ny, 8):
                row = (to + layer) * ny + y
                xb[row : row + 8, :] = block[at + layer, y : y + 8, :]

    for k in range(fields + 1):
        head, tail = table[k, 0:HALO, :], table[k, ny - HALO : ny, :]
        ye[(fields + 1) * nx + k] = jnp.where(swapped, tail, head)
        yo[(fields + 1) * nx + k] = jnp.where(swapped, head, tail)
    large.all[0].wait()
    y_faces(cells, fields * nx)
    for xb, skip, _ in faces:
        x_face(xb, fields * HALO, cells, skip, INNER)
    for k in range(fields):
        large.all[1 + k].wait()
        block = s[k // 2].at[k % 2]
        y_faces(block, k * nx)
        for xb, _, at in faces:
            x_face(xb, k * HALO, block, at, HALO)
    copies.wait()


def load(source, model, observed, depth):
    freqs, _, nx, ny, nz = source.shape
    fields = 2 * freqs
    xs = pltpu.VMEM(((fields * HALO + INNER) * ny + 8, nz), F32)
    ys = pltpu.VMEM(((fields + 1) * nx + fields + 1, HALO, nz), F32)
    return pl.pallas_call(
        load_kernel,
        out_shape=(pltpu.VMEM((2, nx + 2 * HALO, ny + 2 * HALO, nz), F32),) * freqs
        + (
            pltpu.VMEM((nx, ny + 2 * HALO, nz), F32),
            pltpu.VMEM((fields + 1, ny + 2 * HALO, nz), F32),
            xs,
            xs,
            ys,
            ys,
        ),
        in_specs=[HBM] * 4,
        scratch_shapes=[
            pltpu.VMEM(observed.shape, F32),
            pltpu.VMEM(depth.shape, jnp.int32),
            pltpu.VMEM((fields + 1, ny, nz), F32),
            pltpu.SemaphoreType.DMA((3, 32)),
        ],
        compiler_params=params(LOAD_MIB),
        name="load",
    )(source, model, observed, depth)


class Grid:
    def __init__(self, nx, ny, nz):
        self.nx, self.ny, self.nz = nx, ny, nz
        self.xe = nx + 2 * HALO
        self.tiles = ny // 8
        self.own = range(self.tiles)
        self.both = range(self.tiles + 1)
        lane = lax.broadcasted_iota(jnp.int32, (8, nz), 1)
        self.first = lane == 0
        self.last = lane == nz - 1
        self.depths = lane.astype(F32)
        sub = lax.broadcasted_iota(jnp.int32, (8, nz), 0)
        self.top = sub == 7
        self.bottom = sub == 0
        has_left = lax.axis_index("gy") > 0
        has_right = lax.axis_index("gy") < lax.axis_size("gy") - 1
        self.left = jnp.where(has_left, 1.0, 0.0)
        self.right = jnp.where(has_right, 1.0, 0.0)
        self.inside = jnp.where(sub < HALO, self.right, self.left)

    def tile(self, t):
        if t < self.tiles:
            return pl.ds(t, 8, stride=self.tiles)
        return pl.ds(self.ny, 8)

    def rows(self, ref, p, i, tiles):
        return [ref[p, i, self.tile(t), :] for t in tiles]

    def put(self, ref, p, i, values, tiles):
        for t in tiles:
            ref[p, i, self.tile(t), :] = values[t]

    def beside(self, mid):
        left = jnp.where(self.first, 0.0, pltpu.roll(mid, 1, axis=1))
        right = jnp.where(self.last, 0.0, pltpu.roll(mid, self.nz - 1, axis=1))
        return left + right

    def around(self, mid, below, above, tiles):
        n = self.tiles
        halo = mid[n] if len(mid) > n else None
        first_up = pltpu.roll(mid[0], 7, axis=0)
        last_down = pltpu.roll(mid[n - 1], 1, axis=0)
        if halo is not None:
            halo_up = pltpu.roll(halo, 7, axis=0)
            halo_down = pltpu.roll(halo, 1, axis=0)
        total = {}
        for t in tiles:
            if t == n:
                up = jnp.where(self.top, first_up, halo_up)
                down = jnp.where(self.bottom, last_down, halo_down)
            else:
                up = mid[t + 1] if t + 1 < n else None
                down = mid[t - 1] if t else None
                if up is None:
                    edge = 0.0 if halo is None else halo_up
                    up = jnp.where(self.top, edge, first_up)
                if down is None:
                    edge = 0.0 if halo is None else halo_down
                    down = jnp.where(self.bottom, edge, last_down)
            total[t] = ((below[t] + above[t]) + (up + down)) + self.beside(mid[t])
        return total

    def apply(self, src, i, lo, hi, sign, coef, tiles, wide=True, cut=None):
        cr, ci = coef
        mids, totals = [], []
        for p in range(2):
            mid = self.rows(src, p, i, self.both if wide else self.own)
            below = {t: src[p, lo, self.tile(t), :] for t in tiles}
            above = {t: src[p, hi, self.tile(t), :] for t in tiles}
            if cut is not None and cut[0] < 0:
                below = {t: v * cut[1] for t, v in below.items()}
            if cut is not None and cut[0] > 0:
                above = {t: v * cut[1] for t, v in above.items()}
            mids.append(mid)
            totals.append(self.around(mid, below, above, tiles))
        out_re, out_im = {}, {}
        for t in tiles:
            re, im = mids[0][t], mids[1][t]
            if sign > 0:
                out_re[t] = cr[t] * re - ci[t] * im - totals[0][t]
                out_im[t] = cr[t] * im + ci[t] * re - totals[1][t]
            else:
                out_re[t] = cr[t] * re + ci[t] * im - totals[0][t]
                out_im[t] = cr[t] * im - ci[t] * re - totals[1][t]
        return mids, out_re, out_im

    def squares(self, re, im):
        return {t: re[t] * re[t] + im[t] * im[t] for t in self.own}

    def gather(self, values):
        return functools.reduce(jnp.add, [values[t] for t in self.own])

    def zero(self):
        return jnp.zeros((8, self.nz), F32)

    def prepare(self, i, tiles, freq_sq, w, many, cell, column):
        fields = 2 * len(many)
        weight = {}
        for t in tiles:
            depth = column(fields, t)
            weight[t] = jnp.where(self.depths == depth, penalty, 0.0)
            w[i, t] = weight[t]
        out = []
        for f, field in enumerate(many):
            for t in tiles:
                scaled = freq_sq[f] * cell(t)
                field.cr[i, t] = 6.0 - scaled
                field.ci[i, t] = attenuation * scaled
            out.append(
                [
                    {t: weight[t] * column(2 * f + p, t) for t in tiles}
                    for p in range(2)
                ]
            )
        return out

    def pick(self, ref, lead, t, lane):
        at = jnp.full((8, self.nz), lane, jnp.int32)
        return jnp.take_along_axis(ref[lead, self.tile(t), :], at, axis=1)


class Field:
    def __init__(self, grid, refs, w):
        self.grid = grid
        self.s, self.v0, self.u0, self.v1, self.u1, self.cr, self.ci = refs
        self.w = w

    def coef(self, i, tiles):
        return {t: self.cr[i, t] for t in tiles}, {t: self.ci[i, t] for t in tiles}

    def finish(self, i, tiles, wide, lo=None, hi=None, cut=None):
        g = self.grid
        _, re, im = g.apply(self.s, i, lo, hi, -1, self.coef(i, tiles), tiles, wide, cut)
        for p, value in enumerate((re, im)):
            for t in tiles:
                at = g.tile(t)
                total = self.v0[p, i, at, :] + value[t]
                self.v0[p, i, at, :] = total * g.inside if t == g.tiles else total

    def first_halo(self, i, terms):
        g = self.grid
        n = g.tiles
        coef = self.coef(i, [n])
        _, re, im = g.apply(self.s, i, i - 1, i + 1, -1, coef, [n])
        for p, value in enumerate((re, im)):
            self.v0[p, i, g.tile(n), :] = (value[n] + terms[p][n]) * g.inside
            halo = self.s[p, i, g.tile(n), :]
            low = jnp.where(g.bottom, pltpu.roll(halo, 1, axis=0), 0.0)
            high = jnp.where(g.top, pltpu.roll(halo, 7, axis=0), 0.0)
            for t, change in ((0, low), (n - 1, high)):
                at = g.tile(t)
                self.v0[p, i, at, :] = self.v0[p, i, at, :] - change

    def step(self, stage, i, lo, hi, cut=None, acc=None):
        g = self.grid
        src = (None, self.v0, self.u0, self.v1)[stage]
        dst = (None, self.u0, self.v1, self.u1)[stage]
        tiles = g.own if stage == 3 else g.both
        sign = -1 if stage == 2 else 1
        mids, re, im = g.apply(src, i, lo, hi, sign, self.coef(i, tiles), tiles, True, cut)
        if stage != 3:
            weight = {t: self.w[i, t] for t in tiles}
        if stage == 2:
            for p, out in enumerate((re, im)):
                for t in tiles:
                    out[t] = out[t] + weight[t] * self.v0[p, i, g.tile(t), :]
        if stage != 3:
            re[g.tiles] = re[g.tiles] * g.inside
            im[g.tiles] = im[g.tiles] * g.inside
        g.put(dst, 0, i, re, tiles)
        g.put(dst, 1, i, im, tiles)
        if acc is None:
            return None
        acc = list(acc)
        squares = g.squares(re, im)
        acc[stage] = acc[stage] + g.gather(squares)
        if stage == 1:
            squares = g.squares(*mids)
            acc[0] = acc[0] + g.gather(squares)
        if stage != 3:
            at = 1 if stage == 1 else 3
            weighted = {t: weight[t] * squares[t] for t in g.own}
            acc[at] = acc[at] + g.gather(weighted)
        return tuple(acc)


def early_kernel(freqs, nx, ny, freq_sq, *refs):
    s, (cells, aux), refs = refs[:freqs], refs[freqs : freqs + 2], refs[freqs + 2 :]
    w, splat = refs[3 * freqs :]
    nz = cells.shape[2]
    for f in range(freqs):
        splat[f] = jnp.full((8, nz), freq_sq[f], F32)
    grid = Grid(nx, ny, nz)
    many = [
        Field(grid, (s[f], refs[3 * f], None, None, None, *refs[3 * f + 1 : 3 * f + 3]), w)
        for f in range(freqs)
    ]

    def prepare(i):
        return grid.prepare(
            i,
            grid.own,
            freq_sq,
            w,
            many,
            lambda t: cells[i, grid.tile(t), :],
            lambda k, t: grid.pick(aux, k, t, i),
        )

    for i in (0, nx - 1):
        terms = prepare(i)
        for f in range(freqs):
            for p in range(2):
                grid.put(many[f].v0, p, i, terms[f][p], grid.own)

    def row(i):
        terms = prepare(i)
        for f in range(freqs):
            field = many[f]
            _, re, im = grid.apply(
                field.s, i, i - 1, i + 1, -1, field.coef(i, grid.own), grid.own, False
            )
            for p, value in enumerate((re, im)):
                value = {t: value[t] + terms[f][p][t] for t in grid.own}
                grid.put(field.v0, p, i, value, grid.own)

    def pair(k, _):
        row(2 * k + 1)
        row(2 * k + 2)
        return 0

    lax.fori_loop(0, (nx - 2) // 2, pair, 0)


def early(nx, ny, freq_sq, s, cells, aux):
    freqs = len(s)
    _, xe, _, nz = s[0].shape
    field = pltpu.VMEM(s[0].shape, F32)
    coef = pltpu.VMEM((xe, ny // 8 + 1, 8, nz), F32)
    return pl.pallas_call(
        functools.partial(early_kernel, freqs, nx, ny),
        out_shape=(field, coef, coef) * freqs
        + (coef, pltpu.VMEM((freqs, 8, nz), F32)),
        in_specs=[SMEM] + [VMEM] * (freqs + 2),
        compiler_params=params(8),
        name="early",
    )(freq_sq, *s, cells, aux)


def corner_faces(freqs, nx, ny, s, cells, aux, ce, co):
    fields = 2 * freqs
    nz = cells.shape[2]
    sub = lax.broadcasted_iota(jnp.int32, (2 * HALO, nz), 0)
    even_x = parity("gx")
    near = [aux[k, ny:, :] for k in range(fields + 1)]
    for side, cb in enumerate((ce, co)):
        last = even_x if side == 0 else jnp.logical_not(even_x)
        at = [jnp.where(last, nx - d, d - 1) for d in range(1, HALO)]
        for k in range(fields):
            one, two, three = (s[k // 2][k % 2, x, ny:, :] for x in at)
            one = jnp.where(sub == 3, pltpu.roll(three, 3, axis=0), one)
            cb[k] = jnp.where(sub == 4, pltpu.roll(three, 5, axis=0), one)
            if k % 2 == 0:
                kept = two
                continue
            two = jnp.where(
                sub < 4, pltpu.roll(two, 2, axis=0), pltpu.roll(two, 6, axis=0)
            )
            outer = (sub < 2) | (sub > 5)
            cb[fields + k // 2] = jnp.where(outer, kept, two)
        one, two = cells[at[0], ny:, :], cells[at[1], ny:, :]
        one = jnp.where(sub == 2, pltpu.roll(two, 2, axis=0), one)
        cb[fields + freqs] = jnp.where(sub == 5, pltpu.roll(two, 6, axis=0), one)
        skip = jnp.where(last, nx - INNER, 0)
        cb[fields + freqs + 1] = lane_slab(near, fields, skip, 2 * HALO, nz)


def place_corners(freqs, nx, ny, cb, s, cells, aux, above):
    fields = 2 * freqs
    nz = cb.shape[2]
    sub = lax.broadcasted_iota(jnp.int32, (2 * HALO, nz), 0)
    slot = [jnp.where(above, nx + d - 1, nx + 2 * HALO - d) for d in range(1, HALO)]
    layer = [jnp.where(above, d - 1, INNER - d) for d in range(1, HALO)]
    for k in range(fields):
        field, p = s[k // 2], k % 2
        one = cb[k]
        field[p, slot[0], ny:, :] = one
        field[p, slot[2], ny:, :] = jnp.where(
            sub == 0, pltpu.roll(one, 5, axis=0), pltpu.roll(one, 3, axis=0)
        )
        two = cb[fields + k // 2]
        if p:
            two = jnp.where(
                sub < 4, pltpu.roll(two, 6, axis=0), pltpu.roll(two, 2, axis=0)
            )
        field[p, slot[1], ny:, :] = two
    one = cb[fields + freqs]
    cells[layer[0], ny:, :] = one
    cells[layer[1], ny:, :] = jnp.where(
        sub == 0, pltpu.roll(one, 6, axis=0), pltpu.roll(one, 2, axis=0)
    )
    cells[layer[2], ny:, :] = jnp.zeros((2 * HALO, nz), F32)
    aux[ny:, :] = cb[fields + freqs + 1]


def inner_kernel(freqs, nx, ny, half, freq_sq, *refs):
    if half == 0:
        ye, yo = refs[:2]
        count = 4 * freqs + 3
        refs = refs[2 + count :]
        s, (cells, aux), refs = refs[:freqs], refs[freqs : freqs + 2], refs[freqs + 2 :]
        known, refs = refs[: 3 * freqs + 1], refs[3 * freqs + 1 :]
        news, (moments, ce, co) = refs[: 3 * freqs], refs[3 * freqs :]
    else:
        s, known = refs[:freqs], refs[freqs : 4 * freqs + 1]
        partial = refs[7 * freqs + 1]
        refs = refs[7 * freqs + 2 :]
        news, (moments,) = refs[: 3 * freqs], refs[3 * freqs :]
    nz = s[0].shape[3]
    fields = 2 * freqs
    w = known[3 * freqs]
    grid = Grid(nx, ny, nz)
    many = []
    for f in range(freqs):
        v0, cr, ci = known[3 * f : 3 * f + 3]
        u0, v1, u1 = news[3 * f : 3 * f + 3]
        many.append(Field(grid, (s[f], v0, u0, v1, u1, cr, ci), w))
    if half == 0:
        swapped = jnp.broadcast_to(parity("gy"), (HALO, nz))

        def halo(at):
            even, odd = ye[at], yo[at]
            high = jnp.where(swapped, even, odd) * grid.right
            low = jnp.where(swapped, odd, even) * grid.left
            return jnp.concatenate([high, low], axis=0)

        def merge(x, _):
            cells[x, ny:, :] = halo(fields * nx + x)
            for k in range(fields):
                s[k // 2][k % 2, x, ny:, :] = halo(k * nx + x)
            return 0

        lax.fori_loop(0, nx, merge, 0, unroll=4)
        for k in range(fields + 1):
            aux[k, ny:, :] = halo((fields + 1) * nx + k)
        corner_faces(freqs, nx, ny, s, cells, aux, ce, co)

    def prepare(i):
        return grid.prepare(
            i,
            [grid.tiles],
            freq_sq,
            w,
            many,
            lambda t: cells[i, grid.tile(t), :],
            lambda k, t: grid.pick(aux, k, t, i),
        )

    if half == 0:
        for i in (0, nx - 1):
            terms = prepare(i)
            for f in range(freqs):
                for p in range(2):
                    grid.put(many[f].v0, p, i, terms[f][p], [grid.tiles])

    def step(j, acc, active):
        acc = list(acc)
        for k in reversed(active):
            i = j - 2 * k
            if k == 0:
                terms = prepare(i)
            for f in range(freqs):
                if k == 0:
                    many[f].first_halo(i, terms[f])
                else:
                    acc[f] = many[f].step(k, i, i - 1, i + 1, acc=acc[f])
        return tuple(acc)

    def heads(i, _):
        terms = prepare(i)
        for f in range(freqs):
            many[f].first_halo(i, terms[f])
        return 0

    spans = [(1 + 3 * k, nx - 1 + k) for k in range(4)]
    middle = nx // 2 + SHIFT
    edges = sorted({e for span in spans for e in span} | {middle})
    acc = tuple(tuple(grid.zero() for _ in range(4)) for _ in range(freqs))
    if half == 0:
        lax.fori_loop(1, nx - 1, heads, 0, unroll=3)
    for lo, hi in zip(edges[:-1], edges[1:]):
        if (lo < middle) != (half == 0):
            continue
        active = [k for k, (a, b) in enumerate(spans) if k and a <= lo and hi <= b]
        if active:
            acc = lax.fori_loop(lo, hi, functools.partial(step, active=active), acc)
    for f in range(freqs):
        for m in range(4):
            value = acc[f][m]
            moments[f, m] = value if half == 0 else value + partial[f, m]


def inner_part(nx, ny, freq_sq, ye, yo, s, cells, aux, known):
    freqs = len(s)
    nz = cells.shape[2]
    slabs = 3 * freqs + 2
    field = pltpu.VMEM(s[0].shape, F32)
    corner = pltpu.VMEM((slabs, 2 * HALO, nz), F32)
    kept = (*s, cells, aux, *known)
    news = (field,) * (3 * freqs) + (pltpu.VMEM((freqs, 4, 8, nz), F32),)
    got = pl.pallas_call(
        functools.partial(inner_kernel, freqs, nx, ny, 0),
        out_shape=tuple(pltpu.VMEM(k.shape, F32) for k in kept)
        + news
        + (corner, corner),
        in_specs=[VMEM] * (3 + len(kept)),
        input_output_aliases={3 + k: k for k in range(len(kept))},
        compiler_params=params(8),
        name="inner_first",
    )(freq_sq, ye, yo, *kept)
    s, known = got[:freqs], got[freqs + 2 : len(kept)]
    news_got, (ce, co) = got[len(kept) : -2], got[-2:]

    def rest():
        first = freqs + len(known)
        again = pl.pallas_call(
            functools.partial(inner_kernel, freqs, nx, ny, 1, None),
            out_shape=news,
            in_specs=[VMEM] * (freqs + len(known) + len(news)),
            input_output_aliases={first + k: k for k in range(len(news))},
            compiler_params=params(8),
            name="inner_second",
        )(*s, *known, *news_got)
        state = []
        for f in range(freqs):
            v0, cr, ci = known[3 * f : 3 * f + 3]
            state += [s[f], v0, *again[3 * f : 3 * f + 3], cr, ci]
        return state + [known[-1]], again[-1]

    return ce, co, rest


def edge_kernel(peers, freqs, nx, ny, freq_sq, xe, xo, ce, co, *refs):
    count = 7 * freqs + 1
    moments, refs = refs[count], refs[count + 1 :]
    state, (part, cells, aux) = refs[:count], refs[count:]
    fields = 2 * freqs
    nz = state[0].shape[3]
    w = state[-1]
    even_x = parity("gx")
    group = nz // 8
    for side, (xb, cb) in enumerate(((xe, ce), (xo, co))):
        above = even_x if side == 0 else jnp.logical_not(even_x)
        slot = jnp.where(above, nx, nx + HALO)
        half = jnp.where(above, 0, 1)
        for layer in range(HALO):
            for k in range(fields):
                block = state[7 * (k // 2)]
                for y in range(0, ny, 8):
                    row = (k * HALO + layer) * ny + y
                    block[k % 2, slot + layer, y : y + 8, :] = xb[row : row + 8, :]
            if layer < INNER:
                for y in range(0, ny, 8):
                    row = (fields * HALO + layer) * ny + y
                    cells[half, layer, y : y + 8, :] = xb[row : row + 8, :]
        at = (fields * HALO + INNER) * ny
        folded = xb[at : at + ny // 8, :]
        for g in range(8):
            rows = pl.ds(g * (ny // 8), ny // 8)
            aux[half, rows, :] = pltpu.roll(folded, (nz - g * group) % nz, axis=1)
        place_corners(
            freqs, nx, ny, cb, state[: 7 * freqs : 7], cells.at[half], aux.at[half], above
        )
    for k in range(fields):
        for i in (nx + HALO - 1, nx + HALO):
            state[7 * (k // 2)][k % 2, i, ny:, :] = jnp.zeros((2 * HALO, nz), F32)
    grid = Grid(nx, ny, nz)
    many = [Field(grid, state[7 * f : 7 * f + 7], w) for f in range(freqs)]
    for half in range(2):
        for layer in range(INNER):
            i = nx + layer if half == 0 else nx + HALO + 1 + layer
            terms = grid.prepare(
                i,
                grid.both,
                freq_sq,
                w,
                many,
                lambda t: cells[half, layer, grid.tile(t), :],
                lambda k, t: grid.pick(aux, half, t, INNER * k + layer),
            )
            for f in range(freqs):
                for p in range(2):
                    grid.put(many[f].v0, p, i, terms[f][p], grid.both)

    left = jnp.where(lax.axis_index("gx") > 0, 1.0, 0.0)
    right = jnp.where(lax.axis_index("gx") < lax.axis_size("gx") - 1, 1.0, 0.0)
    wrap = grid.xe
    acc = [tuple(grid.zero() for _ in range(4)) for _ in range(freqs)]
    for stage in range(4):
        for k in range(HALO):
            for x in (k - INNER + stage, nx - 1 - stage + k):
                i, lo, hi = x % wrap, (x - 1) % wrap, (x + 1) % wrap
                own = 0 <= x < nx
                cut = None
                if x == 0:
                    cut = (-1, left)
                if x == nx - 1:
                    cut = (1, right)
                for f in range(freqs):
                    if stage == 0:
                        many[f].finish(i, grid.both, True, lo, hi, cut)
                        continue
                    got = many[f].step(
                        stage, i, lo, hi, cut, acc[f] if own else None
                    )
                    if own:
                        acc[f] = got

    rows = []
    for f in range(freqs):
        for m in range(4):
            both = acc[f][m] + moments[f, m]
            rows.append(jnp.sum(both, axis=0, keepdims=True))
    sums = jnp.sum(jnp.concatenate(rows, axis=0), axis=1, keepdims=True)
    sums = jnp.broadcast_to(sums, (4 * freqs, nz))
    for peer in range(peers):
        part[peer] = sums


def edge_part(peers, freqs, nx, ny, freq_sq, xe, xo, ce, co, state, moments):
    nz = state[0].shape[3]
    outs = tuple(pltpu.VMEM(k.shape, F32) for k in state)
    return pl.pallas_call(
        functools.partial(edge_kernel, peers, freqs, nx, ny),
        out_shape=outs + (jax.ShapeDtypeStruct((peers, 4 * freqs, nz), F32),),
        in_specs=[VMEM] * (6 + len(state)),
        input_output_aliases={5 + k: k for k in range(len(state))},
        scratch_shapes=[
            pltpu.VMEM((2, INNER, ny + 2 * HALO, nz), F32),
            pltpu.VMEM((2, ny + 2 * HALO, nz), F32),
        ],
        compiler_params=params(8),
        name="edge_part",
    )(freq_sq, xe, xo, ce, co, *state, moments)


def steps(sums, freqs):
    total = jnp.sum(sums[...], axis=0)
    shape = (8, total.shape[1])
    out = []
    for f in range(freqs):
        m0, m1, m2, m3 = (
            jnp.broadcast_to(total[4 * f + k : 4 * f + k + 1, :], shape)
            for k in range(4)
        )
        first = m0 / m1
        new = first * (first * m2 - m1)
        product = m1 - first * (2.0 * m2 - first * m3)
        ratio = new / m0
        second = new / (product - ratio * new / first)
        out.append((first + second * (1.0 + ratio), -first * second))
    return out


def gradient_kernel(freqs, nx, ny, freq_sq, sums, *refs):
    out = refs[-1]
    weights = steps(sums, freqs)
    scale = [-freq_sq[f] for f in range(freqs)]

    def row(x, _):
        for y in range(0, ny, 8):
            at = pl.ds(y, 8)
            total = None
            for f in range(freqs):
                s, v0, u0, v1, u1 = refs[5 * f : 5 * f + 5]
                a, b = weights[f]
                wave_re = a * v0[0, x, at, :] + b * v1[0, x, at, :]
                wave_im = a * v0[1, x, at, :] + b * v1[1, x, at, :]
                miss_re = a * u0[0, x, at, :] + b * u1[0, x, at, :]
                miss_im = a * u0[1, x, at, :] + b * u1[1, x, at, :]
                miss_re = miss_re - s[0, x, at, :]
                miss_im = miss_im - s[1, x, at, :]
                left = (wave_re + attenuation * wave_im) * miss_re
                right = (wave_im - attenuation * wave_re) * miss_im
                term = scale[f] * (left + right)
                total = term if total is None else total + term
            out[x, at, :] = total
        return 0

    lax.fori_loop(0, nx, row, 0, unroll=2)


def wave_kernel(freqs, nx, ny, sums, *refs):
    out, block, sem = refs[2 * freqs :]
    weights = steps(sums, freqs)
    copies = Copies(sem)
    for f in range(freqs):
        a, b = weights[f]
        v0, v1 = refs[2 * f : 2 * f + 2]
        for p in range(2):
            k = 2 * f + p

            def row(x, _):
                for y in range(0, ny, 8):
                    at = pl.ds(y, 8)
                    block[k, x, at, :] = a * v0[p, x, at, :] + b * v1[p, x, at, :]
                return 0

            lax.fori_loop(0, nx, row, 0, unroll=8)
            copies.add(block.at[k], out.at[f, p])
    copies.wait()


def results(freqs, nx, ny, freq_sq, sums, state):
    nz = state[0].shape[3]
    fields, pairs = [], []
    for f in range(freqs):
        s, v0, u0, v1, u1 = state[7 * f : 7 * f + 5]
        fields += [s, v0, u0, v1, u1]
        pairs += [v0, v1]
    gradient = pl.pallas_call(
        functools.partial(gradient_kernel, freqs, nx, ny),
        out_shape=jax.ShapeDtypeStruct((nx, ny, nz), F32),
        in_specs=[VMEM] * (2 + len(fields)),
        out_specs=VMEM,
        compiler_params=params(8),
        name="gradient_part",
    )(freq_sq, sums, *fields)
    wave = pl.pallas_call(
        functools.partial(wave_kernel, freqs, nx, ny),
        out_shape=jax.ShapeDtypeStruct((freqs, 2, nx, ny, nz), F32),
        in_specs=[VMEM] * (1 + len(pairs)),
        out_specs=HBM,
        scratch_shapes=[
            pltpu.VMEM((2 * freqs, nx, ny, nz), F32),
            pltpu.SemaphoreType.DMA((2 * freqs,)),
        ],
        compiler_params=params(8),
        name="wavefield",
    )(sums, *pairs)
    return gradient, wave


def add_kernel(one, two, out, block, sem):
    nx, ny, _ = one.shape
    copies = Copies(sem)
    parts = sem.shape[0]
    step = nx // parts
    for part in range(parts):

        def row(x, _):
            for y in range(0, ny, 8):
                at = pl.ds(y, 8)
                block[x, at, :] = one[x, at, :] + two[x, at, :]
            return 0

        lax.fori_loop(part * step, (part + 1) * step, row, 0, unroll=4)
        span = pl.ds(part * step, step)
        copies.add(block.at[span], out.at[span])
    copies.wait()


def add(one, two):
    return pl.pallas_call(
        add_kernel,
        out_shape=jax.ShapeDtypeStruct(one.shape, F32),
        in_specs=[VMEM] * 2,
        out_specs=HBM,
        scratch_shapes=[pltpu.VMEM(one.shape, F32), pltpu.SemaphoreType.DMA((2,))],
        compiler_params=params(4),
        name="add",
    )(one, two)


def swap(cells, axis, odd):
    names = ("gx", "gy", "af")
    sizes = [lax.axis_size(name) for name in names]
    along = names.index(axis)
    pairs = []
    for flat in range(sizes[0] * sizes[1] * sizes[2]):
        place = [flat // (sizes[1] * sizes[2]), flat // sizes[2] % sizes[1], flat % sizes[2]]
        mate = ((place[along] + odd) ^ 1) - odd
        if 0 <= mate < sizes[along]:
            place[along] = mate
        elif sizes[2] % 2 == 0:
            place[2] ^= 1
        else:
            continue
        pairs.append((flat, (place[0] * sizes[1] + place[1]) * sizes[2] + place[2]))
    return lax.ppermute(cells, names, pairs)


def on_device(model, freq_sq, source, observed, receiver_depth):
    nx, ny, nz = model.shape
    freqs = freq_sq.shape[0]
    *s, cells, aux, xe, xo, ye, yo = load(source, model, observed, receiver_depth)
    ye, yo = swap(ye, "gy", 0), swap(yo, "gy", 1)
    xe, xo = swap(xe, "gx", 0), swap(xo, "gx", 1)
    *known, splat = early(nx, ny, freq_sq, s, cells, aux)
    ce, co, rest = inner_part(nx, ny, splat, ye, yo, s, cells, aux, known)
    ce, co = swap(ce, "gx", 0), swap(co, "gx", 1)
    state, moments = rest()
    peers = lax.axis_size("gx") * lax.axis_size("gy")
    *state, part = edge_part(
        peers, freqs, nx, ny, splat, xe, xo, ce, co, state, moments
    )
    sums = lax.all_to_all(part, ("gx", "gy"), 0, 0)
    gradient, wave = results(freqs, nx, ny, splat, sums, state)
    if lax.axis_size("af") == 2:
        gradient = add(gradient, lax.ppermute(gradient, "af", [(0, 1), (1, 0)]))
    else:
        gradient = lax.psum(gradient, "af")
    return wave, gradient


def solution(mesh):
    in_specs = (
        P("gx", "gy", None),
        P("af"),
        P("af", None, "gx", "gy", None),
        P("af", None, "gx", "gy"),
        P("gx", "gy"),
    )
    out_specs = (P("af", None, "gx", "gy", None), P("gx", "gy", None))
    return jax.shard_map(
        on_device, mesh=mesh, in_specs=in_specs, out_specs=out_specs, check_vma=False
    )
```

```python
import functools

import jax
import jax.numpy as jnp
from jax import lax
from jax.experimental import pallas as pl
from jax.experimental.pallas import tpu as pltpu
from jax.sharding import PartitionSpec as P

ITERS = 2
attenuation = 0.2
penalty = 4.0

HALO = 2 * ITERS
INNER = HALO - 1
F32 = jnp.float32
ANY = pl.BlockSpec(memory_space=pl.ANY)
HBM = pl.BlockSpec(memory_space=pltpu.HBM)
VMEM = pl.BlockSpec(memory_space=pltpu.VMEM)
SMEM = pl.BlockSpec(memory_space=pltpu.SMEM)
MIB = 1 << 20
LOAD_MIB = 55
SHIFT = -4


def params(mib):
    return pltpu.CompilerParams(vmem_limit_bytes=mib * MIB)


def cost(us):
    return pl.CostEstimate(
        flops=int(us * 1e3), bytes_accessed=int(us * 1e3), transcendentals=0
    )


def parity(axis):
    return lax.rem(lax.axis_index(axis), 2) == 0


class Copies:
    def __init__(self, sem):
        self.sem, self.all = sem, []

    def add(self, src, dst):
        copy = pltpu.make_async_copy(src, dst, self.sem.at[len(self.all)])
        copy.start()
        self.all.append(copy)

    def wait(self):
        for copy in self.all:
            copy.wait()


def lane_slab(table, fields, skip, rows, nz):
    lane = lax.broadcasted_iota(jnp.int32, (rows, nz), 1)
    lanes = jnp.zeros((rows, nz), F32)
    for k in range(fields + 1):
        inside = (lane >= INNER * k) & (lane < INNER * k + INNER)
        shift = lax.rem(INNER * k + nz - skip, nz)
        lanes = jnp.where(inside, pltpu.roll(table[k], shift, axis=1), lanes)
    return lanes


def fold(slab, nz):
    rows, width = slab.shape[0] // 8, nz // 8
    lane = lax.broadcasted_iota(jnp.int32, (rows, nz), 1)
    out = jnp.zeros((rows, nz), F32)
    for g in range(8):
        piece = slab[g * rows : (g + 1) * rows, :]
        inside = (lane >= g * width) & (lane < (g + 1) * width)
        out = jnp.where(inside, pltpu.roll(piece, g * width, axis=1), out)
    return out


def load_kernel(source, model, observed, depth, *refs):
    freqs, _, nx, ny, nz = source.shape
    fields = 2 * freqs
    s, (cells, aux, xe, xo, ye, yo, seen, sunk, table, sem) = refs[:freqs], refs[freqs:]
    small = Copies(sem.at[0])
    small.add(observed, seen)
    small.add(depth, sunk)
    large = Copies(sem.at[1])
    large.add(model, cells.at[:, pl.ds(0, ny), :])
    for f in range(freqs):
        for p in range(2):
            large.add(source.at[f, p], s[f].at[p, pl.ds(0, nx), pl.ds(0, ny), :])
    even_x, even_y = parity("gx"), parity("gy")
    small.wait()
    for f in range(freqs):
        for p in range(2):
            table[2 * f + p, :, 0:nx] = seen[f, p].T
    table[fields, :, 0:nx] = sunk[...].astype(F32).T
    copies = Copies(sem.at[2])
    copies.add(table, aux.at[:, pl.ds(0, ny), :])
    faces = []
    for side, xb in enumerate((xe, xo)):
        last = even_x if side == 0 else jnp.logical_not(even_x)
        skip = jnp.where(last, nx - INNER, 0)
        faces.append((xb, skip, jnp.where(last, nx - HALO, 0)))
        at = (fields * HALO + INNER) * ny
        xb[at : at + ny // 8, :] = fold(lane_slab(table, fields, skip, ny, nz), nz)
    swapped = jnp.broadcast_to(even_y, (HALO, nz))

    def y_faces(block, at):
        def row(x, _):
            head, tail = block[x, 0:HALO, :], block[x, ny - HALO : ny, :]
            ye[at + x] = jnp.where(swapped, tail, head)
            yo[at + x] = jnp.where(swapped, head, tail)
            return 0

        lax.fori_loop(0, nx, row, 0, unroll=8)

    def x_face(xb, to, block, at, layers):
        for layer in range(layers):
            for y in range(0, ny, 8):
                row = (to + layer) * ny + y
                xb[row : row + 8, :] = block[at + layer, y : y + 8, :]

    lane = lax.broadcasted_iota(jnp.int32, (HALO, nz), 1)
    at = fields * nx + nx // 4 * 3
    for slab in range(-(-(fields + 1) // (nz // nx))):
        pair = [jnp.zeros((HALO, nz), F32)] * 2
        for g in range(nz // nx):
            k = slab * (nz // nx) + g
            if k > fields:
                continue
            inside = (lane >= g * nx) & (lane < (g + 1) * nx)
            for end, rows in enumerate((table[k, 0:HALO, :], table[k, ny - HALO : ny, :])):
                moved = pltpu.roll(rows, g * nx, axis=1)
                pair[end] = jnp.where(inside, moved, pair[end])
        ye[at + slab] = jnp.where(swapped, pair[1], pair[0])
        yo[at + slab] = jnp.where(swapped, pair[0], pair[1])
    large.all[0].wait()
    sub = lax.broadcasted_iota(jnp.int32, (8, nz), 0)

    def model_rows(g, _):
        heads = [cells[4 * g + j, 0:8, :] for j in range(4)]
        tails = [cells[4 * g + j, ny - 8 : ny, :] for j in range(4)]
        for j in range(3):
            head = jnp.where(sub == 3, pltpu.roll(heads[3], 3 - j, axis=0), heads[j])
            tail = jnp.where(sub == 4, pltpu.roll(tails[3], 7 - j, axis=0), tails[j])
            head, tail = head[0:HALO, :], tail[8 - HALO : 8, :]
            ye[fields * nx + 3 * g + j] = jnp.where(swapped, tail, head)
            yo[fields * nx + 3 * g + j] = jnp.where(swapped, head, tail)
        return 0

    lax.fori_loop(0, nx // 4, model_rows, 0, unroll=2)
    for xb, skip, _ in faces:
        x_face(xb, fields * HALO, cells, skip, INNER)
    for k in range(fields):
        large.all[1 + k].wait()
        block = s[k // 2].at[k % 2]
        y_faces(block, k * nx)
        for xb, _, at in faces:
            x_face(xb, k * HALO, block, at, HALO)
    copies.wait()


def load(source, model, observed, depth):
    freqs, _, nx, ny, nz = source.shape
    fields = 2 * freqs
    xs = pltpu.VMEM(((fields * HALO + INNER) * ny + 8, nz), F32)
    slabs = fields * nx + nx // 4 * 3 + -(-(fields + 1) // (nz // nx))
    ys = pltpu.VMEM((slabs, HALO, nz), F32)
    return pl.pallas_call(
        load_kernel,
        out_shape=(pltpu.VMEM((2, nx + 2 * HALO, ny + 2 * HALO, nz), F32),) * freqs
        + (
            pltpu.VMEM((nx, ny + 2 * HALO, nz), F32),
            pltpu.VMEM((fields + 1, ny + 2 * HALO, nz), F32),
            xs,
            xs,
            ys,
            ys,
        ),
        in_specs=[HBM] * 4,
        scratch_shapes=[
            pltpu.VMEM(observed.shape, F32),
            pltpu.VMEM(depth.shape, jnp.int32),
            pltpu.VMEM((fields + 1, ny, nz), F32),
            pltpu.SemaphoreType.DMA((3, 32)),
        ],
        compiler_params=params(LOAD_MIB),
        name="load",
    )(source, model, observed, depth)


class Grid:
    def __init__(self, nx, ny, nz):
        self.nx, self.ny, self.nz = nx, ny, nz
        self.xe = nx + 2 * HALO
        self.tiles = ny // 8
        self.own = range(self.tiles)
        self.both = range(self.tiles + 1)
        lane = lax.broadcasted_iota(jnp.int32, (8, nz), 1)
        self.first = lane == 0
        self.last = lane == nz - 1
        self.depths = lane.astype(F32)
        sub = lax.broadcasted_iota(jnp.int32, (8, nz), 0)
        self.top = sub == 7
        self.bottom = sub == 0
        has_left = lax.axis_index("gy") > 0
        has_right = lax.axis_index("gy") < lax.axis_size("gy") - 1
        self.left = jnp.where(has_left, 1.0, 0.0)
        self.right = jnp.where(has_right, 1.0, 0.0)
        self.inside = jnp.where(sub < HALO, self.right, self.left)

    def tile(self, t):
        if t < self.tiles:
            return pl.ds(t, 8, stride=self.tiles)
        return pl.ds(self.ny, 8)

    def rows(self, ref, p, i, tiles):
        return [ref[p, i, self.tile(t), :] for t in tiles]

    def put(self, ref, p, i, values, tiles):
        for t in tiles:
            ref[p, i, self.tile(t), :] = values[t]

    def beside(self, mid):
        left = jnp.where(self.first, 0.0, pltpu.roll(mid, 1, axis=1))
        right = jnp.where(self.last, 0.0, pltpu.roll(mid, self.nz - 1, axis=1))
        return left + right

    def around(self, mid, below, above, tiles):
        n = self.tiles
        halo = mid[n] if len(mid) > n else None
        first_up = pltpu.roll(mid[0], 7, axis=0)
        last_down = pltpu.roll(mid[n - 1], 1, axis=0)
        if halo is not None:
            halo_up = pltpu.roll(halo, 7, axis=0)
            halo_down = pltpu.roll(halo, 1, axis=0)
        total = {}
        for t in tiles:
            if t == n:
                up = jnp.where(self.top, first_up, halo_up)
                down = jnp.where(self.bottom, last_down, halo_down)
            else:
                up = mid[t + 1] if t + 1 < n else None
                down = mid[t - 1] if t else None
                if up is None:
                    edge = 0.0 if halo is None else halo_up
                    up = jnp.where(self.top, edge, first_up)
                if down is None:
                    edge = 0.0 if halo is None else halo_down
                    down = jnp.where(self.bottom, edge, last_down)
            total[t] = ((below[t] + above[t]) + (up + down)) + self.beside(mid[t])
        return total

    def apply(self, src, i, lo, hi, sign, coef, tiles, wide=True, cut=None):
        cr, ci = coef
        mids, totals = [], []
        for p in range(2):
            mid = self.rows(src, p, i, self.both if wide else self.own)
            below = {t: src[p, lo, self.tile(t), :] for t in tiles}
            above = {t: src[p, hi, self.tile(t), :] for t in tiles}
            if cut is not None and cut[0] < 0:
                below = {t: v * cut[1] for t, v in below.items()}
            if cut is not None and cut[0] > 0:
                above = {t: v * cut[1] for t, v in above.items()}
            mids.append(mid)
            totals.append(self.around(mid, below, above, tiles))
        out_re, out_im = {}, {}
        for t in tiles:
            re, im = mids[0][t], mids[1][t]
            if sign > 0:
                out_re[t] = cr[t] * re - ci[t] * im - totals[0][t]
                out_im[t] = cr[t] * im + ci[t] * re - totals[1][t]
            else:
                out_re[t] = cr[t] * re + ci[t] * im - totals[0][t]
                out_im[t] = cr[t] * im - ci[t] * re - totals[1][t]
        return mids, out_re, out_im

    def squares(self, re, im):
        return {t: re[t] * re[t] + im[t] * im[t] for t in self.own}

    def gather(self, values):
        return functools.reduce(jnp.add, [values[t] for t in self.own])

    def zero(self):
        return jnp.zeros((8, self.nz), F32)

    def prepare(self, i, tiles, freq_sq, w, many, cell, column):
        fields = 2 * len(many)
        weight = {}
        for t in tiles:
            depth = column(fields, t)
            weight[t] = jnp.where(self.depths == depth, penalty, 0.0)
            w[i, t] = weight[t]
        out = []
        for f, field in enumerate(many):
            for t in tiles:
                scaled = freq_sq[f] * cell(t)
                field.cr[i, t] = 6.0 - scaled
                field.ci[i, t] = attenuation * scaled
            out.append(
                [
                    {t: weight[t] * column(2 * f + p, t) for t in tiles}
                    for p in range(2)
                ]
            )
        return out

    def pick(self, ref, lead, t, lane):
        at = jnp.full((8, self.nz), lane, jnp.int32)
        return jnp.take_along_axis(ref[lead, self.tile(t), :], at, axis=1)


class Field:
    def __init__(self, grid, refs, w):
        self.grid = grid
        self.s, self.v0, self.u0, self.v1, self.u1, self.cr, self.ci = refs
        self.w = w

    def coef(self, i, tiles):
        return {t: self.cr[i, t] for t in tiles}, {t: self.ci[i, t] for t in tiles}

    def finish(self, i, tiles, wide, lo=None, hi=None, cut=None):
        g = self.grid
        _, re, im = g.apply(self.s, i, lo, hi, -1, self.coef(i, tiles), tiles, wide, cut)
        for p, value in enumerate((re, im)):
            for t in tiles:
                at = g.tile(t)
                total = self.v0[p, i, at, :] + value[t]
                self.v0[p, i, at, :] = total * g.inside if t == g.tiles else total

    def first_halo(self, i, terms):
        g = self.grid
        n = g.tiles
        coef = self.coef(i, [n])
        _, re, im = g.apply(self.s, i, i - 1, i + 1, -1, coef, [n])
        for p, value in enumerate((re, im)):
            self.v0[p, i, g.tile(n), :] = (value[n] + terms[p][n]) * g.inside
            halo = self.s[p, i, g.tile(n), :]
            low = jnp.where(g.bottom, pltpu.roll(halo, 1, axis=0), 0.0)
            high = jnp.where(g.top, pltpu.roll(halo, 7, axis=0), 0.0)
            for t, change in ((0, low), (n - 1, high)):
                at = g.tile(t)
                self.v0[p, i, at, :] = self.v0[p, i, at, :] - change

    def step(self, stage, i, lo, hi, cut=None, acc=None):
        g = self.grid
        src = (None, self.v0, self.u0, self.v1)[stage]
        dst = (None, self.u0, self.v1, self.u1)[stage]
        tiles = g.own if stage == 3 else g.both
        sign = -1 if stage == 2 else 1
        mids, re, im = g.apply(src, i, lo, hi, sign, self.coef(i, tiles), tiles, True, cut)
        if stage != 3:
            weight = {t: self.w[i, t] for t in tiles}
        if stage == 2:
            for p, out in enumerate((re, im)):
                for t in tiles:
                    out[t] = out[t] + weight[t] * self.v0[p, i, g.tile(t), :]
        if stage != 3:
            re[g.tiles] = re[g.tiles] * g.inside
            im[g.tiles] = im[g.tiles] * g.inside
        g.put(dst, 0, i, re, tiles)
        g.put(dst, 1, i, im, tiles)
        if acc is None:
            return None
        acc = list(acc)
        squares = g.squares(re, im)
        acc[stage] = acc[stage] + g.gather(squares)
        if stage == 1:
            squares = g.squares(*mids)
            acc[0] = acc[0] + g.gather(squares)
        if stage != 3:
            at = 1 if stage == 1 else 3
            weighted = {t: weight[t] * squares[t] for t in g.own}
            acc[at] = acc[at] + g.gather(weighted)
        return tuple(acc)


def early_kernel(freqs, nx, ny, freq_sq, *refs):
    s, (cells, aux), refs = refs[:freqs], refs[freqs : freqs + 2], refs[freqs + 2 :]
    w, splat = refs[3 * freqs :]
    nz = cells.shape[2]
    for f in range(freqs):
        splat[f] = jnp.full((8, nz), freq_sq[f], F32)
    grid = Grid(nx, ny, nz)
    many = [
        Field(grid, (s[f], refs[3 * f], None, None, None, *refs[3 * f + 1 : 3 * f + 3]), w)
        for f in range(freqs)
    ]

    def prepare(i):
        return grid.prepare(
            i,
            grid.own,
            freq_sq,
            w,
            many,
            lambda t: cells[i, grid.tile(t), :],
            lambda k, t: grid.pick(aux, k, t, i),
        )

    for i in (0, nx - 1):
        terms = prepare(i)
        for f in range(freqs):
            for p in range(2):
                grid.put(many[f].v0, p, i, terms[f][p], grid.own)

    def row(i):
        terms = prepare(i)
        for f in range(freqs):
            field = many[f]
            _, re, im = grid.apply(
                field.s, i, i - 1, i + 1, -1, field.coef(i, grid.own), grid.own, False
            )
            for p, value in enumerate((re, im)):
                value = {t: value[t] + terms[f][p][t] for t in grid.own}
                grid.put(field.v0, p, i, value, grid.own)

    def pair(k, _):
        row(2 * k + 1)
        row(2 * k + 2)
        return 0

    lax.fori_loop(0, (nx - 2) // 2, pair, 0)


def early(nx, ny, freq_sq, s, cells, aux):
    freqs = len(s)
    _, xe, _, nz = s[0].shape
    field = pltpu.VMEM(s[0].shape, F32)
    coef = pltpu.VMEM((xe, ny // 8 + 1, 8, nz), F32)
    return pl.pallas_call(
        functools.partial(early_kernel, freqs, nx, ny),
        out_shape=(field, coef, coef) * freqs
        + (coef, pltpu.VMEM((freqs, 8, nz), F32)),
        in_specs=[SMEM] + [VMEM] * (freqs + 2),
        compiler_params=params(8),
        name="early",
    )(freq_sq, *s, cells, aux)


def corner_faces(freqs, nx, ny, s, cells, aux, ce, co):
    fields = 2 * freqs
    nz = cells.shape[2]
    sub = lax.broadcasted_iota(jnp.int32, (2 * HALO, nz), 0)
    even_x = parity("gx")
    near = [aux[k, ny:, :] for k in range(fields + 1)]
    for side, cb in enumerate((ce, co)):
        last = even_x if side == 0 else jnp.logical_not(even_x)
        at = [jnp.where(last, nx - d, d - 1) for d in range(1, HALO)]
        for k in range(fields):
            one, two, three = (s[k // 2][k % 2, x, ny:, :] for x in at)
            one = jnp.where(sub == 3, pltpu.roll(three, 3, axis=0), one)
            cb[k] = jnp.where(sub == 4, pltpu.roll(three, 5, axis=0), one)
            if k % 2 == 0:
                kept = two
                continue
            two = jnp.where(
                sub < 4, pltpu.roll(two, 2, axis=0), pltpu.roll(two, 6, axis=0)
            )
            outer = (sub < 2) | (sub > 5)
            cb[fields + k // 2] = jnp.where(outer, kept, two)
        one, two = cells[at[0], ny:, :], cells[at[1], ny:, :]
        one = jnp.where(sub == 2, pltpu.roll(two, 2, axis=0), one)
        cb[fields + freqs] = jnp.where(sub == 5, pltpu.roll(two, 6, axis=0), one)
        skip = jnp.where(last, nx - INNER, 0)
        cb[fields + freqs + 1] = lane_slab(near, fields, skip, 2 * HALO, nz)


def place_corners(freqs, nx, ny, cb, s, cells, aux, above):
    fields = 2 * freqs
    nz = cb.shape[2]
    sub = lax.broadcasted_iota(jnp.int32, (2 * HALO, nz), 0)
    slot = [jnp.where(above, nx + d - 1, nx + 2 * HALO - d) for d in range(1, HALO)]
    layer = [jnp.where(above, d - 1, INNER - d) for d in range(1, HALO)]
    for k in range(fields):
        field, p = s[k // 2], k % 2
        one = cb[k]
        field[p, slot[0], ny:, :] = one
        field[p, slot[2], ny:, :] = jnp.where(
            sub == 0, pltpu.roll(one, 5, axis=0), pltpu.roll(one, 3, axis=0)
        )
        two = cb[fields + k // 2]
        if p:
            two = jnp.where(
                sub < 4, pltpu.roll(two, 6, axis=0), pltpu.roll(two, 2, axis=0)
            )
        field[p, slot[1], ny:, :] = two
    one = cb[fields + freqs]
    cells[layer[0], ny:, :] = one
    cells[layer[1], ny:, :] = jnp.where(
        sub == 0, pltpu.roll(one, 6, axis=0), pltpu.roll(one, 2, axis=0)
    )
    cells[layer[2], ny:, :] = jnp.zeros((2 * HALO, nz), F32)
    aux[ny:, :] = cb[fields + freqs + 1]


def inner_kernel(freqs, nx, ny, half, freq_sq, *refs):
    if half == 0:
        ye, yo = refs[:2]
        count = 4 * freqs + 3
        refs = refs[2 + count :]
        s, (cells, aux), refs = refs[:freqs], refs[freqs : freqs + 2], refs[freqs + 2 :]
        known, refs = refs[: 3 * freqs + 1], refs[3 * freqs + 1 :]
        news, (moments, ce, co) = refs[: 3 * freqs], refs[3 * freqs :]
    else:
        s, known = refs[:freqs], refs[freqs : 4 * freqs + 1]
        partial = refs[7 * freqs + 1]
        refs = refs[7 * freqs + 2 :]
        news, (moments,) = refs[: 3 * freqs], refs[3 * freqs :]
    nz = s[0].shape[3]
    fields = 2 * freqs
    w = known[3 * freqs]
    grid = Grid(nx, ny, nz)
    many = []
    for f in range(freqs):
        v0, cr, ci = known[3 * f : 3 * f + 3]
        u0, v1, u1 = news[3 * f : 3 * f + 3]
        many.append(Field(grid, (s[f], v0, u0, v1, u1, cr, ci), w))
    if half == 0:
        swapped = jnp.broadcast_to(parity("gy"), (HALO, nz))

        def halo(at):
            even, odd = ye[at], yo[at]
            high = jnp.where(swapped, even, odd) * grid.right
            low = jnp.where(swapped, odd, even) * grid.left
            return jnp.concatenate([high, low], axis=0)

        sub = lax.broadcasted_iota(jnp.int32, (8, nz), 0)

        def model_rows(g, _):
            tiles = [halo(fields * nx + 3 * g + j) for j in range(3)]
            last = tiles[0]
            for j in range(3):
                cells[4 * g + j, ny:, :] = tiles[j]
                last = jnp.where(sub == j, pltpu.roll(tiles[j], 5 + j, axis=0), last)
                last = jnp.where(sub == 5 + j, pltpu.roll(tiles[j], 1 + j, axis=0), last)
            cells[4 * g + 3, ny:, :] = last
            return 0

        def merge(x, _):
            for k in range(fields):
                s[k // 2][k % 2, x, ny:, :] = halo(k * nx + x)
            return 0

        lax.fori_loop(0, nx // 4, model_rows, 0, unroll=2)
        lax.fori_loop(0, nx, merge, 0, unroll=4)
        for k in range(fields + 1):
            slab, g = divmod(k, nz // nx)
            tile = halo(fields * nx + nx // 4 * 3 + slab)
            aux[k, ny:, :] = pltpu.roll(tile, (nz - g * nx) % nz, axis=1) if g else tile
        corner_faces(freqs, nx, ny, s, cells, aux, ce, co)

    def prepare(i):
        return grid.prepare(
            i,
            [grid.tiles],
            freq_sq,
            w,
            many,
            lambda t: cells[i, grid.tile(t), :],
            lambda k, t: grid.pick(aux, k, t, i),
        )

    if half == 0:
        for i in (0, nx - 1):
            terms = prepare(i)
            for f in range(freqs):
                for p in range(2):
                    grid.put(many[f].v0, p, i, terms[f][p], [grid.tiles])

    def step(j, acc, active):
        acc = list(acc)
        for k in reversed(active):
            i = j - 2 * k
            if k == 0:
                terms = prepare(i)
            for f in range(freqs):
                if k == 0:
                    many[f].first_halo(i, terms[f])
                else:
                    acc[f] = many[f].step(k, i, i - 1, i + 1, acc=acc[f])
        return tuple(acc)

    def heads(i, _):
        terms = prepare(i)
        for f in range(freqs):
            many[f].first_halo(i, terms[f])
        return 0

    spans = [(1 + 3 * k, nx - 1 + k) for k in range(4)]
    middle = nx // 2 + SHIFT
    edges = sorted({e for span in spans for e in span} | {middle})
    acc = tuple(tuple(grid.zero() for _ in range(4)) for _ in range(freqs))
    if half == 0:
        lax.fori_loop(1, nx - 1, heads, 0, unroll=3)
    for lo, hi in zip(edges[:-1], edges[1:]):
        if (lo < middle) != (half == 0):
            continue
        active = [k for k, (a, b) in enumerate(spans) if k and a <= lo and hi <= b]
        if active:
            acc = lax.fori_loop(lo, hi, functools.partial(step, active=active), acc)
    for f in range(freqs):
        for m in range(4):
            value = acc[f][m]
            moments[f, m] = value if half == 0 else value + partial[f, m]


def inner_part(nx, ny, freq_sq, ye, yo, s, cells, aux, known):
    freqs = len(s)
    nz = cells.shape[2]
    slabs = 3 * freqs + 2
    field = pltpu.VMEM(s[0].shape, F32)
    corner = pltpu.VMEM((slabs, 2 * HALO, nz), F32)
    kept = (*s, cells, aux, *known)
    news = (field,) * (3 * freqs) + (pltpu.VMEM((freqs, 4, 8, nz), F32),)
    got = pl.pallas_call(
        functools.partial(inner_kernel, freqs, nx, ny, 0),
        out_shape=tuple(pltpu.VMEM(k.shape, F32) for k in kept)
        + news
        + (corner, corner),
        in_specs=[VMEM] * (3 + len(kept)),
        input_output_aliases={3 + k: k for k in range(len(kept))},
        compiler_params=params(8),
        name="inner_first",
    )(freq_sq, ye, yo, *kept)
    s, known = got[:freqs], got[freqs + 2 : len(kept)]
    news_got, (ce, co) = got[len(kept) : -2], got[-2:]

    def rest():
        first = freqs + len(known)
        again = pl.pallas_call(
            functools.partial(inner_kernel, freqs, nx, ny, 1, None),
            out_shape=news,
            in_specs=[VMEM] * (freqs + len(known) + len(news)),
            input_output_aliases={first + k: k for k in range(len(news))},
            compiler_params=params(8),
            name="inner_second",
        )(*s, *known, *news_got)
        state = []
        for f in range(freqs):
            v0, cr, ci = known[3 * f : 3 * f + 3]
            state += [s[f], v0, *again[3 * f : 3 * f + 3], cr, ci]
        return state + [known[-1]], again[-1]

    return ce, co, rest


def edge_kernel(peers, freqs, nx, ny, freq_sq, xe, xo, ce, co, *refs):
    count = 7 * freqs + 1
    moments, refs = refs[count], refs[count + 1 :]
    state, (part, cells, aux) = refs[:count], refs[count:]
    fields = 2 * freqs
    nz = state[0].shape[3]
    w = state[-1]
    even_x = parity("gx")
    group = nz // 8
    for side, (xb, cb) in enumerate(((xe, ce), (xo, co))):
        above = even_x if side == 0 else jnp.logical_not(even_x)
        slot = jnp.where(above, nx, nx + HALO)
        half = jnp.where(above, 0, 1)
        for layer in range(HALO):
            for k in range(fields):
                block = state[7 * (k // 2)]
                for y in range(0, ny, 8):
                    row = (k * HALO + layer) * ny + y
                    block[k % 2, slot + layer, y : y + 8, :] = xb[row : row + 8, :]
            if layer < INNER:
                for y in range(0, ny, 8):
                    row = (fields * HALO + layer) * ny + y
                    cells[half, layer, y : y + 8, :] = xb[row : row + 8, :]
        at = (fields * HALO + INNER) * ny
        folded = xb[at : at + ny // 8, :]
        for g in range(8):
            rows = pl.ds(g * (ny // 8), ny // 8)
            aux[half, rows, :] = pltpu.roll(folded, (nz - g * group) % nz, axis=1)
        place_corners(
            freqs, nx, ny, cb, state[: 7 * freqs : 7], cells.at[half], aux.at[half], above
        )
    for k in range(fields):
        for i in (nx + HALO - 1, nx + HALO):
            state[7 * (k // 2)][k % 2, i, ny:, :] = jnp.zeros((2 * HALO, nz), F32)
    grid = Grid(nx, ny, nz)
    many = [Field(grid, state[7 * f : 7 * f + 7], w) for f in range(freqs)]
    for half in range(2):
        for layer in range(INNER):
            i = nx + layer if half == 0 else nx + HALO + 1 + layer
            terms = grid.prepare(
                i,
                grid.both,
                freq_sq,
                w,
                many,
                lambda t: cells[half, layer, grid.tile(t), :],
                lambda k, t: grid.pick(aux, half, t, INNER * k + layer),
            )
            for f in range(freqs):
                for p in range(2):
                    grid.put(many[f].v0, p, i, terms[f][p], grid.both)

    left = jnp.where(lax.axis_index("gx") > 0, 1.0, 0.0)
    right = jnp.where(lax.axis_index("gx") < lax.axis_size("gx") - 1, 1.0, 0.0)
    wrap = grid.xe
    acc = [tuple(grid.zero() for _ in range(4)) for _ in range(freqs)]
    for stage in range(4):
        for k in range(HALO):
            for x in (k - INNER + stage, nx - 1 - stage + k):
                i, lo, hi = x % wrap, (x - 1) % wrap, (x + 1) % wrap
                own = 0 <= x < nx
                cut = None
                if x == 0:
                    cut = (-1, left)
                if x == nx - 1:
                    cut = (1, right)
                for f in range(freqs):
                    if stage == 0:
                        many[f].finish(i, grid.both, True, lo, hi, cut)
                        continue
                    got = many[f].step(
                        stage, i, lo, hi, cut, acc[f] if own else None
                    )
                    if own:
                        acc[f] = got

    rows = []
    for f in range(freqs):
        for m in range(4):
            both = acc[f][m] + moments[f, m]
            rows.append(jnp.sum(both, axis=0, keepdims=True))
    sums = jnp.sum(jnp.concatenate(rows, axis=0), axis=1, keepdims=True)
    sums = jnp.broadcast_to(sums, (4 * freqs, nz))
    for peer in range(peers):
        part[peer] = sums


def edge_part(peers, freqs, nx, ny, freq_sq, xe, xo, ce, co, state, moments):
    nz = state[0].shape[3]
    outs = tuple(pltpu.VMEM(k.shape, F32) for k in state)
    return pl.pallas_call(
        functools.partial(edge_kernel, peers, freqs, nx, ny),
        out_shape=outs + (jax.ShapeDtypeStruct((peers, 4 * freqs, nz), F32),),
        in_specs=[VMEM] * (6 + len(state)),
        input_output_aliases={5 + k: k for k in range(len(state))},
        scratch_shapes=[
            pltpu.VMEM((2, INNER, ny + 2 * HALO, nz), F32),
            pltpu.VMEM((2, ny + 2 * HALO, nz), F32),
        ],
        compiler_params=params(8),
        name="edge_part",
    )(freq_sq, xe, xo, ce, co, *state, moments)


def steps(sums, freqs):
    total = jnp.sum(sums[...], axis=0)
    shape = (8, total.shape[1])
    out = []
    for f in range(freqs):
        m0, m1, m2, m3 = (
            jnp.broadcast_to(total[4 * f + k : 4 * f + k + 1, :], shape)
            for k in range(4)
        )
        first = m0 / m1
        new = first * (first * m2 - m1)
        product = m1 - first * (2.0 * m2 - first * m3)
        ratio = new / m0
        second = new / (product - ratio * new / first)
        out.append((first + second * (1.0 + ratio), -first * second))
    return out


def gradient_kernel(freqs, nx, ny, freq_sq, sums, *refs):
    out = refs[-1]
    weights = steps(sums, freqs)
    scale = [-freq_sq[f] for f in range(freqs)]

    def row(x, _):
        for y in range(0, ny, 8):
            at = pl.ds(y, 8)
            total = None
            for f in range(freqs):
                s, v0, u0, v1, u1 = refs[5 * f : 5 * f + 5]
                a, b = weights[f]
                wave_re = a * v0[0, x, at, :] + b * v1[0, x, at, :]
                wave_im = a * v0[1, x, at, :] + b * v1[1, x, at, :]
                miss_re = a * u0[0, x, at, :] + b * u1[0, x, at, :]
                miss_im = a * u0[1, x, at, :] + b * u1[1, x, at, :]
                miss_re = miss_re - s[0, x, at, :]
                miss_im = miss_im - s[1, x, at, :]
                left = (wave_re + attenuation * wave_im) * miss_re
                right = (wave_im - attenuation * wave_re) * miss_im
                term = scale[f] * (left + right)
                total = term if total is None else total + term
            out[x, at, :] = total
        return 0

    lax.fori_loop(0, nx, row, 0, unroll=2)


def wave_kernel(freqs, nx, ny, sums, *refs):
    out, block, sem = refs[2 * freqs :]
    weights = steps(sums, freqs)
    copies = Copies(sem)
    for f in range(freqs):
        a, b = weights[f]
        v0, v1 = refs[2 * f : 2 * f + 2]
        for p in range(2):
            k = 2 * f + p

            def row(x, _):
                for y in range(0, ny, 8):
                    at = pl.ds(y, 8)
                    block[k, x, at, :] = a * v0[p, x, at, :] + b * v1[p, x, at, :]
                return 0

            lax.fori_loop(0, nx, row, 0, unroll=8)
            copies.add(block.at[k], out.at[f, p])
    copies.wait()


def results(freqs, nx, ny, freq_sq, sums, state):
    nz = state[0].shape[3]
    fields, pairs = [], []
    for f in range(freqs):
        s, v0, u0, v1, u1 = state[7 * f : 7 * f + 5]
        fields += [s, v0, u0, v1, u1]
        pairs += [v0, v1]
    gradient = pl.pallas_call(
        functools.partial(gradient_kernel, freqs, nx, ny),
        out_shape=jax.ShapeDtypeStruct((nx, ny, nz), F32),
        in_specs=[VMEM] * (2 + len(fields)),
        out_specs=VMEM,
        compiler_params=params(8),
        name="gradient_part",
    )(freq_sq, sums, *fields)
    wave = pl.pallas_call(
        functools.partial(wave_kernel, freqs, nx, ny),
        out_shape=jax.ShapeDtypeStruct((freqs, 2, nx, ny, nz), F32),
        in_specs=[VMEM] * (1 + len(pairs)),
        out_specs=HBM,
        scratch_shapes=[
            pltpu.VMEM((2 * freqs, nx, ny, nz), F32),
            pltpu.SemaphoreType.DMA((2 * freqs,)),
        ],
        compiler_params=params(8),
        name="wavefield",
    )(sums, *pairs)
    return gradient, wave


def add_kernel(one, two, out, block, sem):
    nx, ny, _ = one.shape
    copies = Copies(sem)
    parts = sem.shape[0]
    step = nx // parts
    for part in range(parts):

        def row(x, _):
            for y in range(0, ny, 8):
                at = pl.ds(y, 8)
                block[x, at, :] = one[x, at, :] + two[x, at, :]
            return 0

        lax.fori_loop(part * step, (part + 1) * step, row, 0, unroll=4)
        span = pl.ds(part * step, step)
        copies.add(block.at[span], out.at[span])
    copies.wait()


def add(one, two):
    return pl.pallas_call(
        add_kernel,
        out_shape=jax.ShapeDtypeStruct(one.shape, F32),
        in_specs=[VMEM] * 2,
        out_specs=HBM,
        scratch_shapes=[pltpu.VMEM(one.shape, F32), pltpu.SemaphoreType.DMA((2,))],
        compiler_params=params(4),
        name="add",
    )(one, two)


def swap(cells, axis, odd):
    names = ("gx", "gy", "af")
    sizes = [lax.axis_size(name) for name in names]
    along = names.index(axis)
    pairs = []
    for flat in range(sizes[0] * sizes[1] * sizes[2]):
        place = [flat // (sizes[1] * sizes[2]), flat // sizes[2] % sizes[1], flat % sizes[2]]
        mate = ((place[along] + odd) ^ 1) - odd
        if 0 <= mate < sizes[along]:
            place[along] = mate
        elif sizes[2] % 2 == 0:
            place[2] ^= 1
        else:
            continue
        pairs.append((flat, (place[0] * sizes[1] + place[1]) * sizes[2] + place[2]))
    return lax.ppermute(cells, names, pairs)


def on_device(model, freq_sq, source, observed, receiver_depth):
    nx, ny, nz = model.shape
    freqs = freq_sq.shape[0]
    *s, cells, aux, xe, xo, ye, yo = load(source, model, observed, receiver_depth)
    ye, yo = swap(ye, "gy", 0), swap(yo, "gy", 1)
    xe, xo = swap(xe, "gx", 0), swap(xo, "gx", 1)
    *known, splat = early(nx, ny, freq_sq, s, cells, aux)
    ce, co, rest = inner_part(nx, ny, splat, ye, yo, s, cells, aux, known)
    ce, co = swap(ce, "gx", 0), swap(co, "gx", 1)
    state, moments = rest()
    peers = lax.axis_size("gx") * lax.axis_size("gy")
    *state, part = edge_part(
        peers, freqs, nx, ny, splat, xe, xo, ce, co, state, moments
    )
    sums = lax.all_to_all(part, ("gx", "gy"), 0, 0)
    gradient, wave = results(freqs, nx, ny, splat, sums, state)
    if lax.axis_size("af") == 2:
        gradient = add(gradient, lax.ppermute(gradient, "af", [(0, 1), (1, 0)]))
    else:
        gradient = lax.psum(gradient, "af")
    return wave, gradient


def solution(mesh):
    in_specs = (
        P("gx", "gy", None),
        P("af"),
        P("af", None, "gx", "gy", None),
        P("af", None, "gx", "gy"),
        P("gx", "gy"),
    )
    out_specs = (P("af", None, "gx", "gy", None), P("gx", "gy", None))
    return jax.shard_map(
        on_device, mesh=mesh, in_specs=in_specs, out_specs=out_specs, check_vma=False
    )
```

```python
import functools

import jax
import jax.numpy as jnp
from jax import lax
from jax.experimental import pallas as pl
from jax.experimental.pallas import tpu as pltpu
from jax.sharding import PartitionSpec as P

ITERS = 2
attenuation = 0.2
penalty = 4.0

HALO = 2 * ITERS
INNER = HALO - 1
F32 = jnp.float32
ANY = pl.BlockSpec(memory_space=pl.ANY)
HBM = pl.BlockSpec(memory_space=pltpu.HBM)
VMEM = pl.BlockSpec(memory_space=pltpu.VMEM)
SMEM = pl.BlockSpec(memory_space=pltpu.SMEM)
MIB = 1 << 20
LOAD_MIB = 55
SHIFT = -4


def params(mib):
    return pltpu.CompilerParams(vmem_limit_bytes=mib * MIB)


def cost(us):
    return pl.CostEstimate(
        flops=int(us * 1e3), bytes_accessed=int(us * 1e3), transcendentals=0
    )


def parity(axis):
    return lax.rem(lax.axis_index(axis), 2) == 0


class Copies:
    def __init__(self, sem):
        self.sem, self.all = sem, []

    def add(self, src, dst):
        copy = pltpu.make_async_copy(src, dst, self.sem.at[len(self.all)])
        copy.start()
        self.all.append(copy)

    def wait(self):
        for copy in self.all:
            copy.wait()


def lane_slab(table, fields, skip, rows, nz):
    lane = lax.broadcasted_iota(jnp.int32, (rows, nz), 1)
    lanes = jnp.zeros((rows, nz), F32)
    for k in range(fields + 1):
        inside = (lane >= INNER * k) & (lane < INNER * k + INNER)
        shift = lax.rem(INNER * k + nz - skip, nz)
        lanes = jnp.where(inside, pltpu.roll(table[k], shift, axis=1), lanes)
    return lanes


def fold(slab, nz):
    rows, width = slab.shape[0] // 8, nz // 8
    lane = lax.broadcasted_iota(jnp.int32, (rows, nz), 1)
    out = jnp.zeros((rows, nz), F32)
    for g in range(8):
        piece = slab[g * rows : (g + 1) * rows, :]
        inside = (lane >= g * width) & (lane < (g + 1) * width)
        out = jnp.where(inside, pltpu.roll(piece, g * width, axis=1), out)
    return out


def load_kernel(source, model, observed, depth, *refs):
    freqs, _, nx, ny, nz = source.shape
    fields = 2 * freqs
    s, (cells, aux, xe, xo, ye, yo, seen, sunk, table, sem) = refs[:freqs], refs[freqs:]
    small = Copies(sem.at[0])
    small.add(observed, seen)
    small.add(depth, sunk)
    large = Copies(sem.at[1])
    large.add(model, cells.at[:, pl.ds(0, ny), :])
    for f in range(freqs):
        for p in range(2):
            large.add(source.at[f, p], s[f].at[p, pl.ds(0, nx), pl.ds(0, ny), :])
    even_x, even_y = parity("gx"), parity("gy")
    small.wait()
    for f in range(freqs):
        for p in range(2):
            table[2 * f + p, :, 0:nx] = seen[f, p].T
    table[fields, :, 0:nx] = sunk[...].astype(F32).T
    copies = Copies(sem.at[2])
    copies.add(table, aux.at[:, pl.ds(0, ny), :])
    faces = []
    for side, xb in enumerate((xe, xo)):
        last = even_x if side == 0 else jnp.logical_not(even_x)
        skip = jnp.where(last, nx - INNER, 0)
        faces.append((xb, skip, jnp.where(last, nx - HALO, 0)))
        at = (fields * HALO + INNER) * ny
        xb[at : at + ny // 8, :] = fold(lane_slab(table, fields, skip, ny, nz), nz)
    swapped = jnp.broadcast_to(even_y, (HALO, nz))

    def y_faces(block, at):
        def row(x, _):
            head, tail = block[x, 0:HALO, :], block[x, ny - HALO : ny, :]
            ye[at + x] = jnp.where(swapped, tail, head)
            yo[at + x] = jnp.where(swapped, head, tail)
            return 0

        lax.fori_loop(0, nx, row, 0, unroll=8)

    def x_face(xb, to, block, at, layers):
        for layer in range(layers):
            for y in range(0, ny, 8):
                row = (to + layer) * ny + y
                xb[row : row + 8, :] = block[at + layer, y : y + 8, :]

    lane = lax.broadcasted_iota(jnp.int32, (HALO, nz), 1)
    at = fields * nx + nx // 4 * 3
    for slab in range(-(-(fields + 1) // (nz // nx))):
        pair = [jnp.zeros((HALO, nz), F32)] * 2
        for g in range(nz // nx):
            k = slab * (nz // nx) + g
            if k > fields:
                continue
            inside = (lane >= g * nx) & (lane < (g + 1) * nx)
            for end, rows in enumerate((table[k, 0:HALO, :], table[k, ny - HALO : ny, :])):
                moved = pltpu.roll(rows, g * nx, axis=1)
                pair[end] = jnp.where(inside, moved, pair[end])
        ye[at + slab] = jnp.where(swapped, pair[1], pair[0])
        yo[at + slab] = jnp.where(swapped, pair[0], pair[1])
    large.all[0].wait()
    sub = lax.broadcasted_iota(jnp.int32, (8, nz), 0)

    def model_rows(g, _):
        heads = [cells[4 * g + j, 0:8, :] for j in range(4)]
        tails = [cells[4 * g + j, ny - 8 : ny, :] for j in range(4)]
        for j in range(3):
            head = jnp.where(sub == 3, pltpu.roll(heads[3], 3 - j, axis=0), heads[j])
            tail = jnp.where(sub == 4, pltpu.roll(tails[3], 7 - j, axis=0), tails[j])
            head, tail = head[0:HALO, :], tail[8 - HALO : 8, :]
            ye[fields * nx + 3 * g + j] = jnp.where(swapped, tail, head)
            yo[fields * nx + 3 * g + j] = jnp.where(swapped, head, tail)
        return 0

    lax.fori_loop(0, nx // 4, model_rows, 0, unroll=2)
    for xb, skip, _ in faces:
        x_face(xb, fields * HALO, cells, skip, INNER)
    for k in range(fields):
        large.all[1 + k].wait()
        block = s[k // 2].at[k % 2]
        y_faces(block, k * nx)
        for xb, _, at in faces:
            x_face(xb, k * HALO, block, at, HALO)
    copies.wait()


def load(source, model, observed, depth):
    freqs, _, nx, ny, nz = source.shape
    fields = 2 * freqs
    xs = pltpu.VMEM(((fields * HALO + INNER) * ny + 8, nz), F32)
    slabs = fields * nx + nx // 4 * 3 + -(-(fields + 1) // (nz // nx))
    ys = pltpu.VMEM((slabs, HALO, nz), F32)
    return pl.pallas_call(
        load_kernel,
        out_shape=(pltpu.VMEM((2, nx + 2 * HALO, ny + 2 * HALO, nz), F32),) * freqs
        + (
            pltpu.VMEM((nx, ny + 2 * HALO, nz), F32),
            pltpu.VMEM((fields + 1, ny + 2 * HALO, nz), F32),
            xs,
            xs,
            ys,
            ys,
        ),
        in_specs=[HBM] * 4,
        scratch_shapes=[
            pltpu.VMEM(observed.shape, F32),
            pltpu.VMEM(depth.shape, jnp.int32),
            pltpu.VMEM((fields + 1, ny, nz), F32),
            pltpu.SemaphoreType.DMA((3, 32)),
        ],
        compiler_params=params(LOAD_MIB),
        name="load",
    )(source, model, observed, depth)


class Grid:
    def __init__(self, nx, ny, nz):
        self.nx, self.ny, self.nz = nx, ny, nz
        self.xe = nx + 2 * HALO
        self.tiles = ny // 8
        self.own = range(self.tiles)
        self.both = range(self.tiles + 1)
        lane = lax.broadcasted_iota(jnp.int32, (8, nz), 1)
        self.first = lane == 0
        self.last = lane == nz - 1
        self.depths = lane.astype(F32)
        sub = lax.broadcasted_iota(jnp.int32, (8, nz), 0)
        self.top = sub == 7
        self.bottom = sub == 0
        has_left = lax.axis_index("gy") > 0
        has_right = lax.axis_index("gy") < lax.axis_size("gy") - 1
        self.left = jnp.where(has_left, 1.0, 0.0)
        self.right = jnp.where(has_right, 1.0, 0.0)
        self.inside = jnp.where(sub < HALO, self.right, self.left)

    def tile(self, t):
        if t < self.tiles:
            return pl.ds(t, 8, stride=self.tiles)
        return pl.ds(self.ny, 8)

    def rows(self, ref, p, i, tiles):
        return [ref[p, i, self.tile(t), :] for t in tiles]

    def put(self, ref, p, i, values, tiles):
        for t in tiles:
            ref[p, i, self.tile(t), :] = values[t]

    def beside(self, mid):
        left = jnp.where(self.first, 0.0, pltpu.roll(mid, 1, axis=1))
        right = jnp.where(self.last, 0.0, pltpu.roll(mid, self.nz - 1, axis=1))
        return left + right

    def around(self, mid, below, above, tiles):
        n = self.tiles
        halo = mid[n] if len(mid) > n else None
        first_up = pltpu.roll(mid[0], 7, axis=0)
        last_down = pltpu.roll(mid[n - 1], 1, axis=0)
        if halo is not None:
            halo_up = pltpu.roll(halo, 7, axis=0)
            halo_down = pltpu.roll(halo, 1, axis=0)
        total = {}
        for t in tiles:
            if t == n:
                up = jnp.where(self.top, first_up, halo_up)
                down = jnp.where(self.bottom, last_down, halo_down)
            else:
                up = mid[t + 1] if t + 1 < n else None
                down = mid[t - 1] if t else None
                if up is None:
                    edge = 0.0 if halo is None else halo_up
                    up = jnp.where(self.top, edge, first_up)
                if down is None:
                    edge = 0.0 if halo is None else halo_down
                    down = jnp.where(self.bottom, edge, last_down)
            total[t] = ((below[t] + above[t]) + (up + down)) + self.beside(mid[t])
        return total

    def apply(self, src, i, lo, hi, sign, coef, tiles, wide=True, cut=None):
        cr, ci = coef
        mids, totals = [], []
        for p in range(2):
            mid = self.rows(src, p, i, self.both if wide else self.own)
            below = {t: src[p, lo, self.tile(t), :] for t in tiles}
            above = {t: src[p, hi, self.tile(t), :] for t in tiles}
            if cut is not None and cut[0] < 0:
                below = {t: v * cut[1] for t, v in below.items()}
            if cut is not None and cut[0] > 0:
                above = {t: v * cut[1] for t, v in above.items()}
            mids.append(mid)
            totals.append(self.around(mid, below, above, tiles))
        out_re, out_im = {}, {}
        for t in tiles:
            re, im = mids[0][t], mids[1][t]
            if sign > 0:
                out_re[t] = cr[t] * re - ci[t] * im - totals[0][t]
                out_im[t] = cr[t] * im + ci[t] * re - totals[1][t]
            else:
                out_re[t] = cr[t] * re + ci[t] * im - totals[0][t]
                out_im[t] = cr[t] * im - ci[t] * re - totals[1][t]
        return mids, out_re, out_im

    def squares(self, re, im):
        return {t: re[t] * re[t] + im[t] * im[t] for t in self.own}

    def gather(self, values):
        return functools.reduce(jnp.add, [values[t] for t in self.own])

    def zero(self):
        return jnp.zeros((8, self.nz), F32)

    def prepare(self, i, tiles, freq_sq, w, many, cell, column):
        fields = 2 * len(many)
        weight = {}
        for t in tiles:
            depth = column(fields, t)
            weight[t] = jnp.where(self.depths == depth, penalty, 0.0)
            w[i, t] = weight[t]
        out = []
        for f, field in enumerate(many):
            for t in tiles:
                scaled = freq_sq[f] * cell(t)
                field.cr[i, t] = 6.0 - scaled
                field.ci[i, t] = attenuation * scaled
            out.append(
                [
                    {t: weight[t] * column(2 * f + p, t) for t in tiles}
                    for p in range(2)
                ]
            )
        return out

    def pick(self, ref, t, lane):
        at = jnp.full((8, self.nz), lane, jnp.int32)
        return jnp.take_along_axis(ref[self.tile(t), :], at, axis=1)


class Field:
    def __init__(self, grid, refs, w):
        self.grid = grid
        self.s, self.v0, self.u0, self.v1, self.u1, self.cr, self.ci = refs
        self.w = w

    def coef(self, i, tiles):
        return {t: self.cr[i, t] for t in tiles}, {t: self.ci[i, t] for t in tiles}

    def finish(self, i, tiles, wide, lo=None, hi=None, cut=None):
        g = self.grid
        _, re, im = g.apply(self.s, i, lo, hi, -1, self.coef(i, tiles), tiles, wide, cut)
        for p, value in enumerate((re, im)):
            for t in tiles:
                at = g.tile(t)
                total = self.v0[p, i, at, :] + value[t]
                self.v0[p, i, at, :] = total * g.inside if t == g.tiles else total

    def first_halo(self, i, terms):
        g = self.grid
        n = g.tiles
        coef = self.coef(i, [n])
        _, re, im = g.apply(self.s, i, i - 1, i + 1, -1, coef, [n])
        for p, value in enumerate((re, im)):
            self.v0[p, i, g.tile(n), :] = (value[n] + terms[p][n]) * g.inside
            halo = self.s[p, i, g.tile(n), :]
            low = jnp.where(g.bottom, pltpu.roll(halo, 1, axis=0), 0.0)
            high = jnp.where(g.top, pltpu.roll(halo, 7, axis=0), 0.0)
            for t, change in ((0, low), (n - 1, high)):
                at = g.tile(t)
                self.v0[p, i, at, :] = self.v0[p, i, at, :] - change

    def step(self, stage, i, lo, hi, cut=None, acc=None):
        g = self.grid
        src = (None, self.v0, self.u0, self.v1)[stage]
        dst = (None, self.u0, self.v1, self.u1)[stage]
        tiles = g.own if stage == 3 else g.both
        sign = -1 if stage == 2 else 1
        mids, re, im = g.apply(src, i, lo, hi, sign, self.coef(i, tiles), tiles, True, cut)
        if stage != 3:
            weight = {t: self.w[i, t] for t in tiles}
        if stage == 2:
            for p, out in enumerate((re, im)):
                for t in tiles:
                    out[t] = out[t] + weight[t] * self.v0[p, i, g.tile(t), :]
        if stage != 3:
            re[g.tiles] = re[g.tiles] * g.inside
            im[g.tiles] = im[g.tiles] * g.inside
        g.put(dst, 0, i, re, tiles)
        g.put(dst, 1, i, im, tiles)
        if acc is None:
            return None
        acc = list(acc)
        squares = g.squares(re, im)
        acc[stage] = acc[stage] + g.gather(squares)
        if stage == 1:
            squares = g.squares(*mids)
            acc[0] = acc[0] + g.gather(squares)
        if stage != 3:
            at = 1 if stage == 1 else 3
            weighted = {t: weight[t] * squares[t] for t in g.own}
            acc[at] = acc[at] + g.gather(weighted)
        return tuple(acc)


def early_kernel(freqs, nx, ny, freq_sq, *refs):
    s, (cells, aux), refs = refs[:freqs], refs[freqs : freqs + 2], refs[freqs + 2 :]
    w, splat = refs[3 * freqs :]
    nz = cells.shape[2]
    for f in range(freqs):
        splat[f] = jnp.full((8, nz), freq_sq[f], F32)
    grid = Grid(nx, ny, nz)
    many = [
        Field(grid, (s[f], refs[3 * f], None, None, None, *refs[3 * f + 1 : 3 * f + 3]), w)
        for f in range(freqs)
    ]

    def prepare(i):
        return grid.prepare(
            i,
            grid.own,
            freq_sq,
            w,
            many,
            lambda t: cells[i, grid.tile(t), :],
            lambda k, t: grid.pick(aux.at[k], t, i),
        )

    for i in (0, nx - 1):
        terms = prepare(i)
        for f in range(freqs):
            for p in range(2):
                grid.put(many[f].v0, p, i, terms[f][p], grid.own)

    def row(i):
        terms = prepare(i)
        for f in range(freqs):
            field = many[f]
            _, re, im = grid.apply(
                field.s, i, i - 1, i + 1, -1, field.coef(i, grid.own), grid.own, False
            )
            for p, value in enumerate((re, im)):
                value = {t: value[t] + terms[f][p][t] for t in grid.own}
                grid.put(field.v0, p, i, value, grid.own)

    def pair(k, _):
        row(2 * k + 1)
        row(2 * k + 2)
        return 0

    lax.fori_loop(0, (nx - 2) // 2, pair, 0)


def early(nx, ny, freq_sq, s, cells, aux):
    freqs = len(s)
    _, xe, _, nz = s[0].shape
    field = pltpu.VMEM(s[0].shape, F32)
    coef = pltpu.VMEM((xe, ny // 8 + 1, 8, nz), F32)
    return pl.pallas_call(
        functools.partial(early_kernel, freqs, nx, ny),
        out_shape=(field, coef, coef) * freqs
        + (coef, pltpu.VMEM((freqs, 8, nz), F32)),
        in_specs=[SMEM] + [VMEM] * (freqs + 2),
        compiler_params=params(8),
        name="early",
    )(freq_sq, *s, cells, aux)


def corner_faces(freqs, nx, ny, s, cells, aux, ce, co):
    fields = 2 * freqs
    nz = cells.shape[2]
    sub = lax.broadcasted_iota(jnp.int32, (2 * HALO, nz), 0)
    even_x = parity("gx")
    near = [aux[k, ny:, :] for k in range(fields + 1)]
    for side, cb in enumerate((ce, co)):
        last = even_x if side == 0 else jnp.logical_not(even_x)
        at = [jnp.where(last, nx - d, d - 1) for d in range(1, HALO)]
        for k in range(fields):
            one, two, three = (s[k // 2][k % 2, x, ny:, :] for x in at)
            one = jnp.where(sub == 3, pltpu.roll(three, 3, axis=0), one)
            cb[k] = jnp.where(sub == 4, pltpu.roll(three, 5, axis=0), one)
            if k % 2 == 0:
                kept = two
                continue
            two = jnp.where(
                sub < 4, pltpu.roll(two, 2, axis=0), pltpu.roll(two, 6, axis=0)
            )
            outer = (sub < 2) | (sub > 5)
            cb[fields + k // 2] = jnp.where(outer, kept, two)
        one, two = cells[at[0], ny:, :], cells[at[1], ny:, :]
        one = jnp.where(sub == 2, pltpu.roll(two, 2, axis=0), one)
        cb[fields + freqs] = jnp.where(sub == 5, pltpu.roll(two, 6, axis=0), one)
        skip = jnp.where(last, nx - INNER, 0)
        cb[fields + freqs + 1] = lane_slab(near, fields, skip, 2 * HALO, nz)


def place_corners(freqs, nx, ny, cb, s, cells, aux, above):
    fields = 2 * freqs
    nz = cb.shape[2]
    sub = lax.broadcasted_iota(jnp.int32, (2 * HALO, nz), 0)
    slot = [jnp.where(above, nx + d - 1, nx + 2 * HALO - d) for d in range(1, HALO)]
    layer = [jnp.where(above, d - 1, INNER - d) for d in range(1, HALO)]
    for k in range(fields):
        field, p = s[k // 2], k % 2
        one = cb[k]
        field[p, slot[0], ny:, :] = one
        field[p, slot[2], ny:, :] = jnp.where(
            sub == 0, pltpu.roll(one, 5, axis=0), pltpu.roll(one, 3, axis=0)
        )
        two = cb[fields + k // 2]
        if p:
            two = jnp.where(
                sub < 4, pltpu.roll(two, 6, axis=0), pltpu.roll(two, 2, axis=0)
            )
        field[p, slot[1], ny:, :] = two
    one = cb[fields + freqs]
    cells[layer[0], ny:, :] = one
    cells[layer[1], ny:, :] = jnp.where(
        sub == 0, pltpu.roll(one, 6, axis=0), pltpu.roll(one, 2, axis=0)
    )
    cells[layer[2], ny:, :] = jnp.zeros((2 * HALO, nz), F32)
    aux[ny:, :] = cb[fields + freqs + 1]


def inner_kernel(freqs, nx, ny, half, freq_sq, *refs):
    if half == 0:
        ye, yo = refs[:2]
        count = 4 * freqs + 3
        refs = refs[2 + count :]
        s, (cells, aux), refs = refs[:freqs], refs[freqs : freqs + 2], refs[freqs + 2 :]
        known, refs = refs[: 3 * freqs + 1], refs[3 * freqs + 1 :]
        news, (moments, ce, co) = refs[: 3 * freqs], refs[3 * freqs :]
    else:
        s, known = refs[:freqs], refs[freqs : 4 * freqs + 1]
        partial = refs[7 * freqs + 1]
        refs = refs[7 * freqs + 2 :]
        news, (moments,) = refs[: 3 * freqs], refs[3 * freqs :]
    nz = s[0].shape[3]
    fields = 2 * freqs
    w = known[3 * freqs]
    grid = Grid(nx, ny, nz)
    many = []
    for f in range(freqs):
        v0, cr, ci = known[3 * f : 3 * f + 3]
        u0, v1, u1 = news[3 * f : 3 * f + 3]
        many.append(Field(grid, (s[f], v0, u0, v1, u1, cr, ci), w))
    if half == 0:
        swapped = jnp.broadcast_to(parity("gy"), (HALO, nz))

        def halo(at):
            even, odd = ye[at], yo[at]
            high = jnp.where(swapped, even, odd) * grid.right
            low = jnp.where(swapped, odd, even) * grid.left
            return jnp.concatenate([high, low], axis=0)

        sub = lax.broadcasted_iota(jnp.int32, (8, nz), 0)

        def model_rows(g, _):
            tiles = [halo(fields * nx + 3 * g + j) for j in range(3)]
            last = tiles[0]
            for j in range(3):
                cells[4 * g + j, ny:, :] = tiles[j]
                last = jnp.where(sub == j, pltpu.roll(tiles[j], 5 + j, axis=0), last)
                last = jnp.where(sub == 5 + j, pltpu.roll(tiles[j], 1 + j, axis=0), last)
            cells[4 * g + 3, ny:, :] = last
            return 0

        def merge(x, _):
            for k in range(fields):
                s[k // 2][k % 2, x, ny:, :] = halo(k * nx + x)
            return 0

        lax.fori_loop(0, nx // 4, model_rows, 0, unroll=2)
        lax.fori_loop(0, nx, merge, 0, unroll=4)
        for k in range(fields + 1):
            slab, g = divmod(k, nz // nx)
            tile = halo(fields * nx + nx // 4 * 3 + slab)
            aux[k, ny:, :] = pltpu.roll(tile, (nz - g * nx) % nz, axis=1) if g else tile
        corner_faces(freqs, nx, ny, s, cells, aux, ce, co)

    def prepare(i):
        return grid.prepare(
            i,
            [grid.tiles],
            freq_sq,
            w,
            many,
            lambda t: cells[i, grid.tile(t), :],
            lambda k, t: grid.pick(aux.at[k], t, i),
        )

    if half == 0:
        for i in (0, nx - 1):
            terms = prepare(i)
            for f in range(freqs):
                for p in range(2):
                    grid.put(many[f].v0, p, i, terms[f][p], [grid.tiles])

    def step(j, acc, active):
        acc = list(acc)
        for k in reversed(active):
            i = j - 2 * k
            if k == 0:
                terms = prepare(i)
            for f in range(freqs):
                if k == 0:
                    many[f].first_halo(i, terms[f])
                else:
                    acc[f] = many[f].step(k, i, i - 1, i + 1, acc=acc[f])
        return tuple(acc)

    def heads(i, _):
        terms = prepare(i)
        for f in range(freqs):
            many[f].first_halo(i, terms[f])
        return 0

    spans = [(1 + 3 * k, nx - 1 + k) for k in range(4)]
    middle = nx // 2 + SHIFT
    edges = sorted({e for span in spans for e in span} | {middle})
    acc = tuple(tuple(grid.zero() for _ in range(4)) for _ in range(freqs))
    if half == 0:
        lax.fori_loop(1, nx - 1, heads, 0, unroll=3)
    for lo, hi in zip(edges[:-1], edges[1:]):
        if (lo < middle) != (half == 0):
            continue
        active = [k for k, (a, b) in enumerate(spans) if k and a <= lo and hi <= b]
        if active:
            acc = lax.fori_loop(
                lo,
                hi,
                functools.partial(step, active=active),
                acc,
                unroll=3 if hi - lo > 4 else hi - lo,
            )
    for f in range(freqs):
        for m in range(4):
            value = acc[f][m]
            moments[f, m] = value if half == 0 else value + partial[f, m]


def inner_part(nx, ny, freq_sq, ye, yo, s, cells, aux, known):
    freqs = len(s)
    nz = cells.shape[2]
    slabs = 3 * freqs + 2
    field = pltpu.VMEM(s[0].shape, F32)
    corner = pltpu.VMEM((slabs, 2 * HALO, nz), F32)
    kept = (*s, cells, aux, *known)
    news = (field,) * (3 * freqs) + (pltpu.VMEM((freqs, 4, 8, nz), F32),)
    got = pl.pallas_call(
        functools.partial(inner_kernel, freqs, nx, ny, 0),
        out_shape=tuple(pltpu.VMEM(k.shape, F32) for k in kept)
        + news
        + (corner, corner),
        in_specs=[VMEM] * (3 + len(kept)),
        input_output_aliases={3 + k: k for k in range(len(kept))},
        compiler_params=params(8),
        name="inner_first",
    )(freq_sq, ye, yo, *kept)
    s, known = got[:freqs], got[freqs + 2 : len(kept)]
    news_got, (ce, co) = got[len(kept) : -2], got[-2:]

    def rest():
        first = freqs + len(known)
        again = pl.pallas_call(
            functools.partial(inner_kernel, freqs, nx, ny, 1, None),
            out_shape=news,
            in_specs=[VMEM] * (freqs + len(known) + len(news)),
            input_output_aliases={first + k: k for k in range(len(news))},
            compiler_params=params(8),
            name="inner_second",
        )(*s, *known, *news_got)
        state = []
        for f in range(freqs):
            v0, cr, ci = known[3 * f : 3 * f + 3]
            state += [s[f], v0, *again[3 * f : 3 * f + 3], cr, ci]
        return state + [known[-1]], again[-1]

    return ce, co, rest


def edge_kernel(side, peers, freqs, nx, ny, freq_sq, xb, cb, *refs):
    count = 7 * freqs + 1
    moments, refs = refs[count], refs[count + 1 :]
    state, (out, cells, aux) = refs[:count], refs[count:]
    fields = 2 * freqs
    nz = state[0].shape[3]
    w = state[-1]
    above = parity("gx") if side == 0 else jnp.logical_not(parity("gx"))
    group = nz // 8
    wrap = nx + 2 * HALO

    def row_at(distance):
        return jnp.where(above, (nx - 1 + distance) % wrap, -distance % wrap)

    slot = jnp.where(above, nx, nx + HALO)
    for layer in range(HALO):
        for k in range(fields):
            block = state[7 * (k // 2)]
            for y in range(0, ny, 8):
                row = (k * HALO + layer) * ny + y
                block[k % 2, slot + layer, y : y + 8, :] = xb[row : row + 8, :]
        if layer < INNER:
            for y in range(0, ny, 8):
                row = (fields * HALO + layer) * ny + y
                cells[layer, y : y + 8, :] = xb[row : row + 8, :]
    at = (fields * HALO + INNER) * ny
    folded = xb[at : at + ny // 8, :]
    for g in range(8):
        rows = pl.ds(g * (ny // 8), ny // 8)
        aux[rows, :] = pltpu.roll(folded, (nz - g * group) % nz, axis=1)
    place_corners(freqs, nx, ny, cb, state[: 7 * freqs : 7], cells, aux, above)
    for k in range(fields):
        state[7 * (k // 2)][k % 2, row_at(HALO), ny:, :] = jnp.zeros(
            (2 * HALO, nz), F32
        )
    grid = Grid(nx, ny, nz)
    many = [Field(grid, state[7 * f : 7 * f + 7], w) for f in range(freqs)]
    for layer in range(INNER):
        i = jnp.where(above, nx + layer, nx + HALO + 1 + layer)
        terms = grid.prepare(
            i,
            grid.both,
            freq_sq,
            w,
            many,
            lambda t: cells[layer, grid.tile(t), :],
            lambda k, t: grid.pick(aux, t, INNER * k + layer),
        )
        for f in range(freqs):
            for p in range(2):
                grid.put(many[f].v0, p, i, terms[f][p], grid.both)

    place = lax.axis_index("gx")
    more = jnp.where(above, place < lax.axis_size("gx") - 1, place > 0)
    cut = (-1, jnp.where(more, 1.0, 0.0))
    acc = [tuple(grid.zero() for _ in range(4)) for _ in range(freqs)]
    for stage in range(4):
        for k in range(HALO):
            distance = INNER - stage - k
            i, lo, hi = (row_at(distance + d) for d in (0, 1, -1))
            own = distance <= 0
            ends = cut if distance == 0 else None
            for f in range(freqs):
                if stage == 0:
                    many[f].finish(i, grid.both, True, lo, hi, ends)
                    continue
                got = many[f].step(stage, i, lo, hi, ends, acc[f] if own else None)
                if own:
                    acc[f] = got

    if side == 0:
        for f in range(freqs):
            for m in range(4):
                out[f, m] = acc[f][m] + moments[f, m]
        return
    rows = []
    for f in range(freqs):
        for m in range(4):
            both = acc[f][m] + moments[f, m]
            rows.append(jnp.sum(both, axis=0, keepdims=True))
    sums = jnp.sum(jnp.concatenate(rows, axis=0), axis=1, keepdims=True)
    sums = jnp.broadcast_to(sums, (4 * freqs, nz))
    for peer in range(peers):
        out[peer] = sums


def edge_part(side, peers, freqs, nx, ny, freq_sq, xb, cb, state, moments):
    nz = state[0].shape[3]
    outs = tuple(pltpu.VMEM(k.shape, F32) for k in state)
    if side == 0:
        last = pltpu.VMEM(moments.shape, F32)
    else:
        last = jax.ShapeDtypeStruct((peers, 4 * freqs, nz), F32)
    *state, out = pl.pallas_call(
        functools.partial(edge_kernel, side, peers, freqs, nx, ny),
        out_shape=outs + (last,),
        in_specs=[VMEM] * (4 + len(state)),
        input_output_aliases={3 + k: k for k in range(len(state))},
        scratch_shapes=[
            pltpu.VMEM((INNER, ny + 2 * HALO, nz), F32),
            pltpu.VMEM((ny + 2 * HALO, nz), F32),
        ],
        compiler_params=params(8),
        name="edge_odd" if side else "edge_even",
    )(freq_sq, xb, cb, *state, moments)
    return state, out


def steps(sums, freqs):
    total = jnp.sum(sums[...], axis=0)
    shape = (8, total.shape[1])
    out = []
    for f in range(freqs):
        m0, m1, m2, m3 = (
            jnp.broadcast_to(total[4 * f + k : 4 * f + k + 1, :], shape)
            for k in range(4)
        )
        first = m0 / m1
        new = first * (first * m2 - m1)
        product = m1 - first * (2.0 * m2 - first * m3)
        ratio = new / m0
        second = new / (product - ratio * new / first)
        out.append((first + second * (1.0 + ratio), -first * second))
    return out


def gradient_kernel(freqs, nx, ny, freq_sq, sums, *refs):
    out = refs[-1]
    weights = steps(sums, freqs)
    scale = [-freq_sq[f] for f in range(freqs)]

    def row(x, _):
        for y in range(0, ny, 8):
            at = pl.ds(y, 8)
            total = None
            for f in range(freqs):
                s, v0, u0, v1, u1 = refs[5 * f : 5 * f + 5]
                a, b = weights[f]
                wave_re = a * v0[0, x, at, :] + b * v1[0, x, at, :]
                wave_im = a * v0[1, x, at, :] + b * v1[1, x, at, :]
                miss_re = a * u0[0, x, at, :] + b * u1[0, x, at, :]
                miss_im = a * u0[1, x, at, :] + b * u1[1, x, at, :]
                miss_re = miss_re - s[0, x, at, :]
                miss_im = miss_im - s[1, x, at, :]
                left = (wave_re + attenuation * wave_im) * miss_re
                right = (wave_im - attenuation * wave_re) * miss_im
                term = scale[f] * (left + right)
                total = term if total is None else total + term
            out[x, at, :] = total
        return 0

    lax.fori_loop(0, nx, row, 0, unroll=2)


def wave_kernel(freqs, nx, ny, sums, *refs):
    out, block, sem = refs[2 * freqs :]
    weights = steps(sums, freqs)
    copies = Copies(sem)
    for f in range(freqs):
        a, b = weights[f]
        v0, v1 = refs[2 * f : 2 * f + 2]
        for p in range(2):
            k = 2 * f + p

            def row(x, _):
                for y in range(0, ny, 8):
                    at = pl.ds(y, 8)
                    block[k, x, at, :] = a * v0[p, x, at, :] + b * v1[p, x, at, :]
                return 0

            lax.fori_loop(0, nx, row, 0, unroll=8)
            copies.add(block.at[k], out.at[f, p])
    copies.wait()


def results(freqs, nx, ny, freq_sq, sums, state):
    nz = state[0].shape[3]
    fields, pairs = [], []
    for f in range(freqs):
        s, v0, u0, v1, u1 = state[7 * f : 7 * f + 5]
        fields += [s, v0, u0, v1, u1]
        pairs += [v0, v1]
    gradient = pl.pallas_call(
        functools.partial(gradient_kernel, freqs, nx, ny),
        out_shape=jax.ShapeDtypeStruct((nx, ny, nz), F32),
        in_specs=[VMEM] * (2 + len(fields)),
        out_specs=VMEM,
        compiler_params=params(8),
        name="gradient_part",
    )(freq_sq, sums, *fields)
    wave = pl.pallas_call(
        functools.partial(wave_kernel, freqs, nx, ny),
        out_shape=jax.ShapeDtypeStruct((freqs, 2, nx, ny, nz), F32),
        in_specs=[VMEM] * (1 + len(pairs)),
        out_specs=HBM,
        scratch_shapes=[
            pltpu.VMEM((2 * freqs, nx, ny, nz), F32),
            pltpu.SemaphoreType.DMA((2 * freqs,)),
        ],
        compiler_params=params(8),
        name="wavefield",
    )(sums, *pairs)
    return gradient, wave


def add_kernel(one, two, out, block, sem):
    nx, ny, _ = one.shape
    copies = Copies(sem)
    parts = sem.shape[0]
    step = nx // parts
    for part in range(parts):

        def row(x, _):
            for y in range(0, ny, 8):
                at = pl.ds(y, 8)
                block[x, at, :] = one[x, at, :] + two[x, at, :]
            return 0

        lax.fori_loop(part * step, (part + 1) * step, row, 0, unroll=4)
        span = pl.ds(part * step, step)
        copies.add(block.at[span], out.at[span])
    copies.wait()


def add(one, two):
    return pl.pallas_call(
        add_kernel,
        out_shape=jax.ShapeDtypeStruct(one.shape, F32),
        in_specs=[VMEM] * 2,
        out_specs=HBM,
        scratch_shapes=[pltpu.VMEM(one.shape, F32), pltpu.SemaphoreType.DMA((2,))],
        compiler_params=params(4),
        name="add",
    )(one, two)


def swap(cells, axis, odd):
    names = ("gx", "gy", "af")
    sizes = [lax.axis_size(name) for name in names]
    along = names.index(axis)
    pairs = []
    for flat in range(sizes[0] * sizes[1] * sizes[2]):
        place = [flat // (sizes[1] * sizes[2]), flat // sizes[2] % sizes[1], flat % sizes[2]]
        mate = ((place[along] + odd) ^ 1) - odd
        if 0 <= mate < sizes[along]:
            place[along] = mate
        elif sizes[2] % 2 == 0:
            place[2] ^= 1
        else:
            continue
        pairs.append((flat, (place[0] * sizes[1] + place[1]) * sizes[2] + place[2]))
    return lax.ppermute(cells, names, pairs)


def on_device(model, freq_sq, source, observed, receiver_depth):
    nx, ny, nz = model.shape
    freqs = freq_sq.shape[0]
    *s, cells, aux, xe, xo, ye, yo = load(source, model, observed, receiver_depth)
    ye, yo = swap(ye, "gy", 0), swap(yo, "gy", 1)
    xe, xo = swap(xe, "gx", 0), swap(xo, "gx", 1)
    *known, splat = early(nx, ny, freq_sq, s, cells, aux)
    ce, co, rest = inner_part(nx, ny, splat, ye, yo, s, cells, aux, known)
    ce, co = swap(ce, "gx", 0), swap(co, "gx", 1)
    state, moments = rest()
    peers = lax.axis_size("gx") * lax.axis_size("gy")
    state, moments = edge_part(
        0, peers, freqs, nx, ny, splat, xe, ce, state, moments
    )
    state, part = edge_part(1, peers, freqs, nx, ny, splat, xo, co, state, moments)
    sums = lax.all_to_all(part, ("gx", "gy"), 0, 0)
    gradient, wave = results(freqs, nx, ny, splat, sums, state)
    if lax.axis_size("af") == 2:
        gradient = add(gradient, lax.ppermute(gradient, "af", [(0, 1), (1, 0)]))
    else:
        gradient = lax.psum(gradient, "af")
    return wave, gradient


def solution(mesh):
    in_specs = (
        P("gx", "gy", None),
        P("af"),
        P("af", None, "gx", "gy", None),
        P("af", None, "gx", "gy"),
        P("gx", "gy"),
    )
    out_specs = (P("af", None, "gx", "gy", None), P("gx", "gy", None))
    return jax.shard_map(
        on_device, mesh=mesh, in_specs=in_specs, out_specs=out_specs, check_vma=False
    )
```

```python
import functools

import jax
import jax.numpy as jnp
from jax import lax
from jax.experimental import pallas as pl
from jax.experimental.pallas import tpu as pltpu
from jax.sharding import PartitionSpec as P

ITERS = 2
attenuation = 0.2
penalty = 4.0

HALO = 2 * ITERS
INNER = HALO - 1
F32 = jnp.float32
ANY = pl.BlockSpec(memory_space=pl.ANY)
HBM = pl.BlockSpec(memory_space=pltpu.HBM)
VMEM = pl.BlockSpec(memory_space=pltpu.VMEM)
SMEM = pl.BlockSpec(memory_space=pltpu.SMEM)
MIB = 1 << 20
LOAD_MIB = 55
SHIFT = -4


def params(mib):
    return pltpu.CompilerParams(vmem_limit_bytes=mib * MIB)


def cost(us):
    return pl.CostEstimate(
        flops=int(us * 1e3), bytes_accessed=int(us * 1e3), transcendentals=0
    )


def parity(axis):
    return lax.rem(lax.axis_index(axis), 2) == 0


class Copies:
    def __init__(self, sem):
        self.sem, self.all = sem, []

    def add(self, src, dst):
        copy = pltpu.make_async_copy(src, dst, self.sem.at[len(self.all)])
        copy.start()
        self.all.append(copy)

    def wait(self):
        for copy in self.all:
            copy.wait()


def lane_slab(table, fields, skip, rows, nz):
    lane = lax.broadcasted_iota(jnp.int32, (rows, nz), 1)
    lanes = jnp.zeros((rows, nz), F32)
    for k in range(fields + 1):
        inside = (lane >= INNER * k) & (lane < INNER * k + INNER)
        shift = lax.rem(INNER * k + nz - skip, nz)
        lanes = jnp.where(inside, pltpu.roll(table[k], shift, axis=1), lanes)
    return lanes


def fold(slab, nz):
    rows, width = slab.shape[0] // 8, nz // 8
    lane = lax.broadcasted_iota(jnp.int32, (rows, nz), 1)
    out = jnp.zeros((rows, nz), F32)
    for g in range(8):
        piece = slab[g * rows : (g + 1) * rows, :]
        inside = (lane >= g * width) & (lane < (g + 1) * width)
        out = jnp.where(inside, pltpu.roll(piece, g * width, axis=1), out)
    return out


def load_kernel(source, model, observed, depth, *refs):
    freqs, _, nx, ny, nz = source.shape
    fields = 2 * freqs
    s, (cells, aux, xe, xo, ye, yo, seen, sunk, table, sem) = refs[:freqs], refs[freqs:]
    small = Copies(sem.at[0])
    small.add(observed, seen)
    small.add(depth, sunk)
    large = Copies(sem.at[1])
    large.add(model, cells.at[:, pl.ds(0, ny), :])
    for f in range(freqs):
        for p in range(2):
            large.add(source.at[f, p], s[f].at[p, pl.ds(0, nx), pl.ds(0, ny), :])
    even_x, even_y = parity("gx"), parity("gy")
    small.wait()
    for f in range(freqs):
        for p in range(2):
            table[2 * f + p, :, 0:nx] = seen[f, p].T
    table[fields, :, 0:nx] = sunk[...].astype(F32).T
    copies = Copies(sem.at[2])
    copies.add(table, aux.at[:, pl.ds(0, ny), :])
    faces = []
    for side, xb in enumerate((xe, xo)):
        last = even_x if side == 0 else jnp.logical_not(even_x)
        skip = jnp.where(last, nx - INNER, 0)
        faces.append((xb, skip, jnp.where(last, nx - HALO, 0)))
        at = (fields * HALO + INNER) * ny
        xb[at : at + ny // 8, :] = fold(lane_slab(table, fields, skip, ny, nz), nz)
    swapped = jnp.broadcast_to(even_y, (HALO, nz))

    def y_faces(block, at):
        def row(x, _):
            head, tail = block[x, 0:HALO, :], block[x, ny - HALO : ny, :]
            ye[at + x] = jnp.where(swapped, tail, head)
            yo[at + x] = jnp.where(swapped, head, tail)
            return 0

        lax.fori_loop(0, nx, row, 0, unroll=8)

    def x_face(xb, to, block, at, layers):
        for layer in range(layers):
            for y in range(0, ny, 8):
                row = (to + layer) * ny + y
                xb[row : row + 8, :] = block[at + layer, y : y + 8, :]

    lane = lax.broadcasted_iota(jnp.int32, (HALO, nz), 1)
    at = fields * nx + nx // 4 * 3
    for slab in range(-(-(fields + 1) // (nz // nx))):
        pair = [jnp.zeros((HALO, nz), F32)] * 2
        for g in range(nz // nx):
            k = slab * (nz // nx) + g
            if k > fields:
                continue
            inside = (lane >= g * nx) & (lane < (g + 1) * nx)
            for end, rows in enumerate((table[k, 0:HALO, :], table[k, ny - HALO : ny, :])):
                moved = pltpu.roll(rows, g * nx, axis=1)
                pair[end] = jnp.where(inside, moved, pair[end])
        ye[at + slab] = jnp.where(swapped, pair[1], pair[0])
        yo[at + slab] = jnp.where(swapped, pair[0], pair[1])
    large.all[0].wait()
    sub = lax.broadcasted_iota(jnp.int32, (8, nz), 0)

    def model_rows(g, _):
        heads = [cells[4 * g + j, 0:8, :] for j in range(4)]
        tails = [cells[4 * g + j, ny - 8 : ny, :] for j in range(4)]
        for j in range(3):
            head = jnp.where(sub == 3, pltpu.roll(heads[3], 3 - j, axis=0), heads[j])
            tail = jnp.where(sub == 4, pltpu.roll(tails[3], 7 - j, axis=0), tails[j])
            head, tail = head[0:HALO, :], tail[8 - HALO : 8, :]
            ye[fields * nx + 3 * g + j] = jnp.where(swapped, tail, head)
            yo[fields * nx + 3 * g + j] = jnp.where(swapped, head, tail)
        return 0

    lax.fori_loop(0, nx // 4, model_rows, 0, unroll=2)
    for xb, skip, _ in faces:
        x_face(xb, fields * HALO, cells, skip, INNER)
    for k in range(fields):
        large.all[1 + k].wait()
        block = s[k // 2].at[k % 2]
        y_faces(block, k * nx)
        for xb, _, at in faces:
            x_face(xb, k * HALO, block, at, HALO)
    copies.wait()


def load(source, model, observed, depth):
    freqs, _, nx, ny, nz = source.shape
    fields = 2 * freqs
    xs = pltpu.VMEM(((fields * HALO + INNER) * ny + 8, nz), F32)
    slabs = fields * nx + nx // 4 * 3 + -(-(fields + 1) // (nz // nx))
    ys = pltpu.VMEM((slabs, HALO, nz), F32)
    return pl.pallas_call(
        load_kernel,
        out_shape=(pltpu.VMEM((2, nx + 2 * HALO, ny + 2 * HALO, nz), F32),) * freqs
        + (
            pltpu.VMEM((nx, ny + 2 * HALO, nz), F32),
            pltpu.VMEM((fields + 1, ny + 2 * HALO, nz), F32),
            xs,
            xs,
            ys,
            ys,
        ),
        in_specs=[HBM] * 4,
        scratch_shapes=[
            pltpu.VMEM(observed.shape, F32),
            pltpu.VMEM(depth.shape, jnp.int32),
            pltpu.VMEM((fields + 1, ny, nz), F32),
            pltpu.SemaphoreType.DMA((3, 32)),
        ],
        compiler_params=params(LOAD_MIB),
        name="load",
    )(source, model, observed, depth)


class Grid:
    def __init__(self, nx, ny, nz):
        self.nx, self.ny, self.nz = nx, ny, nz
        self.xe = nx + 2 * HALO
        self.tiles = ny // 8
        self.own = range(self.tiles)
        self.both = range(self.tiles + 1)
        lane = lax.broadcasted_iota(jnp.int32, (8, nz), 1)
        self.first = lane == 0
        self.last = lane == nz - 1
        self.depths = lane.astype(F32)
        sub = lax.broadcasted_iota(jnp.int32, (8, nz), 0)
        self.top = sub == 7
        self.bottom = sub == 0
        has_left = lax.axis_index("gy") > 0
        has_right = lax.axis_index("gy") < lax.axis_size("gy") - 1
        self.left = jnp.where(has_left, 1.0, 0.0)
        self.right = jnp.where(has_right, 1.0, 0.0)
        self.inside = jnp.where(sub < HALO, self.right, self.left)

    def tile(self, t):
        if t < self.tiles:
            return pl.ds(t, 8, stride=self.tiles)
        return pl.ds(self.ny, 8)

    def rows(self, ref, p, i, tiles):
        return [ref[p, i, self.tile(t), :] for t in tiles]

    def put(self, ref, p, i, values, tiles):
        for t in tiles:
            ref[p, i, self.tile(t), :] = values[t]

    def beside(self, mid):
        left = jnp.where(self.first, 0.0, pltpu.roll(mid, 1, axis=1))
        right = jnp.where(self.last, 0.0, pltpu.roll(mid, self.nz - 1, axis=1))
        return left + right

    def around(self, mid, below, above, tiles):
        n = self.tiles
        halo = mid[n] if len(mid) > n else None
        first_up = pltpu.roll(mid[0], 7, axis=0)
        last_down = pltpu.roll(mid[n - 1], 1, axis=0)
        if halo is not None:
            halo_up = pltpu.roll(halo, 7, axis=0)
            halo_down = pltpu.roll(halo, 1, axis=0)
        total = {}
        for t in tiles:
            if t == n:
                up = jnp.where(self.top, first_up, halo_up)
                down = jnp.where(self.bottom, last_down, halo_down)
            else:
                up = mid[t + 1] if t + 1 < n else None
                down = mid[t - 1] if t else None
                if up is None:
                    edge = 0.0 if halo is None else halo_up
                    up = jnp.where(self.top, edge, first_up)
                if down is None:
                    edge = 0.0 if halo is None else halo_down
                    down = jnp.where(self.bottom, edge, last_down)
            total[t] = ((below[t] + above[t]) + (up + down)) + self.beside(mid[t])
        return total

    def apply(self, src, i, lo, hi, sign, coef, tiles, wide=True, cut=None):
        cr, ci = coef
        mids, totals = [], []
        for p in range(2):
            mid = self.rows(src, p, i, self.both if wide else self.own)
            below = {t: src[p, lo, self.tile(t), :] for t in tiles}
            above = {t: src[p, hi, self.tile(t), :] for t in tiles}
            if cut is not None and cut[0] < 0:
                below = {t: v * cut[1] for t, v in below.items()}
            if cut is not None and cut[0] > 0:
                above = {t: v * cut[1] for t, v in above.items()}
            mids.append(mid)
            totals.append(self.around(mid, below, above, tiles))
        out_re, out_im = {}, {}
        for t in tiles:
            re, im = mids[0][t], mids[1][t]
            if sign > 0:
                out_re[t] = cr[t] * re - ci[t] * im - totals[0][t]
                out_im[t] = cr[t] * im + ci[t] * re - totals[1][t]
            else:
                out_re[t] = cr[t] * re + ci[t] * im - totals[0][t]
                out_im[t] = cr[t] * im - ci[t] * re - totals[1][t]
        return mids, out_re, out_im

    def squares(self, re, im):
        return {t: re[t] * re[t] + im[t] * im[t] for t in self.own}

    def gather(self, values):
        return functools.reduce(jnp.add, [values[t] for t in self.own])

    def zero(self):
        return jnp.zeros((8, self.nz), F32)

    def prepare(self, i, tiles, freq_sq, w, many, cell, column):
        fields = 2 * len(many)
        weight = {}
        for t in tiles:
            depth = column(fields, t)
            weight[t] = jnp.where(self.depths == depth, penalty, 0.0)
            w[i, t] = weight[t]
        out = []
        for f, field in enumerate(many):
            for t in tiles:
                scaled = freq_sq[f] * cell(t)
                field.cr[i, t] = 6.0 - scaled
                field.ci[i, t] = attenuation * scaled
            out.append(
                [
                    {t: weight[t] * column(2 * f + p, t) for t in tiles}
                    for p in range(2)
                ]
            )
        return out

    def pick(self, ref, t, lane):
        at = jnp.full((8, self.nz), lane, jnp.int32)
        return jnp.take_along_axis(ref[self.tile(t), :], at, axis=1)


class Field:
    def __init__(self, grid, refs, w):
        self.grid = grid
        self.s, self.v0, self.u0, self.v1, self.u1, self.cr, self.ci = refs
        self.w = w

    def coef(self, i, tiles):
        return {t: self.cr[i, t] for t in tiles}, {t: self.ci[i, t] for t in tiles}

    def finish(self, i, tiles, wide, lo=None, hi=None, cut=None):
        g = self.grid
        _, re, im = g.apply(self.s, i, lo, hi, -1, self.coef(i, tiles), tiles, wide, cut)
        for p, value in enumerate((re, im)):
            for t in tiles:
                at = g.tile(t)
                total = self.v0[p, i, at, :] + value[t]
                self.v0[p, i, at, :] = total * g.inside if t == g.tiles else total

    def first_halo(self, i, terms):
        g = self.grid
        n = g.tiles
        coef = self.coef(i, [n])
        _, re, im = g.apply(self.s, i, i - 1, i + 1, -1, coef, [n])
        for p, value in enumerate((re, im)):
            self.v0[p, i, g.tile(n), :] = (value[n] + terms[p][n]) * g.inside
            halo = self.s[p, i, g.tile(n), :]
            low = jnp.where(g.bottom, pltpu.roll(halo, 1, axis=0), 0.0)
            high = jnp.where(g.top, pltpu.roll(halo, 7, axis=0), 0.0)
            for t, change in ((0, low), (n - 1, high)):
                at = g.tile(t)
                self.v0[p, i, at, :] = self.v0[p, i, at, :] - change

    def step(self, stage, i, lo, hi, cut=None, acc=None):
        g = self.grid
        src = (None, self.v0, self.u0, self.v1)[stage]
        dst = (None, self.u0, self.v1, self.u1)[stage]
        tiles = g.own if stage == 3 else g.both
        sign = -1 if stage == 2 else 1
        mids, re, im = g.apply(src, i, lo, hi, sign, self.coef(i, tiles), tiles, True, cut)
        if stage != 3:
            weight = {t: self.w[i, t] for t in tiles}
        if stage == 2:
            for p, out in enumerate((re, im)):
                for t in tiles:
                    out[t] = out[t] + weight[t] * self.v0[p, i, g.tile(t), :]
        if stage != 3:
            re[g.tiles] = re[g.tiles] * g.inside
            im[g.tiles] = im[g.tiles] * g.inside
        g.put(dst, 0, i, re, tiles)
        g.put(dst, 1, i, im, tiles)
        if acc is None:
            return None
        acc = list(acc)
        squares = g.squares(re, im)
        acc[stage] = acc[stage] + g.gather(squares)
        if stage == 1:
            squares = g.squares(*mids)
            acc[0] = acc[0] + g.gather(squares)
        if stage != 3:
            at = 1 if stage == 1 else 3
            weighted = {t: weight[t] * squares[t] for t in g.own}
            acc[at] = acc[at] + g.gather(weighted)
        return tuple(acc)


def early_kernel(freqs, nx, ny, freq_sq, *refs):
    s, (cells, aux), refs = refs[:freqs], refs[freqs : freqs + 2], refs[freqs + 2 :]
    w, splat = refs[3 * freqs :]
    nz = cells.shape[2]
    for f in range(freqs):
        splat[f] = jnp.full((8, nz), freq_sq[f], F32)
    grid = Grid(nx, ny, nz)
    many = [
        Field(grid, (s[f], refs[3 * f], None, None, None, *refs[3 * f + 1 : 3 * f + 3]), w)
        for f in range(freqs)
    ]

    def prepare(i):
        return grid.prepare(
            i,
            grid.own,
            freq_sq,
            w,
            many,
            lambda t: cells[i, grid.tile(t), :],
            lambda k, t: grid.pick(aux.at[k], t, i),
        )

    for i in (0, nx - 1):
        terms = prepare(i)
        for f in range(freqs):
            for p in range(2):
                grid.put(many[f].v0, p, i, terms[f][p], grid.own)

    def row(i):
        terms = prepare(i)
        for f in range(freqs):
            field = many[f]
            _, re, im = grid.apply(
                field.s, i, i - 1, i + 1, -1, field.coef(i, grid.own), grid.own, False
            )
            for p, value in enumerate((re, im)):
                value = {t: value[t] + terms[f][p][t] for t in grid.own}
                grid.put(field.v0, p, i, value, grid.own)

    def pair(k, _):
        row(2 * k + 1)
        row(2 * k + 2)
        return 0

    lax.fori_loop(0, (nx - 2) // 2, pair, 0)


def early(nx, ny, freq_sq, s, cells, aux):
    freqs = len(s)
    _, xe, _, nz = s[0].shape
    field = pltpu.VMEM(s[0].shape, F32)
    coef = pltpu.VMEM((xe, ny // 8 + 1, 8, nz), F32)
    return pl.pallas_call(
        functools.partial(early_kernel, freqs, nx, ny),
        out_shape=(field, coef, coef) * freqs
        + (coef, pltpu.VMEM((freqs, 8, nz), F32)),
        in_specs=[SMEM] + [VMEM] * (freqs + 2),
        compiler_params=params(8),
        name="early",
    )(freq_sq, *s, cells, aux)


def corner_faces(freqs, nx, ny, s, cells, aux, ce, co):
    fields = 2 * freqs
    nz = cells.shape[2]
    sub = lax.broadcasted_iota(jnp.int32, (2 * HALO, nz), 0)
    even_x = parity("gx")
    near = [aux[k, ny:, :] for k in range(fields + 1)]
    for side, cb in enumerate((ce, co)):
        last = even_x if side == 0 else jnp.logical_not(even_x)
        at = [jnp.where(last, nx - d, d - 1) for d in range(1, HALO)]
        for k in range(fields):
            one, two, three = (s[k // 2][k % 2, x, ny:, :] for x in at)
            one = jnp.where(sub == 3, pltpu.roll(three, 3, axis=0), one)
            cb[k] = jnp.where(sub == 4, pltpu.roll(three, 5, axis=0), one)
            if k % 2 == 0:
                kept = two
                continue
            two = jnp.where(
                sub < 4, pltpu.roll(two, 2, axis=0), pltpu.roll(two, 6, axis=0)
            )
            outer = (sub < 2) | (sub > 5)
            cb[fields + k // 2] = jnp.where(outer, kept, two)
        one, two = cells[at[0], ny:, :], cells[at[1], ny:, :]
        one = jnp.where(sub == 2, pltpu.roll(two, 2, axis=0), one)
        cb[fields + freqs] = jnp.where(sub == 5, pltpu.roll(two, 6, axis=0), one)
        skip = jnp.where(last, nx - INNER, 0)
        cb[fields + freqs + 1] = lane_slab(near, fields, skip, 2 * HALO, nz)


def place_corners(freqs, nx, ny, cb, s, cells, aux, above):
    fields = 2 * freqs
    nz = cb.shape[2]
    sub = lax.broadcasted_iota(jnp.int32, (2 * HALO, nz), 0)
    slot = [jnp.where(above, nx + d - 1, nx + 2 * HALO - d) for d in range(1, HALO)]
    layer = [jnp.where(above, d - 1, INNER - d) for d in range(1, HALO)]
    for k in range(fields):
        field, p = s[k // 2], k % 2
        one = cb[k]
        field[p, slot[0], ny:, :] = one
        field[p, slot[2], ny:, :] = jnp.where(
            sub == 0, pltpu.roll(one, 5, axis=0), pltpu.roll(one, 3, axis=0)
        )
        two = cb[fields + k // 2]
        if p:
            two = jnp.where(
                sub < 4, pltpu.roll(two, 6, axis=0), pltpu.roll(two, 2, axis=0)
            )
        field[p, slot[1], ny:, :] = two
    one = cb[fields + freqs]
    cells[layer[0], ny:, :] = one
    cells[layer[1], ny:, :] = jnp.where(
        sub == 0, pltpu.roll(one, 6, axis=0), pltpu.roll(one, 2, axis=0)
    )
    cells[layer[2], ny:, :] = jnp.zeros((2 * HALO, nz), F32)
    aux[ny:, :] = cb[fields + freqs + 1]


def inner_kernel(freqs, nx, ny, half, freq_sq, *refs):
    if half == 0:
        ye, yo = refs[:2]
        count = 4 * freqs + 3
        refs = refs[2 + count :]
        s, (cells, aux), refs = refs[:freqs], refs[freqs : freqs + 2], refs[freqs + 2 :]
        known, refs = refs[: 3 * freqs + 1], refs[3 * freqs + 1 :]
        news, (moments, ce, co) = refs[: 3 * freqs], refs[3 * freqs :]
    else:
        s, known = refs[:freqs], refs[freqs : 4 * freqs + 1]
        partial = refs[7 * freqs + 1]
        refs = refs[7 * freqs + 2 :]
        news, (moments,) = refs[: 3 * freqs], refs[3 * freqs :]
    nz = s[0].shape[3]
    fields = 2 * freqs
    w = known[3 * freqs]
    grid = Grid(nx, ny, nz)
    many = []
    for f in range(freqs):
        v0, cr, ci = known[3 * f : 3 * f + 3]
        u0, v1, u1 = news[3 * f : 3 * f + 3]
        many.append(Field(grid, (s[f], v0, u0, v1, u1, cr, ci), w))
    if half == 0:
        swapped = jnp.broadcast_to(parity("gy"), (HALO, nz))

        def halo(at):
            even, odd = ye[at], yo[at]
            high = jnp.where(swapped, even, odd) * grid.right
            low = jnp.where(swapped, odd, even) * grid.left
            return jnp.concatenate([high, low], axis=0)

        sub = lax.broadcasted_iota(jnp.int32, (8, nz), 0)

        def model_rows(g, _):
            tiles = [halo(fields * nx + 3 * g + j) for j in range(3)]
            last = tiles[0]
            for j in range(3):
                cells[4 * g + j, ny:, :] = tiles[j]
                last = jnp.where(sub == j, pltpu.roll(tiles[j], 5 + j, axis=0), last)
                last = jnp.where(sub == 5 + j, pltpu.roll(tiles[j], 1 + j, axis=0), last)
            cells[4 * g + 3, ny:, :] = last
            return 0

        def merge(x, _):
            for k in range(fields):
                s[k // 2][k % 2, x, ny:, :] = halo(k * nx + x)
            return 0

        lax.fori_loop(0, nx // 4, model_rows, 0, unroll=2)
        lax.fori_loop(0, nx, merge, 0, unroll=4)
        for k in range(fields + 1):
            slab, g = divmod(k, nz // nx)
            tile = halo(fields * nx + nx // 4 * 3 + slab)
            aux[k, ny:, :] = pltpu.roll(tile, (nz - g * nx) % nz, axis=1) if g else tile
        corner_faces(freqs, nx, ny, s, cells, aux, ce, co)

    def prepare(i):
        return grid.prepare(
            i,
            [grid.tiles],
            freq_sq,
            w,
            many,
            lambda t: cells[i, grid.tile(t), :],
            lambda k, t: grid.pick(aux.at[k], t, i),
        )

    if half == 0:
        for i in (0, nx - 1):
            terms = prepare(i)
            for f in range(freqs):
                for p in range(2):
                    grid.put(many[f].v0, p, i, terms[f][p], [grid.tiles])

    def step(j, acc, active):
        acc = list(acc)
        for k in reversed(active):
            i = j - 2 * k
            if k == 0:
                terms = prepare(i)
            for f in range(freqs):
                if k == 0:
                    many[f].first_halo(i, terms[f])
                else:
                    acc[f] = many[f].step(k, i, i - 1, i + 1, acc=acc[f])
        return tuple(acc)

    def heads(i, _):
        terms = prepare(i)
        for f in range(freqs):
            many[f].first_halo(i, terms[f])
        return 0

    spans = [(1 + 3 * k, nx - 1 + k) for k in range(4)]
    middle = nx // 2 + SHIFT
    edges = sorted({e for span in spans for e in span} | {middle})
    acc = tuple(tuple(grid.zero() for _ in range(4)) for _ in range(freqs))
    if half == 0:
        lax.fori_loop(1, nx - 1, heads, 0, unroll=3)
    for lo, hi in zip(edges[:-1], edges[1:]):
        if (lo < middle) != (half == 0):
            continue
        active = [k for k, (a, b) in enumerate(spans) if k and a <= lo and hi <= b]
        if active:
            acc = lax.fori_loop(
                lo,
                hi,
                functools.partial(step, active=active),
                acc,
                unroll=3 if hi - lo > 4 else hi - lo,
            )
    for f in range(freqs):
        for m in range(4):
            value = acc[f][m]
            moments[f, m] = value if half == 0 else value + partial[f, m]


def inner_part(nx, ny, freq_sq, ye, yo, s, cells, aux, known):
    freqs = len(s)
    nz = cells.shape[2]
    slabs = 3 * freqs + 2
    field = pltpu.VMEM(s[0].shape, F32)
    corner = pltpu.VMEM((slabs, 2 * HALO, nz), F32)
    kept = (*s, cells, aux, *known)
    news = (field,) * (3 * freqs) + (pltpu.VMEM((freqs, 4, 8, nz), F32),)
    got = pl.pallas_call(
        functools.partial(inner_kernel, freqs, nx, ny, 0),
        out_shape=tuple(pltpu.VMEM(k.shape, F32) for k in kept)
        + news
        + (corner, corner),
        in_specs=[VMEM] * (3 + len(kept)),
        input_output_aliases={3 + k: k for k in range(len(kept))},
        compiler_params=params(8),
        name="inner_first",
    )(freq_sq, ye, yo, *kept)
    s, known = got[:freqs], got[freqs + 2 : len(kept)]
    news_got, (ce, co) = got[len(kept) : -2], got[-2:]

    def rest():
        first = freqs + len(known)
        again = pl.pallas_call(
            functools.partial(inner_kernel, freqs, nx, ny, 1, None),
            out_shape=news,
            in_specs=[VMEM] * (freqs + len(known) + len(news)),
            input_output_aliases={first + k: k for k in range(len(news))},
            compiler_params=params(8),
            name="inner_second",
        )(*s, *known, *news_got)
        state = []
        for f in range(freqs):
            v0, cr, ci = known[3 * f : 3 * f + 3]
            state += [s[f], v0, *again[3 * f : 3 * f + 3], cr, ci]
        return state + [known[-1]], again[-1]

    return ce, co, rest


def edge_kernel(side, peers, freqs, nx, ny, freq_sq, xb, cb, *refs):
    count = 7 * freqs + 1
    moments, refs = refs[count], refs[count + 1 :]
    state, (out, cells, aux) = refs[:count], refs[count:]
    fields = 2 * freqs
    nz = state[0].shape[3]
    w = state[-1]
    above = parity("gx") if side == 0 else jnp.logical_not(parity("gx"))
    group = nz // 8
    wrap = nx + 2 * HALO

    def row_at(distance):
        return jnp.where(above, (nx - 1 + distance) % wrap, -distance % wrap)

    slot = jnp.where(above, nx, nx + HALO)
    for layer in range(HALO):
        for k in range(fields):
            block = state[7 * (k // 2)]
            for y in range(0, ny, 8):
                row = (k * HALO + layer) * ny + y
                block[k % 2, slot + layer, y : y + 8, :] = xb[row : row + 8, :]
        if layer < INNER:
            for y in range(0, ny, 8):
                row = (fields * HALO + layer) * ny + y
                cells[layer, y : y + 8, :] = xb[row : row + 8, :]
    at = (fields * HALO + INNER) * ny
    folded = xb[at : at + ny // 8, :]
    for g in range(8):
        rows = pl.ds(g * (ny // 8), ny // 8)
        aux[rows, :] = pltpu.roll(folded, (nz - g * group) % nz, axis=1)
    place_corners(freqs, nx, ny, cb, state[: 7 * freqs : 7], cells, aux, above)
    for k in range(fields):
        state[7 * (k // 2)][k % 2, row_at(HALO), ny:, :] = jnp.zeros(
            (2 * HALO, nz), F32
        )
    grid = Grid(nx, ny, nz)
    many = [Field(grid, state[7 * f : 7 * f + 7], w) for f in range(freqs)]
    for layer in range(INNER):
        i = jnp.where(above, nx + layer, nx + HALO + 1 + layer)
        terms = grid.prepare(
            i,
            grid.both,
            freq_sq,
            w,
            many,
            lambda t: cells[layer, grid.tile(t), :],
            lambda k, t: grid.pick(aux, t, INNER * k + layer),
        )
        for f in range(freqs):
            for p in range(2):
                grid.put(many[f].v0, p, i, terms[f][p], grid.both)

    place = lax.axis_index("gx")
    more = jnp.where(above, place < lax.axis_size("gx") - 1, place > 0)
    cut = (-1, jnp.where(more, 1.0, 0.0))
    acc = [tuple(grid.zero() for _ in range(4)) for _ in range(freqs)]
    for stage in range(4):
        for k in range(HALO):
            distance = INNER - stage - k
            i, lo, hi = (row_at(distance + d) for d in (0, 1, -1))
            own = distance <= 0
            ends = cut if distance == 0 else None
            for f in range(freqs):
                if stage == 0:
                    many[f].finish(i, grid.both, True, lo, hi, ends)
                    continue
                got = many[f].step(stage, i, lo, hi, ends, acc[f] if own else None)
                if own:
                    acc[f] = got

    if side == 0:
        for f in range(freqs):
            for m in range(4):
                out[f, m] = acc[f][m] + moments[f, m]
        return
    rows = []
    for f in range(freqs):
        for m in range(4):
            both = acc[f][m] + moments[f, m]
            rows.append(jnp.sum(both, axis=0, keepdims=True))
    sums = jnp.sum(jnp.concatenate(rows, axis=0), axis=1, keepdims=True)
    lane = lax.broadcasted_iota(jnp.int32, (4 * freqs, nz), 1)
    sub = lax.broadcasted_iota(jnp.int32, (4 * freqs, nz), 0)
    sums = jnp.where(lane == sub, jnp.broadcast_to(sums, (4 * freqs, nz)), 0.0)
    out[...] = jnp.broadcast_to(jnp.sum(sums, axis=0, keepdims=True), out.shape)


def edge_part(side, peers, freqs, nx, ny, freq_sq, xb, cb, state, moments):
    nz = state[0].shape[3]
    outs = tuple(pltpu.VMEM(k.shape, F32) for k in state)
    if side == 0:
        last = pltpu.VMEM(moments.shape, F32)
    else:
        last = jax.ShapeDtypeStruct((peers, nz), F32)
    *state, out = pl.pallas_call(
        functools.partial(edge_kernel, side, peers, freqs, nx, ny),
        out_shape=outs + (last,),
        in_specs=[VMEM] * (4 + len(state)),
        input_output_aliases={3 + k: k for k in range(len(state))},
        scratch_shapes=[
            pltpu.VMEM((INNER, ny + 2 * HALO, nz), F32),
            pltpu.VMEM((ny + 2 * HALO, nz), F32),
        ],
        compiler_params=params(8),
        name="edge_odd" if side else "edge_even",
    )(freq_sq, xb, cb, *state, moments)
    return state, out


def steps(sums, freqs):
    total = jnp.sum(sums[...], axis=0, keepdims=True)
    shape = (8, total.shape[1])
    out = []
    for f in range(freqs):
        m0, m1, m2, m3 = (
            jnp.broadcast_to(total[:, 4 * f + k : 4 * f + k + 1], shape)
            for k in range(4)
        )
        first = m0 / m1
        new = first * (first * m2 - m1)
        product = m1 - first * (2.0 * m2 - first * m3)
        ratio = new / m0
        second = new / (product - ratio * new / first)
        out.append((first + second * (1.0 + ratio), -first * second))
    return out


def gradient_kernel(freqs, nx, ny, freq_sq, sums, *refs):
    out = refs[-1]
    weights = steps(sums, freqs)
    scale = [-freq_sq[f] for f in range(freqs)]

    def row(x, _):
        for y in range(0, ny, 8):
            at = pl.ds(y, 8)
            total = None
            for f in range(freqs):
                s, v0, u0, v1, u1 = refs[5 * f : 5 * f + 5]
                a, b = weights[f]
                wave_re = a * v0[0, x, at, :] + b * v1[0, x, at, :]
                wave_im = a * v0[1, x, at, :] + b * v1[1, x, at, :]
                miss_re = a * u0[0, x, at, :] + b * u1[0, x, at, :]
                miss_im = a * u0[1, x, at, :] + b * u1[1, x, at, :]
                miss_re = miss_re - s[0, x, at, :]
                miss_im = miss_im - s[1, x, at, :]
                left = (wave_re + attenuation * wave_im) * miss_re
                right = (wave_im - attenuation * wave_re) * miss_im
                term = scale[f] * (left + right)
                total = term if total is None else total + term
            out[x, at, :] = total
        return 0

    lax.fori_loop(0, nx, row, 0, unroll=2)


def wave_kernel(freqs, nx, ny, sums, *refs):
    out, block, sem = refs[2 * freqs :]
    weights = steps(sums, freqs)
    copies = Copies(sem)
    for f in range(freqs):
        a, b = weights[f]
        v0, v1 = refs[2 * f : 2 * f + 2]
        for p in range(2):
            k = 2 * f + p

            def row(x, _):
                for y in range(0, ny, 8):
                    at = pl.ds(y, 8)
                    block[k, x, at, :] = a * v0[p, x, at, :] + b * v1[p, x, at, :]
                return 0

            lax.fori_loop(0, nx, row, 0, unroll=8)
            copies.add(block.at[k], out.at[f, p])
    copies.wait()


def results(freqs, nx, ny, freq_sq, sums, state):
    nz = state[0].shape[3]
    fields, pairs = [], []
    for f in range(freqs):
        s, v0, u0, v1, u1 = state[7 * f : 7 * f + 5]
        fields += [s, v0, u0, v1, u1]
        pairs += [v0, v1]
    gradient = pl.pallas_call(
        functools.partial(gradient_kernel, freqs, nx, ny),
        out_shape=jax.ShapeDtypeStruct((nx, ny, nz), F32),
        in_specs=[VMEM] * (2 + len(fields)),
        out_specs=VMEM,
        compiler_params=params(8),
        name="gradient_part",
    )(freq_sq, sums, *fields)
    wave = pl.pallas_call(
        functools.partial(wave_kernel, freqs, nx, ny),
        out_shape=jax.ShapeDtypeStruct((freqs, 2, nx, ny, nz), F32),
        in_specs=[VMEM] * (1 + len(pairs)),
        out_specs=HBM,
        scratch_shapes=[
            pltpu.VMEM((2 * freqs, nx, ny, nz), F32),
            pltpu.SemaphoreType.DMA((2 * freqs,)),
        ],
        compiler_params=params(8),
        name="wavefield",
    )(sums, *pairs)
    return gradient, wave


def add_kernel(one, two, out, block, sem):
    nx, ny, _ = one.shape
    copies = Copies(sem)
    parts = sem.shape[0]
    step = nx // parts
    for part in range(parts):

        def row(x, _):
            for y in range(0, ny, 8):
                at = pl.ds(y, 8)
                block[x, at, :] = one[x, at, :] + two[x, at, :]
            return 0

        lax.fori_loop(part * step, (part + 1) * step, row, 0, unroll=4)
        span = pl.ds(part * step, step)
        copies.add(block.at[span], out.at[span])
    copies.wait()


def add(one, two):
    return pl.pallas_call(
        add_kernel,
        out_shape=jax.ShapeDtypeStruct(one.shape, F32),
        in_specs=[VMEM] * 2,
        out_specs=HBM,
        scratch_shapes=[pltpu.VMEM(one.shape, F32), pltpu.SemaphoreType.DMA((2,))],
        compiler_params=params(4),
        name="add",
    )(one, two)


def swap(cells, axis, odd):
    names = ("gx", "gy", "af")
    sizes = [lax.axis_size(name) for name in names]
    along = names.index(axis)
    pairs = []
    for flat in range(sizes[0] * sizes[1] * sizes[2]):
        place = [flat // (sizes[1] * sizes[2]), flat // sizes[2] % sizes[1], flat % sizes[2]]
        mate = ((place[along] + odd) ^ 1) - odd
        if 0 <= mate < sizes[along]:
            place[along] = mate
        elif sizes[2] % 2 == 0:
            place[2] ^= 1
        else:
            continue
        pairs.append((flat, (place[0] * sizes[1] + place[1]) * sizes[2] + place[2]))
    return lax.ppermute(cells, names, pairs)


def on_device(model, freq_sq, source, observed, receiver_depth):
    nx, ny, nz = model.shape
    freqs = freq_sq.shape[0]
    *s, cells, aux, xe, xo, ye, yo = load(source, model, observed, receiver_depth)
    ye, yo = swap(ye, "gy", 0), swap(yo, "gy", 1)
    xe, xo = swap(xe, "gx", 0), swap(xo, "gx", 1)
    *known, splat = early(nx, ny, freq_sq, s, cells, aux)
    ce, co, rest = inner_part(nx, ny, splat, ye, yo, s, cells, aux, known)
    ce, co = swap(ce, "gx", 0), swap(co, "gx", 1)
    state, moments = rest()
    peers = lax.axis_size("gx") * lax.axis_size("gy")
    state, moments = edge_part(
        0, peers, freqs, nx, ny, splat, xe, ce, state, moments
    )
    state, part = edge_part(1, peers, freqs, nx, ny, splat, xo, co, state, moments)
    sums = lax.all_to_all(part, ("gx", "gy"), 0, 0)
    gradient, wave = results(freqs, nx, ny, splat, sums, state)
    if lax.axis_size("af") == 2:
        gradient = add(gradient, lax.ppermute(gradient, "af", [(0, 1), (1, 0)]))
    else:
        gradient = lax.psum(gradient, "af")
    return wave, gradient


def solution(mesh):
    in_specs = (
        P("gx", "gy", None),
        P("af"),
        P("af", None, "gx", "gy", None),
        P("af", None, "gx", "gy"),
        P("gx", "gy"),
    )
    out_specs = (P("af", None, "gx", "gy", None), P("gx", "gy", None))
    return jax.shard_map(
        on_device, mesh=mesh, in_specs=in_specs, out_specs=out_specs, check_vma=False
    )
```

```python
import functools

import jax
import jax.numpy as jnp
from jax import lax
from jax.experimental import pallas as pl
from jax.experimental.pallas import tpu as pltpu
from jax.sharding import PartitionSpec as P

ITERS = 2
attenuation = 0.2
penalty = 4.0

HALO = 2 * ITERS
INNER = HALO - 1
F32 = jnp.float32
ANY = pl.BlockSpec(memory_space=pl.ANY)
HBM = pl.BlockSpec(memory_space=pltpu.HBM)
VMEM = pl.BlockSpec(memory_space=pltpu.VMEM)
SMEM = pl.BlockSpec(memory_space=pltpu.SMEM)
MIB = 1 << 20
LOAD_MIB = 55
SHIFT = -4


def params(mib):
    return pltpu.CompilerParams(vmem_limit_bytes=mib * MIB)


def cost(us):
    return pl.CostEstimate(
        flops=int(us * 1e3), bytes_accessed=int(us * 1e3), transcendentals=0
    )


def parity(axis):
    return lax.rem(lax.axis_index(axis), 2) == 0


class Copies:
    def __init__(self, sem):
        self.sem, self.all = sem, []

    def add(self, src, dst):
        copy = pltpu.make_async_copy(src, dst, self.sem.at[len(self.all)])
        copy.start()
        self.all.append(copy)

    def wait(self):
        for copy in self.all:
            copy.wait()


def lane_slab(table, fields, skip, rows, nz):
    lane = lax.broadcasted_iota(jnp.int32, (rows, nz), 1)
    lanes = jnp.zeros((rows, nz), F32)
    for k in range(fields + 1):
        inside = (lane >= INNER * k) & (lane < INNER * k + INNER)
        shift = lax.rem(INNER * k + nz - skip, nz)
        lanes = jnp.where(inside, pltpu.roll(table[k], shift, axis=1), lanes)
    return lanes


def fold(slab, nz):
    rows, width = slab.shape[0] // 8, nz // 8
    lane = lax.broadcasted_iota(jnp.int32, (rows, nz), 1)
    out = jnp.zeros((rows, nz), F32)
    for g in range(8):
        piece = slab[g * rows : (g + 1) * rows, :]
        inside = (lane >= g * width) & (lane < (g + 1) * width)
        out = jnp.where(inside, pltpu.roll(piece, g * width, axis=1), out)
    return out


def load_kernel(source, model, observed, depth, *refs):
    freqs, _, nx, ny, nz = source.shape
    fields = 2 * freqs
    s, (cells, aux, xe, xo, ye, yo, seen, sunk, table, sem) = refs[:freqs], refs[freqs:]
    small = Copies(sem.at[0])
    small.add(observed, seen)
    small.add(depth, sunk)
    large = Copies(sem.at[1])
    large.add(model, cells.at[:, pl.ds(0, ny), :])
    for f in range(freqs):
        for p in range(2):
            large.add(source.at[f, p], s[f].at[p, pl.ds(0, nx), pl.ds(0, ny), :])
    even_x, even_y = parity("gx"), parity("gy")
    small.wait()
    for f in range(freqs):
        for p in range(2):
            table[2 * f + p, :, 0:nx] = seen[f, p].T
    table[fields, :, 0:nx] = sunk[...].astype(F32).T
    copies = Copies(sem.at[2])
    copies.add(table, aux.at[:, pl.ds(0, ny), :])
    faces = []
    for side, xb in enumerate((xe, xo)):
        last = even_x if side == 0 else jnp.logical_not(even_x)
        skip = jnp.where(last, nx - INNER, 0)
        faces.append((xb, skip, jnp.where(last, nx - HALO, 0)))
        at = (fields * HALO + INNER) * ny
        xb[at : at + ny // 8, :] = fold(lane_slab(table, fields, skip, ny, nz), nz)
    swapped = jnp.broadcast_to(even_y, (HALO, nz))

    def y_faces(block, at):
        def row(x, _):
            head, tail = block[x, 0:HALO, :], block[x, ny - HALO : ny, :]
            ye[at + x] = jnp.where(swapped, tail, head)
            yo[at + x] = jnp.where(swapped, head, tail)
            return 0

        lax.fori_loop(0, nx, row, 0, unroll=8)

    def x_face(xb, to, block, at, layers):
        for layer in range(layers):
            for y in range(0, ny, 8):
                row = (to + layer) * ny + y
                xb[row : row + 8, :] = block[at + layer, y : y + 8, :]

    lane = lax.broadcasted_iota(jnp.int32, (HALO, nz), 1)
    at = fields * nx + nx // 4 * 3
    for slab in range(-(-(fields + 1) // (nz // nx))):
        pair = [jnp.zeros((HALO, nz), F32)] * 2
        for g in range(nz // nx):
            k = slab * (nz // nx) + g
            if k > fields:
                continue
            inside = (lane >= g * nx) & (lane < (g + 1) * nx)
            for end, rows in enumerate((table[k, 0:HALO, :], table[k, ny - HALO : ny, :])):
                moved = pltpu.roll(rows, g * nx, axis=1)
                pair[end] = jnp.where(inside, moved, pair[end])
        ye[at + slab] = jnp.where(swapped, pair[1], pair[0])
        yo[at + slab] = jnp.where(swapped, pair[0], pair[1])
    large.all[0].wait()
    sub = lax.broadcasted_iota(jnp.int32, (8, nz), 0)

    def model_rows(g, _):
        heads = [cells[4 * g + j, 0:8, :] for j in range(4)]
        tails = [cells[4 * g + j, ny - 8 : ny, :] for j in range(4)]
        for j in range(3):
            head = jnp.where(sub == 3, pltpu.roll(heads[3], 3 - j, axis=0), heads[j])
            tail = jnp.where(sub == 4, pltpu.roll(tails[3], 7 - j, axis=0), tails[j])
            head, tail = head[0:HALO, :], tail[8 - HALO : 8, :]
            ye[fields * nx + 3 * g + j] = jnp.where(swapped, tail, head)
            yo[fields * nx + 3 * g + j] = jnp.where(swapped, head, tail)
        return 0

    lax.fori_loop(0, nx // 4, model_rows, 0, unroll=2)
    for xb, skip, _ in faces:
        x_face(xb, fields * HALO, cells, skip, INNER)
    for k in range(fields):
        large.all[1 + k].wait()
        block = s[k // 2].at[k % 2]
        y_faces(block, k * nx)
        for xb, _, at in faces:
            x_face(xb, k * HALO, block, at, HALO)
    copies.wait()


def load(source, model, observed, depth):
    freqs, _, nx, ny, nz = source.shape
    fields = 2 * freqs
    xs = pltpu.VMEM(((fields * HALO + INNER) * ny + 8, nz), F32)
    slabs = fields * nx + nx // 4 * 3 + -(-(fields + 1) // (nz // nx))
    ys = pltpu.VMEM((slabs, HALO, nz), F32)
    return pl.pallas_call(
        load_kernel,
        out_shape=(pltpu.VMEM((2, nx + 2 * HALO, ny + 2 * HALO, nz), F32),) * freqs
        + (
            pltpu.VMEM((nx, ny + 2 * HALO, nz), F32),
            pltpu.VMEM((fields + 1, ny + 2 * HALO, nz), F32),
            xs,
            xs,
            ys,
            ys,
        ),
        in_specs=[HBM] * 4,
        scratch_shapes=[
            pltpu.VMEM(observed.shape, F32),
            pltpu.VMEM(depth.shape, jnp.int32),
            pltpu.VMEM((fields + 1, ny, nz), F32),
            pltpu.SemaphoreType.DMA((3, 32)),
        ],
        compiler_params=params(LOAD_MIB),
        name="load",
    )(source, model, observed, depth)


class Grid:
    def __init__(self, nx, ny, nz):
        self.nx, self.ny, self.nz = nx, ny, nz
        self.xe = nx + 2 * HALO
        self.tiles = ny // 8
        self.own = range(self.tiles)
        self.both = range(self.tiles + 1)
        lane = lax.broadcasted_iota(jnp.int32, (8, nz), 1)
        self.first = lane == 0
        self.last = lane == nz - 1
        self.depths = lane.astype(F32)
        sub = lax.broadcasted_iota(jnp.int32, (8, nz), 0)
        self.top = sub == 7
        self.bottom = sub == 0
        has_left = lax.axis_index("gy") > 0
        has_right = lax.axis_index("gy") < lax.axis_size("gy") - 1
        self.left = jnp.where(has_left, 1.0, 0.0)
        self.right = jnp.where(has_right, 1.0, 0.0)
        self.inside = jnp.where(sub < HALO, self.right, self.left)

    def tile(self, t):
        if t < self.tiles:
            return pl.ds(t, 8, stride=self.tiles)
        return pl.ds(self.ny, 8)

    def rows(self, ref, p, i, tiles):
        return [ref[p, i, self.tile(t), :] for t in tiles]

    def put(self, ref, p, i, values, tiles):
        for t in tiles:
            ref[p, i, self.tile(t), :] = values[t]

    def beside(self, mid):
        left = jnp.where(self.first, 0.0, pltpu.roll(mid, 1, axis=1))
        right = jnp.where(self.last, 0.0, pltpu.roll(mid, self.nz - 1, axis=1))
        return left + right

    def around(self, mid, below, above, tiles):
        n = self.tiles
        halo = mid[n] if len(mid) > n else None
        first_up = pltpu.roll(mid[0], 7, axis=0)
        last_down = pltpu.roll(mid[n - 1], 1, axis=0)
        if halo is not None:
            halo_up = pltpu.roll(halo, 7, axis=0)
            halo_down = pltpu.roll(halo, 1, axis=0)
        total = {}
        for t in tiles:
            if t == n:
                up = jnp.where(self.top, first_up, halo_up)
                down = jnp.where(self.bottom, last_down, halo_down)
            else:
                up = mid[t + 1] if t + 1 < n else None
                down = mid[t - 1] if t else None
                if up is None:
                    edge = 0.0 if halo is None else halo_up
                    up = jnp.where(self.top, edge, first_up)
                if down is None:
                    edge = 0.0 if halo is None else halo_down
                    down = jnp.where(self.bottom, edge, last_down)
            total[t] = ((below[t] + above[t]) + (up + down)) + self.beside(mid[t])
        return total

    def apply(self, src, i, lo, hi, sign, coef, tiles, wide=True, cut=None):
        cr, ci = coef
        mids, totals = [], []
        for p in range(2):
            mid = self.rows(src, p, i, self.both if wide else self.own)
            below = {t: src[p, lo, self.tile(t), :] for t in tiles}
            above = {t: src[p, hi, self.tile(t), :] for t in tiles}
            if cut is not None and cut[0] < 0:
                below = {t: v * cut[1] for t, v in below.items()}
            if cut is not None and cut[0] > 0:
                above = {t: v * cut[1] for t, v in above.items()}
            mids.append(mid)
            totals.append(self.around(mid, below, above, tiles))
        out_re, out_im = {}, {}
        for t in tiles:
            re, im = mids[0][t], mids[1][t]
            if sign > 0:
                out_re[t] = cr[t] * re - ci[t] * im - totals[0][t]
                out_im[t] = cr[t] * im + ci[t] * re - totals[1][t]
            else:
                out_re[t] = cr[t] * re + ci[t] * im - totals[0][t]
                out_im[t] = cr[t] * im - ci[t] * re - totals[1][t]
        return mids, out_re, out_im

    def squares(self, re, im):
        return {t: re[t] * re[t] + im[t] * im[t] for t in self.own}

    def gather(self, values):
        return functools.reduce(jnp.add, [values[t] for t in self.own])

    def zero(self):
        return jnp.zeros((8, self.nz), F32)

    def prepare(self, i, tiles, freq_sq, w, many, cell, column):
        fields = 2 * len(many)
        weight = {}
        for t in tiles:
            depth = column(fields, t)
            weight[t] = jnp.where(self.depths == depth, penalty, 0.0)
            w[i, t] = weight[t]
        out = []
        for f, field in enumerate(many):
            for t in tiles:
                scaled = freq_sq[f] * cell(t)
                field.cr[i, t] = 6.0 - scaled
                field.ci[i, t] = attenuation * scaled
            out.append(
                [
                    {t: weight[t] * column(2 * f + p, t) for t in tiles}
                    for p in range(2)
                ]
            )
        return out

    def pick(self, ref, t, lane):
        at = jnp.full((8, self.nz), lane, jnp.int32)
        return jnp.take_along_axis(ref[self.tile(t), :], at, axis=1)


class Field:
    def __init__(self, grid, refs, w):
        self.grid = grid
        self.s, self.v0, self.u0, self.v1, self.u1, self.cr, self.ci = refs
        self.w = w

    def coef(self, i, tiles):
        return {t: self.cr[i, t] for t in tiles}, {t: self.ci[i, t] for t in tiles}

    def finish(self, i, tiles, wide, lo=None, hi=None, cut=None):
        g = self.grid
        _, re, im = g.apply(self.s, i, lo, hi, -1, self.coef(i, tiles), tiles, wide, cut)
        for p, value in enumerate((re, im)):
            for t in tiles:
                at = g.tile(t)
                total = self.v0[p, i, at, :] + value[t]
                self.v0[p, i, at, :] = total * g.inside if t == g.tiles else total

    def first_halo(self, i, terms):
        g = self.grid
        n = g.tiles
        coef = self.coef(i, [n])
        _, re, im = g.apply(self.s, i, i - 1, i + 1, -1, coef, [n])
        for p, value in enumerate((re, im)):
            self.v0[p, i, g.tile(n), :] = (value[n] + terms[p][n]) * g.inside
            halo = self.s[p, i, g.tile(n), :]
            low = jnp.where(g.bottom, pltpu.roll(halo, 1, axis=0), 0.0)
            high = jnp.where(g.top, pltpu.roll(halo, 7, axis=0), 0.0)
            for t, change in ((0, low), (n - 1, high)):
                at = g.tile(t)
                self.v0[p, i, at, :] = self.v0[p, i, at, :] - change

    def step(self, stage, i, lo, hi, cut=None, acc=None):
        g = self.grid
        src = (None, self.v0, self.u0, self.v1)[stage]
        dst = (None, self.u0, self.v1, self.u1)[stage]
        tiles = g.own if stage == 3 else g.both
        sign = -1 if stage == 2 else 1
        mids, re, im = g.apply(src, i, lo, hi, sign, self.coef(i, tiles), tiles, True, cut)
        if stage != 3:
            weight = {t: self.w[i, t] for t in tiles}
        if stage == 2:
            for p, out in enumerate((re, im)):
                for t in tiles:
                    out[t] = out[t] + weight[t] * self.v0[p, i, g.tile(t), :]
        if stage != 3:
            re[g.tiles] = re[g.tiles] * g.inside
            im[g.tiles] = im[g.tiles] * g.inside
        g.put(dst, 0, i, re, tiles)
        g.put(dst, 1, i, im, tiles)
        if acc is None:
            return None
        acc = list(acc)
        squares = g.squares(re, im)
        acc[stage] = acc[stage] + g.gather(squares)
        if stage == 1:
            squares = g.squares(*mids)
            acc[0] = acc[0] + g.gather(squares)
        if stage != 3:
            at = 1 if stage == 1 else 3
            weighted = {t: weight[t] * squares[t] for t in g.own}
            acc[at] = acc[at] + g.gather(weighted)
        return tuple(acc)


def early_kernel(freqs, nx, ny, freq_sq, *refs):
    s, (cells, aux), refs = refs[:freqs], refs[freqs : freqs + 2], refs[freqs + 2 :]
    w, splat = refs[3 * freqs :]
    nz = cells.shape[2]
    for f in range(freqs):
        splat[f] = jnp.full((8, nz), freq_sq[f], F32)
    grid = Grid(nx, ny, nz)
    many = [
        Field(grid, (s[f], refs[3 * f], None, None, None, *refs[3 * f + 1 : 3 * f + 3]), w)
        for f in range(freqs)
    ]

    def prepare(i):
        return grid.prepare(
            i,
            grid.own,
            freq_sq,
            w,
            many,
            lambda t: cells[i, grid.tile(t), :],
            lambda k, t: grid.pick(aux.at[k], t, i),
        )

    for i in (0, nx - 1):
        terms = prepare(i)
        for f in range(freqs):
            for p in range(2):
                grid.put(many[f].v0, p, i, terms[f][p], grid.own)

    def row(i):
        terms = prepare(i)
        for f in range(freqs):
            field = many[f]
            _, re, im = grid.apply(
                field.s, i, i - 1, i + 1, -1, field.coef(i, grid.own), grid.own, False
            )
            for p, value in enumerate((re, im)):
                value = {t: value[t] + terms[f][p][t] for t in grid.own}
                grid.put(field.v0, p, i, value, grid.own)

    def pair(k, _):
        row(2 * k + 1)
        row(2 * k + 2)
        return 0

    lax.fori_loop(0, (nx - 2) // 2, pair, 0)


def early(nx, ny, freq_sq, s, cells, aux):
    freqs = len(s)
    _, xe, _, nz = s[0].shape
    field = pltpu.VMEM(s[0].shape, F32)
    coef = pltpu.VMEM((xe, ny // 8 + 1, 8, nz), F32)
    return pl.pallas_call(
        functools.partial(early_kernel, freqs, nx, ny),
        out_shape=(field, coef, coef) * freqs
        + (coef, pltpu.VMEM((freqs, 8, nz), F32)),
        in_specs=[SMEM] + [VMEM] * (freqs + 2),
        compiler_params=params(8),
        name="early",
    )(freq_sq, *s, cells, aux)


def corner_faces(freqs, nx, ny, s, cells, aux, ce, co):
    fields = 2 * freqs
    nz = cells.shape[2]
    sub = lax.broadcasted_iota(jnp.int32, (2 * HALO, nz), 0)
    even_x = parity("gx")
    near = [aux[k, ny:, :] for k in range(fields + 1)]
    for side, cb in enumerate((ce, co)):
        last = even_x if side == 0 else jnp.logical_not(even_x)
        at = [jnp.where(last, nx - d, d - 1) for d in range(1, HALO)]
        for k in range(fields):
            one, two, three = (s[k // 2][k % 2, x, ny:, :] for x in at)
            one = jnp.where(sub == 3, pltpu.roll(three, 3, axis=0), one)
            cb[k] = jnp.where(sub == 4, pltpu.roll(three, 5, axis=0), one)
            if k % 2 == 0:
                kept = two
                continue
            two = jnp.where(
                sub < 4, pltpu.roll(two, 2, axis=0), pltpu.roll(two, 6, axis=0)
            )
            outer = (sub < 2) | (sub > 5)
            cb[fields + k // 2] = jnp.where(outer, kept, two)
        one, two = cells[at[0], ny:, :], cells[at[1], ny:, :]
        one = jnp.where(sub == 2, pltpu.roll(two, 2, axis=0), one)
        cb[fields + freqs] = jnp.where(sub == 5, pltpu.roll(two, 6, axis=0), one)
        skip = jnp.where(last, nx - INNER, 0)
        cb[fields + freqs + 1] = lane_slab(near, fields, skip, 2 * HALO, nz)


def place_corners(freqs, nx, ny, cb, s, cells, aux, above):
    fields = 2 * freqs
    nz = cb.shape[2]
    sub = lax.broadcasted_iota(jnp.int32, (2 * HALO, nz), 0)
    slot = [jnp.where(above, nx + d - 1, nx + 2 * HALO - d) for d in range(1, HALO)]
    layer = [jnp.where(above, d - 1, INNER - d) for d in range(1, HALO)]
    for k in range(fields):
        field, p = s[k // 2], k % 2
        one = cb[k]
        field[p, slot[0], ny:, :] = one
        field[p, slot[2], ny:, :] = jnp.where(
            sub == 0, pltpu.roll(one, 5, axis=0), pltpu.roll(one, 3, axis=0)
        )
        two = cb[fields + k // 2]
        if p:
            two = jnp.where(
                sub < 4, pltpu.roll(two, 6, axis=0), pltpu.roll(two, 2, axis=0)
            )
        field[p, slot[1], ny:, :] = two
    one = cb[fields + freqs]
    cells[layer[0], ny:, :] = one
    cells[layer[1], ny:, :] = jnp.where(
        sub == 0, pltpu.roll(one, 6, axis=0), pltpu.roll(one, 2, axis=0)
    )
    cells[layer[2], ny:, :] = jnp.zeros((2 * HALO, nz), F32)
    aux[ny:, :] = cb[fields + freqs + 1]


def inner_kernel(freqs, nx, ny, half, freq_sq, *refs):
    if half == 0:
        ye, yo = refs[:2]
        count = 4 * freqs + 3
        refs = refs[2 + count :]
        s, (cells, aux), refs = refs[:freqs], refs[freqs : freqs + 2], refs[freqs + 2 :]
        known, refs = refs[: 3 * freqs + 1], refs[3 * freqs + 1 :]
        news, (moments, ce, co) = refs[: 3 * freqs], refs[3 * freqs :]
    else:
        s, known = refs[:freqs], refs[freqs : 4 * freqs + 1]
        partial = refs[7 * freqs + 1]
        refs = refs[7 * freqs + 2 :]
        news, (moments,) = refs[: 3 * freqs], refs[3 * freqs :]
    nz = s[0].shape[3]
    fields = 2 * freqs
    w = known[3 * freqs]
    grid = Grid(nx, ny, nz)
    many = []
    for f in range(freqs):
        v0, cr, ci = known[3 * f : 3 * f + 3]
        u0, v1, u1 = news[3 * f : 3 * f + 3]
        many.append(Field(grid, (s[f], v0, u0, v1, u1, cr, ci), w))
    if half == 0:
        swapped = jnp.broadcast_to(parity("gy"), (HALO, nz))

        def halo(at):
            even, odd = ye[at], yo[at]
            high = jnp.where(swapped, even, odd) * grid.right
            low = jnp.where(swapped, odd, even) * grid.left
            return jnp.concatenate([high, low], axis=0)

        sub = lax.broadcasted_iota(jnp.int32, (8, nz), 0)

        def model_rows(g, _):
            tiles = [halo(fields * nx + 3 * g + j) for j in range(3)]
            last = tiles[0]
            for j in range(3):
                cells[4 * g + j, ny:, :] = tiles[j]
                last = jnp.where(sub == j, pltpu.roll(tiles[j], 5 + j, axis=0), last)
                last = jnp.where(sub == 5 + j, pltpu.roll(tiles[j], 1 + j, axis=0), last)
            cells[4 * g + 3, ny:, :] = last
            return 0

        def merge(x, _):
            for k in range(fields):
                s[k // 2][k % 2, x, ny:, :] = halo(k * nx + x)
            return 0

        lax.fori_loop(0, nx // 4, model_rows, 0, unroll=2)
        lax.fori_loop(0, nx, merge, 0, unroll=4)
        for k in range(fields + 1):
            slab, g = divmod(k, nz // nx)
            tile = halo(fields * nx + nx // 4 * 3 + slab)
            aux[k, ny:, :] = pltpu.roll(tile, (nz - g * nx) % nz, axis=1) if g else tile
        corner_faces(freqs, nx, ny, s, cells, aux, ce, co)

    def prepare(i):
        return grid.prepare(
            i,
            [grid.tiles],
            freq_sq,
            w,
            many,
            lambda t: cells[i, grid.tile(t), :],
            lambda k, t: grid.pick(aux.at[k], t, i),
        )

    if half == 0:
        for i in (0, nx - 1):
            terms = prepare(i)
            for f in range(freqs):
                for p in range(2):
                    grid.put(many[f].v0, p, i, terms[f][p], [grid.tiles])

    def step(j, acc, active):
        acc = list(acc)
        for k in reversed(active):
            i = j - 2 * k
            if k == 0:
                terms = prepare(i)
            for f in range(freqs):
                if k == 0:
                    many[f].first_halo(i, terms[f])
                else:
                    acc[f] = many[f].step(k, i, i - 1, i + 1, acc=acc[f])
        return tuple(acc)

    def heads(i, _):
        terms = prepare(i)
        for f in range(freqs):
            many[f].first_halo(i, terms[f])
        return 0

    spans = [(1 + 3 * k, nx - 1 + k) for k in range(4)]
    middle = nx // 2 + SHIFT
    edges = sorted({e for span in spans for e in span} | {middle})
    acc = tuple(tuple(grid.zero() for _ in range(4)) for _ in range(freqs))
    if half == 0:
        lax.fori_loop(1, nx - 1, heads, 0, unroll=3)
    for lo, hi in zip(edges[:-1], edges[1:]):
        if (lo < middle) != (half == 0):
            continue
        active = [k for k, (a, b) in enumerate(spans) if k and a <= lo and hi <= b]
        if active:
            acc = lax.fori_loop(
                lo,
                hi,
                functools.partial(step, active=active),
                acc,
                unroll=3 if hi - lo > 4 else hi - lo,
            )
    for f in range(freqs):
        for m in range(4):
            value = acc[f][m]
            moments[f, m] = value if half == 0 else value + partial[f, m]


def inner_part(nx, ny, freq_sq, ye, yo, s, cells, aux, known):
    freqs = len(s)
    nz = cells.shape[2]
    slabs = 3 * freqs + 2
    field = pltpu.VMEM(s[0].shape, F32)
    corner = pltpu.VMEM((slabs, 2 * HALO, nz), F32)
    kept = (*s, cells, aux, *known)
    news = (field,) * (3 * freqs) + (pltpu.VMEM((freqs, 4, 8, nz), F32),)
    got = pl.pallas_call(
        functools.partial(inner_kernel, freqs, nx, ny, 0),
        out_shape=tuple(pltpu.VMEM(k.shape, F32) for k in kept)
        + news
        + (corner, corner),
        in_specs=[VMEM] * (3 + len(kept)),
        input_output_aliases={3 + k: k for k in range(len(kept))},
        compiler_params=params(8),
        name="inner_first",
    )(freq_sq, ye, yo, *kept)
    s, known = got[:freqs], got[freqs + 2 : len(kept)]
    news_got, (ce, co) = got[len(kept) : -2], got[-2:]

    def rest():
        first = freqs + len(known)
        again = pl.pallas_call(
            functools.partial(inner_kernel, freqs, nx, ny, 1, None),
            out_shape=news,
            in_specs=[VMEM] * (freqs + len(known) + len(news)),
            input_output_aliases={first + k: k for k in range(len(news))},
            compiler_params=params(8),
            name="inner_second",
        )(*s, *known, *news_got)
        state = []
        for f in range(freqs):
            v0, cr, ci = known[3 * f : 3 * f + 3]
            state += [s[f], v0, *again[3 * f : 3 * f + 3], cr, ci]
        return state + [known[-1]], again[-1]

    return ce, co, rest


def edge_kernel(side, peers, freqs, nx, ny, freq_sq, xb, cb, *refs):
    count = 7 * freqs + 1
    moments, refs = refs[count], refs[count + 1 :]
    state, (out, cells, aux) = refs[:count], refs[count:]
    fields = 2 * freqs
    nz = state[0].shape[3]
    w = state[-1]
    above = parity("gx") if side == 0 else jnp.logical_not(parity("gx"))
    group = nz // 8
    wrap = nx + 2 * HALO

    def row_at(distance):
        return jnp.where(above, (nx - 1 + distance) % wrap, -distance % wrap)

    slot = jnp.where(above, nx, nx + HALO)
    for layer in range(HALO):
        for k in range(fields):
            block = state[7 * (k // 2)]
            for y in range(0, ny, 8):
                row = (k * HALO + layer) * ny + y
                block[k % 2, slot + layer, y : y + 8, :] = xb[row : row + 8, :]
        if layer < INNER:
            for y in range(0, ny, 8):
                row = (fields * HALO + layer) * ny + y
                cells[layer, y : y + 8, :] = xb[row : row + 8, :]
    at = (fields * HALO + INNER) * ny
    folded = xb[at : at + ny // 8, :]
    for g in range(8):
        rows = pl.ds(g * (ny // 8), ny // 8)
        aux[rows, :] = pltpu.roll(folded, (nz - g * group) % nz, axis=1)
    place_corners(freqs, nx, ny, cb, state[: 7 * freqs : 7], cells, aux, above)
    for k in range(fields):
        state[7 * (k // 2)][k % 2, row_at(HALO), ny:, :] = jnp.zeros(
            (2 * HALO, nz), F32
        )
    grid = Grid(nx, ny, nz)
    many = [Field(grid, state[7 * f : 7 * f + 7], w) for f in range(freqs)]
    for layer in range(INNER):
        i = jnp.where(above, nx + layer, nx + HALO + 1 + layer)
        terms = grid.prepare(
            i,
            grid.both,
            freq_sq,
            w,
            many,
            lambda t: cells[layer, grid.tile(t), :],
            lambda k, t: grid.pick(aux, t, INNER * k + layer),
        )
        for f in range(freqs):
            for p in range(2):
                grid.put(many[f].v0, p, i, terms[f][p], grid.both)

    place = lax.axis_index("gx")
    more = jnp.where(above, place < lax.axis_size("gx") - 1, place > 0)
    cut = (-1, jnp.where(more, 1.0, 0.0))
    acc = [tuple(grid.zero() for _ in range(4)) for _ in range(freqs)]
    for stage in range(4):
        for k in range(HALO):
            distance = INNER - stage - k
            i, lo, hi = (row_at(distance + d) for d in (0, 1, -1))
            own = distance <= 0
            ends = cut if distance == 0 else None
            for f in range(freqs):
                if stage == 0:
                    many[f].finish(i, grid.both, True, lo, hi, ends)
                    continue
                got = many[f].step(stage, i, lo, hi, ends, acc[f] if own else None)
                if own:
                    acc[f] = got

    if side == 0:
        for f in range(freqs):
            for m in range(4):
                out[f, m] = acc[f][m] + moments[f, m]
        return
    rows = []
    for f in range(freqs):
        for m in range(4):
            both = acc[f][m] + moments[f, m]
            rows.append(jnp.sum(both, axis=0, keepdims=True))
    sums = jnp.sum(jnp.concatenate(rows, axis=0), axis=1, keepdims=True)
    lane = lax.broadcasted_iota(jnp.int32, (4 * freqs, nz), 1)
    sub = lax.broadcasted_iota(jnp.int32, (4 * freqs, nz), 0)
    sums = jnp.where(lane == sub, jnp.broadcast_to(sums, (4 * freqs, nz)), 0.0)
    out[...] = jnp.broadcast_to(jnp.sum(sums, axis=0, keepdims=True), out.shape)


def edge_part(side, peers, freqs, nx, ny, freq_sq, xb, cb, state, moments):
    nz = state[0].shape[3]
    outs = tuple(pltpu.VMEM(k.shape, F32) for k in state)
    if side == 0:
        last = pltpu.VMEM(moments.shape, F32)
    else:
        last = jax.ShapeDtypeStruct((peers, nz), F32)
    *state, out = pl.pallas_call(
        functools.partial(edge_kernel, side, peers, freqs, nx, ny),
        out_shape=outs + (last,),
        in_specs=[VMEM] * (4 + len(state)),
        input_output_aliases={3 + k: k for k in range(len(state))},
        scratch_shapes=[
            pltpu.VMEM((INNER, ny + 2 * HALO, nz), F32),
            pltpu.VMEM((ny + 2 * HALO, nz), F32),
        ],
        compiler_params=params(8),
        name="edge_odd" if side else "edge_even",
    )(freq_sq, xb, cb, *state, moments)
    return state, out


def steps(sums, freqs):
    total = jnp.sum(sums[...], axis=0, keepdims=True)
    shape = (8, total.shape[1])
    out = []
    for f in range(freqs):
        m0, m1, m2, m3 = (
            jnp.broadcast_to(total[:, 4 * f + k : 4 * f + k + 1], shape)
            for k in range(4)
        )
        first = m0 / m1
        new = first * (first * m2 - m1)
        product = m1 - first * (2.0 * m2 - first * m3)
        ratio = new / m0
        second = new / (product - ratio * new / first)
        out.append((first + second * (1.0 + ratio), -first * second))
    return out


def gradient_kernel(freqs, nx, ny, freq_sq, sums, *refs):
    out = refs[-1]
    weights = steps(sums, freqs)
    scale = [-freq_sq[f] for f in range(freqs)]

    def row(x, _):
        for y in range(0, ny, 8):
            at = pl.ds(y, 8)
            total = None
            for f in range(freqs):
                s, v0, u0, v1, u1 = refs[5 * f : 5 * f + 5]
                a, b = weights[f]
                wave_re = a * v0[0, x, at, :] + b * v1[0, x, at, :]
                wave_im = a * v0[1, x, at, :] + b * v1[1, x, at, :]
                miss_re = a * u0[0, x, at, :] + b * u1[0, x, at, :]
                miss_im = a * u0[1, x, at, :] + b * u1[1, x, at, :]
                miss_re = miss_re - s[0, x, at, :]
                miss_im = miss_im - s[1, x, at, :]
                left = (wave_re + attenuation * wave_im) * miss_re
                right = (wave_im - attenuation * wave_re) * miss_im
                term = scale[f] * (left + right)
                total = term if total is None else total + term
            out[x, at, :] = total
        return 0

    lax.fori_loop(0, nx, row, 0, unroll=4)


def wave_kernel(freqs, nx, ny, sums, *refs):
    out, block, sem = refs[2 * freqs :]
    weights = steps(sums, freqs)
    copies = Copies(sem)
    for f in range(freqs):
        a, b = weights[f]
        v0, v1 = refs[2 * f : 2 * f + 2]
        for p in range(2):
            k = 2 * f + p

            def row(x, _):
                for y in range(0, ny, 8):
                    at = pl.ds(y, 8)
                    block[k, x, at, :] = a * v0[p, x, at, :] + b * v1[p, x, at, :]
                return 0

            lax.fori_loop(0, nx, row, 0, unroll=8)
            copies.add(block.at[k], out.at[f, p])
    copies.wait()


def results(freqs, nx, ny, freq_sq, sums, state):
    nz = state[0].shape[3]
    fields, pairs = [], []
    for f in range(freqs):
        s, v0, u0, v1, u1 = state[7 * f : 7 * f + 5]
        fields += [s, v0, u0, v1, u1]
        pairs += [v0, v1]
    gradient = pl.pallas_call(
        functools.partial(gradient_kernel, freqs, nx, ny),
        out_shape=jax.ShapeDtypeStruct((nx, ny, nz), F32),
        in_specs=[VMEM] * (2 + len(fields)),
        out_specs=VMEM,
        compiler_params=params(8),
        name="gradient_part",
    )(freq_sq, sums, *fields)
    wave = pl.pallas_call(
        functools.partial(wave_kernel, freqs, nx, ny),
        out_shape=jax.ShapeDtypeStruct((freqs, 2, nx, ny, nz), F32),
        in_specs=[VMEM] * (1 + len(pairs)),
        out_specs=HBM,
        scratch_shapes=[
            pltpu.VMEM((2 * freqs, nx, ny, nz), F32),
            pltpu.SemaphoreType.DMA((2 * freqs,)),
        ],
        compiler_params=params(8),
        name="wavefield",
    )(sums, *pairs)
    return gradient, wave


def add_kernel(one, two, out, block, sem):
    nx, ny, _ = one.shape
    copies = Copies(sem)
    parts = sem.shape[0]
    step = nx // parts
    for part in range(parts):

        def row(x, _):
            for y in range(0, ny, 8):
                at = pl.ds(y, 8)
                block[x, at, :] = one[x, at, :] + two[x, at, :]
            return 0

        lax.fori_loop(part * step, (part + 1) * step, row, 0, unroll=4)
        span = pl.ds(part * step, step)
        copies.add(block.at[span], out.at[span])
    copies.wait()


def add(one, two):
    return pl.pallas_call(
        add_kernel,
        out_shape=jax.ShapeDtypeStruct(one.shape, F32),
        in_specs=[VMEM] * 2,
        out_specs=HBM,
        scratch_shapes=[pltpu.VMEM(one.shape, F32), pltpu.SemaphoreType.DMA((4,))],
        compiler_params=params(4),
        name="add",
    )(one, two)


def swap(cells, axis, odd):
    names = ("gx", "gy", "af")
    sizes = [lax.axis_size(name) for name in names]
    along = names.index(axis)
    pairs = []
    for flat in range(sizes[0] * sizes[1] * sizes[2]):
        place = [flat // (sizes[1] * sizes[2]), flat // sizes[2] % sizes[1], flat % sizes[2]]
        mate = ((place[along] + odd) ^ 1) - odd
        if 0 <= mate < sizes[along]:
            place[along] = mate
        elif sizes[2] % 2 == 0:
            place[2] ^= 1
        else:
            continue
        pairs.append((flat, (place[0] * sizes[1] + place[1]) * sizes[2] + place[2]))
    return lax.ppermute(cells, names, pairs)


def on_device(model, freq_sq, source, observed, receiver_depth):
    nx, ny, nz = model.shape
    freqs = freq_sq.shape[0]
    *s, cells, aux, xe, xo, ye, yo = load(source, model, observed, receiver_depth)
    ye, yo = swap(ye, "gy", 0), swap(yo, "gy", 1)
    xe, xo = swap(xe, "gx", 0), swap(xo, "gx", 1)
    *known, splat = early(nx, ny, freq_sq, s, cells, aux)
    ce, co, rest = inner_part(nx, ny, splat, ye, yo, s, cells, aux, known)
    ce, co = swap(ce, "gx", 0), swap(co, "gx", 1)
    state, moments = rest()
    peers = lax.axis_size("gx") * lax.axis_size("gy")
    state, moments = edge_part(
        0, peers, freqs, nx, ny, splat, xe, ce, state, moments
    )
    state, part = edge_part(1, peers, freqs, nx, ny, splat, xo, co, state, moments)
    sums = lax.all_to_all(part, ("gx", "gy"), 0, 0)
    gradient, wave = results(freqs, nx, ny, splat, sums, state)
    if lax.axis_size("af") == 2:
        gradient = add(gradient, lax.ppermute(gradient, "af", [(0, 1), (1, 0)]))
    else:
        gradient = lax.psum(gradient, "af")
    return wave, gradient


def solution(mesh):
    in_specs = (
        P("gx", "gy", None),
        P("af"),
        P("af", None, "gx", "gy", None),
        P("af", None, "gx", "gy"),
        P("gx", "gy"),
    )
    out_specs = (P("af", None, "gx", "gy", None), P("gx", "gy", None))
    return jax.shard_map(
        on_device, mesh=mesh, in_specs=in_specs, out_specs=out_specs, check_vma=False
    )
```

```python
import functools

import jax
import jax.numpy as jnp
from jax import lax
from jax.experimental import pallas as pl
from jax.experimental.pallas import tpu as pltpu
from jax.sharding import PartitionSpec as P

ITERS = 2
attenuation = 0.2
penalty = 4.0

HALO = 2 * ITERS
INNER = HALO - 1
F32 = jnp.float32
ANY = pl.BlockSpec(memory_space=pl.ANY)
HBM = pl.BlockSpec(memory_space=pltpu.HBM)
VMEM = pl.BlockSpec(memory_space=pltpu.VMEM)
SMEM = pl.BlockSpec(memory_space=pltpu.SMEM)
MIB = 1 << 20
LOAD_MIB = 55
SHIFT = -4


def params(mib):
    return pltpu.CompilerParams(vmem_limit_bytes=mib * MIB)


def cost(us):
    return pl.CostEstimate(
        flops=int(us * 1e3), bytes_accessed=int(us * 1e3), transcendentals=0
    )


def parity(axis):
    return lax.rem(lax.axis_index(axis), 2) == 0


class Copies:
    def __init__(self, sem):
        self.sem, self.all = sem, []

    def add(self, src, dst):
        copy = pltpu.make_async_copy(src, dst, self.sem.at[len(self.all)])
        copy.start()
        self.all.append(copy)

    def wait(self):
        for copy in self.all:
            copy.wait()


def lane_slab(table, fields, skip, rows, nz):
    lane = lax.broadcasted_iota(jnp.int32, (rows, nz), 1)
    lanes = jnp.zeros((rows, nz), F32)
    for k in range(fields + 1):
        inside = (lane >= INNER * k) & (lane < INNER * k + INNER)
        shift = lax.rem(INNER * k + nz - skip, nz)
        lanes = jnp.where(inside, pltpu.roll(table[k], shift, axis=1), lanes)
    return lanes


def fold(slab, nz):
    rows, width = slab.shape[0] // 8, nz // 8
    lane = lax.broadcasted_iota(jnp.int32, (rows, nz), 1)
    out = jnp.zeros((rows, nz), F32)
    for g in range(8):
        piece = slab[g * rows : (g + 1) * rows, :]
        inside = (lane >= g * width) & (lane < (g + 1) * width)
        out = jnp.where(inside, pltpu.roll(piece, g * width, axis=1), out)
    return out


def load_kernel(source, model, observed, depth, *refs):
    freqs, _, nx, ny, nz = source.shape
    fields = 2 * freqs
    s, (cells, aux, xe, xo, ye, yo, seen, sunk, table, sem) = refs[:freqs], refs[freqs:]
    small = Copies(sem.at[0])
    small.add(observed, seen)
    small.add(depth, sunk)
    large = Copies(sem.at[1])
    large.add(model, cells.at[:, pl.ds(0, ny), :])
    for f in range(freqs):
        for p in range(2):
            large.add(source.at[f, p], s[f].at[p, pl.ds(0, nx), pl.ds(0, ny), :])
    even_x, even_y = parity("gx"), parity("gy")
    small.wait()
    for f in range(freqs):
        for p in range(2):
            table[2 * f + p, :, 0:nx] = seen[f, p].T
    table[fields, :, 0:nx] = sunk[...].astype(F32).T
    copies = Copies(sem.at[2])
    copies.add(table, aux.at[:, pl.ds(0, ny), :])
    faces = []
    for side, xb in enumerate((xe, xo)):
        last = even_x if side == 0 else jnp.logical_not(even_x)
        skip = jnp.where(last, nx - INNER, 0)
        faces.append((xb, skip, jnp.where(last, nx - HALO, 0)))
        at = (fields * HALO + INNER) * ny
        xb[at : at + ny // 8, :] = fold(lane_slab(table, fields, skip, ny, nz), nz)
    swapped = jnp.broadcast_to(even_y, (HALO, nz))

    def y_faces(block, at):
        def row(x, _):
            head, tail = block[x, 0:HALO, :], block[x, ny - HALO : ny, :]
            ye[at + x] = jnp.where(swapped, tail, head)
            yo[at + x] = jnp.where(swapped, head, tail)
            return 0

        lax.fori_loop(0, nx, row, 0, unroll=8)

    def x_face(xb, to, block, at, layers):
        for layer in range(layers):
            for y in range(0, ny, 8):
                row = (to + layer) * ny + y
                xb[row : row + 8, :] = block[at + layer, y : y + 8, :]

    lane = lax.broadcasted_iota(jnp.int32, (HALO, nz), 1)
    at = fields * nx + nx // 4 * 3
    for slab in range(-(-(fields + 1) // (nz // nx))):
        pair = [jnp.zeros((HALO, nz), F32)] * 2
        for g in range(nz // nx):
            k = slab * (nz // nx) + g
            if k > fields:
                continue
            inside = (lane >= g * nx) & (lane < (g + 1) * nx)
            for end, rows in enumerate((table[k, 0:HALO, :], table[k, ny - HALO : ny, :])):
                moved = pltpu.roll(rows, g * nx, axis=1)
                pair[end] = jnp.where(inside, moved, pair[end])
        ye[at + slab] = jnp.where(swapped, pair[1], pair[0])
        yo[at + slab] = jnp.where(swapped, pair[0], pair[1])
    large.all[0].wait()
    sub = lax.broadcasted_iota(jnp.int32, (8, nz), 0)

    def model_rows(g, _):
        heads = [cells[4 * g + j, 0:8, :] for j in range(4)]
        tails = [cells[4 * g + j, ny - 8 : ny, :] for j in range(4)]
        for j in range(3):
            head = jnp.where(sub == 3, pltpu.roll(heads[3], 3 - j, axis=0), heads[j])
            tail = jnp.where(sub == 4, pltpu.roll(tails[3], 7 - j, axis=0), tails[j])
            head, tail = head[0:HALO, :], tail[8 - HALO : 8, :]
            ye[fields * nx + 3 * g + j] = jnp.where(swapped, tail, head)
            yo[fields * nx + 3 * g + j] = jnp.where(swapped, head, tail)
        return 0

    lax.fori_loop(0, nx // 4, model_rows, 0, unroll=4)
    for xb, skip, _ in faces:
        x_face(xb, fields * HALO, cells, skip, INNER)
    for k in range(fields):
        large.all[1 + k].wait()
        block = s[k // 2].at[k % 2]
        y_faces(block, k * nx)
        for xb, _, at in faces:
            x_face(xb, k * HALO, block, at, HALO)
    copies.wait()


def load(source, model, observed, depth):
    freqs, _, nx, ny, nz = source.shape
    fields = 2 * freqs
    xs = pltpu.VMEM(((fields * HALO + INNER) * ny + 8, nz), F32)
    slabs = fields * nx + nx // 4 * 3 + -(-(fields + 1) // (nz // nx))
    ys = pltpu.VMEM((slabs, HALO, nz), F32)
    return pl.pallas_call(
        load_kernel,
        out_shape=(pltpu.VMEM((2, nx + 2 * HALO, ny + 2 * HALO, nz), F32),) * freqs
        + (
            pltpu.VMEM((nx, ny + 2 * HALO, nz), F32),
            pltpu.VMEM((fields + 1, ny + 2 * HALO, nz), F32),
            xs,
            xs,
            ys,
            ys,
        ),
        in_specs=[HBM] * 4,
        scratch_shapes=[
            pltpu.VMEM(observed.shape, F32),
            pltpu.VMEM(depth.shape, jnp.int32),
            pltpu.VMEM((fields + 1, ny, nz), F32),
            pltpu.SemaphoreType.DMA((3, 32)),
        ],
        compiler_params=params(LOAD_MIB),
        name="load",
    )(source, model, observed, depth)


class Grid:
    def __init__(self, nx, ny, nz):
        self.nx, self.ny, self.nz = nx, ny, nz
        self.xe = nx + 2 * HALO
        self.tiles = ny // 8
        self.own = range(self.tiles)
        self.both = range(self.tiles + 1)
        lane = lax.broadcasted_iota(jnp.int32, (8, nz), 1)
        self.first = lane == 0
        self.last = lane == nz - 1
        self.depths = lane.astype(F32)
        sub = lax.broadcasted_iota(jnp.int32, (8, nz), 0)
        self.top = sub == 7
        self.bottom = sub == 0
        has_left = lax.axis_index("gy") > 0
        has_right = lax.axis_index("gy") < lax.axis_size("gy") - 1
        self.left = jnp.where(has_left, 1.0, 0.0)
        self.right = jnp.where(has_right, 1.0, 0.0)
        self.inside = jnp.where(sub < HALO, self.right, self.left)

    def tile(self, t):
        if t < self.tiles:
            return pl.ds(t, 8, stride=self.tiles)
        return pl.ds(self.ny, 8)

    def rows(self, ref, p, i, tiles):
        return [ref[p, i, self.tile(t), :] for t in tiles]

    def put(self, ref, p, i, values, tiles):
        for t in tiles:
            ref[p, i, self.tile(t), :] = values[t]

    def beside(self, mid):
        left = jnp.where(self.first, 0.0, pltpu.roll(mid, 1, axis=1))
        right = jnp.where(self.last, 0.0, pltpu.roll(mid, self.nz - 1, axis=1))
        return left + right

    def around(self, mid, below, above, tiles):
        n = self.tiles
        halo = mid[n] if len(mid) > n else None
        first_up = pltpu.roll(mid[0], 7, axis=0)
        last_down = pltpu.roll(mid[n - 1], 1, axis=0)
        if halo is not None:
            halo_up = pltpu.roll(halo, 7, axis=0)
            halo_down = pltpu.roll(halo, 1, axis=0)
        total = {}
        for t in tiles:
            if t == n:
                up = jnp.where(self.top, first_up, halo_up)
                down = jnp.where(self.bottom, last_down, halo_down)
            else:
                up = mid[t + 1] if t + 1 < n else None
                down = mid[t - 1] if t else None
                if up is None:
                    edge = 0.0 if halo is None else halo_up
                    up = jnp.where(self.top, edge, first_up)
                if down is None:
                    edge = 0.0 if halo is None else halo_down
                    down = jnp.where(self.bottom, edge, last_down)
            total[t] = ((below[t] + above[t]) + (up + down)) + self.beside(mid[t])
        return total

    def apply(self, src, i, lo, hi, sign, coef, tiles, wide=True, cut=None):
        cr, ci = coef
        mids, totals = [], []
        for p in range(2):
            mid = self.rows(src, p, i, self.both if wide else self.own)
            below = {t: src[p, lo, self.tile(t), :] for t in tiles}
            above = {t: src[p, hi, self.tile(t), :] for t in tiles}
            if cut is not None and cut[0] < 0:
                below = {t: v * cut[1] for t, v in below.items()}
            if cut is not None and cut[0] > 0:
                above = {t: v * cut[1] for t, v in above.items()}
            mids.append(mid)
            totals.append(self.around(mid, below, above, tiles))
        out_re, out_im = {}, {}
        for t in tiles:
            re, im = mids[0][t], mids[1][t]
            if sign > 0:
                out_re[t] = cr[t] * re - ci[t] * im - totals[0][t]
                out_im[t] = cr[t] * im + ci[t] * re - totals[1][t]
            else:
                out_re[t] = cr[t] * re + ci[t] * im - totals[0][t]
                out_im[t] = cr[t] * im - ci[t] * re - totals[1][t]
        return mids, out_re, out_im

    def squares(self, re, im):
        return {t: re[t] * re[t] + im[t] * im[t] for t in self.own}

    def gather(self, values):
        return functools.reduce(jnp.add, [values[t] for t in self.own])

    def zero(self):
        return jnp.zeros((8, self.nz), F32)

    def prepare(self, i, tiles, freq_sq, w, many, cell, column):
        fields = 2 * len(many)
        weight = {}
        for t in tiles:
            depth = column(fields, t)
            weight[t] = jnp.where(self.depths == depth, penalty, 0.0)
            w[i, t] = weight[t]
        out = []
        for f, field in enumerate(many):
            for t in tiles:
                scaled = freq_sq[f] * cell(t)
                field.cr[i, t] = 6.0 - scaled
                field.ci[i, t] = attenuation * scaled
            out.append(
                [
                    {t: weight[t] * column(2 * f + p, t) for t in tiles}
                    for p in range(2)
                ]
            )
        return out

    def pick(self, ref, t, lane):
        at = jnp.full((8, self.nz), lane, jnp.int32)
        return jnp.take_along_axis(ref[self.tile(t), :], at, axis=1)


class Field:
    def __init__(self, grid, refs, w):
        self.grid = grid
        self.s, self.v0, self.u0, self.v1, self.u1, self.cr, self.ci = refs
        self.w = w

    def coef(self, i, tiles):
        return {t: self.cr[i, t] for t in tiles}, {t: self.ci[i, t] for t in tiles}

    def finish(self, i, tiles, wide, lo=None, hi=None, cut=None):
        g = self.grid
        _, re, im = g.apply(self.s, i, lo, hi, -1, self.coef(i, tiles), tiles, wide, cut)
        for p, value in enumerate((re, im)):
            for t in tiles:
                at = g.tile(t)
                total = self.v0[p, i, at, :] + value[t]
                self.v0[p, i, at, :] = total * g.inside if t == g.tiles else total

    def first_halo(self, i, terms):
        g = self.grid
        n = g.tiles
        coef = self.coef(i, [n])
        _, re, im = g.apply(self.s, i, i - 1, i + 1, -1, coef, [n])
        for p, value in enumerate((re, im)):
            self.v0[p, i, g.tile(n), :] = (value[n] + terms[p][n]) * g.inside
            halo = self.s[p, i, g.tile(n), :]
            low = jnp.where(g.bottom, pltpu.roll(halo, 1, axis=0), 0.0)
            high = jnp.where(g.top, pltpu.roll(halo, 7, axis=0), 0.0)
            for t, change in ((0, low), (n - 1, high)):
                at = g.tile(t)
                self.v0[p, i, at, :] = self.v0[p, i, at, :] - change

    def step(self, stage, i, lo, hi, cut=None, acc=None):
        g = self.grid
        src = (None, self.v0, self.u0, self.v1)[stage]
        dst = (None, self.u0, self.v1, self.u1)[stage]
        tiles = g.own if stage == 3 else g.both
        sign = -1 if stage == 2 else 1
        mids, re, im = g.apply(src, i, lo, hi, sign, self.coef(i, tiles), tiles, True, cut)
        if stage != 3:
            weight = {t: self.w[i, t] for t in tiles}
        if stage == 2:
            for p, out in enumerate((re, im)):
                for t in tiles:
                    out[t] = out[t] + weight[t] * self.v0[p, i, g.tile(t), :]
        if stage != 3:
            re[g.tiles] = re[g.tiles] * g.inside
            im[g.tiles] = im[g.tiles] * g.inside
        g.put(dst, 0, i, re, tiles)
        g.put(dst, 1, i, im, tiles)
        if acc is None:
            return None
        acc = list(acc)
        squares = g.squares(re, im)
        acc[stage] = acc[stage] + g.gather(squares)
        if stage == 1:
            squares = g.squares(*mids)
            acc[0] = acc[0] + g.gather(squares)
        if stage != 3:
            at = 1 if stage == 1 else 3
            weighted = {t: weight[t] * squares[t] for t in g.own}
            acc[at] = acc[at] + g.gather(weighted)
        return tuple(acc)


def early_kernel(freqs, nx, ny, freq_sq, *refs):
    s, (cells, aux), refs = refs[:freqs], refs[freqs : freqs + 2], refs[freqs + 2 :]
    w, splat = refs[3 * freqs :]
    nz = cells.shape[2]
    for f in range(freqs):
        splat[f] = jnp.full((8, nz), freq_sq[f], F32)
    grid = Grid(nx, ny, nz)
    many = [
        Field(grid, (s[f], refs[3 * f], None, None, None, *refs[3 * f + 1 : 3 * f + 3]), w)
        for f in range(freqs)
    ]

    def prepare(i):
        return grid.prepare(
            i,
            grid.own,
            freq_sq,
            w,
            many,
            lambda t: cells[i, grid.tile(t), :],
            lambda k, t: grid.pick(aux.at[k], t, i),
        )

    for i in (0, nx - 1):
        terms = prepare(i)
        for f in range(freqs):
            for p in range(2):
                grid.put(many[f].v0, p, i, terms[f][p], grid.own)

    def row(i):
        terms = prepare(i)
        for f in range(freqs):
            field = many[f]
            _, re, im = grid.apply(
                field.s, i, i - 1, i + 1, -1, field.coef(i, grid.own), grid.own, False
            )
            for p, value in enumerate((re, im)):
                value = {t: value[t] + terms[f][p][t] for t in grid.own}
                grid.put(field.v0, p, i, value, grid.own)

    def pair(k, _):
        row(2 * k + 1)
        row(2 * k + 2)
        return 0

    lax.fori_loop(0, (nx - 2) // 2, pair, 0)


def early(nx, ny, freq_sq, s, cells, aux):
    freqs = len(s)
    _, xe, _, nz = s[0].shape
    field = pltpu.VMEM(s[0].shape, F32)
    coef = pltpu.VMEM((xe, ny // 8 + 1, 8, nz), F32)
    return pl.pallas_call(
        functools.partial(early_kernel, freqs, nx, ny),
        out_shape=(field, coef, coef) * freqs
        + (coef, pltpu.VMEM((freqs, 8, nz), F32)),
        in_specs=[SMEM] + [VMEM] * (freqs + 2),
        compiler_params=params(8),
        name="early",
    )(freq_sq, *s, cells, aux)


def corner_faces(freqs, nx, ny, s, cells, aux, ce, co):
    fields = 2 * freqs
    nz = cells.shape[2]
    sub = lax.broadcasted_iota(jnp.int32, (2 * HALO, nz), 0)
    even_x = parity("gx")
    near = [aux[k, ny:, :] for k in range(fields + 1)]
    for side, cb in enumerate((ce, co)):
        last = even_x if side == 0 else jnp.logical_not(even_x)
        at = [jnp.where(last, nx - d, d - 1) for d in range(1, HALO)]
        for k in range(fields):
            one, two, three = (s[k // 2][k % 2, x, ny:, :] for x in at)
            one = jnp.where(sub == 3, pltpu.roll(three, 3, axis=0), one)
            cb[k] = jnp.where(sub == 4, pltpu.roll(three, 5, axis=0), one)
            if k % 2 == 0:
                kept = two
                continue
            two = jnp.where(
                sub < 4, pltpu.roll(two, 2, axis=0), pltpu.roll(two, 6, axis=0)
            )
            outer = (sub < 2) | (sub > 5)
            cb[fields + k // 2] = jnp.where(outer, kept, two)
        one, two = cells[at[0], ny:, :], cells[at[1], ny:, :]
        one = jnp.where(sub == 2, pltpu.roll(two, 2, axis=0), one)
        cb[fields + freqs] = jnp.where(sub == 5, pltpu.roll(two, 6, axis=0), one)
        skip = jnp.where(last, nx - INNER, 0)
        cb[fields + freqs + 1] = lane_slab(near, fields, skip, 2 * HALO, nz)


def place_corners(freqs, nx, ny, cb, s, cells, aux, above):
    fields = 2 * freqs
    nz = cb.shape[2]
    sub = lax.broadcasted_iota(jnp.int32, (2 * HALO, nz), 0)
    slot = [jnp.where(above, nx + d - 1, nx + 2 * HALO - d) for d in range(1, HALO)]
    layer = [jnp.where(above, d - 1, INNER - d) for d in range(1, HALO)]
    for k in range(fields):
        field, p = s[k // 2], k % 2
        one = cb[k]
        field[p, slot[0], ny:, :] = one
        field[p, slot[2], ny:, :] = jnp.where(
            sub == 0, pltpu.roll(one, 5, axis=0), pltpu.roll(one, 3, axis=0)
        )
        two = cb[fields + k // 2]
        if p:
            two = jnp.where(
                sub < 4, pltpu.roll(two, 6, axis=0), pltpu.roll(two, 2, axis=0)
            )
        field[p, slot[1], ny:, :] = two
    one = cb[fields + freqs]
    cells[layer[0], ny:, :] = one
    cells[layer[1], ny:, :] = jnp.where(
        sub == 0, pltpu.roll(one, 6, axis=0), pltpu.roll(one, 2, axis=0)
    )
    cells[layer[2], ny:, :] = jnp.zeros((2 * HALO, nz), F32)
    aux[ny:, :] = cb[fields + freqs + 1]


def inner_kernel(freqs, nx, ny, half, freq_sq, *refs):
    if half == 0:
        ye, yo = refs[:2]
        count = 4 * freqs + 3
        refs = refs[2 + count :]
        s, (cells, aux), refs = refs[:freqs], refs[freqs : freqs + 2], refs[freqs + 2 :]
        known, refs = refs[: 3 * freqs + 1], refs[3 * freqs + 1 :]
        news, (moments, ce, co) = refs[: 3 * freqs], refs[3 * freqs :]
    else:
        s, known = refs[:freqs], refs[freqs : 4 * freqs + 1]
        partial = refs[7 * freqs + 1]
        refs = refs[7 * freqs + 2 :]
        news, (moments,) = refs[: 3 * freqs], refs[3 * freqs :]
    nz = s[0].shape[3]
    fields = 2 * freqs
    w = known[3 * freqs]
    grid = Grid(nx, ny, nz)
    many = []
    for f in range(freqs):
        v0, cr, ci = known[3 * f : 3 * f + 3]
        u0, v1, u1 = news[3 * f : 3 * f + 3]
        many.append(Field(grid, (s[f], v0, u0, v1, u1, cr, ci), w))
    if half == 0:
        swapped = jnp.broadcast_to(parity("gy"), (HALO, nz))

        def halo(at):
            even, odd = ye[at], yo[at]
            high = jnp.where(swapped, even, odd) * grid.right
            low = jnp.where(swapped, odd, even) * grid.left
            return jnp.concatenate([high, low], axis=0)

        sub = lax.broadcasted_iota(jnp.int32, (8, nz), 0)

        def model_rows(g, _):
            tiles = [halo(fields * nx + 3 * g + j) for j in range(3)]
            last = tiles[0]
            for j in range(3):
                cells[4 * g + j, ny:, :] = tiles[j]
                last = jnp.where(sub == j, pltpu.roll(tiles[j], 5 + j, axis=0), last)
                last = jnp.where(sub == 5 + j, pltpu.roll(tiles[j], 1 + j, axis=0), last)
            cells[4 * g + 3, ny:, :] = last
            return 0

        def merge(x, _):
            for k in range(fields):
                s[k // 2][k % 2, x, ny:, :] = halo(k * nx + x)
            return 0

        lax.fori_loop(0, nx // 4, model_rows, 0, unroll=4)
        lax.fori_loop(0, nx, merge, 0, unroll=8)
        for k in range(fields + 1):
            slab, g = divmod(k, nz // nx)
            tile = halo(fields * nx + nx // 4 * 3 + slab)
            aux[k, ny:, :] = pltpu.roll(tile, (nz - g * nx) % nz, axis=1) if g else tile
        corner_faces(freqs, nx, ny, s, cells, aux, ce, co)

    def prepare(i):
        return grid.prepare(
            i,
            [grid.tiles],
            freq_sq,
            w,
            many,
            lambda t: cells[i, grid.tile(t), :],
            lambda k, t: grid.pick(aux.at[k], t, i),
        )

    if half == 0:
        for i in (0, nx - 1):
            terms = prepare(i)
            for f in range(freqs):
                for p in range(2):
                    grid.put(many[f].v0, p, i, terms[f][p], [grid.tiles])

    def step(j, acc, active):
        acc = list(acc)
        for k in reversed(active):
            i = j - 2 * k
            if k == 0:
                terms = prepare(i)
            for f in range(freqs):
                if k == 0:
                    many[f].first_halo(i, terms[f])
                else:
                    acc[f] = many[f].step(k, i, i - 1, i + 1, acc=acc[f])
        return tuple(acc)

    def heads(i, _):
        terms = prepare(i)
        for f in range(freqs):
            many[f].first_halo(i, terms[f])
        return 0

    spans = [(1 + 3 * k, nx - 1 + k) for k in range(4)]
    middle = nx // 2 + SHIFT
    edges = sorted({e for span in spans for e in span} | {middle})
    acc = tuple(tuple(grid.zero() for _ in range(4)) for _ in range(freqs))
    if half == 0:
        lax.fori_loop(1, nx - 1, heads, 0, unroll=5)
    for lo, hi in zip(edges[:-1], edges[1:]):
        if (lo < middle) != (half == 0):
            continue
        active = [k for k, (a, b) in enumerate(spans) if k and a <= lo and hi <= b]
        if active:
            acc = lax.fori_loop(
                lo,
                hi,
                functools.partial(step, active=active),
                acc,
                unroll=3 if hi - lo > 4 else hi - lo,
            )
    for f in range(freqs):
        for m in range(4):
            value = acc[f][m]
            moments[f, m] = value if half == 0 else value + partial[f, m]


def inner_part(nx, ny, freq_sq, ye, yo, s, cells, aux, known):
    freqs = len(s)
    nz = cells.shape[2]
    slabs = 3 * freqs + 2
    field = pltpu.VMEM(s[0].shape, F32)
    corner = pltpu.VMEM((slabs, 2 * HALO, nz), F32)
    kept = (*s, cells, aux, *known)
    news = (field,) * (3 * freqs) + (pltpu.VMEM((freqs, 4, 8, nz), F32),)
    got = pl.pallas_call(
        functools.partial(inner_kernel, freqs, nx, ny, 0),
        out_shape=tuple(pltpu.VMEM(k.shape, F32) for k in kept)
        + news
        + (corner, corner),
        in_specs=[VMEM] * (3 + len(kept)),
        input_output_aliases={3 + k: k for k in range(len(kept))},
        compiler_params=params(8),
        name="inner_first",
    )(freq_sq, ye, yo, *kept)
    s, known = got[:freqs], got[freqs + 2 : len(kept)]
    news_got, (ce, co) = got[len(kept) : -2], got[-2:]

    def rest():
        first = freqs + len(known)
        again = pl.pallas_call(
            functools.partial(inner_kernel, freqs, nx, ny, 1, None),
            out_shape=news,
            in_specs=[VMEM] * (freqs + len(known) + len(news)),
            input_output_aliases={first + k: k for k in range(len(news))},
            compiler_params=params(8),
            name="inner_second",
        )(*s, *known, *news_got)
        state = []
        for f in range(freqs):
            v0, cr, ci = known[3 * f : 3 * f + 3]
            state += [s[f], v0, *again[3 * f : 3 * f + 3], cr, ci]
        return state + [known[-1]], again[-1]

    return ce, co, rest


def edge_kernel(side, peers, freqs, nx, ny, freq_sq, xb, cb, *refs):
    count = 7 * freqs + 1
    moments, refs = refs[count], refs[count + 1 :]
    state, (out, cells, aux) = refs[:count], refs[count:]
    fields = 2 * freqs
    nz = state[0].shape[3]
    w = state[-1]
    above = parity("gx") if side == 0 else jnp.logical_not(parity("gx"))
    group = nz // 8
    wrap = nx + 2 * HALO

    def row_at(distance):
        return jnp.where(above, (nx - 1 + distance) % wrap, -distance % wrap)

    slot = jnp.where(above, nx, nx + HALO)
    for layer in range(HALO):
        for k in range(fields):
            block = state[7 * (k // 2)]
            for y in range(0, ny, 8):
                row = (k * HALO + layer) * ny + y
                block[k % 2, slot + layer, y : y + 8, :] = xb[row : row + 8, :]
        if layer < INNER:
            for y in range(0, ny, 8):
                row = (fields * HALO + layer) * ny + y
                cells[layer, y : y + 8, :] = xb[row : row + 8, :]
    at = (fields * HALO + INNER) * ny
    folded = xb[at : at + ny // 8, :]
    for g in range(8):
        rows = pl.ds(g * (ny // 8), ny // 8)
        aux[rows, :] = pltpu.roll(folded, (nz - g * group) % nz, axis=1)
    place_corners(freqs, nx, ny, cb, state[: 7 * freqs : 7], cells, aux, above)
    for k in range(fields):
        state[7 * (k // 2)][k % 2, row_at(HALO), ny:, :] = jnp.zeros(
            (2 * HALO, nz), F32
        )
    grid = Grid(nx, ny, nz)
    many = [Field(grid, state[7 * f : 7 * f + 7], w) for f in range(freqs)]
    for layer in range(INNER):
        i = jnp.where(above, nx + layer, nx + HALO + 1 + layer)
        terms = grid.prepare(
            i,
            grid.both,
            freq_sq,
            w,
            many,
            lambda t: cells[layer, grid.tile(t), :],
            lambda k, t: grid.pick(aux, t, INNER * k + layer),
        )
        for f in range(freqs):
            for p in range(2):
                grid.put(many[f].v0, p, i, terms[f][p], grid.both)

    place = lax.axis_index("gx")
    more = jnp.where(above, place < lax.axis_size("gx") - 1, place > 0)
    cut = (-1, jnp.where(more, 1.0, 0.0))
    acc = [tuple(grid.zero() for _ in range(4)) for _ in range(freqs)]
    for stage in range(4):
        for k in range(HALO):
            distance = INNER - stage - k
            i, lo, hi = (row_at(distance + d) for d in (0, 1, -1))
            own = distance <= 0
            ends = cut if distance == 0 else None
            for f in range(freqs):
                if stage == 0:
                    many[f].finish(i, grid.both, True, lo, hi, ends)
                    continue
                got = many[f].step(stage, i, lo, hi, ends, acc[f] if own else None)
                if own:
                    acc[f] = got

    if side == 0:
        for f in range(freqs):
            for m in range(4):
                out[f, m] = acc[f][m] + moments[f, m]
        return
    rows = []
    for f in range(freqs):
        for m in range(4):
            both = acc[f][m] + moments[f, m]
            rows.append(jnp.sum(both, axis=0, keepdims=True))
    sums = jnp.sum(jnp.concatenate(rows, axis=0), axis=1, keepdims=True)
    lane = lax.broadcasted_iota(jnp.int32, (4 * freqs, nz), 1)
    sub = lax.broadcasted_iota(jnp.int32, (4 * freqs, nz), 0)
    sums = jnp.where(lane == sub, jnp.broadcast_to(sums, (4 * freqs, nz)), 0.0)
    out[...] = jnp.broadcast_to(jnp.sum(sums, axis=0, keepdims=True), out.shape)


def edge_part(side, peers, freqs, nx, ny, freq_sq, xb, cb, state, moments):
    nz = state[0].shape[3]
    outs = tuple(pltpu.VMEM(k.shape, F32) for k in state)
    if side == 0:
        last = pltpu.VMEM(moments.shape, F32)
    else:
        last = jax.ShapeDtypeStruct((peers, nz), F32)
    *state, out = pl.pallas_call(
        functools.partial(edge_kernel, side, peers, freqs, nx, ny),
        out_shape=outs + (last,),
        in_specs=[VMEM] * (4 + len(state)),
        input_output_aliases={3 + k: k for k in range(len(state))},
        scratch_shapes=[
            pltpu.VMEM((INNER, ny + 2 * HALO, nz), F32),
            pltpu.VMEM((ny + 2 * HALO, nz), F32),
        ],
        compiler_params=params(8),
        name="edge_odd" if side else "edge_even",
    )(freq_sq, xb, cb, *state, moments)
    return state, out


def steps(sums, freqs):
    total = jnp.sum(sums[...], axis=0, keepdims=True)
    shape = (8, total.shape[1])
    out = []
    for f in range(freqs):
        m0, m1, m2, m3 = (
            jnp.broadcast_to(total[:, 4 * f + k : 4 * f + k + 1], shape)
            for k in range(4)
        )
        first = m0 / m1
        new = first * (first * m2 - m1)
        product = m1 - first * (2.0 * m2 - first * m3)
        ratio = new / m0
        second = new / (product - ratio * new / first)
        out.append((first + second * (1.0 + ratio), -first * second))
    return out


def gradient_kernel(freqs, nx, ny, freq_sq, sums, *refs):
    out = refs[-1]
    weights = steps(sums, freqs)
    scale = [-freq_sq[f] for f in range(freqs)]

    def row(x, _):
        for y in range(0, ny, 8):
            at = pl.ds(y, 8)
            total = None
            for f in range(freqs):
                s, v0, u0, v1, u1 = refs[5 * f : 5 * f + 5]
                a, b = weights[f]
                wave_re = a * v0[0, x, at, :] + b * v1[0, x, at, :]
                wave_im = a * v0[1, x, at, :] + b * v1[1, x, at, :]
                miss_re = a * u0[0, x, at, :] + b * u1[0, x, at, :]
                miss_im = a * u0[1, x, at, :] + b * u1[1, x, at, :]
                miss_re = miss_re - s[0, x, at, :]
                miss_im = miss_im - s[1, x, at, :]
                left = (wave_re + attenuation * wave_im) * miss_re
                right = (wave_im - attenuation * wave_re) * miss_im
                term = scale[f] * (left + right)
                total = term if total is None else total + term
            out[x, at, :] = total
        return 0

    lax.fori_loop(0, nx, row, 0, unroll=4)


def wave_kernel(freqs, nx, ny, sums, *refs):
    out, block, sem = refs[2 * freqs :]
    weights = steps(sums, freqs)
    copies = Copies(sem)
    for f in range(freqs):
        a, b = weights[f]
        v0, v1 = refs[2 * f : 2 * f + 2]
        for p in range(2):
            k = 2 * f + p

            def row(x, _):
                for y in range(0, ny, 8):
                    at = pl.ds(y, 8)
                    block[k, x, at, :] = a * v0[p, x, at, :] + b * v1[p, x, at, :]
                return 0

            lax.fori_loop(0, nx, row, 0, unroll=8)
            copies.add(block.at[k], out.at[f, p])
    copies.wait()


def results(freqs, nx, ny, freq_sq, sums, state):
    nz = state[0].shape[3]
    fields, pairs = [], []
    for f in range(freqs):
        s, v0, u0, v1, u1 = state[7 * f : 7 * f + 5]
        fields += [s, v0, u0, v1, u1]
        pairs += [v0, v1]
    gradient = pl.pallas_call(
        functools.partial(gradient_kernel, freqs, nx, ny),
        out_shape=jax.ShapeDtypeStruct((nx, ny, nz), F32),
        in_specs=[VMEM] * (2 + len(fields)),
        out_specs=VMEM,
        compiler_params=params(8),
        name="gradient_part",
    )(freq_sq, sums, *fields)
    wave = pl.pallas_call(
        functools.partial(wave_kernel, freqs, nx, ny),
        out_shape=jax.ShapeDtypeStruct((freqs, 2, nx, ny, nz), F32),
        in_specs=[VMEM] * (1 + len(pairs)),
        out_specs=HBM,
        scratch_shapes=[
            pltpu.VMEM((2 * freqs, nx, ny, nz), F32),
            pltpu.SemaphoreType.DMA((2 * freqs,)),
        ],
        compiler_params=params(8),
        name="wavefield",
    )(sums, *pairs)
    return gradient, wave


def add_kernel(one, two, out, block, sem):
    nx, ny, _ = one.shape
    copies = Copies(sem)
    parts = sem.shape[0]
    step = nx // parts
    for part in range(parts):

        def row(x, _):
            for y in range(0, ny, 8):
                at = pl.ds(y, 8)
                block[x, at, :] = one[x, at, :] + two[x, at, :]
            return 0

        lax.fori_loop(part * step, (part + 1) * step, row, 0, unroll=4)
        span = pl.ds(part * step, step)
        copies.add(block.at[span], out.at[span])
    copies.wait()


def add(one, two):
    return pl.pallas_call(
        add_kernel,
        out_shape=jax.ShapeDtypeStruct(one.shape, F32),
        in_specs=[VMEM] * 2,
        out_specs=HBM,
        scratch_shapes=[pltpu.VMEM(one.shape, F32), pltpu.SemaphoreType.DMA((4,))],
        compiler_params=params(4),
        name="add",
    )(one, two)


def swap(cells, axis, odd):
    names = ("gx", "gy", "af")
    sizes = [lax.axis_size(name) for name in names]
    along = names.index(axis)
    pairs = []
    for flat in range(sizes[0] * sizes[1] * sizes[2]):
        place = [flat // (sizes[1] * sizes[2]), flat // sizes[2] % sizes[1], flat % sizes[2]]
        mate = ((place[along] + odd) ^ 1) - odd
        if 0 <= mate < sizes[along]:
            place[along] = mate
        elif sizes[2] % 2 == 0:
            place[2] ^= 1
        else:
            continue
        pairs.append((flat, (place[0] * sizes[1] + place[1]) * sizes[2] + place[2]))
    return lax.ppermute(cells, names, pairs)


def on_device(model, freq_sq, source, observed, receiver_depth):
    nx, ny, nz = model.shape
    freqs = freq_sq.shape[0]
    *s, cells, aux, xe, xo, ye, yo = load(source, model, observed, receiver_depth)
    ye, yo = swap(ye, "gy", 0), swap(yo, "gy", 1)
    xe, xo = swap(xe, "gx", 0), swap(xo, "gx", 1)
    *known, splat = early(nx, ny, freq_sq, s, cells, aux)
    ce, co, rest = inner_part(nx, ny, splat, ye, yo, s, cells, aux, known)
    ce, co = swap(ce, "gx", 0), swap(co, "gx", 1)
    state, moments = rest()
    peers = lax.axis_size("gx") * lax.axis_size("gy")
    state, moments = edge_part(
        0, peers, freqs, nx, ny, splat, xe, ce, state, moments
    )
    state, part = edge_part(1, peers, freqs, nx, ny, splat, xo, co, state, moments)
    sums = lax.all_to_all(part, ("gx", "gy"), 0, 0)
    gradient, wave = results(freqs, nx, ny, splat, sums, state)
    if lax.axis_size("af") == 2:
        gradient = add(gradient, lax.ppermute(gradient, "af", [(0, 1), (1, 0)]))
    else:
        gradient = lax.psum(gradient, "af")
    return wave, gradient


def solution(mesh):
    in_specs = (
        P("gx", "gy", None),
        P("af"),
        P("af", None, "gx", "gy", None),
        P("af", None, "gx", "gy"),
        P("gx", "gy"),
    )
    out_specs = (P("af", None, "gx", "gy", None), P("gx", "gy", None))
    return jax.shard_map(
        on_device, mesh=mesh, in_specs=in_specs, out_specs=out_specs, check_vma=False
    )
```
